32 devices in a mesh: row: 8 (over y, x, core), col: 4 (over z).
Axes of the slice: x: 2, y: 2, z: 4, core: 2. Of those that a mesh axis runs over, the one named last changes fastest.
Arguments:
- x_dosage: bfloat16 [16384, 2048], P('row', 'col'), may hold values from 0 to 2
- y_dosage: bfloat16 [2048, 8192], P('row', 'col'), may hold values from 0 to 2
- freq: float32 [2048], replicated, may hold values from 0.05 to 0.5
- weight: float32 [2048], replicated, may hold values from 0.5 to 3.47
- sex_rows: int32 [16384], P('row'), may hold values 0 or 1
- sex_cols: int32 [8192], P('col'), may hold values 0 or 1
Outputs:
- relation: bfloat16 [16384, 8192], P('row', 'col')
- inbreeding: float32 [16384], P('row')
The draws below stay inside these ranges and needn't reach their ends.
All inputs are finite; a program needn't handle non-finite values. No bound on the sum of `sex_rows` or of `sex_cols` on one device may be relied on, other than what follows from the above.
Results may differ from the reference program's by a relative error of at most 0.0057.
Values may be sent and summed in bfloat16 or wider, within the bound.
No kernel may reach another device: no remote copies, remote signals or barrier semaphores. Data moves between devices by JAX's collectives and lax.ppermute only.
A program may use at most 128 MiB of HBM per device.

```python
import math
import jax
import jax.numpy as jnp
from jax import lax

SR = 2048
VG = 256
STEPS = 4
N1 = 16384
N2 = 8192
M = 2048
N_ROW = 8


def freq_of(key):
    return jax.random.uniform(jax.random.fold_in(key, 11), (M,), jnp.float32, 0.05, 0.5)


def draw_freq(key, part):
    return freq_of(key)


def draw_weight(key, part):
    position = jnp.arange(M, dtype=jnp.float32) / jnp.float32(max(M - 1, 1))
    base = jax.random.uniform(jax.random.fold_in(key, 13), (M,), jnp.float32, math.log(0.5), math.log(2.0))
    return jnp.exp(base) * jnp.exp(0.5 * math.log(3.0) * position)


def spread_draw(key, shape):
    unit = jax.random.uniform(jax.random.fold_in(key, 17), shape, jnp.float32, 0.0, 2.0)
    return unit


def draw_x_dosage(key, part):
    freq = freq_of(key)
    unit = spread_draw(jax.random.fold_in(key, 23), (N1, M))
    return (2.0 * freq[None, :] * unit).astype(jnp.bfloat16)


def draw_y_dosage(key, part):
    freq = freq_of(key)
    unit = spread_draw(jax.random.fold_in(key, 29), (M, N2))
    return (2.0 * freq[:, None] * unit).astype(jnp.bfloat16)


def with_ends(entries, rng, least, top_value):
    dims = entries.shape
    index_at = [jax.random.randint(jax.random.fold_in(rng, axis), (), 0, dims[axis]) for axis in range(len(dims))]
    entries = entries.at[tuple(index_at)].set(least)
    longest = dims.index(max(dims))
    index_at[longest] = (index_at[longest] + 1) % dims[longest]
    return entries.at[tuple(index_at)].set(top_value)


def setup_inputs(seed: int = 0) -> dict:
    arg_keys = jax.random.split(jax.random.key(seed), 7)
    x_dosage = draw_x_dosage(jax.random.fold_in(arg_keys[6], 71), 0)
    y_dosage = draw_y_dosage(jax.random.fold_in(arg_keys[6], 71), 0)
    freq = draw_freq(jax.random.fold_in(arg_keys[6], 71), 0)
    weight = draw_weight(jax.random.fold_in(arg_keys[6], 71), 0)
    sex_rows = with_ends((jax.random.randint(arg_keys[4], (N1,), 0, 2) < 1).astype(jnp.int32), jax.random.fold_in(arg_keys[4], 1), 0, 1)
    sex_cols = with_ends((jax.random.randint(arg_keys[5], (N2,), 0, 2) < 1).astype(jnp.int32), jax.random.fold_in(arg_keys[5], 1), 0, 1)
    return dict(x_dosage=x_dosage, y_dosage=y_dosage, freq=freq, weight=weight, sex_rows=sex_rows, sex_cols=sex_cols)


def standardize(dosage, freq, weight, male):
    value = dosage.astype(jnp.float32)
    female_z = weight * (value - 2.0 * freq) / jnp.sqrt(2.0 * freq * (1.0 - freq))
    male_z = weight * (0.5 * value - freq) / jnp.sqrt(freq * (1.0 - freq))
    return jnp.where(male > 0, male_z, female_z).astype(jnp.bfloat16)

def reference(x_dosage, y_dosage, freq, weight, sex_rows, sex_cols):
    zx = standardize(x_dosage, freq[None, :], weight[None, :], sex_rows[:, None])
    zy = standardize(y_dosage, freq[:, None], weight[:, None], sex_cols[None, :])
    scale = jnp.sqrt(jnp.float32(STEPS * VG))
    blocks = []
    for group_row in range(N_ROW):
        total = jnp.zeros((SR, N2), jnp.float32)
        for step in range(STEPS):
            group = (group_row + step) % N_ROW
            left = zx[group_row * SR:(group_row + 1) * SR, group * VG:(group + 1) * VG]
            right = zy[group * VG:(group + 1) * VG, :]
            total = total + jnp.dot(left, right, preferred_element_type=jnp.float32)
        blocks.append((total / scale).astype(jnp.bfloat16))
    relation = jnp.concatenate(blocks, axis=0)
    squares = lax.optimization_barrier(jnp.sum(jnp.square(zx.astype(jnp.float32)), axis=1))
    inbreeding = squares / jnp.float32(M) - 1.0
    return (relation, inbreeding)
```

```python
import functools

import jax
import jax.numpy as jnp
import numpy as np
from jax import lax
from jax.experimental import pallas as pl
from jax.experimental.pallas import tpu as pltpu
from jax.sharding import PartitionSpec as P

STEPS = 4
HALVES = 2
DEPTH = 2
TILES = 4
VMEM_LIMIT = 48 * 2**20


class Lane:
    def __init__(self, rows, cols, groups_here, towards_zero):
        self.cols = cols
        self.place = (lambda c: c) if towards_zero else (lambda c: cols - 1 - c)
        self.chunks = []
        for r in range(rows):
            slots = {}
            todo = []
            for half in range(HALVES):
                for s in range(STEPS):
                    p = self.place((r + s) % rows // groups_here)
                    if p > 0:
                        todo.append((half, p, s))
            todo.sort()
            slot = 1
            while todo:
                ready = [k for k in todo if 1 + DEPTH * (k[1] - 1) <= slot]
                if ready:
                    todo.remove(ready[0])
                    slots[slot] = ready[0]
                slot += 1
            self.chunks.append(slots)
        self.rounds = max([max(slots, default=0) for slots in self.chunks])

    def sent(self, r, c, t):
        p = self.place(c)
        key = self.chunks[r].get(t + DEPTH * (p - 1)) if p > 0 else None
        if key is None or key[1] < p:
            return None
        return key

    def pairs(self, t):
        found = []
        for r in range(len(self.chunks)):
            for c in range(self.cols):
                if self.sent(r, c, t) is not None:
                    p = self.place(c) - 1
                    to = p if self.place(0) == 0 else self.cols - 1 - p
                    found.append((r * self.cols + c, r * self.cols + to))
        return found

    def own(self, r, c, t):
        key = self.sent(r, c, t)
        return key if key is not None and key[1] == self.place(c) else None

    def arrival(self, r, c, half, s):
        p = self.place(c)
        for slot, key in self.chunks[r].items():
            if key[0] == half and key[2] == s and key[1] > p:
                return slot - DEPTH * p
        return None


def relay_kernel(at, table, x, held, out, sem):
    half_rows, width = out.shape

    @pl.when(table[at] == 1)
    def _():
        row = pl.multiple_of(table[at + 1] * half_rows, half_rows)
        col = pl.multiple_of(table[at + 2] * width, width)
        copy = pltpu.make_async_copy(x.at[pl.ds(row, half_rows), pl.ds(col, width)], out, sem)
        copy.start()
        copy.wait()


def relay(at, table, x, held):
    return pl.pallas_call(
        functools.partial(relay_kernel, at),
        out_shape=jax.ShapeDtypeStruct(held.shape, held.dtype),
        grid_spec=pltpu.PrefetchScalarGridSpec(
            num_scalar_prefetch=1,
            grid=(1,),
            in_specs=[pl.BlockSpec(memory_space=pl.ANY)] * 2,
            out_specs=pl.BlockSpec(memory_space=pl.ANY),
            scratch_shapes=[pltpu.SemaphoreType.DMA],
        ),
        input_output_aliases={2: 0},
        name="relay",
    )(table, x, held)


def product_kernel(half, at, candidates, scale, n_buffers, table, *refs):
    x, buffers = refs[0], refs[1 : 1 + n_buffers]
    factor, twice, male, zy = refs[1 + n_buffers : 5 + n_buffers]
    out, raw, sems = refs[-3:]
    half_rows = raw.shape[0]
    width = raw.shape[1] // STEPS
    tile_rows = half_rows // TILES
    i = pl.program_id(0)

    def fetch(source, row, col, s):
        for tile in range(TILES):
            pltpu.make_async_copy(
                source.at[pl.ds(row + tile * tile_rows, tile_rows), pl.ds(col, width)],
                raw.at[pl.ds(tile * tile_rows, tile_rows), pl.ds(s * width, width)],
                sems.at[tile, s],
            ).start()

    @pl.when(i == 0)
    def _():
        for s in range(STEPS):
            place = table[at + s]
            for number in candidates[s]:
                if number >= 0:

                    @pl.when(place == number)
                    def _(number=number, s=s):
                        fetch(buffers[number], 0, 0, s)

                else:

                    @pl.when(place < 0)
                    def _(s=s, place=place):
                        col = pl.multiple_of((-1 - place) * width, width)
                        fetch(x, half * half_rows, col, s)

    rows = pl.ds(pl.multiple_of(i * tile_rows, tile_rows), tile_rows)
    for s in range(STEPS):
        part = raw.at[rows, pl.ds(s * width, width)]
        pltpu.make_async_copy(part, part, sems.at[i, s]).wait()
    value = raw[rows, :].astype(jnp.float32) - twice[...]
    zx = (value * factor[...] * male[...]).astype(jnp.bfloat16)
    total = jnp.dot(zx, zy[...], preferred_element_type=jnp.float32)
    out[...] = (total * scale).astype(out.dtype)


def product(half, at, candidates, table, x, buffers, factor, twice, male, zy, before):
    rows, n = x.shape[0], zy.shape[1]
    half_rows = rows // HALVES
    tile_rows = half_rows // TILES
    depth = zy.shape[0]
    scale = float(1.0 / np.sqrt(np.float32(depth)))
    whole = lambda i, table: (0, 0)
    specs = [pl.BlockSpec(memory_space=pl.ANY)] * (1 + len(buffers)) + [
        pl.BlockSpec((1, depth), whole),
        pl.BlockSpec((1, depth), whole),
        pl.BlockSpec((tile_rows, 1), lambda i, table: (half * TILES + i, 0)),
        pl.BlockSpec((depth, n), whole),
    ]
    args = [table, x, *buffers, factor, twice, male, zy]
    aliases = {}
    if before is not None:
        aliases = {len(args): 0}
        specs.append(pl.BlockSpec(memory_space=pl.ANY))
        args.append(before)
    return pl.pallas_call(
        functools.partial(product_kernel, half, at, candidates, scale, len(buffers)),
        out_shape=jax.ShapeDtypeStruct((rows, n), jnp.bfloat16),
        grid_spec=pltpu.PrefetchScalarGridSpec(
            num_scalar_prefetch=1,
            grid=(TILES,),
            in_specs=specs,
            out_specs=pl.BlockSpec((tile_rows, n), lambda i, table: (half * TILES + i, 0)),
            scratch_shapes=[
                pltpu.VMEM((half_rows, depth), jnp.bfloat16),
                pltpu.SemaphoreType.DMA((TILES, STEPS)),
            ],
        ),
        input_output_aliases=aliases,
        compiler_params=pltpu.CompilerParams(vmem_limit_bytes=VMEM_LIMIT),
        cost_estimate=pl.CostEstimate(
            flops=2 * half_rows * depth * n,
            bytes_accessed=2 * (half_rows * depth + depth * n + half_rows * n),
            transcendentals=0,
        ),
        name="product",
    )(*args)


def col_sum(value, cols):
    if cols & (cols - 1):
        return lax.psum(value, "col")
    bit = 1
    while bit < cols:
        value = value + lax.ppermute(value, "col", [(i, i ^ bit) for i in range(cols)])
        bit *= 2
    return value


def local(rows, cols, x, y, freq, weight, sex_rows, sex_cols):
    group_size = y.shape[0]
    local_vars = x.shape[1]
    groups_here = local_vars // group_size
    half_rows = x.shape[0] // HALVES
    lanes = [Lane(rows, cols, groups_here, towards) for towards in (True, False)]

    numbers = np.zeros((rows * cols, 0), np.int32)

    def add(columns):
        nonlocal numbers
        at = numbers.shape[1]
        numbers = np.concatenate([numbers, np.asarray(columns, np.int32)], axis=1)
        return at

    devices = [(r, c) for r in range(rows) for c in range(cols)]
    own_at = {}
    for d, lane in enumerate(lanes):
        for t in range(1, lane.rounds + 1):
            entry = []
            for r, c in devices:
                key = lane.own(r, c, t)
                entry.append((0, 0, 0) if key is None else (1, key[0], (r + key[2]) % rows % groups_here))
            own_at[d, t] = add(entry)
    used = {}
    place_at = {}
    candidates = {}
    for half in range(HALVES):
        arrivals = {
            (r, c, s, d): lane.arrival(r, c, half, s)
            for r, c in devices
            for s in range(STEPS)
            for d, lane in enumerate(lanes)
        }
        used[half] = sorted({(t, d) for (_, _, _, d), t in arrivals.items() if t is not None})
        entry = []
        for r, c in devices:
            places = []
            for s in range(STEPS):
                place = -1 - (r + s) % rows % groups_here
                for d in range(len(lanes)):
                    if arrivals[r, c, s, d] is not None:
                        place = used[half].index((arrivals[r, c, s, d], d))
                places.append(place)
            entry.append(places)
        place_at[half] = add(entry)
        candidates[half] = [sorted({max(e[s], -1) for e in entry}) for s in range(STEPS)]

    row_place = lax.axis_index("row")
    col_place = lax.axis_index("col")
    table = lax.dynamic_slice(jnp.asarray(numbers), (row_place * cols + col_place, 0), (1, numbers.shape[1]))[0]

    buffers = {}
    for t in range(1, max(lane.rounds for lane in lanes) + 1):
        for d, lane in enumerate(lanes):
            if t > lane.rounds:
                continue
            pairs = lane.pairs(t)
            if not pairs:
                continue
            at = own_at[d, t]
            held = buffers.get((d, t - DEPTH))
            if held is None:
                start = (table[at + 1] * half_rows, table[at + 2] * group_size)
                held = lax.dynamic_slice(x, start, (half_rows, group_size))
            elif numbers[:, at].any():
                held = buffers[d, t - DEPTH] = relay(at, table, x, held)
            buffers[d, t] = lax.ppermute(held, ("row", "col"), pairs)

    back = [(i, (i - 1) % rows) for i in range(rows)]
    window = [y]
    for _ in range(STEPS - 1):
        window.append(lax.ppermute(window[-1], "row", back))

    factor = weight / jnp.sqrt(2.0 * freq * (1.0 - freq))
    span = STEPS * group_size

    def in_window(value):
        twice = jnp.concatenate([value, value])
        return lax.dynamic_slice(twice, (row_place * group_size,), (span,))

    window_factor = in_window(factor)
    window_twice = in_window(2.0 * freq)
    male_scale = np.float32(np.sqrt(0.5))
    male_rows = jnp.where(sex_rows > 0, male_scale, np.float32(1.0))[:, None]
    male_cols = jnp.where(sex_cols > 0, male_scale, np.float32(1.0))[None, :]
    zy = []
    for s, block in enumerate(window):
        part = slice(s * group_size, (s + 1) * group_size)
        value = block.astype(jnp.float32) - window_twice[part, None]
        zy.append((value * window_factor[part, None] * male_cols).astype(jnp.bfloat16))
    zy = jnp.concatenate(zy, axis=0)

    here = lambda value: lax.dynamic_slice(value, (col_place * local_vars,), (local_vars,))[None, :]
    zx = ((x.astype(jnp.float32) - here(2.0 * freq)) * here(factor) * male_rows).astype(jnp.bfloat16)
    squares = col_sum(jnp.sum(jnp.square(zx.astype(jnp.float32)), axis=1), cols)
    inbreeding = squares / jnp.float32(freq.shape[0]) - 1.0

    relation = None
    for half in range(HALVES):
        relation = product(
            half,
            place_at[half],
            candidates[half],
            table,
            x,
            [buffers[d, t] for t, d in used[half]],
            window_factor[None, :],
            window_twice[None, :],
            male_rows,
            zy,
            relation,
        )
    return relation, inbreeding


def solution(mesh):
    rows, cols = mesh.shape["row"], mesh.shape["col"]
    return jax.shard_map(
        functools.partial(local, rows, cols),
        mesh=mesh,
        in_specs=(P("row", "col"), P("row", "col"), P(), P(), P("row"), P("col")),
        out_specs=(P("row", "col"), P("row")),
        check_vma=False,
    )
```

```python
import functools

import jax
import jax.numpy as jnp
import numpy as np
from jax import lax
from jax.experimental import pallas as pl
from jax.experimental.pallas import tpu as pltpu
from jax.sharding import PartitionSpec as P

STEPS = 4
HALVES = 2
DEPTH = 2
TILES = 4
VMEM_LIMIT = 48 * 2**20


class Lane:
    def __init__(self, rows, cols, groups_here, towards_zero):
        self.cols = cols
        self.place = (lambda c: c) if towards_zero else (lambda c: cols - 1 - c)
        self.chunks = []
        for r in range(rows):
            slots = {}
            todo = []
            for half in range(HALVES):
                for s in range(STEPS):
                    p = self.place((r + s) % rows // groups_here)
                    if p > 0:
                        todo.append((half, p, s))
            todo.sort()
            slot = 1
            while todo:
                ready = [k for k in todo if 1 + DEPTH * (k[1] - 1) <= slot]
                if ready:
                    todo.remove(ready[0])
                    slots[slot] = ready[0]
                slot += 1
            self.chunks.append(slots)
        self.rounds = max([max(slots, default=0) for slots in self.chunks])

    def sent(self, r, c, t):
        p = self.place(c)
        key = self.chunks[r].get(t + DEPTH * (p - 1)) if p > 0 else None
        if key is None or key[1] < p:
            return None
        return key

    def pairs(self, t):
        found = []
        for r in range(len(self.chunks)):
            for c in range(self.cols):
                if self.sent(r, c, t) is not None:
                    p = self.place(c) - 1
                    to = p if self.place(0) == 0 else self.cols - 1 - p
                    found.append((r * self.cols + c, r * self.cols + to))
        return found

    def own(self, r, c, t):
        key = self.sent(r, c, t)
        return key if key is not None and key[1] == self.place(c) else None

    def arrival(self, r, c, half, s):
        p = self.place(c)
        for slot, key in self.chunks[r].items():
            if key[0] == half and key[2] == s and key[1] > p:
                return slot - DEPTH * p
        return None


def product_kernel(half, at, candidates, scale, n_buffers, table, *refs):
    x, buffers = refs[0], refs[1 : 1 + n_buffers]
    factor, twice, male, zy = refs[1 + n_buffers : 5 + n_buffers]
    out, raw, sems = refs[-3:]
    half_rows = raw.shape[0]
    width = raw.shape[1] // STEPS
    tile_rows = half_rows // TILES
    i = pl.program_id(0)

    def fetch(source, row, col, s):
        for tile in range(TILES):
            pltpu.make_async_copy(
                source.at[pl.ds(row + tile * tile_rows, tile_rows), pl.ds(col, width)],
                raw.at[pl.ds(tile * tile_rows, tile_rows), pl.ds(s * width, width)],
                sems.at[tile, s],
            ).start()

    @pl.when(i == 0)
    def _():
        for s in range(STEPS):
            place = table[at + s]
            for number in candidates[s]:
                if number >= 0:

                    @pl.when(place == number)
                    def _(number=number, s=s):
                        fetch(buffers[number], 0, 0, s)

                else:

                    @pl.when(place < 0)
                    def _(s=s, place=place):
                        col = pl.multiple_of((-1 - place) * width, width)
                        fetch(x, half * half_rows, col, s)

    rows = pl.ds(pl.multiple_of(i * tile_rows, tile_rows), tile_rows)
    for s in range(STEPS):
        part = raw.at[rows, pl.ds(s * width, width)]
        pltpu.make_async_copy(part, part, sems.at[i, s]).wait()
    value = raw[rows, :].astype(jnp.float32) - twice[...]
    zx = (value * factor[...] * male[...]).astype(jnp.bfloat16)
    total = jnp.dot(zx, zy[...], preferred_element_type=jnp.float32)
    out[...] = (total * scale).astype(out.dtype)


def product(half, at, candidates, table, x, buffers, factor, twice, male, zy, before):
    rows, n = x.shape[0], zy.shape[1]
    half_rows = rows // HALVES
    tile_rows = half_rows // TILES
    depth = zy.shape[0]
    scale = float(1.0 / np.sqrt(np.float32(depth)))
    whole = lambda i, table: (0, 0)
    specs = [pl.BlockSpec(memory_space=pl.ANY)] * (1 + len(buffers)) + [
        pl.BlockSpec((1, depth), whole),
        pl.BlockSpec((1, depth), whole),
        pl.BlockSpec((tile_rows, 1), lambda i, table: (half * TILES + i, 0)),
        pl.BlockSpec((depth, n), whole),
    ]
    args = [table, x, *buffers, factor, twice, male, zy]
    aliases = {}
    if before is not None:
        aliases = {len(args): 0}
        specs.append(pl.BlockSpec(memory_space=pl.ANY))
        args.append(before)
    return pl.pallas_call(
        functools.partial(product_kernel, half, at, candidates, scale, len(buffers)),
        out_shape=jax.ShapeDtypeStruct((rows, n), jnp.bfloat16),
        grid_spec=pltpu.PrefetchScalarGridSpec(
            num_scalar_prefetch=1,
            grid=(TILES,),
            in_specs=specs,
            out_specs=pl.BlockSpec((tile_rows, n), lambda i, table: (half * TILES + i, 0)),
            scratch_shapes=[
                pltpu.VMEM((half_rows, depth), jnp.bfloat16),
                pltpu.SemaphoreType.DMA((TILES, STEPS)),
            ],
        ),
        input_output_aliases=aliases,
        compiler_params=pltpu.CompilerParams(vmem_limit_bytes=VMEM_LIMIT),
        cost_estimate=pl.CostEstimate(
            flops=2 * half_rows * depth * n,
            bytes_accessed=2 * (half_rows * depth + depth * n + half_rows * n),
            transcendentals=0,
        ),
        name="product",
    )(*args)


def col_sum(value, cols):
    if cols & (cols - 1):
        return lax.psum(value, "col")
    bit = 1
    while bit < cols:
        value = value + lax.ppermute(value, "col", [(i, i ^ bit) for i in range(cols)])
        bit *= 2
    return value


def local(rows, cols, x, y, freq, weight, sex_rows, sex_cols):
    group_size = y.shape[0]
    local_vars = x.shape[1]
    groups_here = local_vars // group_size
    half_rows = x.shape[0] // HALVES
    lanes = [Lane(rows, cols, groups_here, towards) for towards in (True, False)]

    numbers = np.zeros((rows * cols, 0), np.int32)

    def add(columns):
        nonlocal numbers
        at = numbers.shape[1]
        numbers = np.concatenate([numbers, np.asarray(columns, np.int32)], axis=1)
        return at

    devices = [(r, c) for r in range(rows) for c in range(cols)]
    own_at = {}
    for d, lane in enumerate(lanes):
        for t in range(1, lane.rounds + 1):
            entry = []
            for r, c in devices:
                key = lane.own(r, c, t)
                entry.append((0, 0, 0) if key is None else (1, key[0], (r + key[2]) % rows % groups_here))
            own_at[d, t] = add(entry)
    used = {}
    place_at = {}
    candidates = {}
    for half in range(HALVES):
        arrivals = {
            (r, c, s, d): lane.arrival(r, c, half, s)
            for r, c in devices
            for s in range(STEPS)
            for d, lane in enumerate(lanes)
        }
        used[half] = sorted({(t, d) for (_, _, _, d), t in arrivals.items() if t is not None})
        entry = []
        for r, c in devices:
            places = []
            for s in range(STEPS):
                place = -1 - (r + s) % rows % groups_here
                for d in range(len(lanes)):
                    if arrivals[r, c, s, d] is not None:
                        place = used[half].index((arrivals[r, c, s, d], d))
                places.append(place)
            entry.append(places)
        place_at[half] = add(entry)
        candidates[half] = [sorted({max(e[s], -1) for e in entry}) for s in range(STEPS)]

    row_place = lax.axis_index("row")
    col_place = lax.axis_index("col")
    table = lax.dynamic_slice(jnp.asarray(numbers), (row_place * cols + col_place, 0), (1, numbers.shape[1]))[0]

    buffers = {}
    for t in range(1, max(lane.rounds for lane in lanes) + 1):
        for d, lane in enumerate(lanes):
            if t > lane.rounds:
                continue
            pairs = lane.pairs(t)
            if not pairs:
                continue
            at = own_at[d, t]
            held = buffers.get((d, t - DEPTH))
            if held is None or numbers[:, at].any():
                start = (table[at + 1] * half_rows, table[at + 2] * group_size)
                mine = lax.dynamic_slice(x, start, (half_rows, group_size))
                held = mine if held is None else jnp.where(table[at] == 1, mine, held)
            buffers[d, t] = lax.ppermute(held, ("row", "col"), pairs)

    back = [(i, (i - 1) % rows) for i in range(rows)]
    window = [y]
    for _ in range(STEPS - 1):
        window.append(lax.ppermute(window[-1], "row", back))

    factor = weight / jnp.sqrt(2.0 * freq * (1.0 - freq))
    span = STEPS * group_size

    def in_window(value):
        twice = jnp.concatenate([value, value])
        return lax.dynamic_slice(twice, (row_place * group_size,), (span,))

    window_factor = in_window(factor)
    window_twice = in_window(2.0 * freq)
    male_scale = np.float32(np.sqrt(0.5))
    male_rows = jnp.where(sex_rows > 0, male_scale, np.float32(1.0))[:, None]
    male_cols = jnp.where(sex_cols > 0, male_scale, np.float32(1.0))[None, :]
    zy = []
    for s, block in enumerate(window):
        part = slice(s * group_size, (s + 1) * group_size)
        value = block.astype(jnp.float32) - window_twice[part, None]
        zy.append((value * window_factor[part, None] * male_cols).astype(jnp.bfloat16))
    zy = jnp.concatenate(zy, axis=0)

    here = lambda value: lax.dynamic_slice(value, (col_place * local_vars,), (local_vars,))[None, :]
    zx = ((x.astype(jnp.float32) - here(2.0 * freq)) * here(factor) * male_rows).astype(jnp.bfloat16)
    squares = col_sum(jnp.sum(jnp.square(zx.astype(jnp.float32)), axis=1), cols)
    inbreeding = squares / jnp.float32(freq.shape[0]) - 1.0

    relation = None
    for half in range(HALVES):
        relation = product(
            half,
            place_at[half],
            candidates[half],
            table,
            x,
            [buffers[d, t] for t, d in used[half]],
            window_factor[None, :],
            window_twice[None, :],
            male_rows,
            zy,
            relation,
        )
    return relation, inbreeding


def solution(mesh):
    rows, cols = mesh.shape["row"], mesh.shape["col"]
    return jax.shard_map(
        functools.partial(local, rows, cols),
        mesh=mesh,
        in_specs=(P("row", "col"), P("row", "col"), P(), P(), P("row"), P("col")),
        out_specs=(P("row", "col"), P("row")),
        check_vma=False,
    )
```

```python
import functools
import itertools

import jax
import jax.numpy as jnp
import numpy as np
from jax import lax
from jax.experimental import pallas as pl
from jax.experimental.pallas import tpu as pltpu
from jax.sharding import PartitionSpec as P

STEPS = 4
HALVES = 2
DEPTH = 2
HOP = 2
COL_TILE = 512
ROW_TILE = 128
VMEM_LIMIT = 40 * 2**20


class Item:
    def __init__(self, row, half, s, place, home=None):
        self.row, self.half, self.s, self.place = row, half, s, place
        self.home = home


def line_slots(items, cut):
    ends, inner = {}, {}
    todo = sorted(items, key=lambda i: (i.home is None, i.half, i.place, i.s))
    slot = 1
    while todo:
        for item in todo:
            first = 1 + DEPTH * (item.place - 1) + (HOP if item.home is not None else 0)
            if first <= slot:
                ends[slot] = item
                if item.place > 1:
                    inner[slot] = item
                todo.remove(item)
                break
        slot += 1
    for item in sorted(cut, key=lambda i: (i.place, i.half, i.s)):
        slot = 1 + DEPTH * (item.place - 1)
        if item.place > 1:
            while slot in inner:
                slot += 1
            inner[slot] = item
    return ends, inner


class Lane:
    def __init__(self, rows, cols, groups_here, towards_zero):
        self.rows, self.cols = rows, cols
        self.towards_zero = towards_zero
        self.items = []
        for r in range(rows):
            mine = [
                Item(r, half, s, self.place((r + s) % rows // groups_here))
                for half in range(HALVES)
                for s in range(STEPS)
            ]
            self.items.append([i for i in mine if i.place > 0])
        self.away = []
        self.lines = [line_slots(items, []) for items in self.items]
        if rows % 2 == 0 and cols > 3:
            for r in range(rows // 2):
                self.balance(r, r + rows // 2)
                self.balance(r + rows // 2, r)
        self.rounds = max(
            [max(ends, default=0) for ends, _ in self.lines] + [max(inner, default=0) - DEPTH for _, inner in self.lines]
        )

    def place(self, c):
        return c if self.towards_zero else self.cols - 1 - c

    col = place

    def balance(self, r, other):
        if len(self.items[r]) < len(self.items[other]) or any(i.row == other for i in self.away):
            return
        places = sorted({i.place for i in self.items[r]})
        best = None
        for counts in itertools.product(range(HALVES + 1), repeat=len(places)):
            gone = []
            for place, count in zip(places, counts):
                here = [i for i in self.items[r] if i.place == place]
                here.sort(key=lambda i: (-i.half, -i.s))
                gone += here[:count]
            visitors = [Item(other, i.half, i.s, i.place, home=r) for i in gone]
            mine = line_slots([i for i in self.items[r] if i not in gone], gone)
            theirs = line_slots(self.items[other] + visitors, [])
            score = (
                max(max(mine[0], default=0), max(theirs[0], default=0)),
                abs(len(mine[0]) - len(theirs[0])),
                max([slot for slot, i in theirs[0].items() if i.home is not None], default=0),
                len(gone),
            )
            if best is None or score < best[0]:
                best = score, gone, mine, theirs
        _, gone, mine, theirs = best
        self.away += gone
        if gone:
            self.lines[r], self.lines[other] = mine, theirs

    def sent(self, r, c, t):
        p = self.place(c)
        ends, inner = self.lines[r]
        if p == 0:
            return None
        item = ends.get(t) if p == 1 else inner.get(t + DEPTH * (p - 1))
        return item if item is not None and item.place >= p else None

    def pairs(self, t):
        found = []
        for r in range(self.rows):
            for c in range(self.cols):
                if self.sent(r, c, t) is not None:
                    found.append((r * self.cols + c, r * self.cols + self.col(self.place(c) - 1)))
        return found

    def arrival(self, r, c, half, s):
        p = self.place(c)
        for i in self.items[r]:
            if (i.half, i.s) == (half, s) and i.place > p:
                if p == 0 and i in self.away:
                    for ends, _ in self.lines:
                        for slot, v in ends.items():
                            if v.home == r and (v.half, v.s) == (half, s):
                                return slot, True
                ends, inner = self.lines[r]
                for slot, v in (ends if p == 0 else inner).items():
                    if v is i:
                        return slot - DEPTH * p, False
        return None


def lookup(values, device):
    known = [v for v in values if v is not None]
    if len(set(known)) <= 1:
        return known[0] if known else 0
    values = [known[0] if v is None else v for v in values]
    result = jnp.uint32(0)
    place = (device % 32).astype(jnp.uint32)
    for bit in range(max(values).bit_length()):
        ones = [v >> bit & 1 for v in values]
        words = [sum(b << i for i, b in enumerate(ones[at : at + 32])) for at in range(0, len(ones), 32)]
        word = jnp.uint32(words[0])
        for i, other in enumerate(words[1:], 1):
            word = jnp.where(device // 32 == i, jnp.uint32(other), word)
        result = result | (((word >> place) & jnp.uint32(1)) << jnp.uint32(bit))
    return result.astype(jnp.int32)


def product_kernel(half, candidates, scale, n_buffers, places, *refs):
    x, buffers = refs[0], refs[1 : 1 + n_buffers]
    factor, twice, male = refs[1 + n_buffers : 4 + n_buffers]
    zy = refs[4 + n_buffers : 4 + n_buffers + STEPS]
    out, raw, zx, sems = refs[-4:]
    half_rows = raw.shape[0]
    width = raw.shape[1] // STEPS

    @pl.when(pl.program_id(0) == 0)
    def _():
        for s in range(STEPS):
            place = places[s]
            target = raw.at[:, pl.ds(s * width, width)]
            for number in candidates[s]:
                if number >= 0:

                    @pl.when(place == number)
                    def _(number=number, target=target, s=s):
                        pltpu.make_async_copy(buffers[number], target, sems.at[s]).start()

                else:

                    @pl.when(place < 0)
                    def _(place=place, target=target, s=s):
                        col = pl.multiple_of((-1 - place) * width, width)
                        mine = x.at[pl.ds(half * half_rows, half_rows), pl.ds(col, width)]
                        pltpu.make_async_copy(mine, target, sems.at[s]).start()

        for s in range(STEPS):
            columns = pl.ds(s * width, width)
            part = raw.at[:, columns]
            pltpu.make_async_copy(part, part, sems.at[s]).wait()

            @pl.loop(0, half_rows // ROW_TILE)
            def _(i, columns=columns):
                rows = pl.ds(pl.multiple_of(i * ROW_TILE, ROW_TILE), ROW_TILE)
                value = raw[rows, columns].astype(jnp.float32) - twice[:, columns]
                zx[rows, columns] = (value * factor[:, columns] * male[rows, :]).astype(zx.dtype)

    right = jnp.concatenate([block[...] for block in zy], axis=0)
    total = jnp.dot(zx[...], right, preferred_element_type=jnp.float32)
    out[...] = (total * scale).astype(out.dtype)


def product(half, places, candidates, x, buffers, factor, twice, male, zy, before):
    rows, n = x.shape[0], zy[0].shape[1]
    half_rows = rows // HALVES
    group_size = zy[0].shape[0]
    depth = group_size * STEPS
    scale = float(1.0 / np.sqrt(np.float32(depth)))
    whole = lambda j, places: (0, 0)
    specs = [pl.BlockSpec(memory_space=pl.ANY)] * (1 + len(buffers)) + [
        pl.BlockSpec((1, depth), whole),
        pl.BlockSpec((1, depth), whole),
        pl.BlockSpec((half_rows, 1), lambda j, places: (half, 0)),
    ]
    specs += [pl.BlockSpec((group_size, COL_TILE), lambda j, places: (0, j))] * STEPS
    args = [places, x, *buffers, factor, twice, male, *zy]
    aliases = {}
    if before is not None:
        aliases = {len(args): 0}
        specs.append(pl.BlockSpec(memory_space=pl.ANY))
        args.append(before)
    return pl.pallas_call(
        functools.partial(product_kernel, half, candidates, scale, len(buffers)),
        out_shape=jax.ShapeDtypeStruct((rows, n), jnp.bfloat16),
        grid_spec=pltpu.PrefetchScalarGridSpec(
            num_scalar_prefetch=1,
            grid=(n // COL_TILE,),
            in_specs=specs,
            out_specs=pl.BlockSpec((half_rows, COL_TILE), lambda j, places: (half, j)),
            scratch_shapes=[
                pltpu.VMEM((half_rows, depth), jnp.bfloat16),
                pltpu.VMEM((half_rows, depth), jnp.bfloat16),
                pltpu.SemaphoreType.DMA((STEPS,)),
            ],
        ),
        input_output_aliases=aliases,
        compiler_params=pltpu.CompilerParams(vmem_limit_bytes=VMEM_LIMIT),
        cost_estimate=pl.CostEstimate(
            flops=2 * half_rows * depth * n,
            bytes_accessed=2 * (half_rows * depth + depth * n + half_rows * n),
            transcendentals=0,
        ),
        name="product",
    )(*args)


def col_sum(value, cols):
    if cols & (cols - 1):
        return lax.psum(value, "col")
    bit = 1
    while bit < cols:
        value = value + lax.ppermute(value, "col", [(i, i ^ bit) for i in range(cols)])
        bit *= 2
    return value


def local(rows, cols, x, y, freq, weight, sex_rows, sex_cols):
    group_size = y.shape[0]
    local_vars = x.shape[1]
    groups_here = local_vars // group_size
    half_rows = x.shape[0] // HALVES
    lanes = [Lane(rows, cols, groups_here, towards) for towards in (True, False)]
    devices = [(r, c) for r in range(rows) for c in range(cols)]
    both = ("row", "col")

    row_place = lax.axis_index("row")
    col_place = lax.axis_index("col")
    device = row_place * cols + col_place

    def local_group(item):
        return ((item.row if item.home is None else item.home) + item.s) % rows % groups_here

    def own_chunk(x, items):
        half = lookup([None if i is None else i.half for i in items], device)
        group = lookup([None if i is None else local_group(i) for i in items], device)
        return lax.dynamic_slice(x, (half * half_rows, group * group_size), (half_rows, group_size))

    crossings = []
    crossing_of = {}
    for d, lane in enumerate(lanes):
        for r in range(rows):
            for item in lane.lines[r][0].values():
                if item.home is None:
                    continue
                source = (item.home, lane.col(item.place))
                target = (r, lane.col(item.place))
                for number, crossing in enumerate(crossings):
                    if source not in crossing and target not in [to for to, _ in crossing.values()]:
                        break
                else:
                    number = len(crossings)
                    crossings.append({})
                crossings[number][source] = (target, item)
                crossing_of[d, r, item.half, item.s] = number

    def number(rc):
        return rc[0] * cols + rc[1]

    buffers = {}
    crossed = {}
    window = [y]
    back = [(i, (i - 1) % rows) for i in range(rows)]
    last = max(lane.rounds for lane in lanes)
    for t in range(1, last + 1):
        for d, lane in enumerate(lanes):
            pairs = lane.pairs(t)
            if not pairs:
                continue
            sent = [lane.sent(r, c, t) for r, c in devices]
            own = [i if i is not None and i.place == lane.place(c) else None for i, (r, c) in zip(sent, devices)]
            home = [i if i is not None and i.home is None else None for i in own]
            visits = [
                None if i is None or i.home is None else crossing_of[d, r, i.half, i.s]
                for i, (r, c) in zip(own, devices)
            ]
            forwards = any(i is not None and o is None for i, o in zip(sent, own))
            sources = [(None, buffers[d, t - DEPTH])] if forwards else []
            for visit in sorted({v for v in visits if v is not None}):
                sources.append(([v == visit for v in visits], crossed[visit]))
            held = None
            if any(home):
                tied = lax.optimization_barrier((x, *[b for _, b in sources]))
                sources = [(mask, b) for (mask, _), b in zip(sources, tied[1:])]
                held = own_chunk(tied[0], home)
            for mask, buffer in sources[::-1]:
                if held is None:
                    held = buffer
                elif mask is not None:
                    held = jnp.where(lookup([int(m) for m in mask], device) == 1, buffer, held)
                else:
                    kept = [
                        None if i is None else int(i.place != lane.place(c)) for i, (r, c) in zip(sent, devices)
                    ]
                    held = jnp.where(lookup(kept, device) == 1, buffer, held)
            if t in (4, 6, 7) and d == 0 and len(window) < STEPS:
                held, window[-1] = lax.optimization_barrier((held, window[-1]))
            buffers[d, t] = lax.ppermute(held, both, pairs)
        if t == 1:
            for crossing in crossings:
                own = [crossing[rc][1] if rc in crossing else None for rc in devices]
                held = own_chunk(lax.optimization_barrier(x), own)
                pairs = [(number(rc), number(to)) for rc, (to, _) in crossing.items()]
                crossed[crossings.index(crossing)] = lax.ppermute(held, both, pairs)
        if t in (1, 4, 6, 7) and len(window) < STEPS:
            window.append(lax.ppermute(window[-1], "row", back))
        pairs, by_lane = [], []
        for d, lane in enumerate(lanes):
            for r in range(rows):
                item = lane.lines[r][0].get(t)
                if item is not None and item.home is not None:
                    end = lane.col(0)
                    pairs.append((number((r, end)), number((item.home, end))))
                    by_lane.append(d)
        if pairs:
            if len(set(by_lane)) == 1:
                held = buffers[by_lane[0], t]
            else:
                held = jnp.where(col_place == lanes[0].col(0), buffers[0, t], buffers[1, t])
            buffers["back", t] = lax.ppermute(held, both, pairs)
    while len(window) < STEPS:
        window.append(lax.ppermute(window[-1], "row", back))

    factor = weight / jnp.sqrt(2.0 * freq * (1.0 - freq))
    span = STEPS * group_size

    def in_window(value):
        return lax.dynamic_slice(jnp.concatenate([value, value]), (row_place * group_size,), (span,))

    window_factor = in_window(factor)
    window_twice = in_window(2.0 * freq)
    male_scale = np.float32(np.sqrt(0.5))
    male_rows = jnp.where(sex_rows > 0, male_scale, np.float32(1.0))[:, None]
    male_cols = jnp.where(sex_cols > 0, male_scale, np.float32(1.0))[None, :]
    zy = []
    for s, block in enumerate(window):
        part = slice(s * group_size, (s + 1) * group_size)
        value = block.astype(jnp.float32) - window_twice[part, None]
        zy.append((value * window_factor[part, None] * male_cols).astype(jnp.bfloat16))

    here = lambda value: lax.dynamic_slice(value, (col_place * local_vars,), (local_vars,))[None, :]
    zx = ((x.astype(jnp.float32) - here(2.0 * freq)) * here(factor) * male_rows).astype(jnp.bfloat16)
    squares = col_sum(jnp.sum(jnp.square(zx.astype(jnp.float32)), axis=1), cols)
    inbreeding = squares / jnp.float32(freq.shape[0]) - 1.0

    relation = None
    for half in range(HALVES):
        found = []
        for r, c in devices:
            keys = []
            for s in range(STEPS):
                key = -1 - (r + s) % rows % groups_here
                for d, lane in enumerate(lanes):
                    arrival = lane.arrival(r, c, half, s)
                    if arrival is not None:
                        key = ("back" if arrival[1] else d, arrival[0])
                keys.append(key)
            found.append(keys)
        used = sorted({k for keys in found for k in keys if isinstance(k, tuple)}, key=lambda k: (k[1], str(k[0])))
        found = np.asarray([[k if isinstance(k, int) else used.index(k) for k in keys] for keys in found], np.int32)
        candidates = [sorted({max(int(k), -1) for k in found[:, s]}) for s in range(STEPS)]
        relation = product(
            half,
            lax.dynamic_slice(jnp.asarray(found), (device, 0), (1, STEPS))[0],
            candidates,
            x,
            [buffers[key] for key in used],
            window_factor[None, :],
            window_twice[None, :],
            male_rows,
            zy,
            relation,
        )
    return relation, inbreeding


def solution(mesh):
    rows, cols = mesh.shape["row"], mesh.shape["col"]
    return jax.shard_map(
        functools.partial(local, rows, cols),
        mesh=mesh,
        in_specs=(P("row", "col"), P("row", "col"), P(), P(), P("row"), P("col")),
        out_specs=(P("row", "col"), P("row")),
        check_vma=False,
    )
```

```python
import functools
import itertools

import jax
import jax.numpy as jnp
import numpy as np
from jax import lax
from jax.experimental import pallas as pl
from jax.experimental.pallas import tpu as pltpu
from jax.sharding import PartitionSpec as P

STEPS = 4
PIECES = 4
PARTS = ((0, 2), (2, 3), (3, 4))
DEPTH = 1
HOP = 2
COL_TILE = 512
ROW_TILE = 32
VMEM_LIMIT = 40 * 2**20


class Item:
    def __init__(self, row, blocks, place, home=None):
        self.row, self.blocks, self.place = row, blocks, place
        self.home = home

    @property
    def owner(self):
        return self.row if self.home is None else self.home


def items_of(row, steps, place):
    items = []
    for a, b in zip(steps[::2], steps[1::2]):
        items += [Item(row, ((q, a), (q, b)), place) for q in range(PIECES)]
    if len(steps) % 2:
        items += [Item(row, ((q, steps[-1]), (q + 1, steps[-1])), place) for q in range(0, PIECES, 2)]
    return items


def line_slots(items, cut):
    ends, inner = {}, {}
    todo = sorted(items, key=lambda i: (i.home is None, i.blocks[0][0], i.place, i.blocks))
    slot = 1
    while todo:
        for item in todo:
            first = 1 + DEPTH * (item.place - 1) + (HOP if item.home is not None else 0)
            if first <= slot:
                ends[slot] = item
                if item.place > 1:
                    inner[slot] = item
                todo.remove(item)
                break
        slot += 1
    for item in sorted(cut, key=lambda i: (i.place, i.blocks)):
        slot = 1 + DEPTH * (item.place - 1)
        if item.place > 1:
            while slot in inner:
                slot += 1
            inner[slot] = item
    return ends, inner


class Lane:
    def __init__(self, rows, cols, groups_here, towards_zero):
        self.rows, self.cols = rows, cols
        self.towards_zero = towards_zero
        self.items = []
        for r in range(rows):
            steps_at = {}
            for s in range(STEPS):
                steps_at.setdefault(self.place((r + s) % rows // groups_here), []).append(s)
            mine = [i for place, steps in steps_at.items() for i in items_of(r, steps, place)]
            self.items.append([i for i in mine if i.place > 0])
        self.away = []
        self.lines = [line_slots(items, []) for items in self.items]
        if rows % 2 == 0 and cols > 3:
            for r in range(rows // 2):
                self.balance(r, r + rows // 2)
                self.balance(r + rows // 2, r)
        self.rounds = max(
            [max(ends, default=0) for ends, _ in self.lines] + [max(inner, default=0) - DEPTH for _, inner in self.lines]
        )

    def place(self, c):
        return c if self.towards_zero else self.cols - 1 - c

    col = place

    def balance(self, r, other):
        if len(self.items[r]) < len(self.items[other]) or any(i.row == other for i in self.away):
            return
        places = sorted({i.place for i in self.items[r]})
        best = None
        for counts in itertools.product(range(3), repeat=len(places)):
            gone = []
            for place, count in zip(places, counts):
                here = [i for i in self.items[r] if i.place == place]
                here.sort(key=lambda i: i.blocks, reverse=True)
                gone += here[:count]
            visitors = [Item(other, i.blocks, i.place, home=r) for i in gone]
            mine = line_slots([i for i in self.items[r] if i not in gone], gone)
            theirs = line_slots(self.items[other] + visitors, [])
            score = (
                max(max(mine[0], default=0), max(theirs[0], default=0)),
                abs(len(mine[0]) - len(theirs[0])),
                max([slot for slot, i in theirs[0].items() if i.home is not None], default=0),
                len(gone),
            )
            if best is None or score < best[0]:
                best = score, gone, mine, theirs
        _, gone, mine, theirs = best
        self.away += gone
        if gone:
            self.lines[r], self.lines[other] = mine, theirs

    def sent(self, r, c, t):
        p = self.place(c)
        ends, inner = self.lines[r]
        if p == 0:
            return None
        item = ends.get(t) if p == 1 else inner.get(t + DEPTH * (p - 1))
        return item if item is not None and item.place >= p else None

    def pairs(self, t):
        found = []
        for r in range(self.rows):
            for c in range(self.cols):
                if self.sent(r, c, t) is not None:
                    found.append((r * self.cols + c, r * self.cols + self.col(self.place(c) - 1)))
        return found

    def arrival(self, r, c, block):
        p = self.place(c)
        for i in self.items[r]:
            if block not in i.blocks or i.place <= p:
                continue
            sub = i.blocks.index(block)
            ends, inner = self.lines[r]
            if p == 0 and i in self.away:
                for other, _ in self.lines:
                    for slot, v in other.items():
                        if v.home == r and v.blocks == i.blocks:
                            return slot, True, sub
            for slot, v in (ends if p == 0 else inner).items():
                if v is i:
                    return slot - DEPTH * p, False, sub
        return None


def lookup(values, device):
    known = [v for v in values if v is not None]
    if len(set(known)) <= 1:
        return known[0] if known else 0
    values = [known[0] if v is None else v for v in values]
    result = jnp.uint32(0)
    place = (device % 32).astype(jnp.uint32)
    for bit in range(max(values).bit_length()):
        ones = [v >> bit & 1 for v in values]
        words = [sum(b << i for i, b in enumerate(ones[at : at + 32])) for at in range(0, len(ones), 32)]
        word = jnp.uint32(words[0])
        for i, other in enumerate(words[1:], 1):
            word = jnp.where(device // 32 == i, jnp.uint32(other), word)
        result = result | (((word >> place) & jnp.uint32(1)) << jnp.uint32(bit))
    return result.astype(jnp.int32)


def window_kernel(*refs):
    blocks = refs[:STEPS]
    factor, twice, male, out = refs[STEPS:]
    group_size = blocks[0].shape[0]
    for s, block in enumerate(blocks):

        @pl.loop(0, group_size // ROW_TILE)
        def _(i, s=s, block=block):
            here = pl.ds(pl.multiple_of(i * ROW_TILE, ROW_TILE), ROW_TILE)
            rows = pl.ds(pl.multiple_of(s * group_size + i * ROW_TILE, ROW_TILE), ROW_TILE)
            value = block[here, :].astype(jnp.float32) - twice[rows, :]
            out[rows, :] = (value * factor[rows, :] * male[...]).astype(out.dtype)


def standardized_window(blocks, factor, twice, male):
    group_size, n = blocks[0].shape
    depth = STEPS * group_size
    column = lambda j: (0, 0)
    return pl.pallas_call(
        window_kernel,
        out_shape=jax.ShapeDtypeStruct((depth, n), jnp.bfloat16),
        grid=(n // COL_TILE,),
        in_specs=[pl.BlockSpec((group_size, COL_TILE), lambda j: (0, j))] * STEPS
        + [pl.BlockSpec((depth, 1), column)] * 2
        + [pl.BlockSpec((1, COL_TILE), lambda j: (0, j))],
        out_specs=pl.BlockSpec((depth, COL_TILE), lambda j: (0, j)),
        compiler_params=pltpu.CompilerParams(vmem_limit_bytes=VMEM_LIMIT),
        cost_estimate=pl.CostEstimate(flops=4 * depth * n, bytes_accessed=4 * depth * n, transcendentals=0),
        name="window",
    )(*blocks, factor, twice, male)


def product_kernel(first, candidates, scale, n_buffers, places, *refs):
    x, buffers = refs[0], refs[1 : 1 + n_buffers]
    factor, twice, male, zy = refs[1 + n_buffers : 5 + n_buffers]
    out, raw, zx, sems = refs[-4:]
    width = raw.shape[1] // STEPS
    piece_rows = buffers[0].shape[0] // 2
    pieces = raw.shape[0] // piece_rows

    @pl.when(pl.program_id(0) == 0)
    def _():
        for q in range(pieces):
            for s in range(STEPS):
                place = places[q * STEPS + s]
                target = raw.at[pl.ds(q * piece_rows, piece_rows), pl.ds(s * width, width)]
                for number in candidates[q * STEPS + s]:
                    if number >= 0:

                        @pl.when(place == number)
                        def _(number=number, target=target, q=q):
                            block = buffers[number // 2].at[pl.ds(number % 2 * piece_rows, piece_rows), :]
                            pltpu.make_async_copy(block, target, sems.at[q]).start()

                    else:

                        @pl.when(place < 0)
                        def _(place=place, target=target, q=q):
                            col = pl.multiple_of((-1 - place) * width, width)
                            block = x.at[pl.ds((first + q) * piece_rows, piece_rows), pl.ds(col, width)]
                            pltpu.make_async_copy(block, target, sems.at[q]).start()

        for q in range(pieces):
            part = raw.at[pl.ds(q * piece_rows, piece_rows), :]
            pltpu.make_async_copy(part, part, sems.at[q]).wait()

            @pl.loop(0, piece_rows // ROW_TILE)
            def _(i, q=q):
                rows = pl.ds(pl.multiple_of(q * piece_rows + i * ROW_TILE, ROW_TILE), ROW_TILE)
                value = raw[rows, :].astype(jnp.float32) - twice[...]
                zx[rows, :] = (value * factor[...] * male[rows, :]).astype(zx.dtype)

    total = jnp.dot(zx[...], zy[...], preferred_element_type=jnp.float32)
    out[...] = (total * scale).astype(out.dtype)


def product(part, places, candidates, x, buffers, factor, twice, male, zy, before):
    rows, (depth, n) = x.shape[0], zy.shape
    first, stop = part
    part_rows = rows // PIECES * (stop - first)
    number = first // (stop - first)
    scale = float(1.0 / np.sqrt(np.float32(depth)))
    whole = lambda j, places: (0, 0)
    specs = [pl.BlockSpec(memory_space=pl.ANY)] * (1 + len(buffers)) + [
        pl.BlockSpec((1, depth), whole),
        pl.BlockSpec((1, depth), whole),
        pl.BlockSpec((part_rows, 1), lambda j, places: (number, 0)),
        pl.BlockSpec((depth, COL_TILE), lambda j, places: (0, j)),
    ]
    args = [places, x, *buffers, factor, twice, male, zy]
    aliases = {}
    if before is not None:
        aliases = {len(args): 0}
        specs.append(pl.BlockSpec(memory_space=pl.ANY))
        args.append(before)
    return pl.pallas_call(
        functools.partial(product_kernel, first, candidates, scale, len(buffers)),
        out_shape=jax.ShapeDtypeStruct((rows, n), jnp.bfloat16),
        grid_spec=pltpu.PrefetchScalarGridSpec(
            num_scalar_prefetch=1,
            grid=(n // COL_TILE,),
            in_specs=specs,
            out_specs=pl.BlockSpec((part_rows, COL_TILE), lambda j, places: (number, j)),
            scratch_shapes=[
                pltpu.VMEM((part_rows, depth), jnp.bfloat16),
                pltpu.VMEM((part_rows, depth), jnp.bfloat16),
                pltpu.SemaphoreType.DMA((stop - first,)),
            ],
        ),
        input_output_aliases=aliases,
        compiler_params=pltpu.CompilerParams(vmem_limit_bytes=VMEM_LIMIT),
        cost_estimate=pl.CostEstimate(
            flops=2 * part_rows * depth * n,
            bytes_accessed=2 * (part_rows * depth + depth * n + part_rows * n),
            transcendentals=0,
        ),
        name="product",
    )(*args)


def col_sum(value, cols):
    if cols & (cols - 1):
        return lax.psum(value, "col")
    bit = 1
    while bit < cols:
        value = value + lax.ppermute(value, "col", [(i, i ^ bit) for i in range(cols)])
        bit *= 2
    return value


def local(rows, cols, x, y, freq, weight, sex_rows, sex_cols):
    group_size = y.shape[0]
    local_vars = x.shape[1]
    groups_here = local_vars // group_size
    piece_rows = x.shape[0] // PIECES
    lanes = [Lane(rows, cols, groups_here, towards) for towards in (True, False)]
    devices = [(r, c) for r in range(rows) for c in range(cols)]
    both = ("row", "col")

    row_place = lax.axis_index("row")
    col_place = lax.axis_index("col")
    device = row_place * cols + col_place

    def number(r, c):
        return r * cols + c

    def own_chunk(x, items):
        blocks = []
        for k in range(2):
            piece = lookup([None if i is None else i.blocks[k][0] for i in items], device)
            group = lookup(
                [None if i is None else (i.owner + i.blocks[k][1]) % rows % groups_here for i in items], device
            )
            start = (piece * piece_rows, group * group_size)
            blocks.append(lax.dynamic_slice(x, start, (piece_rows, group_size)))
        return jnp.concatenate(blocks, axis=0)

    crossings = []
    crossing_of = {}
    for d, lane in enumerate(lanes):
        for r in range(rows):
            for slot, item in sorted(lane.lines[r][0].items()):
                if item.home is None:
                    continue
                source, target = (item.home, lane.col(item.place)), (r, lane.col(item.place))
                for k, crossing in enumerate(crossings):
                    if source not in crossing and target not in [to for to, _ in crossing.values()]:
                        break
                else:
                    k = len(crossings)
                    crossings.append({})
                crossings[k][source] = (target, item)
                crossing_of[d, r, item.blocks] = k

    def lane_of(phase, r):
        return (r + phase) % 2

    buffers = {}
    crossed = {}
    window = [y]
    back = [(i, (i - 1) % rows) for i in range(rows)]

    def send(phase, t):
        lane = {r: lanes[lane_of(phase, r)] for r in range(rows)}
        sent = [lane[r].sent(r, c, t) for r, c in devices]
        pairs = [
            (number(r, c), number(r, lane[r].col(lane[r].place(c) - 1)))
            for i, (r, c) in zip(sent, devices)
            if i is not None
        ]
        if not pairs:
            return
        at = [lane[r].place(c) for r, c in devices]
        kinds = []
        for i, p, (r, c) in zip(sent, at, devices):
            if i is None:
                kinds.append(None)
            elif i.place != p:
                kinds.append(1)
            elif i.home is None:
                kinds.append(0)
            else:
                kinds.append(2 + crossing_of[lane_of(phase, r), r, i.blocks])
        sources = []
        for kind in sorted({k for k in kinds if k}):
            sources.append((kind, buffers[phase, t - DEPTH] if kind == 1 else crossed[kind - 2]))
        ties = [b for _, b in sources]
        other = buffers.get((1 - phase, t - 1 - (1 - phase)))
        if other is not None:
            ties.append(other)
        if phase == 0 and t in (3, 5, 7) and len(window) < STEPS:
            ties.append(window[-1])
        tied = lax.optimization_barrier((x, *ties))
        if phase == 0 and t in (3, 5, 7) and len(window) < STEPS:
            window[-1] = tied[-1]
        held = None
        if 0 in kinds:
            held = own_chunk(tied[0], [i if k == 0 else None for i, k in zip(sent, kinds)])
        for k, (kind, _) in enumerate(sources):
            buffer = tied[1 + k]
            if held is not None:
                mask = lookup([None if v is None else int(v == kind) for v in kinds], device)
                buffer = jnp.where(mask == 1, buffer, held)
            held = buffer
        buffers[phase, t] = lax.ppermute(held, both, pairs)

    def bring_back(phase, t):
        pairs = []
        for r in range(rows):
            lane = lanes[lane_of(phase, r)]
            item = lane.lines[r][0].get(t)
            if item is not None and item.home is not None:
                pairs.append((number(r, lane.col(0)), number(item.home, lane.col(0))))
        if pairs:
            buffers["back%d" % phase, t] = lax.ppermute(buffers[phase, t], both, pairs)

    for t in range(1, max(lane.rounds for lane in lanes) + 1):
        for phase in range(2):
            send(phase, t)
        if t == 1:
            for crossing in crossings:
                held = own_chunk(
                    lax.optimization_barrier(x), [crossing[rc][1] if rc in crossing else None for rc in devices]
                )
                pairs = [(number(*rc), number(*to)) for rc, (to, _) in crossing.items()]
                crossed[len(crossed)] = lax.ppermute(held, both, pairs)
        if t in (1, 3, 5, 7) and len(window) < STEPS:
            window.append(lax.ppermute(window[-1], "row", back))
        for phase in range(2):
            bring_back(phase, t)
    while len(window) < STEPS:
        window.append(lax.ppermute(window[-1], "row", back))

    factor = weight / jnp.sqrt(2.0 * freq * (1.0 - freq))
    span = STEPS * group_size

    def in_window(value):
        return lax.dynamic_slice(jnp.concatenate([value, value]), (row_place * group_size,), (span,))

    window_factor = in_window(factor)
    window_twice = in_window(2.0 * freq)
    male_scale = np.float32(np.sqrt(0.5))
    male_rows = jnp.where(sex_rows > 0, male_scale, np.float32(1.0))[:, None]
    male_cols = jnp.where(sex_cols > 0, male_scale, np.float32(1.0))[None, :]
    zy = standardized_window(window, window_factor[:, None], window_twice[:, None], male_cols)

    here = lambda value: lax.dynamic_slice(value, (col_place * local_vars,), (local_vars,))[None, :]
    zx = ((x.astype(jnp.float32) - here(2.0 * freq)) * here(factor) * male_rows).astype(jnp.bfloat16)
    squares = col_sum(jnp.sum(jnp.square(zx.astype(jnp.float32)), axis=1), cols)
    inbreeding = squares / jnp.float32(freq.shape[0]) - 1.0

    relation = None
    for part in PARTS:
        found = []
        for r, c in devices:
            keys = []
            for q in range(*part):
                for s in range(STEPS):
                    key = -1 - (r + s) % rows % groups_here
                    for d, lane in enumerate(lanes):
                        arrival = lane.arrival(r, c, (q, s))
                        if arrival is not None:
                            t, returned, sub = arrival
                            phase = (r + d) % 2
                            if returned:
                                phase = "back%d" % ((r + rows // 2 + d) % 2)
                            key = (phase, t), sub
                    keys.append(key)
            found.append(keys)
        used = {k[0] for keys in found for k in keys if isinstance(k, tuple)}
        used = sorted(used, key=lambda k: (k[1], str(k[0])))
        places = np.asarray(
            [[k if isinstance(k, int) else 2 * used.index(k[0]) + k[1] for k in keys] for keys in found], np.int32
        )
        candidates = [sorted({max(int(k), -1) for k in places[:, i]}) for i in range(places.shape[1])]
        relation = product(
            part,
            lax.dynamic_slice(jnp.asarray(places), (device, 0), (1, places.shape[1]))[0],
            candidates,
            x,
            [buffers[key] for key in used],
            window_factor[None, :],
            window_twice[None, :],
            male_rows,
            zy,
            relation,
        )
    return relation, inbreeding


def solution(mesh):
    rows, cols = mesh.shape["row"], mesh.shape["col"]
    return jax.shard_map(
        functools.partial(local, rows, cols),
        mesh=mesh,
        in_specs=(P("row", "col"), P("row", "col"), P(), P(), P("row"), P("col")),
        out_specs=(P("row", "col"), P("row")),
        check_vma=False,
    )
```

```python
import functools
import itertools

import jax
import jax.numpy as jnp
import numpy as np
from jax import lax
from jax.experimental import pallas as pl
from jax.experimental.pallas import tpu as pltpu
from jax.sharding import PartitionSpec as P

STEPS = 4
PIECES = 2
DEPTH = 2
FLIGHT = 3
HOP = 2
COL_TILE = 512
ROW_TILE = 32
VMEM_LIMIT = 60 * 2**20


class Item:
    def __init__(self, row, piece, s, place, home=None):
        self.row, self.piece, self.s, self.place = row, piece, s, place
        self.home = home

    @property
    def owner(self):
        return self.row if self.home is None else self.home

    @property
    def key(self):
        return self.piece, self.s


def line_slots(items, cut):
    ends, inner = {}, {}
    todo = sorted(items, key=lambda i: (i.home is None, i.piece, i.place, i.s))
    slot = 1
    while todo:
        for item in todo:
            first = 1 + DEPTH * (item.place - 1) + (HOP if item.home is not None else 0)
            if first <= slot:
                ends[slot] = item
                if item.place > 1:
                    inner[slot] = item
                todo.remove(item)
                break
        slot += 1
    for item in sorted(cut, key=lambda i: (i.place, i.key)):
        slot = 1 + DEPTH * (item.place - 1)
        if item.place > 1:
            while slot in inner:
                slot += 1
            inner[slot] = item
    return ends, inner


class Lane:
    def __init__(self, rows, cols, groups_here, towards_zero):
        self.rows, self.cols = rows, cols
        self.towards_zero = towards_zero
        self.items = []
        for r in range(rows):
            mine = [
                Item(r, piece, s, self.place((r + s) % rows // groups_here))
                for piece in range(PIECES)
                for s in range(STEPS)
            ]
            self.items.append([i for i in mine if i.place > 0])
        self.away = []
        self.lines = [line_slots(items, []) for items in self.items]
        if rows % 2 == 0 and cols > 3:
            for r in range(rows // 2):
                self.balance(r, r + rows // 2)
                self.balance(r + rows // 2, r)
        self.rounds = max(
            [max(ends, default=0) for ends, _ in self.lines] + [max(inner, default=0) - DEPTH for _, inner in self.lines]
        )

    def place(self, c):
        return c if self.towards_zero else self.cols - 1 - c

    col = place

    def balance(self, r, other):
        if len(self.items[r]) < len(self.items[other]) or any(i.row == other for i in self.away):
            return
        places = sorted({i.place for i in self.items[r]})
        best = None
        for counts in itertools.product(range(3), repeat=len(places)):
            gone = []
            for place, count in zip(places, counts):
                here = [i for i in self.items[r] if i.place == place]
                here.sort(key=lambda i: i.key, reverse=True)
                gone += here[:count]
            visitors = [Item(other, i.piece, i.s, i.place, home=r) for i in gone]
            mine = line_slots([i for i in self.items[r] if i not in gone], gone)
            theirs = line_slots(self.items[other] + visitors, [])
            score = (
                max(max(mine[0], default=0), max(theirs[0], default=0)),
                abs(len(mine[0]) - len(theirs[0])),
                max([slot for slot, i in theirs[0].items() if i.home is not None], default=0),
                len(gone),
            )
            if best is None or score < best[0]:
                best = score, gone, mine, theirs
        _, gone, mine, theirs = best
        self.away += gone
        if gone:
            self.lines[r], self.lines[other] = mine, theirs

    def sent(self, r, c, t):
        p = self.place(c)
        ends, inner = self.lines[r]
        if p == 0:
            return None
        item = ends.get(t) if p == 1 else inner.get(t + DEPTH * (p - 1))
        return item if item is not None and item.place >= p else None

    def pairs(self, t):
        found = []
        for r in range(self.rows):
            for c in range(self.cols):
                if self.sent(r, c, t) is not None:
                    found.append((r * self.cols + c, r * self.cols + self.col(self.place(c) - 1)))
        return found

    def arrival(self, r, c, key):
        p = self.place(c)
        for i in self.items[r]:
            if i.key != key or i.place <= p:
                continue
            ends, inner = self.lines[r]
            if p == 0 and i in self.away:
                for other, _ in self.lines:
                    for slot, v in other.items():
                        if v.home == r and v.key == key:
                            return slot, True
            for slot, v in (ends if p == 0 else inner).items():
                if v is i:
                    return slot - DEPTH * p, False
        return None


def lookup(values, device):
    known = [v for v in values if v is not None]
    if len(set(known)) <= 1:
        return known[0] if known else 0
    values = [known[0] if v is None else v for v in values]
    result = jnp.uint32(0)
    place = (device % 32).astype(jnp.uint32)
    for bit in range(max(values).bit_length()):
        ones = [v >> bit & 1 for v in values]
        words = [sum(b << i for i, b in enumerate(ones[at : at + 32])) for at in range(0, len(ones), 32)]
        word = jnp.uint32(words[0])
        for i, other in enumerate(words[1:], 1):
            word = jnp.where(device // 32 == i, jnp.uint32(other), word)
        result = result | (((word >> place) & jnp.uint32(1)) << jnp.uint32(bit))
    return result.astype(jnp.int32)


def window_kernel(*refs):
    blocks = refs[:STEPS]
    factor, twice, male, out = refs[STEPS:]
    group_size = blocks[0].shape[0]
    for s, block in enumerate(blocks):

        @pl.loop(0, group_size // ROW_TILE)
        def _(i, s=s, block=block):
            here = pl.ds(pl.multiple_of(i * ROW_TILE, ROW_TILE), ROW_TILE)
            rows = pl.ds(pl.multiple_of(s * group_size + i * ROW_TILE, ROW_TILE), ROW_TILE)
            value = block[here, :].astype(jnp.float32) - twice[rows, :]
            out[rows, :] = (value * factor[rows, :] * male[...]).astype(out.dtype)


def standardized_window(blocks, factor, twice, male):
    group_size, n = blocks[0].shape
    depth = STEPS * group_size
    column = lambda j: (0, 0)
    return pl.pallas_call(
        window_kernel,
        out_shape=jax.ShapeDtypeStruct((depth, n), jnp.bfloat16),
        grid=(n // COL_TILE,),
        in_specs=[pl.BlockSpec((group_size, COL_TILE), lambda j: (0, j))] * STEPS
        + [pl.BlockSpec((depth, 1), column)] * 2
        + [pl.BlockSpec((1, COL_TILE), lambda j: (0, j))],
        out_specs=pl.BlockSpec((depth, COL_TILE), lambda j: (0, j)),
        compiler_params=pltpu.CompilerParams(vmem_limit_bytes=VMEM_LIMIT),
        cost_estimate=pl.CostEstimate(flops=4 * depth * n, bytes_accessed=4 * depth * n, transcendentals=0),
        name="window",
    )(*blocks, factor, twice, male)


def product_kernel(piece, candidates, scale, n_buffers, places, *refs):
    x, buffers = refs[0], refs[1 : 1 + n_buffers]
    factor, twice, male, zy = refs[1 + n_buffers : 5 + n_buffers]
    out, raw, zx, sems = refs[-4:]
    piece_rows = raw.shape[0]
    width = raw.shape[1] // STEPS

    @pl.when(pl.program_id(0) == 0)
    def _():
        for s in range(STEPS):
            place = places[s]
            target = raw.at[:, pl.ds(s * width, width)]
            for number in candidates[s]:
                if number >= 0:

                    @pl.when(place == number)
                    def _(number=number, target=target, s=s):
                        pltpu.make_async_copy(buffers[number], target, sems.at[s]).start()

                else:

                    @pl.when(place < 0)
                    def _(place=place, target=target, s=s):
                        col = pl.multiple_of((-1 - place) * width, width)
                        block = x.at[pl.ds(piece * piece_rows, piece_rows), pl.ds(col, width)]
                        pltpu.make_async_copy(block, target, sems.at[s]).start()

        for s in range(STEPS):
            part = raw.at[:, pl.ds(s * width, width)]
            pltpu.make_async_copy(part, part, sems.at[s]).wait()

        @pl.loop(0, piece_rows // ROW_TILE)
        def _(i):
            rows = pl.ds(pl.multiple_of(i * ROW_TILE, ROW_TILE), ROW_TILE)
            value = raw[rows, :].astype(jnp.float32) - twice[...]
            zx[rows, :] = (value * factor[...] * male[rows, :]).astype(zx.dtype)

    total = jnp.dot(zx[...], zy[...], preferred_element_type=jnp.float32)
    out[...] = (total * scale).astype(out.dtype)


def product(piece, places, candidates, x, buffers, factor, twice, male, zy, before):
    rows, (depth, n) = x.shape[0], zy.shape
    piece_rows = rows // PIECES
    scale = float(1.0 / np.sqrt(np.float32(depth)))
    whole = lambda j, places: (0, 0)
    specs = [pl.BlockSpec(memory_space=pl.ANY)] * (1 + len(buffers)) + [
        pl.BlockSpec((1, depth), whole),
        pl.BlockSpec((1, depth), whole),
        pl.BlockSpec((piece_rows, 1), lambda j, places: (piece, 0)),
        pl.BlockSpec((depth, COL_TILE), lambda j, places: (0, j)),
    ]
    args = [places, x, *buffers, factor, twice, male, zy]
    aliases = {}
    if before is not None:
        aliases = {len(args): 0}
        specs.append(pl.BlockSpec(memory_space=pl.ANY))
        args.append(before)
    return pl.pallas_call(
        functools.partial(product_kernel, piece, candidates, scale, len(buffers)),
        out_shape=jax.ShapeDtypeStruct((rows, n), jnp.bfloat16),
        grid_spec=pltpu.PrefetchScalarGridSpec(
            num_scalar_prefetch=1,
            grid=(n // COL_TILE,),
            in_specs=specs,
            out_specs=pl.BlockSpec((piece_rows, COL_TILE), lambda j, places: (piece, j)),
            scratch_shapes=[
                pltpu.VMEM((piece_rows, depth), jnp.bfloat16),
                pltpu.VMEM((piece_rows, depth), jnp.bfloat16),
                pltpu.SemaphoreType.DMA((STEPS,)),
            ],
        ),
        input_output_aliases=aliases,
        compiler_params=pltpu.CompilerParams(vmem_limit_bytes=VMEM_LIMIT),
        cost_estimate=pl.CostEstimate(
            flops=2 * piece_rows * depth * n,
            bytes_accessed=2 * (piece_rows * depth + depth * n + piece_rows * n),
            transcendentals=0,
        ),
        name="product",
    )(*args)


def local(rows, cols, x, y, freq, weight, sex_rows, sex_cols):
    group_size = y.shape[0]
    local_vars = x.shape[1]
    groups_here = local_vars // group_size
    piece_rows = x.shape[0] // PIECES
    lanes = [Lane(rows, cols, groups_here, towards) for towards in (True, False)]
    rounds = max(lane.rounds for lane in lanes)
    devices = [(r, c) for r in range(rows) for c in range(cols)]
    both = ("row", "col")

    row_place = lax.axis_index("row")
    col_place = lax.axis_index("col")
    device = row_place * cols + col_place

    def number(r, c):
        return r * cols + c

    chain = [x]

    def after(*values):
        *values, chain[0] = lax.optimization_barrier((*values, chain[0]))
        return values[0] if len(values) == 1 else values

    def own_chunk(items):
        piece = lookup([None if i is None else i.piece for i in items], device)
        group = lookup([None if i is None else (i.owner + i.s) % rows % groups_here for i in items], device)
        return lax.dynamic_slice(chain[0], (piece * piece_rows, group * group_size), (piece_rows, group_size))

    crossings = []
    crossing_of = {}
    for d, lane in enumerate(lanes):
        for r in range(rows):
            for slot, item in sorted(lane.lines[r][0].items()):
                if item.home is None:
                    continue
                source, target = (item.home, lane.col(item.place)), (r, lane.col(item.place))
                for k, crossing in enumerate(crossings):
                    if source not in crossing and target not in [to for to, _ in crossing.values()]:
                        break
                else:
                    k = len(crossings)
                    crossings.append({})
                crossings[k][source] = (target, item)
                crossing_of[d, r, item.key] = k

    def lane_of(phase, r):
        return (r + phase) % 2

    buffers = {}
    crossed = {}

    def send(phase, t):
        lane = {r: lanes[lane_of(phase, r)] for r in range(rows)}
        sent = [lane[r].sent(r, c, t) for r, c in devices]
        pairs = [
            (number(r, c), number(r, lane[r].col(lane[r].place(c) - 1)))
            for i, (r, c) in zip(sent, devices)
            if i is not None
        ]
        if not pairs:
            return
        kinds = []
        for i, (r, c) in zip(sent, devices):
            if i is None:
                kinds.append(None)
            elif i.place != lane[r].place(c):
                kinds.append(1)
            elif i.home is None:
                kinds.append(0)
            else:
                kinds.append(2 + crossing_of[lane_of(phase, r), r, i.key])
        held = None
        sources = [k for k in sorted(set(kinds) - {None}) if k]
        found = [buffers[phase, t - DEPTH] if k == 1 else crossed[k - 2] for k in sources]
        if 0 in kinds:
            held = own_chunk([i if k == 0 else None for i, k in zip(sent, kinds)])
        for kind, buffer in zip(sources, found):
            if held is not None:
                mask = lookup([None if v is None else int(v == kind) for v in kinds], device)
                buffer = jnp.where(mask == 1, buffer, held)
            held = buffer
        buffers[phase, t] = lax.ppermute(after(held), both, pairs)

    def cross(crossing):
        held = own_chunk([crossing[rc][1] if rc in crossing else None for rc in devices])
        pairs = [(number(*rc), number(*to)) for rc, (to, _) in crossing.items()]
        return lax.ppermute(after(held), both, pairs)

    def bring_back(t):
        pairs, phase_at = [], [None] * len(devices)
        for d, lane in enumerate(lanes):
            for r in range(rows):
                item = lane.lines[r][0].get(t)
                if item is not None and item.home is not None:
                    pairs.append((number(r, lane.col(0)), number(item.home, lane.col(0))))
                    phase_at[pairs[-1][0]] = (r + d) % 2
        if not pairs:
            return None
        phases = sorted(set(phase_at) - {None})
        held = buffers[phases[0], t]
        if len(phases) > 1:
            held = jnp.where(lookup(phase_at, device) == 1, buffers[1, t], held)
        return lax.ppermute(held, both, pairs)

    factor = weight / jnp.sqrt(2.0 * freq * (1.0 - freq))
    twice = 2.0 * freq
    male_scale = np.float32(np.sqrt(0.5))
    male_rows = jnp.where(sex_rows > 0, male_scale, np.float32(1.0))[:, None]
    male_cols = jnp.where(sex_cols > 0, male_scale, np.float32(1.0))[None, :]

    def in_window(value):
        span = STEPS * group_size
        return lax.dynamic_slice(jnp.concatenate([value, value]), (row_place * group_size,), (span,))

    def own_squares(x):
        here = lambda value: lax.dynamic_slice(value, (col_place * local_vars,), (local_vars,))[None, :]
        zx = ((x.astype(jnp.float32) - here(twice)) * here(factor) * male_rows).astype(jnp.bfloat16)
        return jnp.sum(jnp.square(zx.astype(jnp.float32)), axis=1)

    def piece_product(piece, zy, before):
        found = []
        for r, c in devices:
            keys = []
            for s in range(STEPS):
                key = -1 - (r + s) % rows % groups_here
                for d, lane in enumerate(lanes):
                    arrival = lane.arrival(r, c, (piece, s))
                    if arrival is not None:
                        t, returned = arrival
                        key = ("back" if returned else (r + d) % 2, t)
                keys.append(key)
            found.append(keys)
        used = sorted({k for keys in found for k in keys if isinstance(k, tuple)}, key=lambda k: (k[1], str(k[0])))
        places = [[k if isinstance(k, int) else used.index(k) for k in keys] for keys in found]
        places = np.asarray(places, np.int32)
        candidates = [sorted({max(int(k), -1) for k in places[:, s]}) for s in range(STEPS)]
        places = lax.dynamic_slice(jnp.asarray(places), (device, 0), (1, STEPS))[0]
        held = [buffers[key] for key in used]
        window_factor, window_twice = in_window(factor)[None, :], in_window(twice)[None, :]
        return product(piece, places, candidates, x, after(*held), window_factor, window_twice, male_rows, zy, before)

    later = []

    def join_later(place, put, value):
        later.append((place, put, value))

    def join(place):
        for entry in [e for e in later if e[0] <= place]:
            later.remove(entry)
            _, put, value = entry
            put(after(value))

    window = [y]
    back = [(i, (i - 1) % rows) for i in range(rows)]
    squares = [None]
    bits = [1 << k for k in range(cols.bit_length() - 1)] if cols & (cols - 1) == 0 else []

    def start_window(place):
        if len(window) < STEPS:

            def put(value):
                window.append(value)
                start_window(place + 3)

            join_later(place + 3, put, lax.ppermute(after(window[-1]), "row", back))

    def start_cross(place, todo):
        if todo:

            def put(value):
                crossed[len(crossed)] = value
                start_cross(place + 2, todo[1:])

            join_later(place + 2, put, cross(todo[0]))

    def start_sum(place):
        if bits:
            bit = bits.pop(0)

            def put(value):
                squares[0] = squares[0] + value
                start_sum(place + 3)

            join_later(place + 3, put, lax.ppermute(squares[0], "col", [(i, i ^ bit) for i in range(cols)]))

    def landed(phase, t, place):
        if (phase, t) in buffers:
            buffers[phase, t] = after(buffers[phase, t])
        returned = bring_back(t) if phase == 1 else None
        if returned is not None:
            join_later(place + 2, lambda value: buffers.__setitem__(("back", t), value), returned)

    sends = [(phase, t) for t in range(1, rounds + 1) for phase in range(2)]
    relation = zy = None
    done = 0
    last = {}
    for piece in range(PIECES):
        last[piece] = 0
        for d, lane in enumerate(lanes):
            for r, c in devices:
                for s in range(STEPS):
                    arrival = lane.arrival(r, c, (piece, s))
                    if arrival is not None:
                        t, returned = arrival
                        place = sends.index((1 if returned else (r + d) % 2, t)) + FLIGHT + (2 if returned else 0)
                        last[piece] = max(last[piece], place)
    for place, (phase, t) in enumerate(sends):
        if place >= FLIGHT:
            landed(*sends[place - FLIGHT], place)
        join(place)
        send(phase, t)
        if place == 1:
            start_cross(place, crossings)
            start_window(place)
        if place == 2:
            squares[0] = after(own_squares(chain[0]))
        if place == 7:
            start_sum(place)
        if len(window) == STEPS and zy is None:
            zy = standardized_window(after(*window), in_window(factor)[:, None], in_window(twice)[:, None], male_cols)
            zy = after(zy)
        while zy is not None and done < PIECES - 1 and last[done] <= place:
            relation = after(piece_product(done, zy, relation))
            done += 1
    for place in range(len(sends), len(sends) + FLIGHT):
        landed(*sends[place - FLIGHT], place)
        join(place)
    while later:
        join(max(place for place, _, _ in later))
    if not cols & (cols - 1) == 0:
        squares[0] = lax.psum(squares[0], "col")
    inbreeding = squares[0] / jnp.float32(freq.shape[0]) - 1.0
    if zy is None:
        zy = standardized_window(window, in_window(factor)[:, None], in_window(twice)[:, None], male_cols)
    for piece in range(done, PIECES):
        relation = piece_product(piece, zy, relation)
    return relation, inbreeding


def solution(mesh):
    rows, cols = mesh.shape["row"], mesh.shape["col"]
    return jax.shard_map(
        functools.partial(local, rows, cols),
        mesh=mesh,
        in_specs=(P("row", "col"), P("row", "col"), P(), P(), P("row"), P("col")),
        out_specs=(P("row", "col"), P("row")),
        check_vma=False,
    )
```

```python
import functools

import jax
import jax.numpy as jnp
import numpy as np
from jax import lax
from jax.experimental import pallas as pl
from jax.experimental.pallas import tpu as pltpu
from jax.sharding import PartitionSpec as P

STEPS = 4
PIECES = 4
PARTS = ((0, 2), (2, 3), (3, 4))
CHAINS = 2
COL_TILE = 512
ROW_TILE = 32
LANES = 128
VMEM_LIMIT = 40 * 2**20
RELAY_LIMIT = 60 * 2**20


class Line:
    def __init__(self, chunks):
        self.slots = {}
        todo = sorted(chunks)
        slot = 1
        while todo:
            for chunk in todo:
                if chunk[1] <= slot:
                    self.slots[slot] = chunk
                    todo.remove(chunk)
                    break
            slot += 1

    def sent(self, p, t):
        chunk = self.slots.get(t + p - 1) if p > 0 else None
        return chunk if chunk is not None and chunk[1] >= p else None


class Plan:
    def __init__(self, rows, cols, groups_here):
        self.rows, self.cols = rows, cols
        self.lines = {}
        for phase in range(2):
            for r in range(rows):
                place = [self.position(phase, r, (r + s) % rows // groups_here) for s in range(STEPS)]
                order = sorted((q, place[s], s) for q in range(PIECES) for s in range(STEPS) if place[s] > 0)
                for chain in range(CHAINS):
                    self.lines[phase, chain, r] = Line(order[chain::CHAINS])
        self.rounds = max(max(line.slots, default=0) for line in self.lines.values())

    def position(self, phase, r, c):
        return c if (r + phase) % 2 == 0 else self.cols - 1 - c

    def sent(self, phase, chain, r, c, t):
        return self.lines[phase, chain, r].sent(self.position(phase, r, c), t)

    def pairs(self, phase, chain, t):
        found = []
        for r in range(self.rows):
            for c in range(self.cols):
                if self.sent(phase, chain, r, c, t) is not None:
                    to = self.position(phase, r, self.position(phase, r, c) - 1)
                    found.append((r * self.cols + c, r * self.cols + to))
        return found

    def arrival(self, r, c, q, s):
        for (phase, chain, row), line in self.lines.items():
            if row == r:
                p = self.position(phase, r, c)
                for slot, chunk in line.slots.items():
                    if (chunk[0], chunk[2]) == (q, s) and chunk[1] > p:
                        return phase, chain, slot - p
        return None


def lookup(values, device):
    known = [v for v in values if v is not None]
    if len(set(known)) <= 1:
        return known[0] if known else 0
    values = [known[0] if v is None else v for v in values]
    result = jnp.uint32(0)
    place = (device % 32).astype(jnp.uint32)
    for bit in range(max(values).bit_length()):
        ones = [v >> bit & 1 for v in values]
        words = [sum(b << i for i, b in enumerate(ones[at : at + 32])) for at in range(0, len(ones), 32)]
        word = jnp.uint32(words[0])
        for i, other in enumerate(words[1:], 1):
            word = jnp.where(device // 32 == i, jnp.uint32(other), word)
        result = result | (((word >> place) & jnp.uint32(1)) << jnp.uint32(bit))
    return result.astype(jnp.int32)


def relay_kernel(at, table, x, held, out, sem):
    rows, width = out.shape

    @pl.when(table[at] == 1)
    def _():
        row = pl.multiple_of(table[at + 1] * rows, rows)
        col = pl.multiple_of(table[at + 2] * width, width)
        copy = pltpu.make_async_copy(x.at[pl.ds(row, rows), pl.ds(col, width)], out, sem)
        copy.start()
        copy.wait()


def relay(at, table, x, held):
    return pl.pallas_call(
        functools.partial(relay_kernel, at),
        out_shape=jax.ShapeDtypeStruct(held.shape, held.dtype),
        grid_spec=pltpu.PrefetchScalarGridSpec(
            num_scalar_prefetch=1,
            grid=(1,),
            in_specs=[pl.BlockSpec(memory_space=pl.ANY)] * 2,
            out_specs=pl.BlockSpec(memory_space=pl.ANY),
            scratch_shapes=[pltpu.SemaphoreType.DMA],
        ),
        input_output_aliases={2: 0},
        compiler_params=pltpu.CompilerParams(vmem_limit_bytes=RELAY_LIMIT),
        cost_estimate=pl.CostEstimate(flops=0, bytes_accessed=0, transcendentals=0),
        name="relay",
    )(table, x, held)


def window_kernel(*refs):
    blocks = refs[:STEPS]
    factor, twice, male, out = refs[STEPS:]
    group_size, width = blocks[0].shape
    for s, block in enumerate(blocks):

        @pl.loop(0, group_size // ROW_TILE)
        def _(i, s=s, block=block):
            here = pl.ds(pl.multiple_of(i * ROW_TILE, ROW_TILE), ROW_TILE)
            rows = pl.ds(pl.multiple_of(s * group_size + i * ROW_TILE, ROW_TILE), ROW_TILE)
            for k in range(0, width, LANES):
                value = block[here, k : k + LANES].astype(jnp.float32) - twice[rows, :]
                out[rows, k : k + LANES] = (value * factor[rows, :] * male[:, k : k + LANES]).astype(out.dtype)


def standardized_window(blocks, factor, twice, male):
    group_size, n = blocks[0].shape
    depth = STEPS * group_size
    column = lambda j: (0, 0)
    return pl.pallas_call(
        window_kernel,
        out_shape=jax.ShapeDtypeStruct((depth, n), jnp.bfloat16),
        grid=(n // COL_TILE,),
        in_specs=[pl.BlockSpec((group_size, COL_TILE), lambda j: (0, j))] * STEPS
        + [pl.BlockSpec((depth, LANES), column)] * 2
        + [pl.BlockSpec((1, COL_TILE), lambda j: (0, j))],
        out_specs=pl.BlockSpec((depth, COL_TILE), lambda j: (0, j)),
        compiler_params=pltpu.CompilerParams(vmem_limit_bytes=VMEM_LIMIT),
        cost_estimate=pl.CostEstimate(flops=4 * depth * n, bytes_accessed=4 * depth * n, transcendentals=0),
        name="window",
    )(*blocks, factor, twice, male)


def product_kernel(first, candidates, scale, n_buffers, places, *refs):
    x, buffers = refs[0], refs[1 : 1 + n_buffers]
    factor, twice, male, zy = refs[1 + n_buffers : 5 + n_buffers]
    out, raw, zx, sems = refs[-4:]
    width = raw.shape[1] // STEPS
    piece_rows = buffers[0].shape[0]
    pieces = raw.shape[0] // piece_rows

    @pl.when(pl.program_id(0) == 0)
    def _():
        for q in range(pieces):
            for s in range(STEPS):
                place = places[q * STEPS + s]
                target = raw.at[pl.ds(q * piece_rows, piece_rows), pl.ds(s * width, width)]
                for number in candidates[q * STEPS + s]:
                    if number >= 0:

                        @pl.when(place == number)
                        def _(number=number, target=target, q=q):
                            pltpu.make_async_copy(buffers[number], target, sems.at[q]).start()

                    else:

                        @pl.when(place < 0)
                        def _(place=place, target=target, q=q):
                            col = pl.multiple_of((-1 - place) * width, width)
                            block = x.at[pl.ds((first + q) * piece_rows, piece_rows), pl.ds(col, width)]
                            pltpu.make_async_copy(block, target, sems.at[q]).start()

        for q in range(pieces):
            part = raw.at[pl.ds(q * piece_rows, piece_rows), :]
            pltpu.make_async_copy(part, part, sems.at[q]).wait()

            @pl.loop(0, piece_rows // ROW_TILE)
            def _(i, q=q):
                rows = pl.ds(pl.multiple_of(q * piece_rows + i * ROW_TILE, ROW_TILE), ROW_TILE)
                for k in range(0, raw.shape[1], LANES):
                    lanes = slice(k, k + LANES)
                    value = raw[rows, lanes].astype(jnp.float32) - twice[:, lanes]
                    zx[rows, lanes] = (value * factor[:, lanes] * male[rows, :]).astype(zx.dtype)

    total = jnp.dot(zx[...], zy[...], preferred_element_type=jnp.float32)
    out[...] = (total * scale).astype(out.dtype)


def product(part, places, candidates, x, buffers, factor, twice, male, zy, before):
    rows, (depth, n) = x.shape[0], zy.shape
    first, stop = part
    part_rows = rows // PIECES * (stop - first)
    number = first // (stop - first)
    scale = float(1.0 / np.sqrt(np.float32(depth)))
    whole = lambda j, places: (0, 0)
    specs = [pl.BlockSpec(memory_space=pl.ANY)] * (1 + len(buffers)) + [
        pl.BlockSpec((1, depth), whole),
        pl.BlockSpec((1, depth), whole),
        pl.BlockSpec((part_rows, LANES), lambda j, places: (number, 0)),
        pl.BlockSpec((depth, COL_TILE), lambda j, places: (0, j)),
    ]
    args = [places, x, *buffers, factor, twice, male, zy]
    aliases = {}
    if before is not None:
        aliases = {len(args): 0}
        specs.append(pl.BlockSpec(memory_space=pl.ANY))
        args.append(before)
    return pl.pallas_call(
        functools.partial(product_kernel, first, candidates, scale, len(buffers)),
        out_shape=jax.ShapeDtypeStruct((rows, n), jnp.bfloat16),
        grid_spec=pltpu.PrefetchScalarGridSpec(
            num_scalar_prefetch=1,
            grid=(n // COL_TILE,),
            in_specs=specs,
            out_specs=pl.BlockSpec((part_rows, COL_TILE), lambda j, places: (number, j)),
            scratch_shapes=[
                pltpu.VMEM((part_rows, depth), jnp.bfloat16),
                pltpu.VMEM((part_rows, depth), jnp.bfloat16),
                pltpu.SemaphoreType.DMA((stop - first,)),
            ],
        ),
        input_output_aliases=aliases,
        compiler_params=pltpu.CompilerParams(vmem_limit_bytes=VMEM_LIMIT),
        cost_estimate=pl.CostEstimate(
            flops=2 * part_rows * depth * n,
            bytes_accessed=2 * (part_rows * depth + depth * n + part_rows * n),
            transcendentals=0,
        ),
        name="product",
    )(*args)


def local(rows, cols, x, y, freq, weight, sex_rows, sex_cols):
    group_size = y.shape[0]
    local_vars = x.shape[1]
    groups_here = local_vars // group_size
    piece_rows = x.shape[0] // PIECES
    plan = Plan(rows, cols, groups_here)
    devices = [(r, c) for r in range(rows) for c in range(cols)]

    row_place = lax.axis_index("row")
    col_place = lax.axis_index("col")
    device = row_place * cols + col_place

    sends = [(phase, chain, t) for t in range(1, plan.rounds + 1) for chain in range(CHAINS) for phase in range(2)]
    own_of = {}
    for key in sends:
        own_of[key] = []
        for r, c in devices:
            chunk = plan.sent(*key[:2], r, c, key[2])
            mine = chunk is not None and chunk[1] == plan.position(key[0], r, c)
            own_of[key].append((chunk[0], (r + chunk[2]) % rows % groups_here) if mine else None)
    numbers = [[n for key in sends for n in ((1, *own_of[key][i]) if own_of[key][i] else (0, 0, 0))] for i in range(len(devices))]
    table = lax.dynamic_slice(jnp.asarray(numbers, jnp.int32), (device, 0), (1, 3 * len(sends)))[0]

    latest = [x]

    def after(*values):
        *values, latest[0] = lax.optimization_barrier((*values, latest[0]))
        return values[0] if len(values) == 1 else values

    buffers = {}

    def send(key):
        phase, chain, t = key
        pairs = plan.pairs(*key)
        if not pairs:
            return
        own = own_of[key]
        held = buffers.get((phase, chain, t - 1))
        if held is None:
            piece = lookup([None if o is None else o[0] for o in own], device)
            group = lookup([None if o is None else o[1] for o in own], device)
            start = (piece * piece_rows, group * group_size)
            held = after(lax.dynamic_slice(latest[0], start, (piece_rows, group_size)))
        elif any(own):
            held = buffers[phase, chain, t - 1] = relay(3 * sends.index(key), table, x, held)
        buffers[key] = lax.ppermute(beside(key, held), ("row", "col"), pairs)

    factor = weight / jnp.sqrt(2.0 * freq * (1.0 - freq))
    twice = 2.0 * freq
    male_scale = np.float32(np.sqrt(0.5))
    male_rows = jnp.where(sex_rows > 0, male_scale, np.float32(1.0))
    male_cols = jnp.where(sex_cols > 0, male_scale, np.float32(1.0))
    wide = lambda value: jnp.broadcast_to(value[:, None], (value.shape[0], LANES))

    def in_window(value):
        span = STEPS * group_size
        return lax.dynamic_slice(jnp.concatenate([value, value]), (row_place * group_size,), (span,))

    window_factor, window_twice = in_window(factor), in_window(twice)
    male_wide = wide(male_rows)

    def own_squares(x):
        here = lambda value: lax.dynamic_slice(value, (col_place * local_vars,), (local_vars,))[None, :]
        zx = ((x.astype(jnp.float32) - here(twice)) * here(factor) * male_rows[:, None]).astype(jnp.bfloat16)
        return jnp.sum(jnp.square(zx.astype(jnp.float32)), axis=1)

    def part_product(part, zy, before):
        found = []
        for r, c in devices:
            keys = []
            for q in range(*part):
                for s in range(STEPS):
                    arrival = plan.arrival(r, c, q, s)
                    keys.append(-1 - (r + s) % rows % groups_here if arrival is None else arrival)
            found.append(keys)
        used = sorted({k for keys in found for k in keys if isinstance(k, tuple)}, key=lambda k: (k[2], k[1], k[0]))
        places = [[k if isinstance(k, int) else used.index(k) for k in keys] for keys in found]
        places = np.asarray(places, np.int32)
        candidates = [sorted({max(int(k), -1) for k in places[:, i]}) for i in range(places.shape[1])]
        places = lax.dynamic_slice(jnp.asarray(places), (device, 0), (1, places.shape[1]))[0]
        held = [buffers[key] for key in used]
        return product(
            part, places, candidates, x, held, window_factor[None, :], window_twice[None, :], male_wide, zy, before
        )

    back = [(i, (i - 1) % rows) for i in range(rows)]
    window = [y]
    moving = [lax.ppermute(y, "row", back)]
    squares = own_squares(x)
    bits = [1 << k for k in range(cols.bit_length() - 1)] if cols & (cols - 1) == 0 else []
    relation = None

    def beside(key, held):
        phase, chain, t = key
        if phase == chain == 0 and t in (3, 5, 7) and len(window) < STEPS:
            held, block = lax.optimization_barrier((held, moving[0]))
            window.append(block)
            if len(window) < STEPS:
                moving[0] = lax.ppermute(block, "row", back)
        return held

    for key in sends:
        send(key)
    if cols & (cols - 1):
        squares = lax.psum(squares, "col")
    for bit in bits:
        squares = squares + lax.ppermute(squares, "col", [(i, i ^ bit) for i in range(cols)])
    inbreeding = squares / jnp.float32(freq.shape[0]) - 1.0
    while len(window) < STEPS:
        window.append(moving[0])
        if len(window) < STEPS:
            moving[0] = lax.ppermute(window[-1], "row", back)
    zy = standardized_window(window, wide(window_factor), wide(window_twice), male_cols[None, :])
    for part in PARTS:
        relation = part_product(part, zy, relation)
    return relation, inbreeding


def solution(mesh):
    rows, cols = mesh.shape["row"], mesh.shape["col"]
    return jax.shard_map(
        functools.partial(local, rows, cols),
        mesh=mesh,
        in_specs=(P("row", "col"), P("row", "col"), P(), P(), P("row"), P("col")),
        out_specs=(P("row", "col"), P("row")),
        check_vma=False,
    )
```

```python
import functools

import jax
import jax.numpy as jnp
import numpy as np
from jax import lax
from jax.experimental import pallas as pl
from jax.experimental.pallas import tpu as pltpu
from jax.sharding import PartitionSpec as P

STEPS = 4
PIECES = 4
PARTS = ((0, 2), (2, 3), (3, 4))
CHAINS = 2
COL_TILE = 512
ROW_TILE = 32
LANES = 128
VMEM_LIMIT = 20 * 2**20
RELAY_LIMIT = 8 * 2**20


class Line:
    def __init__(self, chunks):
        self.slots = {}
        todo = sorted(chunks)
        slot = 1
        while todo:
            for chunk in todo:
                if chunk[1] <= slot:
                    self.slots[slot] = chunk
                    todo.remove(chunk)
                    break
            slot += 1

    def sent(self, p, t):
        chunk = self.slots.get(t + p - 1) if p > 0 else None
        return chunk if chunk is not None and chunk[1] >= p else None


class Plan:
    def __init__(self, rows, cols, groups_here):
        self.rows, self.cols = rows, cols
        self.lines = {}
        for phase in range(2):
            for r in range(rows):
                place = [self.position(phase, r, (r + s) % rows // groups_here) for s in range(STEPS)]
                order = sorted((q, place[s], s) for q in range(PIECES) for s in range(STEPS) if place[s] > 0)
                for chain in range(CHAINS):
                    self.lines[phase, chain, r] = Line(order[chain::CHAINS])
        self.rounds = max(max(line.slots, default=0) for line in self.lines.values())

    def position(self, phase, r, c):
        return c if (r + phase) % 2 == 0 else self.cols - 1 - c

    def sent(self, phase, chain, r, c, t):
        return self.lines[phase, chain, r].sent(self.position(phase, r, c), t)

    def pairs(self, phase, chain, t):
        found = []
        for r in range(self.rows):
            for c in range(self.cols):
                if self.sent(phase, chain, r, c, t) is not None:
                    to = self.position(phase, r, self.position(phase, r, c) - 1)
                    found.append((r * self.cols + c, r * self.cols + to))
        return found

    def arrival(self, r, c, q, s):
        for (phase, chain, row), line in self.lines.items():
            if row == r:
                p = self.position(phase, r, c)
                for slot, chunk in line.slots.items():
                    if (chunk[0], chunk[2]) == (q, s) and chunk[1] > p:
                        return phase, chain, slot - p
        return None


def lookup(values, device):
    known = [v for v in values if v is not None]
    if len(set(known)) <= 1:
        return known[0] if known else 0
    values = [known[0] if v is None else v for v in values]
    result = jnp.uint32(0)
    place = (device % 32).astype(jnp.uint32)
    for bit in range(max(values).bit_length()):
        ones = [v >> bit & 1 for v in values]
        words = [sum(b << i for i, b in enumerate(ones[at : at + 32])) for at in range(0, len(ones), 32)]
        word = jnp.uint32(words[0])
        for i, other in enumerate(words[1:], 1):
            word = jnp.where(device // 32 == i, jnp.uint32(other), word)
        result = result | (((word >> place) & jnp.uint32(1)) << jnp.uint32(bit))
    return result.astype(jnp.int32)


def relay_kernel(at, table, x, held, out):
    rows, width = out.shape

    @pl.when(table[at] == 1)
    def _():
        row = pl.multiple_of(table[at + 1] * rows, rows)
        col = pl.multiple_of(table[at + 2] * width, width)
        out[...] = x[pl.ds(row, rows), pl.ds(col, width)]

    @pl.when(table[at] == 0)
    def _():
        out[...] = held[...]


def relay(at, table, x, held):
    return pl.pallas_call(
        functools.partial(relay_kernel, at),
        out_shape=jax.ShapeDtypeStruct(held.shape, held.dtype),
        in_specs=[pl.BlockSpec(memory_space=pltpu.SMEM)] + [pl.BlockSpec(memory_space=pltpu.VMEM)] * 2,
        out_specs=pl.BlockSpec(memory_space=pltpu.VMEM),
        input_output_aliases={2: 0},
        compiler_params=pltpu.CompilerParams(vmem_limit_bytes=RELAY_LIMIT),
        cost_estimate=pl.CostEstimate(flops=0, bytes_accessed=0, transcendentals=0),
        name="relay",
    )(table, in_vmem(x), in_vmem(held))


def in_vmem(value):
    return pltpu.with_memory_space_constraint(value, pltpu.VMEM)


VMEM = pl.BlockSpec(memory_space=pltpu.VMEM)


def window_kernel(*refs):
    blocks = refs[:STEPS]
    factor, twice, male, out = refs[STEPS:]
    group_size, width = blocks[0].shape
    for s, block in enumerate(blocks):

        @pl.loop(0, group_size // ROW_TILE)
        def _(i, s=s, block=block):
            here = pl.ds(pl.multiple_of(i * ROW_TILE, ROW_TILE), ROW_TILE)
            rows = pl.ds(pl.multiple_of(s * group_size + i * ROW_TILE, ROW_TILE), ROW_TILE)
            for k in range(0, width, LANES):
                value = block[here, k : k + LANES].astype(jnp.float32) - twice[rows, :]
                out[rows, k : k + LANES] = (value * factor[rows, :] * male[:, k : k + LANES]).astype(out.dtype)


def standardized_window(blocks, factor, twice, male):
    group_size, n = blocks[0].shape
    depth = STEPS * group_size
    return pl.pallas_call(
        window_kernel,
        out_shape=pltpu.VMEM((depth, n), jnp.bfloat16),
        in_specs=[VMEM] * (STEPS + 3),
        out_specs=VMEM,
        compiler_params=pltpu.CompilerParams(vmem_limit_bytes=VMEM_LIMIT),
        cost_estimate=pl.CostEstimate(flops=4 * depth * n, bytes_accessed=4 * depth * n, transcendentals=0),
        name="window",
    )(*[in_vmem(v) for v in (*blocks, factor, twice, male)])


def product_kernel(part, candidates, scale, n_buffers, places, x, *refs):
    buffers = refs[:n_buffers]
    factor, twice, male, zy = refs[n_buffers : n_buffers + 4]
    out, zx, tiles, sems = refs[-4:]
    piece_rows, width = buffers[0].shape
    first, stop = part

    def standardize(source, row, col, q, s):
        @pl.loop(0, piece_rows // ROW_TILE)
        def _(i):
            at = i * ROW_TILE
            here = pl.ds(pl.multiple_of(row + at, ROW_TILE), ROW_TILE)
            rows = pl.ds(pl.multiple_of((q - first) * piece_rows + at, ROW_TILE), ROW_TILE)
            sexes = male[pl.ds(pl.multiple_of(q * piece_rows + at, ROW_TILE), ROW_TILE), :]
            for k in range(0, width, LANES):
                lanes = slice(s * width + k, s * width + k + LANES)
                value = source[here, pl.ds(pl.multiple_of(col + k, LANES), LANES)].astype(jnp.float32)
                zx[rows, lanes] = ((value - twice[:, lanes]) * factor[:, lanes] * sexes).astype(zx.dtype)

    for q in range(first, stop):
        for s in range(STEPS):
            place = places[(q - first) * STEPS + s]
            for number in candidates[(q - first) * STEPS + s]:
                if number >= 0:

                    @pl.when(place == number)
                    def _(number=number, q=q, s=s):
                        standardize(buffers[number], 0, 0, q, s)

                else:

                    @pl.when(place < 0)
                    def _(place=place, q=q, s=s):
                        standardize(x, q * piece_rows, (-1 - place) * width, q, s)

    def copy(j):
        where = out.at[pl.ds(first * piece_rows, zx.shape[0]), pl.ds(j * COL_TILE, COL_TILE)]
        return pltpu.make_async_copy(tiles.at[j % 2], where, sems.at[j % 2])

    count = zy.shape[1] // COL_TILE
    for j in range(count):
        if j >= 2:
            copy(j - 2).wait()
        total = jnp.dot(zx[...], zy[:, j * COL_TILE : (j + 1) * COL_TILE], preferred_element_type=jnp.float32)
        tiles[j % 2] = (total * scale).astype(tiles.dtype)
        copy(j).start()
    for j in range(max(count - 2, 0), count):
        copy(j).wait()


def product(part, places, candidates, x, buffers, factor, twice, male, zy, before):
    rows, (depth, n) = x.shape[0], zy.shape
    part_rows = rows // PIECES * (part[1] - part[0])
    scale = float(1.0 / np.sqrt(np.float32(depth)))
    args = [places, *[in_vmem(v) for v in (x, *buffers, factor, twice, male, zy)]]
    specs = [pl.BlockSpec(memory_space=pltpu.SMEM)] + [VMEM] * (len(args) - 1)
    aliases = {}
    kernel = functools.partial(product_kernel, part, candidates, scale, len(buffers))
    if before is not None:
        aliases = {len(args): 0}
        specs.append(pl.BlockSpec(memory_space=pl.ANY))
        args.append(before)
    return pl.pallas_call(
        kernel,
        out_shape=jax.ShapeDtypeStruct((rows, n), jnp.bfloat16),
        in_specs=specs,
        out_specs=pl.BlockSpec(memory_space=pl.ANY),
        scratch_shapes=[
            pltpu.VMEM((part_rows, depth), jnp.bfloat16),
            pltpu.VMEM((2, part_rows, COL_TILE), jnp.bfloat16),
            pltpu.SemaphoreType.DMA((2,)),
        ],
        input_output_aliases=aliases,
        compiler_params=pltpu.CompilerParams(vmem_limit_bytes=VMEM_LIMIT),
        cost_estimate=pl.CostEstimate(
            flops=2 * part_rows * depth * n,
            bytes_accessed=2 * part_rows * n,
            transcendentals=0,
        ),
        name="product",
    )(*args)


def local(rows, cols, x, y, freq, weight, sex_rows, sex_cols):
    group_size = y.shape[0]
    local_vars = x.shape[1]
    groups_here = local_vars // group_size
    piece_rows = x.shape[0] // PIECES
    plan = Plan(rows, cols, groups_here)
    devices = [(r, c) for r in range(rows) for c in range(cols)]

    row_place = lax.axis_index("row")
    col_place = lax.axis_index("col")
    device = row_place * cols + col_place

    sends = [(phase, chain, t) for t in range(1, plan.rounds + 1) for chain in range(CHAINS) for phase in range(2)]
    own_of = {}
    for key in sends:
        own_of[key] = []
        for r, c in devices:
            chunk = plan.sent(*key[:2], r, c, key[2])
            mine = chunk is not None and chunk[1] == plan.position(key[0], r, c)
            own_of[key].append((chunk[0], (r + chunk[2]) % rows % groups_here) if mine else None)
    numbers = [[n for key in sends for n in ((1, *own_of[key][i]) if own_of[key][i] else (0, 0, 0))] for i in range(len(devices))]
    table = lax.dynamic_slice(jnp.asarray(numbers, jnp.int32), (device, 0), (1, 3 * len(sends)))[0]

    buffers = {}

    def first(key):
        own = own_of[key]
        piece = lookup([None if o is None else o[0] for o in own], device)
        group = lookup([None if o is None else o[1] for o in own], device)
        return lax.dynamic_slice(x, (piece * piece_rows, group * group_size), (piece_rows, group_size))

    firsts = [key for key in sends if key[2] == 1 and plan.pairs(*key)]
    starts = dict(zip(firsts, lax.optimization_barrier([first(key) for key in firsts])))

    def send(key):
        phase, chain, t = key
        pairs = plan.pairs(*key)
        if not pairs:
            return
        own = own_of[key]
        held = buffers.get((phase, chain, t - 1))
        if held is None:
            held = starts.pop(key) if key in starts else first(key)
        elif any(own):
            held = buffers[phase, chain, t - 1] = relay(3 * sends.index(key), table, x, held)
        buffers[key] = lax.ppermute(held, ("row", "col"), pairs)

    factor = weight / jnp.sqrt(2.0 * freq * (1.0 - freq))
    twice = 2.0 * freq
    male_scale = np.float32(np.sqrt(0.5))
    male_rows = jnp.where(sex_rows > 0, male_scale, np.float32(1.0))
    male_cols = jnp.where(sex_cols > 0, male_scale, np.float32(1.0))
    wide = lambda value: jnp.broadcast_to(value[:, None], (value.shape[0], LANES))

    def in_window(value):
        span = STEPS * group_size
        return lax.dynamic_slice(jnp.concatenate([value, value]), (row_place * group_size,), (span,))

    window_factor, window_twice = in_window(factor), in_window(twice)
    male_wide = wide(male_rows)

    def own_squares(x):
        here = lambda value: lax.dynamic_slice(value, (col_place * local_vars,), (local_vars,))[None, :]
        zx = ((x.astype(jnp.float32) - here(twice)) * here(factor) * male_rows[:, None]).astype(jnp.bfloat16)
        return jnp.sum(jnp.square(zx.astype(jnp.float32)), axis=1)

    def part_product(part, zy, before):
        found = []
        for r, c in devices:
            keys = []
            for q in range(*part):
                for s in range(STEPS):
                    arrival = plan.arrival(r, c, q, s)
                    keys.append(-1 - (r + s) % rows % groups_here if arrival is None else arrival)
            found.append(keys)
        used = sorted({k for keys in found for k in keys if isinstance(k, tuple)}, key=lambda k: (k[2], k[1], k[0]))
        places = [[k if isinstance(k, int) else used.index(k) for k in keys] for keys in found]
        places = np.asarray(places, np.int32)
        candidates = [sorted({max(int(k), -1) for k in places[:, i]}) for i in range(places.shape[1])]
        places = lax.dynamic_slice(jnp.asarray(places), (device, 0), (1, places.shape[1]))[0]
        held = [buffers[key] for key in used]
        return product(
            part, places, candidates, x, held, window_factor[None, :], window_twice[None, :], male_wide, zy, before
        )

    back = [(i, (i - 1) % rows) for i in range(rows)]
    window = [y]
    moving = [lax.ppermute(y, "row", back)]
    squares = own_squares(x)
    bits = [1 << k for k in range(cols.bit_length() - 1)] if cols & (cols - 1) == 0 else []
    relation = None

    for key in sends:
        send(key)
    while len(window) < STEPS:
        window.append(moving[0])
        if len(window) < STEPS:
            moving[0] = lax.ppermute(window[-1], "row", back)
    zy = standardized_window(window, wide(window_factor), wide(window_twice), male_cols[None, :])
    if cols & (cols - 1):
        squares = lax.psum(squares, "col")
    for part in PARTS:
        relation = part_product(part, zy, relation)
        if bits:
            bit = bits.pop(0)
            other = lax.ppermute(squares, "col", [(i, i ^ bit) for i in range(cols)])
            relation, other = lax.optimization_barrier((relation, other))
            squares = squares + other
    for bit in bits:
        squares = squares + lax.ppermute(squares, "col", [(i, i ^ bit) for i in range(cols)])
    inbreeding = squares / jnp.float32(freq.shape[0]) - 1.0
    return relation, inbreeding


def solution(mesh):
    rows, cols = mesh.shape["row"], mesh.shape["col"]
    return jax.shard_map(
        functools.partial(local, rows, cols),
        mesh=mesh,
        in_specs=(P("row", "col"), P("row", "col"), P(), P(), P("row"), P("col")),
        out_specs=(P("row", "col"), P("row")),
        check_vma=False,
    )
```

```python
import functools
import itertools

import jax
import jax.numpy as jnp
import numpy as np
from jax import lax
from jax.experimental import pallas as pl
from jax.experimental.pallas import tpu as pltpu
from jax.sharding import PartitionSpec as P

STEPS = 4
PIECES = 2
PARTS = ((0, 1), (1, 2))
DEPTH = 1
HOP = 2
COL_TILE = 512
ROW_TILE = 32
LANES = 128
VMEM_LIMIT = 20 * 2**20
RELAY_LIMIT = 8 * 2**20


class Item:
    def __init__(self, row, piece, s, place, home=None):
        self.row, self.piece, self.s, self.place = row, piece, s, place
        self.home = home

    @property
    def owner(self):
        return self.row if self.home is None else self.home

    @property
    def key(self):
        return self.piece, self.s


def line_slots(items, cut):
    ends, inner = {}, {}
    todo = sorted(items, key=lambda i: (i.home is None, i.piece, i.place, i.s))
    slot = 1
    while todo:
        for item in todo:
            first = 1 + DEPTH * (item.place - 1) + (HOP if item.home is not None else 0)
            if first <= slot:
                ends[slot] = item
                if item.place > 1:
                    inner[slot] = item
                todo.remove(item)
                break
        slot += 1
    for item in sorted(cut, key=lambda i: (i.place, i.key)):
        slot = 1 + DEPTH * (item.place - 1)
        if item.place > 1:
            while slot in inner:
                slot += 1
            inner[slot] = item
    return ends, inner


class Lane:
    def __init__(self, rows, cols, groups_here, towards_zero):
        self.rows, self.cols = rows, cols
        self.towards_zero = towards_zero
        self.items = []
        for r in range(rows):
            mine = [
                Item(r, piece, s, self.place((r + s) % rows // groups_here))
                for piece in range(PIECES)
                for s in range(STEPS)
            ]
            self.items.append([i for i in mine if i.place > 0])
        self.away = []
        self.lines = [line_slots(items, []) for items in self.items]
        if rows % 2 == 0 and cols > 3:
            for r in range(rows // 2):
                self.balance(r, r + rows // 2)
                self.balance(r + rows // 2, r)
        self.rounds = max(
            [max(ends, default=0) for ends, _ in self.lines] + [max(inner, default=0) - DEPTH for _, inner in self.lines]
        )

    def place(self, c):
        return c if self.towards_zero else self.cols - 1 - c

    col = place

    def balance(self, r, other):
        if len(self.items[r]) < len(self.items[other]) or any(i.row == other for i in self.away):
            return
        places = sorted({i.place for i in self.items[r]})
        best = None
        for counts in itertools.product(range(3), repeat=len(places)):
            gone = []
            for place, count in zip(places, counts):
                here = [i for i in self.items[r] if i.place == place]
                here.sort(key=lambda i: i.key, reverse=True)
                gone += here[:count]
            visitors = [Item(other, i.piece, i.s, i.place, home=r) for i in gone]
            mine = line_slots([i for i in self.items[r] if i not in gone], gone)
            theirs = line_slots(self.items[other] + visitors, [])
            score = (
                max(max(mine[0], default=0), max(theirs[0], default=0)),
                abs(len(mine[0]) - len(theirs[0])),
                max([slot for slot, i in theirs[0].items() if i.home is not None], default=0),
                len(gone),
            )
            if best is None or score < best[0]:
                best = score, gone, mine, theirs
        _, gone, mine, theirs = best
        self.away += gone
        if gone:
            self.lines[r], self.lines[other] = mine, theirs

    def sent(self, r, c, t):
        p = self.place(c)
        ends, inner = self.lines[r]
        if p == 0:
            return None
        item = ends.get(t) if p == 1 else inner.get(t + DEPTH * (p - 1))
        return item if item is not None and item.place >= p else None

    def pairs(self, t):
        found = []
        for r in range(self.rows):
            for c in range(self.cols):
                if self.sent(r, c, t) is not None:
                    found.append((r * self.cols + c, r * self.cols + self.col(self.place(c) - 1)))
        return found

    def arrival(self, r, c, key):
        p = self.place(c)
        for i in self.items[r]:
            if i.key != key or i.place <= p:
                continue
            ends, inner = self.lines[r]
            if p == 0 and i in self.away:
                for other, _ in self.lines:
                    for slot, v in other.items():
                        if v.home == r and v.key == key:
                            return slot, True
            for slot, v in (ends if p == 0 else inner).items():
                if v is i:
                    return slot - DEPTH * p, False
        return None


def lookup(values, device):
    known = [v for v in values if v is not None]
    if len(set(known)) <= 1:
        return known[0] if known else 0
    values = [known[0] if v is None else v for v in values]
    result = jnp.uint32(0)
    place = (device % 32).astype(jnp.uint32)
    for bit in range(max(values).bit_length()):
        ones = [v >> bit & 1 for v in values]
        words = [sum(b << i for i, b in enumerate(ones[at : at + 32])) for at in range(0, len(ones), 32)]
        word = jnp.uint32(words[0])
        for i, other in enumerate(words[1:], 1):
            word = jnp.where(device // 32 == i, jnp.uint32(other), word)
        result = result | (((word >> place) & jnp.uint32(1)) << jnp.uint32(bit))
    return result.astype(jnp.int32)


def relay_kernel(at, table, x, *refs):
    *sources, out = refs
    rows, width = out.shape

    @pl.when(table[at] == 0)
    def _():
        row = pl.multiple_of(table[at + 1] * rows, rows)
        col = pl.multiple_of(table[at + 2] * width, width)
        out[...] = x[pl.ds(row, rows), pl.ds(col, width)]

    for i, source in enumerate(sources):

        @pl.when(table[at] == i + 1)
        def _(source=source):
            out[...] = source[...]


def relay(at, table, x, sources):
    return pl.pallas_call(
        functools.partial(relay_kernel, at),
        out_shape=pltpu.VMEM(sources[0].shape, sources[0].dtype),
        in_specs=[pl.BlockSpec(memory_space=pltpu.SMEM)] + [VMEM] * (1 + len(sources)),
        out_specs=VMEM,
        compiler_params=pltpu.CompilerParams(vmem_limit_bytes=RELAY_LIMIT),
        cost_estimate=pl.CostEstimate(flops=0, bytes_accessed=0, transcendentals=0),
        name="relay",
    )(table, *[in_vmem(v) for v in (x, *sources)])


def in_vmem(value):
    return pltpu.with_memory_space_constraint(value, pltpu.VMEM)


VMEM = pl.BlockSpec(memory_space=pltpu.VMEM)


def window_kernel(*refs):
    blocks = refs[:STEPS]
    factor, twice, male, out = refs[STEPS:]
    group_size, width = blocks[0].shape
    for s, block in enumerate(blocks):

        @pl.loop(0, group_size // ROW_TILE)
        def _(i, s=s, block=block):
            here = pl.ds(pl.multiple_of(i * ROW_TILE, ROW_TILE), ROW_TILE)
            rows = pl.ds(pl.multiple_of(s * group_size + i * ROW_TILE, ROW_TILE), ROW_TILE)
            for k in range(0, width, LANES):
                value = block[here, k : k + LANES].astype(jnp.float32) - twice[rows, :]
                out[rows, k : k + LANES] = (value * factor[rows, :] * male[:, k : k + LANES]).astype(out.dtype)


def standardized_window(blocks, factor, twice, male):
    group_size, n = blocks[0].shape
    depth = STEPS * group_size
    return pl.pallas_call(
        window_kernel,
        out_shape=pltpu.VMEM((depth, n), jnp.bfloat16),
        in_specs=[VMEM] * (STEPS + 3),
        out_specs=VMEM,
        compiler_params=pltpu.CompilerParams(vmem_limit_bytes=VMEM_LIMIT),
        cost_estimate=pl.CostEstimate(flops=4 * depth * n, bytes_accessed=4 * depth * n, transcendentals=0),
        name="window",
    )(*[in_vmem(v) for v in (*blocks, factor, twice, male)])


def product_kernel(part, candidates, scale, n_buffers, places, x, *refs):
    buffers = refs[:n_buffers]
    factor, twice, male, zy = refs[n_buffers : n_buffers + 4]
    out, zx, tiles, sems = refs[-4:]
    piece_rows, width = buffers[0].shape
    first, stop = part

    def standardize(source, row, col, q, s):
        @pl.loop(0, piece_rows // ROW_TILE)
        def _(i):
            at = i * ROW_TILE
            here = pl.ds(pl.multiple_of(row + at, ROW_TILE), ROW_TILE)
            rows = pl.ds(pl.multiple_of((q - first) * piece_rows + at, ROW_TILE), ROW_TILE)
            sexes = male[pl.ds(pl.multiple_of(q * piece_rows + at, ROW_TILE), ROW_TILE), :]
            for k in range(0, width, LANES):
                lanes = slice(s * width + k, s * width + k + LANES)
                value = source[here, pl.ds(pl.multiple_of(col + k, LANES), LANES)].astype(jnp.float32)
                zx[rows, lanes] = ((value - twice[:, lanes]) * factor[:, lanes] * sexes).astype(zx.dtype)

    for q in range(first, stop):
        for s in range(STEPS):
            place = places[(q - first) * STEPS + s]
            for number in candidates[(q - first) * STEPS + s]:
                if number >= 0:

                    @pl.when(place == number)
                    def _(number=number, q=q, s=s):
                        standardize(buffers[number], 0, 0, q, s)

                else:

                    @pl.when(place < 0)
                    def _(place=place, q=q, s=s):
                        standardize(x, q * piece_rows, (-1 - place) * width, q, s)

    def copy(j):
        where = out.at[pl.ds(first * piece_rows, zx.shape[0]), pl.ds(j * COL_TILE, COL_TILE)]
        return pltpu.make_async_copy(tiles.at[j % 2], where, sems.at[j % 2])

    count = zy.shape[1] // COL_TILE
    for j in range(count):
        if j >= 2:
            copy(j - 2).wait()
        total = jnp.dot(zx[...], zy[:, j * COL_TILE : (j + 1) * COL_TILE], preferred_element_type=jnp.float32)
        tiles[j % 2] = (total * scale).astype(tiles.dtype)
        copy(j).start()
    for j in range(max(count - 2, 0), count):
        copy(j).wait()


def product(part, places, candidates, x, buffers, factor, twice, male, zy, before):
    rows, (depth, n) = x.shape[0], zy.shape
    part_rows = rows // PIECES * (part[1] - part[0])
    scale = float(1.0 / np.sqrt(np.float32(depth)))
    args = [places, *[in_vmem(v) for v in (x, *buffers, factor, twice, male, zy)]]
    specs = [pl.BlockSpec(memory_space=pltpu.SMEM)] + [VMEM] * (len(args) - 1)
    aliases = {}
    kernel = functools.partial(product_kernel, part, candidates, scale, len(buffers))
    if before is not None:
        aliases = {len(args): 0}
        specs.append(pl.BlockSpec(memory_space=pl.ANY))
        args.append(before)
    return pl.pallas_call(
        kernel,
        out_shape=jax.ShapeDtypeStruct((rows, n), jnp.bfloat16),
        in_specs=specs,
        out_specs=pl.BlockSpec(memory_space=pl.ANY),
        scratch_shapes=[
            pltpu.VMEM((part_rows, depth), jnp.bfloat16),
            pltpu.VMEM((2, part_rows, COL_TILE), jnp.bfloat16),
            pltpu.SemaphoreType.DMA((2,)),
        ],
        input_output_aliases=aliases,
        compiler_params=pltpu.CompilerParams(vmem_limit_bytes=VMEM_LIMIT),
        cost_estimate=pl.CostEstimate(
            flops=2 * part_rows * depth * n,
            bytes_accessed=2 * part_rows * n,
            transcendentals=0,
        ),
        name="product",
    )(*args)


def local(rows, cols, x, y, freq, weight, sex_rows, sex_cols):
    group_size = y.shape[0]
    local_vars = x.shape[1]
    groups_here = local_vars // group_size
    piece_rows = x.shape[0] // PIECES
    lanes = [Lane(rows, cols, groups_here, towards) for towards in (True, False)]
    rounds = max(lane.rounds for lane in lanes)
    devices = [(r, c) for r in range(rows) for c in range(cols)]
    both = ("row", "col")

    row_place = lax.axis_index("row")
    col_place = lax.axis_index("col")
    device = row_place * cols + col_place

    def number(r, c):
        return r * cols + c

    def group_here(item):
        return (item.owner + item.s) % rows % groups_here

    crossings = []
    crossing_of = {}
    for d, lane in enumerate(lanes):
        for r in range(rows):
            for slot, item in sorted(lane.lines[r][0].items()):
                if item.home is None:
                    continue
                source, target = (item.home, lane.col(item.place)), (r, lane.col(item.place))
                for k, crossing in enumerate(crossings):
                    if source not in crossing and target not in [to for to, _ in crossing.values()]:
                        break
                else:
                    k = len(crossings)
                    crossings.append({})
                crossings[k][source] = (target, item)
                crossing_of[d, r, item.key] = k

    def lane_of(phase, r):
        return (r + phase) % 2

    sends = [(phase, t) for t in range(1, rounds + 1) for phase in range(2)]
    pairs_of, kinds_of, own_of = {}, {}, {}
    for phase, t in sends:
        pairs, kinds, own = [], [], []
        for r, c in devices:
            lane = lanes[lane_of(phase, r)]
            item = lane.sent(r, c, t)
            if item is not None:
                pairs.append((number(r, c), number(r, lane.col(lane.place(c) - 1))))
            if item is None:
                kinds.append(None)
            elif item.place != lane.place(c):
                kinds.append("forward")
            elif item.home is not None:
                kinds.append(crossing_of[lane_of(phase, r), r, item.key])
            else:
                kinds.append("own")
            own.append(item if kinds[-1] == "own" else None)
        pairs_of[phase, t], kinds_of[phase, t], own_of[phase, t] = pairs, kinds, own

    returns = {}
    for t in range(1, rounds + 1):
        pairs, phases = [], [None] * len(devices)
        for d, lane in enumerate(lanes):
            for r in range(rows):
                item = lane.lines[r][0].get(t)
                if item is not None and item.home is not None:
                    pairs.append((number(r, lane.col(0)), number(item.home, lane.col(0))))
                    phases[pairs[-1][0]] = (r + d) % 2
        if pairs:
            returns[t] = pairs, phases

    columns = []

    def add(entries):
        columns.append(np.asarray(entries, np.int32))
        return sum(c.shape[1] for c in columns[:-1])

    relays = {}
    for key in sends:
        kinds = kinds_of[key]
        names = sorted(set(kinds) - {None, "own"}, key=str)
        if names and (len(names) > 1 or "own" in kinds):
            entries = []
            for kind, item in zip(kinds, own_of[key]):
                if kind == "own":
                    entries.append((0, item.piece, group_here(item)))
                else:
                    entries.append((1 + names.index(kind) if kind is not None else 1, 0, 0))
            relays[key] = names, add(entries)
    for t, (pairs, phases) in returns.items():
        if len(set(phases) - {None}) > 1:
            relays["back", t] = None, add([(1 + (p or 0), 0, 0) for p in phases])
    table = np.concatenate(columns, axis=1) if columns else np.zeros((len(devices), 1), np.int32)
    table = lax.dynamic_slice(jnp.asarray(table), (device, 0), (1, table.shape[1]))[0]

    def own_chunk(items):
        piece = lookup([None if i is None else i.piece for i in items], device)
        group = lookup([None if i is None else group_here(i) for i in items], device)
        return lax.dynamic_slice(x, (piece * piece_rows, group * group_size), (piece_rows, group_size))

    firsts = {key: own_of[key] for key in sends if key[1] == 1 and any(own_of[key])}
    for k, crossing in enumerate(crossings):
        firsts["cross", k] = [crossing[rc][1] if rc in crossing else None for rc in devices]
    starts = dict(zip(firsts, lax.optimization_barrier([own_chunk(items) for items in firsts.values()])))

    factor = weight / jnp.sqrt(2.0 * freq * (1.0 - freq))
    twice = 2.0 * freq
    male_scale = np.float32(np.sqrt(0.5))
    male_rows = jnp.where(sex_rows > 0, male_scale, np.float32(1.0))
    male_cols = jnp.where(sex_cols > 0, male_scale, np.float32(1.0))
    wide = lambda value: jnp.broadcast_to(value[:, None], (value.shape[0], LANES))

    def in_window(value):
        span = STEPS * group_size
        return lax.dynamic_slice(jnp.concatenate([value, value]), (row_place * group_size,), (span,))

    window_factor, window_twice = in_window(factor), in_window(twice)
    male_wide = wide(male_rows)

    def own_squares():
        here = lambda value: lax.dynamic_slice(value, (col_place * local_vars,), (local_vars,))[None, :]
        zx = ((x.astype(jnp.float32) - here(twice)) * here(factor) * male_rows[:, None]).astype(jnp.bfloat16)
        return jnp.sum(jnp.square(zx.astype(jnp.float32)), axis=1)

    buffers = {}
    last = [0] * len(PARTS)

    def part_product(part, zy, before):
        found = []
        for r, c in devices:
            keys = []
            for q in range(*part):
                for s in range(STEPS):
                    key = -1 - (r + s) % rows % groups_here
                    for d, lane in enumerate(lanes):
                        arrival = lane.arrival(r, c, (q, s))
                        if arrival is not None:
                            t, returned = arrival
                            key = ("back" if returned else (r + d) % 2, t)
                    keys.append(key)
            found.append(keys)
        used = sorted({k for keys in found for k in keys if isinstance(k, tuple)}, key=lambda k: (k[1], str(k[0])))
        places = [[k if isinstance(k, int) else used.index(k) for k in keys] for keys in found]
        places = np.asarray(places, np.int32)
        candidates = [sorted({max(int(k), -1) for k in places[:, i]}) for i in range(places.shape[1])]
        places = lax.dynamic_slice(jnp.asarray(places), (device, 0), (1, places.shape[1]))[0]
        held = [buffers[key] for key in used]
        return product(
            part, places, candidates, x, held, window_factor[None, :], window_twice[None, :], male_wide, zy, before
        )

    for number_of_part, part in enumerate(PARTS):
        for d, lane in enumerate(lanes):
            for r, c in devices:
                for q in range(*part):
                    for s in range(STEPS):
                        arrival = lane.arrival(r, c, (q, s))
                        if arrival is not None:
                            t = arrival[0] + (2 if arrival[1] else 0)
                            last[number_of_part] = max(last[number_of_part], t)

    back = [(i, (i - 1) % rows) for i in range(rows)]
    window = [y]
    while len(window) < STEPS:
        window.append(lax.ppermute(window[-1], "row", back))
    zy = relation = None
    squares = own_squares()
    bits = [1 << k for k in range(cols.bit_length() - 1)] if cols & (cols - 1) == 0 else []
    if cols & (cols - 1):
        squares = lax.psum(squares, "col")

    def sum_beside(value, squares):
        if not bits:
            return value, squares
        bit = bits.pop(0)
        other = lax.ppermute(squares, "col", [(i, i ^ bit) for i in range(cols)])
        value, other = lax.optimization_barrier((value, other))
        return value, squares + other

    def window_product():
        return standardized_window(window, wide(window_factor), wide(window_twice), male_cols[None, :])

    crossed = {}
    done = 0
    for key in sends:
        phase, t = key
        if not pairs_of[key]:
            continue
        if key in relays:
            names, at = relays[key]
            sources = [buffers[phase, t - DEPTH] if name == "forward" else crossed[name] for name in names]
            held = relay(at, table, x, sources)
        elif key in starts:
            held = starts[key]
        elif "forward" in kinds_of[key]:
            held = buffers[phase, t - DEPTH]
        elif "own" in kinds_of[key]:
            held = own_chunk(own_of[key])
        else:
            held = crossed[next(k for k in kinds_of[key] if k is not None)]
        if phase == 1 and t == last[0]:
            zy, squares = sum_beside(window_product(), squares)
            held, zy = lax.optimization_barrier((held, zy))
        if phase == 1 and t == last[0] + 2 and zy is not None:
            relation, squares = sum_beside(part_product(PARTS[0], zy, relation), squares)
            held, relation = lax.optimization_barrier((held, relation))
            done = 1
        if phase == 1 and ("back", t - 2) in buffers:
            held, buffers["back", t - 2] = lax.optimization_barrier((held, buffers["back", t - 2]))
        buffers[key] = lax.ppermute(held, both, pairs_of[key])
        if key == (1, 1):
            for k, crossing in enumerate(crossings):
                pairs = [(number(*rc), number(*to)) for rc, (to, _) in crossing.items()]
                crossed[k] = lax.ppermute(starts["cross", k], both, pairs)
        if phase == 1 and t in returns:
            pairs, phases = returns[t]
            if ("back", t) in relays:
                held = relay(relays["back", t][1], table, x, [buffers[0, t], buffers[1, t]])
            else:
                held = buffers[next(p for p in phases if p is not None), t]
            buffers["back", t] = lax.ppermute(held, both, pairs)
    if zy is None:
        zy = window_product()
    for part in PARTS[done:]:
        relation = part_product(part, zy, relation)
    for bit in bits:
        squares = squares + lax.ppermute(squares, "col", [(i, i ^ bit) for i in range(cols)])
    inbreeding = squares / jnp.float32(freq.shape[0]) - 1.0
    return relation, inbreeding


def solution(mesh):
    rows, cols = mesh.shape["row"], mesh.shape["col"]
    return jax.shard_map(
        functools.partial(local, rows, cols),
        mesh=mesh,
        in_specs=(P("row", "col"), P("row", "col"), P(), P(), P("row"), P("col")),
        out_specs=(P("row", "col"), P("row")),
        check_vma=False,
    )
```

```python
import functools
import itertools

import jax
import jax.numpy as jnp
import numpy as np
from jax import lax
from jax.experimental import pallas as pl
from jax.experimental.pallas import tpu as pltpu
from jax.sharding import PartitionSpec as P

STEPS = 4
PIECES = 1
DEPTH = 1
HOP = 1
COL_TILE = 512
ROW_BLOCK = 512
ROW_TILE = 32
LANES = 128
VMEM_LIMIT = 10 * 2**20
RELAY_LIMIT = 2 * 2**20


class Item:
    def __init__(self, row, piece, s, place, home=None):
        self.row, self.piece, self.s, self.place = row, piece, s, place
        self.home = home

    @property
    def owner(self):
        return self.row if self.home is None else self.home

    @property
    def key(self):
        return self.piece, self.s


def line_slots(items, cut):
    ends, inner = {}, {}
    todo = sorted(items, key=lambda i: (i.home is None, i.piece, i.place, i.s))
    slot = 1
    while todo:
        for item in todo:
            first = 1 + DEPTH * (item.place - 1) + (HOP if item.home is not None else 0)
            if first <= slot:
                ends[slot] = item
                if item.place > 1:
                    inner[slot] = item
                todo.remove(item)
                break
        slot += 1
    for item in sorted(cut, key=lambda i: (i.place, i.key)):
        slot = 1 + DEPTH * (item.place - 1)
        if item.place > 1:
            while slot in inner:
                slot += 1
            inner[slot] = item
    return ends, inner


class Lane:
    def __init__(self, rows, cols, groups_here, towards_zero):
        self.rows, self.cols = rows, cols
        self.towards_zero = towards_zero
        self.items = []
        for r in range(rows):
            mine = [
                Item(r, piece, s, self.place((r + s) % rows // groups_here))
                for piece in range(PIECES)
                for s in range(STEPS)
            ]
            self.items.append([i for i in mine if i.place > 0])
        self.away = []
        self.lines = [line_slots(items, []) for items in self.items]
        if rows % 2 == 0 and cols > 3:
            for r in range(rows // 2):
                self.balance(r, r + rows // 2)
                self.balance(r + rows // 2, r)
        self.rounds = max(
            [max(ends, default=0) for ends, _ in self.lines] + [max(inner, default=0) - DEPTH for _, inner in self.lines]
        )

    def place(self, c):
        return c if self.towards_zero else self.cols - 1 - c

    col = place

    def balance(self, r, other):
        if len(self.items[r]) < len(self.items[other]) or any(i.row == other for i in self.away):
            return
        places = sorted({i.place for i in self.items[r]})
        best = None
        for counts in itertools.product(range(3), repeat=len(places)):
            gone = []
            for place, count in zip(places, counts):
                here = [i for i in self.items[r] if i.place == place]
                here.sort(key=lambda i: i.key, reverse=True)
                gone += here[:count]
            visitors = [Item(other, i.piece, i.s, i.place, home=r) for i in gone]
            mine = line_slots([i for i in self.items[r] if i not in gone], gone)
            theirs = line_slots(self.items[other] + visitors, [])
            score = (
                max(max(mine[0], default=0), max(theirs[0], default=0)),
                abs(len(mine[0]) - len(theirs[0])),
                max([slot for slot, i in theirs[0].items() if i.home is not None], default=0),
                len(gone),
            )
            if best is None or score < best[0]:
                best = score, gone, mine, theirs
        _, gone, mine, theirs = best
        self.away += gone
        if gone:
            self.lines[r], self.lines[other] = mine, theirs

    def sent(self, r, c, t):
        p = self.place(c)
        ends, inner = self.lines[r]
        if p == 0:
            return None
        item = ends.get(t) if p == 1 else inner.get(t + DEPTH * (p - 1))
        return item if item is not None and item.place >= p else None

    def pairs(self, t):
        found = []
        for r in range(self.rows):
            for c in range(self.cols):
                if self.sent(r, c, t) is not None:
                    found.append((r * self.cols + c, r * self.cols + self.col(self.place(c) - 1)))
        return found

    def arrival(self, r, c, key):
        p = self.place(c)
        for i in self.items[r]:
            if i.key != key or i.place <= p:
                continue
            ends, inner = self.lines[r]
            if p == 0 and i in self.away:
                for other, _ in self.lines:
                    for slot, v in other.items():
                        if v.home == r and v.key == key:
                            return slot, True
            for slot, v in (ends if p == 0 else inner).items():
                if v is i:
                    return slot - DEPTH * p, False
        return None


def lookup(values, device):
    known = [v for v in values if v is not None]
    if len(set(known)) <= 1:
        return known[0] if known else 0
    values = [known[0] if v is None else v for v in values]
    result = jnp.uint32(0)
    place = (device % 32).astype(jnp.uint32)
    for bit in range(max(values).bit_length()):
        ones = [v >> bit & 1 for v in values]
        words = [sum(b << i for i, b in enumerate(ones[at : at + 32])) for at in range(0, len(ones), 32)]
        word = jnp.uint32(words[0])
        for i, other in enumerate(words[1:], 1):
            word = jnp.where(device // 32 == i, jnp.uint32(other), word)
        result = result | (((word >> place) & jnp.uint32(1)) << jnp.uint32(bit))
    return result.astype(jnp.int32)


def relay_kernel(at, table, x, *refs):
    *sources, out = refs
    rows, width = out.shape

    @pl.when(table[at] == 0)
    def _():
        row = pl.multiple_of(table[at + 1] * rows, rows)
        col = pl.multiple_of(table[at + 2] * width, width)
        out[...] = x[pl.ds(row, rows), pl.ds(col, width)]

    for i, source in enumerate(sources):

        @pl.when(table[at] == i + 1)
        def _(source=source):
            out[...] = source[...]


def relay(at, table, x, sources):
    return pl.pallas_call(
        functools.partial(relay_kernel, at),
        out_shape=pltpu.VMEM(sources[0].shape, sources[0].dtype),
        in_specs=[pl.BlockSpec(memory_space=pltpu.SMEM)] + [VMEM] * (1 + len(sources)),
        out_specs=VMEM,
        compiler_params=pltpu.CompilerParams(vmem_limit_bytes=RELAY_LIMIT),
        cost_estimate=pl.CostEstimate(flops=0, bytes_accessed=0, transcendentals=0),
        name="relay",
    )(table, *[in_vmem(v) for v in (x, *sources)])


def in_vmem(value):
    return pltpu.with_memory_space_constraint(value, pltpu.VMEM)


VMEM = pl.BlockSpec(memory_space=pltpu.VMEM)


def window_kernel(at, table, *refs):
    blocks = refs[:STEPS]
    factor, twice, male, out = refs[STEPS:]
    group_size, width = blocks[0].shape
    for s, block in enumerate(blocks):
        rank = table[at + s]

        @pl.loop(0, group_size // ROW_TILE)
        def _(i, s=s, block=block, rank=rank):
            here = pl.ds(pl.multiple_of(i * ROW_TILE, ROW_TILE), ROW_TILE)
            rows = pl.ds(pl.multiple_of(s * group_size + i * ROW_TILE, ROW_TILE), ROW_TILE)
            to = pl.ds(pl.multiple_of(rank * group_size + i * ROW_TILE, ROW_TILE), ROW_TILE)
            for k in range(0, width, LANES):
                value = block[here, k : k + LANES].astype(jnp.float32) - twice[rows, :]
                out[to, k : k + LANES] = (value * factor[rows, :] * male[:, k : k + LANES]).astype(out.dtype)


def standardized_window(at, table, blocks, factor, twice, male):
    group_size, n = blocks[0].shape
    depth = STEPS * group_size
    return pl.pallas_call(
        functools.partial(window_kernel, at),
        out_shape=pltpu.VMEM((depth, n), jnp.bfloat16),
        in_specs=[pl.BlockSpec(memory_space=pltpu.SMEM)] + [VMEM] * (STEPS + 3),
        out_specs=VMEM,
        compiler_params=pltpu.CompilerParams(vmem_limit_bytes=VMEM_LIMIT),
        cost_estimate=pl.CostEstimate(flops=4 * depth * n, bytes_accessed=4 * depth * n, transcendentals=0),
        name="window",
    )(table, *[in_vmem(v) for v in (*blocks, factor, twice, male)])


def standardize(table, at, candidates, x, buffers, factor, twice, male, zx, columns, first, count):
    width = columns.stop - columns.start
    place, step = table[at], table[at + 1]

    def from_source(source, col):
        @pl.loop(0, count // ROW_TILE)
        def _(i):
            here = pl.ds(pl.multiple_of(first + i * ROW_TILE, ROW_TILE), ROW_TILE)
            to = pl.ds(pl.multiple_of(i * ROW_TILE, ROW_TILE), ROW_TILE)
            for k in range(0, width, LANES):
                lanes = pl.ds(pl.multiple_of(step * width + k, LANES), LANES)
                value = source[here, pl.ds(pl.multiple_of(col + k, LANES), LANES)].astype(jnp.float32)
                value = (value - twice[:, lanes]) * factor[:, lanes] * male[here, :]
                zx[to, columns.start + k : columns.start + k + LANES] = value.astype(zx.dtype)

    for number in candidates:
        if number >= 0:

            @pl.when(place == number)
            def _(number=number):
                from_source(buffers[number], 0)

        else:

            @pl.when(place < 0)
            def _():
                from_source(x, (-1 - place) * width)


def early_kernel(at, candidates, n_buffers, table, x, *refs):
    buffers = refs[:n_buffers]
    factor, twice, male, zy, total, zx = refs[n_buffers:]
    rows, depth = zx.shape
    width = depth // (STEPS - 1)
    for rank in range(STEPS - 1):
        columns = slice(rank * width, (rank + 1) * width)
        standardize(table, at + 2 * rank, candidates[rank], x, buffers, factor, twice, male, zx, columns, 0, rows)

    @pl.loop(0, rows // ROW_BLOCK)
    def _(i):
        block = pl.ds(pl.multiple_of(i * ROW_BLOCK, ROW_BLOCK), ROW_BLOCK)
        for j in range(0, total.shape[1], COL_TILE):
            right = zy[:depth, j : j + COL_TILE]
            total[block, j : j + COL_TILE] = jnp.dot(zx[block, :], right, preferred_element_type=jnp.float32)


def early_product(at, candidates, table, x, buffers, factor, twice, male, zy):
    rows, (depth, n) = x.shape[0], zy.shape
    depth = depth // STEPS * (STEPS - 1)
    args = [in_vmem(v) for v in (x, *buffers, factor, twice, male, zy)]
    return pl.pallas_call(
        functools.partial(early_kernel, at, candidates, len(buffers)),
        out_shape=pltpu.VMEM((rows, n), jnp.float32),
        in_specs=[pl.BlockSpec(memory_space=pltpu.SMEM)] + [VMEM] * len(args),
        out_specs=VMEM,
        scratch_shapes=[pltpu.VMEM((rows, depth), jnp.bfloat16)],
        compiler_params=pltpu.CompilerParams(vmem_limit_bytes=VMEM_LIMIT),
        cost_estimate=pl.CostEstimate(flops=2 * rows * depth * n, bytes_accessed=0, transcendentals=0),
        name="early",
    )(table, *args)


def last_kernel(at, candidates, scale, n_buffers, table, x, *refs):
    buffers = refs[:n_buffers]
    factor, twice, male, zy, total, out, zx, blocks, sems = refs[n_buffers:]
    rows, n = total.shape
    width = zx.shape[1]

    def copy(i):
        return pltpu.make_async_copy(blocks.at[i % 2], out.at[pl.ds(i * ROW_BLOCK, ROW_BLOCK), :], sems.at[i % 2])

    count = rows // ROW_BLOCK
    for i in range(count):
        first = i * ROW_BLOCK
        standardize(
            table, at, candidates, x, buffers, factor, twice, male, zx, slice(0, width), first, ROW_BLOCK
        )
        if i >= 2:
            copy(i - 2).wait()
        for j in range(0, n, COL_TILE):
            right = zy[zy.shape[0] - width :, j : j + COL_TILE]
            product = jnp.dot(zx[...], right, preferred_element_type=jnp.float32)
            product = product + total[first : first + ROW_BLOCK, j : j + COL_TILE]
            blocks[i % 2, :, j : j + COL_TILE] = (product * scale).astype(blocks.dtype)
        copy(i).start()
    for i in range(max(count - 2, 0), count):
        copy(i).wait()


def last_product(at, candidates, table, x, buffers, factor, twice, male, zy, total):
    rows, (depth, n) = x.shape[0], zy.shape
    width = depth // STEPS
    scale = float(1.0 / np.sqrt(np.float32(depth)))
    args = [in_vmem(v) for v in (x, *buffers, factor, twice, male, zy, total)]
    return pl.pallas_call(
        functools.partial(last_kernel, at, candidates, scale, len(buffers)),
        out_shape=jax.ShapeDtypeStruct((rows, n), jnp.bfloat16),
        in_specs=[pl.BlockSpec(memory_space=pltpu.SMEM)] + [VMEM] * len(args),
        out_specs=pl.BlockSpec(memory_space=pl.ANY),
        scratch_shapes=[
            pltpu.VMEM((ROW_BLOCK, width), jnp.bfloat16),
            pltpu.VMEM((2, ROW_BLOCK, n), jnp.bfloat16),
            pltpu.SemaphoreType.DMA((2,)),
        ],
        compiler_params=pltpu.CompilerParams(vmem_limit_bytes=VMEM_LIMIT),
        cost_estimate=pl.CostEstimate(flops=2 * rows * width * n, bytes_accessed=2 * rows * n, transcendentals=0),
        name="last",
    )(table, *args)


def local(rows, cols, x, y, freq, weight, sex_rows, sex_cols):
    group_size = y.shape[0]
    local_vars = x.shape[1]
    groups_here = local_vars // group_size
    piece_rows = x.shape[0] // PIECES
    lanes = [Lane(rows, cols, groups_here, towards) for towards in (True, False)]
    rounds = max(lane.rounds for lane in lanes)
    devices = [(r, c) for r in range(rows) for c in range(cols)]
    both = ("row", "col")

    row_place = lax.axis_index("row")
    col_place = lax.axis_index("col")
    device = row_place * cols + col_place

    def number(r, c):
        return r * cols + c

    def group_here(item):
        return (item.owner + item.s) % rows % groups_here

    crossings = []
    crossing_of = {}
    for d, lane in enumerate(lanes):
        for r in range(rows):
            for slot, item in sorted(lane.lines[r][0].items()):
                if item.home is None:
                    continue
                source, target = (item.home, lane.col(item.place)), (r, lane.col(item.place))
                for k, crossing in enumerate(crossings):
                    if source not in crossing and target not in [to for to, _ in crossing.values()]:
                        break
                else:
                    k = len(crossings)
                    crossings.append({})
                crossings[k][source] = (target, item)
                crossing_of[d, r, item.key] = k

    def lane_of(phase, r):
        return (r + phase) % 2

    sends = [(phase, t) for t in range(1, rounds + 1) for phase in range(2)]
    pairs_of, kinds_of, own_of = {}, {}, {}
    for phase, t in sends:
        pairs, kinds, own = [], [], []
        for r, c in devices:
            lane = lanes[lane_of(phase, r)]
            item = lane.sent(r, c, t)
            if item is not None:
                pairs.append((number(r, c), number(r, lane.col(lane.place(c) - 1))))
            if item is None:
                kinds.append(None)
            elif item.place != lane.place(c):
                kinds.append("forward")
            elif item.home is not None:
                kinds.append(crossing_of[lane_of(phase, r), r, item.key])
            else:
                kinds.append("own")
            own.append(item if kinds[-1] == "own" else None)
        pairs_of[phase, t], kinds_of[phase, t], own_of[phase, t] = pairs, kinds, own

    returns = {}
    for t in range(1, rounds + 1):
        pairs, phases = [], [None] * len(devices)
        for d, lane in enumerate(lanes):
            for r in range(rows):
                item = lane.lines[r][0].get(t)
                if item is not None and item.home is not None:
                    pairs.append((number(r, lane.col(0)), number(item.home, lane.col(0))))
                    phases[pairs[-1][0]] = (r + d) % 2
        if pairs:
            returns[t] = pairs, phases

    columns = []

    def add(entries):
        columns.append(np.asarray(entries, np.int32))
        return sum(c.shape[1] for c in columns[:-1])

    relays = {}
    for key in sends:
        kinds = kinds_of[key]
        names = sorted(set(kinds) - {None, "own"}, key=str)
        if names and (len(names) > 1 or "own" in kinds):
            entries = []
            for kind, item in zip(kinds, own_of[key]):
                if kind == "own":
                    entries.append((0, item.piece, group_here(item)))
                else:
                    entries.append((1 + names.index(kind) if kind is not None else 1, 0, 0))
            relays[key] = names, add(entries)
    for t, (pairs, phases) in returns.items():
        if len(set(phases) - {None}) > 1:
            relays["back", t] = None, add([(1 + (p or 0), 0, 0) for p in phases])

    order = []
    for r, c in devices:
        arrivals = []
        for s in range(STEPS):
            when, key = 0, -1 - (r + s) % rows % groups_here
            for d, lane in enumerate(lanes):
                arrival = lane.arrival(r, c, (0, s))
                if arrival is not None:
                    t, returned = arrival
                    when, key = (t + 0.7, ("back", t)) if returned else (t, ((r + d) % 2, t))
            arrivals.append((when, s, key))
        order.append(sorted(arrivals, key=lambda a: a[:2]))
    rank_at = add([[[a[1] for a in arrivals].index(s) for s in range(STEPS)] for arrivals in order])
    used, candidates, source_at = [], [], []
    for ranks in (range(STEPS - 1), range(STEPS - 1, STEPS)):
        keys = {arrivals[k][2] for arrivals in order for k in ranks}
        used.append(sorted((k for k in keys if isinstance(k, tuple)), key=lambda k: (k[1], str(k[0]))))
        places = [
            [arrivals[k][2] if isinstance(arrivals[k][2], int) else used[-1].index(arrivals[k][2]) for k in ranks]
            for arrivals in order
        ]
        candidates.append([sorted({max(p[i], -1) for p in places}) for i in range(len(ranks))])
        source_at.append(
            add([[n for p, k in zip(row, ranks) for n in (p, arrivals[k][1])] for row, arrivals in zip(places, order)])
        )
    table = np.concatenate(columns, axis=1)
    table = lax.dynamic_slice(jnp.asarray(table), (device, 0), (1, table.shape[1]))[0]

    def own_chunk(items, x=x):
        piece = lookup([None if i is None else i.piece for i in items], device)
        group = lookup([None if i is None else group_here(i) for i in items], device)
        return lax.dynamic_slice(x, (piece * piece_rows, group * group_size), (piece_rows, group_size))

    factor = weight / jnp.sqrt(2.0 * freq * (1.0 - freq))
    twice = 2.0 * freq
    male_scale = np.float32(np.sqrt(0.5))
    male_rows = jnp.where(sex_rows > 0, male_scale, np.float32(1.0))
    male_cols = jnp.where(sex_cols > 0, male_scale, np.float32(1.0))
    wide = lambda value: jnp.broadcast_to(value[:, None], (value.shape[0], LANES))

    def in_window(value):
        span = STEPS * group_size
        return lax.dynamic_slice(jnp.concatenate([value, value]), (row_place * group_size,), (span,))

    window_factor, window_twice = in_window(factor), in_window(twice)
    male_wide = wide(male_rows)

    def own_squares():
        here = lambda value: lax.dynamic_slice(value, (col_place * local_vars,), (local_vars,))[None, :]
        zx = ((x.astype(jnp.float32) - here(twice)) * here(factor) * male_rows[:, None]).astype(jnp.bfloat16)
        return jnp.sum(jnp.square(zx.astype(jnp.float32)), axis=1)

    back = [(i, (i - 1) % rows) for i in range(rows)]
    window = [y]
    while len(window) < STEPS:
        window.append(lax.ppermute(window[-1], "row", back))
    squares = own_squares()

    starts = {}
    if any(own_of[0, 1]):
        starts[0, 1] = own_chunk(own_of[0, 1])
    for k, crossing in enumerate(crossings):
        starts["cross", k] = own_chunk([crossing[rc][1] if rc in crossing else None for rc in devices])
    later_x, squares = lax.optimization_barrier((x, squares))
    if any(own_of[1, 1]):
        starts[1, 1] = own_chunk(own_of[1, 1], later_x)
    bits = [1 << k for k in range(cols.bit_length() - 1)] if cols & (cols - 1) == 0 else []
    if cols & (cols - 1):
        squares = lax.psum(squares, "col")

    def sum_beside(value, squares):
        if not bits:
            return value, squares
        bit = bits.pop(0)
        other = lax.ppermute(squares, "col", [(i, i ^ bit) for i in range(cols)])
        value, other = lax.optimization_barrier((value, other))
        return value, squares + other

    buffers, crossed = {}, {}
    zy = None
    for key in sends:
        phase, t = key
        if pairs_of[key]:
            if key in relays:
                names, at = relays[key]
                sources = [buffers[phase, t - DEPTH] if name == "forward" else crossed[name] for name in names]
                held = relay(at, table, x, sources)
            elif key in starts:
                held = starts[key]
            elif "forward" in kinds_of[key]:
                held = buffers[phase, t - DEPTH]
            elif "own" in kinds_of[key]:
                held = own_chunk(own_of[key])
            else:
                held = crossed[next(k for k in kinds_of[key] if k is not None)]
            if key == (1, STEPS):
                zy = standardized_window(
                    rank_at, table, window, wide(window_factor), wide(window_twice), male_cols[None, :]
                )
                zy, squares = sum_beside(zy, squares)
                held, zy = lax.optimization_barrier((held, zy))
            buffers[key] = lax.ppermute(held, both, pairs_of[key])
        if key == (0, 1):
            for k, crossing in enumerate(crossings):
                pairs = [(number(*rc), number(*to)) for rc, (to, _) in crossing.items()]
                crossed[k] = lax.ppermute(starts["cross", k], both, pairs)
        if phase == 1 and t in returns:
            pairs, phases = returns[t]
            if ("back", t) in relays:
                held = relay(relays["back", t][1], table, x, [buffers[0, t], buffers[1, t]])
            else:
                held = buffers[next(p for p in phases if p is not None), t]
            buffers["back", t] = lax.ppermute(held, both, pairs)
    if zy is None:
        zy = standardized_window(rank_at, table, window, wide(window_factor), wide(window_twice), male_cols[None, :])
    shared = window_factor[None, :], window_twice[None, :], male_wide, zy
    total = early_product(source_at[0], candidates[0], table, x, [buffers[k] for k in used[0]], *shared)
    total, squares = sum_beside(total, squares)
    relation = last_product(source_at[1], candidates[1][0], table, x, [buffers[k] for k in used[1]], *shared, total)
    for bit in bits:
        squares = squares + lax.ppermute(squares, "col", [(i, i ^ bit) for i in range(cols)])
    inbreeding = squares / jnp.float32(freq.shape[0]) - 1.0
    return relation, inbreeding


def solution(mesh):
    rows, cols = mesh.shape["row"], mesh.shape["col"]
    return jax.shard_map(
        functools.partial(local, rows, cols),
        mesh=mesh,
        in_specs=(P("row", "col"), P("row", "col"), P(), P(), P("row"), P("col")),
        out_specs=(P("row", "col"), P("row")),
        check_vma=False,
    )
```

```python
import functools
import itertools

import jax
import jax.numpy as jnp
import numpy as np
from jax import lax
from jax.experimental import pallas as pl
from jax.experimental.pallas import tpu as pltpu
from jax.sharding import PartitionSpec as P

STEPS = 4
PIECES = 1
DEPTH = 1
HOP = 1
COL_TILE = 512
ROW_BLOCK = 512
ROW_TILE = 32
LANES = 128
VMEM_LIMIT = 10 * 2**20
RELAY_LIMIT = 2 * 2**20


class Item:
    def __init__(self, row, piece, s, place, home=None):
        self.row, self.piece, self.s, self.place = row, piece, s, place
        self.home = home

    @property
    def owner(self):
        return self.row if self.home is None else self.home

    @property
    def key(self):
        return self.piece, self.s


def line_slots(items, cut):
    ends, inner = {}, {}
    todo = sorted(items, key=lambda i: (i.home is None, i.piece, i.place, i.s))
    slot = 1
    while todo:
        for item in todo:
            first = 1 + DEPTH * (item.place - 1) + (HOP if item.home is not None else 0)
            if first <= slot:
                ends[slot] = item
                if item.place > 1:
                    inner[slot] = item
                todo.remove(item)
                break
        slot += 1
    for item in sorted(cut, key=lambda i: (i.place, i.key)):
        slot = 1 + DEPTH * (item.place - 1)
        if item.place > 1:
            while slot in inner:
                slot += 1
            inner[slot] = item
    return ends, inner


class Lane:
    def __init__(self, rows, cols, groups_here, towards_zero):
        self.rows, self.cols = rows, cols
        self.towards_zero = towards_zero
        self.items = []
        for r in range(rows):
            mine = [
                Item(r, piece, s, self.place((r + s) % rows // groups_here))
                for piece in range(PIECES)
                for s in range(STEPS)
            ]
            self.items.append([i for i in mine if i.place > 0])
        self.away = []
        self.lines = [line_slots(items, []) for items in self.items]
        if rows % 2 == 0 and cols > 3:
            for r in range(rows // 2):
                self.balance(r, r + rows // 2)
                self.balance(r + rows // 2, r)
        self.rounds = max(
            [max(ends, default=0) for ends, _ in self.lines] + [max(inner, default=0) - DEPTH for _, inner in self.lines]
        )

    def place(self, c):
        return c if self.towards_zero else self.cols - 1 - c

    col = place

    def balance(self, r, other):
        if len(self.items[r]) < len(self.items[other]) or any(i.row == other for i in self.away):
            return
        places = sorted({i.place for i in self.items[r]})
        best = None
        for counts in itertools.product(range(3), repeat=len(places)):
            gone = []
            for place, count in zip(places, counts):
                here = [i for i in self.items[r] if i.place == place]
                here.sort(key=lambda i: i.key, reverse=True)
                gone += here[:count]
            visitors = [Item(other, i.piece, i.s, i.place, home=r) for i in gone]
            mine = line_slots([i for i in self.items[r] if i not in gone], gone)
            theirs = line_slots(self.items[other] + visitors, [])
            score = (
                max(max(mine[0], default=0), max(theirs[0], default=0)),
                abs(len(mine[0]) - len(theirs[0])),
                max([slot for slot, i in theirs[0].items() if i.home is not None], default=0),
                len(gone),
            )
            if best is None or score < best[0]:
                best = score, gone, mine, theirs
        _, gone, mine, theirs = best
        self.away += gone
        if gone:
            self.lines[r], self.lines[other] = mine, theirs

    def sent(self, r, c, t):
        p = self.place(c)
        ends, inner = self.lines[r]
        if p == 0:
            return None
        item = ends.get(t) if p == 1 else inner.get(t + DEPTH * (p - 1))
        return item if item is not None and item.place >= p else None

    def pairs(self, t):
        found = []
        for r in range(self.rows):
            for c in range(self.cols):
                if self.sent(r, c, t) is not None:
                    found.append((r * self.cols + c, r * self.cols + self.col(self.place(c) - 1)))
        return found

    def arrival(self, r, c, key):
        p = self.place(c)
        for i in self.items[r]:
            if i.key != key or i.place <= p:
                continue
            ends, inner = self.lines[r]
            if p == 0 and i in self.away:
                for other, _ in self.lines:
                    for slot, v in other.items():
                        if v.home == r and v.key == key:
                            return slot, True
            for slot, v in (ends if p == 0 else inner).items():
                if v is i:
                    return slot - DEPTH * p, False
        return None


def lookup(values, device):
    known = [v for v in values if v is not None]
    if len(set(known)) <= 1:
        return known[0] if known else 0
    values = [known[0] if v is None else v for v in values]
    result = jnp.uint32(0)
    place = (device % 32).astype(jnp.uint32)
    for bit in range(max(values).bit_length()):
        ones = [v >> bit & 1 for v in values]
        words = [sum(b << i for i, b in enumerate(ones[at : at + 32])) for at in range(0, len(ones), 32)]
        word = jnp.uint32(words[0])
        for i, other in enumerate(words[1:], 1):
            word = jnp.where(device // 32 == i, jnp.uint32(other), word)
        result = result | (((word >> place) & jnp.uint32(1)) << jnp.uint32(bit))
    return result.astype(jnp.int32)


def relay_kernel(at, table, x, *refs):
    *sources, out = refs
    rows, width = out.shape

    @pl.when(table[at] == 0)
    def _():
        row = pl.multiple_of(table[at + 1] * rows, rows)
        col = pl.multiple_of(table[at + 2] * width, width)
        out[...] = x[pl.ds(row, rows), pl.ds(col, width)]

    for i, source in enumerate(sources):

        @pl.when(table[at] == i + 1)
        def _(source=source):
            out[...] = source[...]


def relay(at, table, x, sources):
    return pl.pallas_call(
        functools.partial(relay_kernel, at),
        out_shape=pltpu.VMEM(sources[0].shape, sources[0].dtype),
        in_specs=[pl.BlockSpec(memory_space=pltpu.SMEM)] + [VMEM] * (1 + len(sources)),
        out_specs=VMEM,
        compiler_params=pltpu.CompilerParams(vmem_limit_bytes=RELAY_LIMIT),
        cost_estimate=pl.CostEstimate(flops=0, bytes_accessed=0, transcendentals=0),
        name="relay",
    )(table, *[in_vmem(v) for v in (x, *sources)])


def in_vmem(value):
    return pltpu.with_memory_space_constraint(value, pltpu.VMEM)


VMEM = pl.BlockSpec(memory_space=pltpu.VMEM)


def window_kernel(at, table, *refs):
    blocks = refs[:STEPS]
    factor, twice, male, out = refs[STEPS:]
    group_size, width = blocks[0].shape
    for s, block in enumerate(blocks):
        rank = table[at + s]

        @pl.loop(0, group_size // ROW_TILE)
        def _(i, s=s, block=block, rank=rank):
            here = pl.ds(pl.multiple_of(i * ROW_TILE, ROW_TILE), ROW_TILE)
            rows = pl.ds(pl.multiple_of(s * group_size + i * ROW_TILE, ROW_TILE), ROW_TILE)
            to = pl.ds(pl.multiple_of(rank * group_size + i * ROW_TILE, ROW_TILE), ROW_TILE)
            for k in range(0, width, LANES):
                value = block[here, k : k + LANES].astype(jnp.float32) - twice[rows, :]
                out[to, k : k + LANES] = (value * factor[rows, :] * male[:, k : k + LANES]).astype(out.dtype)


def standardized_window(at, table, blocks, factor, twice, male):
    group_size, n = blocks[0].shape
    depth = STEPS * group_size
    return pl.pallas_call(
        functools.partial(window_kernel, at),
        out_shape=pltpu.VMEM((depth, n), jnp.bfloat16),
        in_specs=[pl.BlockSpec(memory_space=pltpu.SMEM)] + [VMEM] * (STEPS + 3),
        out_specs=VMEM,
        compiler_params=pltpu.CompilerParams(vmem_limit_bytes=VMEM_LIMIT),
        cost_estimate=pl.CostEstimate(flops=4 * depth * n, bytes_accessed=4 * depth * n, transcendentals=0),
        name="window",
    )(table, *[in_vmem(v) for v in (*blocks, factor, twice, male)])


def standardize(table, at, candidates, x, buffers, factor, twice, male, zx, columns, first, count):
    width = columns.stop - columns.start
    place, step = table[at], table[at + 1]

    def from_source(source, col):
        @pl.loop(0, count // ROW_TILE)
        def _(i):
            here = pl.ds(pl.multiple_of(first + i * ROW_TILE, ROW_TILE), ROW_TILE)
            to = pl.ds(pl.multiple_of(i * ROW_TILE, ROW_TILE), ROW_TILE)
            for k in range(0, width, LANES):
                lanes = pl.ds(pl.multiple_of(step * width + k, LANES), LANES)
                value = source[here, pl.ds(pl.multiple_of(col + k, LANES), LANES)].astype(jnp.float32)
                value = (value - twice[:, lanes]) * factor[:, lanes] * male[here, :]
                zx[to, columns.start + k : columns.start + k + LANES] = value.astype(zx.dtype)

    for number in candidates:
        if number >= 0:

            @pl.when(place == number)
            def _(number=number):
                from_source(buffers[number], 0)

        else:

            @pl.when(place < 0)
            def _():
                from_source(x, (-1 - place) * width)


def early_kernel(at, candidates, n_buffers, table, x, *refs):
    buffers = refs[:n_buffers]
    factor, twice, male, zy, total, zx = refs[n_buffers:]
    rows, depth = zx.shape
    width = depth // (STEPS - 1)
    for rank in range(STEPS - 1):
        columns = slice(rank * width, (rank + 1) * width)
        standardize(table, at + 2 * rank, candidates[rank], x, buffers, factor, twice, male, zx, columns, 0, rows)

    @pl.loop(0, rows // ROW_BLOCK)
    def _(i):
        block = pl.ds(pl.multiple_of(i * ROW_BLOCK, ROW_BLOCK), ROW_BLOCK)
        for j in range(0, total.shape[1], COL_TILE):
            right = zy[:depth, j : j + COL_TILE]
            total[block, j : j + COL_TILE] = jnp.dot(zx[block, :], right, preferred_element_type=jnp.float32)


def early_product(at, candidates, table, x, buffers, factor, twice, male, zy):
    rows, (depth, n) = x.shape[0], zy.shape
    depth = depth // STEPS * (STEPS - 1)
    args = [in_vmem(v) for v in (x, *buffers, factor, twice, male, zy)]
    return pl.pallas_call(
        functools.partial(early_kernel, at, candidates, len(buffers)),
        out_shape=pltpu.VMEM((rows, n), jnp.float32),
        in_specs=[pl.BlockSpec(memory_space=pltpu.SMEM)] + [VMEM] * len(args),
        out_specs=VMEM,
        scratch_shapes=[pltpu.VMEM((rows, depth), jnp.bfloat16)],
        compiler_params=pltpu.CompilerParams(vmem_limit_bytes=VMEM_LIMIT),
        cost_estimate=pl.CostEstimate(flops=2 * rows * depth * n, bytes_accessed=0, transcendentals=0),
        name="early",
    )(table, *args)


def last_kernel(at, candidates, scale, n_buffers, table, x, *refs):
    buffers = refs[:n_buffers]
    factor, twice, male, zy, total, out, zx, blocks, sems = refs[n_buffers:]
    rows, n = total.shape
    width = zx.shape[1]

    def copy(i):
        return pltpu.make_async_copy(blocks.at[i % 2], out.at[pl.ds(i * ROW_BLOCK, ROW_BLOCK), :], sems.at[i % 2])

    count = rows // ROW_BLOCK
    for i in range(count):
        first = i * ROW_BLOCK
        standardize(
            table, at, candidates, x, buffers, factor, twice, male, zx, slice(0, width), first, ROW_BLOCK
        )
        if i >= 2:
            copy(i - 2).wait()
        for j in range(0, n, COL_TILE):
            right = zy[zy.shape[0] - width :, j : j + COL_TILE]
            product = jnp.dot(zx[...], right, preferred_element_type=jnp.float32)
            product = product + total[first : first + ROW_BLOCK, j : j + COL_TILE]
            blocks[i % 2, :, j : j + COL_TILE] = (product * scale).astype(blocks.dtype)
        copy(i).start()
    for i in range(max(count - 2, 0), count):
        copy(i).wait()


def last_product(at, candidates, table, x, buffers, factor, twice, male, zy, total):
    rows, (depth, n) = x.shape[0], zy.shape
    width = depth // STEPS
    scale = float(1.0 / np.sqrt(np.float32(depth)))
    args = [in_vmem(v) for v in (x, *buffers, factor, twice, male, zy, total)]
    return pl.pallas_call(
        functools.partial(last_kernel, at, candidates, scale, len(buffers)),
        out_shape=jax.ShapeDtypeStruct((rows, n), jnp.bfloat16),
        in_specs=[pl.BlockSpec(memory_space=pltpu.SMEM)] + [VMEM] * len(args),
        out_specs=pl.BlockSpec(memory_space=pl.ANY),
        scratch_shapes=[
            pltpu.VMEM((ROW_BLOCK, width), jnp.bfloat16),
            pltpu.VMEM((2, ROW_BLOCK, n), jnp.bfloat16),
            pltpu.SemaphoreType.DMA((2,)),
        ],
        compiler_params=pltpu.CompilerParams(vmem_limit_bytes=VMEM_LIMIT),
        cost_estimate=pl.CostEstimate(flops=2 * rows * width * n, bytes_accessed=2 * rows * n, transcendentals=0),
        name="last",
    )(table, *args)


def local(rows, cols, x, y, freq, weight, sex_rows, sex_cols):
    group_size = y.shape[0]
    local_vars = x.shape[1]
    groups_here = local_vars // group_size
    piece_rows = x.shape[0] // PIECES
    lanes = [Lane(rows, cols, groups_here, towards) for towards in (True, False)]
    rounds = max(lane.rounds for lane in lanes)
    devices = [(r, c) for r in range(rows) for c in range(cols)]
    both = ("row", "col")

    row_place = lax.axis_index("row")
    col_place = lax.axis_index("col")
    device = row_place * cols + col_place

    def number(r, c):
        return r * cols + c

    def group_here(item):
        return (item.owner + item.s) % rows % groups_here

    crossings = []
    crossing_of = {}
    for d, lane in enumerate(lanes):
        for r in range(rows):
            for slot, item in sorted(lane.lines[r][0].items()):
                if item.home is None:
                    continue
                source, target = (item.home, lane.col(item.place)), (r, lane.col(item.place))
                for k, crossing in enumerate(crossings):
                    if source not in crossing and target not in [to for to, _ in crossing.values()]:
                        break
                else:
                    k = len(crossings)
                    crossings.append({})
                crossings[k][source] = (target, item)
                crossing_of[d, r, item.key] = k

    def lane_of(phase, r):
        return (r + phase) % 2

    sends = [(phase, t) for t in range(1, rounds + 1) for phase in range(2)]
    pairs_of, kinds_of, own_of = {}, {}, {}
    for phase, t in sends:
        pairs, kinds, own = [], [], []
        for r, c in devices:
            lane = lanes[lane_of(phase, r)]
            item = lane.sent(r, c, t)
            if item is not None:
                pairs.append((number(r, c), number(r, lane.col(lane.place(c) - 1))))
            if item is None:
                kinds.append(None)
            elif item.place != lane.place(c):
                kinds.append("forward")
            elif item.home is not None:
                kinds.append(crossing_of[lane_of(phase, r), r, item.key])
            else:
                kinds.append("own")
            own.append(item if kinds[-1] == "own" else None)
        pairs_of[phase, t], kinds_of[phase, t], own_of[phase, t] = pairs, kinds, own

    returns = {}
    for t in range(1, rounds + 1):
        pairs, phases = [], [None] * len(devices)
        for d, lane in enumerate(lanes):
            for r in range(rows):
                item = lane.lines[r][0].get(t)
                if item is not None and item.home is not None:
                    pairs.append((number(r, lane.col(0)), number(item.home, lane.col(0))))
                    phases[pairs[-1][0]] = (r + d) % 2
        if pairs:
            returns[t] = pairs, phases

    columns = []

    def add(entries):
        columns.append(np.asarray(entries, np.int32))
        return sum(c.shape[1] for c in columns[:-1])

    relays = {}
    for key in sends:
        kinds = kinds_of[key]
        names = sorted(set(kinds) - {None, "own"}, key=str)
        if names and (len(names) > 1 or "own" in kinds):
            entries = []
            for kind, item in zip(kinds, own_of[key]):
                if kind == "own":
                    entries.append((0, item.piece, group_here(item)))
                else:
                    entries.append((1 + names.index(kind) if kind is not None else 1, 0, 0))
            relays[key] = names, add(entries)
    for t, (pairs, phases) in returns.items():
        if len(set(phases) - {None}) > 1:
            relays["back", t] = None, add([(1 + (p or 0), 0, 0) for p in phases])

    order = []
    for r, c in devices:
        arrivals = []
        for s in range(STEPS):
            when, key = 0, -1 - (r + s) % rows % groups_here
            for d, lane in enumerate(lanes):
                arrival = lane.arrival(r, c, (0, s))
                if arrival is not None:
                    t, returned = arrival
                    when, key = (t + 0.7, ("back", t)) if returned else (t, ((r + d) % 2, t))
            arrivals.append((when, s, key))
        order.append(sorted(arrivals, key=lambda a: a[:2]))
    rank_at = add([[[a[1] for a in arrivals].index(s) for s in range(STEPS)] for arrivals in order])
    used, candidates, source_at = [], [], []
    for ranks in (range(STEPS - 1), range(STEPS - 1, STEPS)):
        keys = {arrivals[k][2] for arrivals in order for k in ranks}
        used.append(sorted((k for k in keys if isinstance(k, tuple)), key=lambda k: (k[1], str(k[0]))))
        places = [
            [arrivals[k][2] if isinstance(arrivals[k][2], int) else used[-1].index(arrivals[k][2]) for k in ranks]
            for arrivals in order
        ]
        candidates.append([sorted({max(p[i], -1) for p in places}) for i in range(len(ranks))])
        source_at.append(
            add([[n for p, k in zip(row, ranks) for n in (p, arrivals[k][1])] for row, arrivals in zip(places, order)])
        )
    table = np.concatenate(columns, axis=1)
    table = lax.dynamic_slice(jnp.asarray(table), (device, 0), (1, table.shape[1]))[0]

    def own_chunk(items, x=x):
        piece = lookup([None if i is None else i.piece for i in items], device)
        group = lookup([None if i is None else group_here(i) for i in items], device)
        return lax.dynamic_slice(x, (piece * piece_rows, group * group_size), (piece_rows, group_size))

    factor = weight / jnp.sqrt(2.0 * freq * (1.0 - freq))
    twice = 2.0 * freq
    male_scale = np.float32(np.sqrt(0.5))
    male_rows = jnp.where(sex_rows > 0, male_scale, np.float32(1.0))
    male_cols = jnp.where(sex_cols > 0, male_scale, np.float32(1.0))
    wide = lambda value: jnp.broadcast_to(value[:, None], (value.shape[0], LANES))

    def in_window(value):
        span = STEPS * group_size
        return lax.dynamic_slice(jnp.concatenate([value, value]), (row_place * group_size,), (span,))

    window_factor, window_twice = in_window(factor), in_window(twice)
    male_wide = wide(male_rows)

    def own_squares():
        here = lambda value: lax.dynamic_slice(value, (col_place * local_vars,), (local_vars,))[None, :]
        zx = ((x.astype(jnp.float32) - here(twice)) * here(factor) * male_rows[:, None]).astype(jnp.bfloat16)
        return jnp.sum(jnp.square(zx.astype(jnp.float32)), axis=1)

    back = [(i, (i - 1) % rows) for i in range(rows)]
    window = [y]
    while len(window) < STEPS:
        window.append(lax.ppermute(window[-1], "row", back))
    squares = own_squares()

    starts = {}
    if any(own_of[1, 1]):
        starts[1, 1] = own_chunk(own_of[1, 1])
    later_x = x
    for k, crossing in enumerate(crossings):
        later_x = lax.optimization_barrier(later_x)
        starts["cross", k] = own_chunk([crossing[rc][1] if rc in crossing else None for rc in devices], later_x)
    later_x, squares = lax.optimization_barrier((later_x, squares))
    if any(own_of[0, 1]):
        starts[0, 1] = own_chunk(own_of[0, 1], later_x)
    bits = [1 << k for k in range(cols.bit_length() - 1)] if cols & (cols - 1) == 0 else []
    if cols & (cols - 1):
        squares = lax.psum(squares, "col")

    def sum_beside(value, squares):
        if not bits:
            return value, squares
        bit = bits.pop(0)
        other = lax.ppermute(squares, "col", [(i, i ^ bit) for i in range(cols)])
        value, other = lax.optimization_barrier((value, other))
        return value, squares + other

    buffers, crossed = {}, {}

    def bring_back(t):
        if t in returns:
            pairs, phases = returns[t]
            if ("back", t) in relays:
                held = relay(relays["back", t][1], table, x, [buffers[0, t], buffers[1, t]])
            else:
                held = buffers[next(p for p in phases if p is not None), t]
            buffers["back", t] = lax.ppermute(held, both, pairs)

    for key in sends:
        phase, t = key
        if pairs_of[key]:
            if key in relays:
                names, at = relays[key]
                sources = [buffers[phase, t - DEPTH] if name == "forward" else crossed[name] for name in names]
                held = relay(at, table, x, sources)
            elif key in starts:
                held = starts[key]
            elif "forward" in kinds_of[key]:
                held = buffers[phase, t - DEPTH]
            elif "own" in kinds_of[key]:
                held = own_chunk(own_of[key])
            else:
                held = crossed[next(k for k in kinds_of[key] if k is not None)]
            if phase == 1 and t in (2, 3):
                held, squares = sum_beside(held, squares)
            if phase == 1 and t - 1 in returns:
                held, table = lax.optimization_barrier((held, table))
            buffers[key] = lax.ppermute(held, both, pairs_of[key])
        if key == (0, 1):
            for k, crossing in enumerate(crossings):
                pairs = [(number(*rc), number(*to)) for rc, (to, _) in crossing.items()]
                crossed[k] = lax.ppermute(starts["cross", k], both, pairs)
        if phase == 1:
            bring_back(t - 1)
    bring_back(rounds)
    zy = standardized_window(rank_at, table, window, wide(window_factor), wide(window_twice), male_cols[None, :])
    shared = window_factor[None, :], window_twice[None, :], male_wide, zy
    total = early_product(source_at[0], candidates[0], table, x, [buffers[k] for k in used[0]], *shared)
    relation = last_product(source_at[1], candidates[1][0], table, x, [buffers[k] for k in used[1]], *shared, total)
    for bit in bits:
        squares = squares + lax.ppermute(squares, "col", [(i, i ^ bit) for i in range(cols)])
    inbreeding = squares / jnp.float32(freq.shape[0]) - 1.0
    return relation, inbreeding


def solution(mesh):
    rows, cols = mesh.shape["row"], mesh.shape["col"]
    return jax.shard_map(
        functools.partial(local, rows, cols),
        mesh=mesh,
        in_specs=(P("row", "col"), P("row", "col"), P(), P(), P("row"), P("col")),
        out_specs=(P("row", "col"), P("row")),
        check_vma=False,
    )
```

```python
import functools
import itertools

import jax
import jax.numpy as jnp
import numpy as np
from jax import lax
from jax.experimental import pallas as pl
from jax.experimental.pallas import tpu as pltpu
from jax.sharding import PartitionSpec as P

STEPS = 4
PIECES = 1
DEPTH = 1
HOP = 1
COL_TILE = 512
ROW_BLOCK = 512
ROW_TILE = 32
LANES = 128
VMEM_LIMIT = 10 * 2**20
RELAY_LIMIT = 2 * 2**20


class Item:
    def __init__(self, row, piece, s, place, home=None):
        self.row, self.piece, self.s, self.place = row, piece, s, place
        self.home = home

    @property
    def owner(self):
        return self.row if self.home is None else self.home

    @property
    def key(self):
        return self.piece, self.s


def line_slots(items, cut):
    ends, inner = {}, {}
    todo = sorted(items, key=lambda i: (i.home is None, i.piece, i.place, i.s))
    slot = 1
    while todo:
        for item in todo:
            first = 1 + DEPTH * (item.place - 1) + (HOP if item.home is not None else 0)
            if first <= slot:
                ends[slot] = item
                if item.place > 1:
                    inner[slot] = item
                todo.remove(item)
                break
        slot += 1
    for item in sorted(cut, key=lambda i: (i.place, i.key)):
        slot = 1 + DEPTH * (item.place - 1)
        if item.place > 1:
            while slot in inner:
                slot += 1
            inner[slot] = item
    return ends, inner


class Lane:
    def __init__(self, rows, cols, groups_here, towards_zero):
        self.rows, self.cols = rows, cols
        self.towards_zero = towards_zero
        self.items = []
        for r in range(rows):
            mine = [
                Item(r, piece, s, self.place((r + s) % rows // groups_here))
                for piece in range(PIECES)
                for s in range(STEPS)
            ]
            self.items.append([i for i in mine if i.place > 0])
        self.away = []
        self.lines = [line_slots(items, []) for items in self.items]
        if rows % 2 == 0 and cols > 3:
            for r in range(rows // 2):
                self.balance(r, r + rows // 2)
                self.balance(r + rows // 2, r)
        self.rounds = max(
            [max(ends, default=0) for ends, _ in self.lines] + [max(inner, default=0) - DEPTH for _, inner in self.lines]
        )

    def place(self, c):
        return c if self.towards_zero else self.cols - 1 - c

    col = place

    def balance(self, r, other):
        if len(self.items[r]) < len(self.items[other]) or any(i.row == other for i in self.away):
            return
        places = sorted({i.place for i in self.items[r]})
        best = None
        for counts in itertools.product(range(3), repeat=len(places)):
            gone = []
            for place, count in zip(places, counts):
                here = [i for i in self.items[r] if i.place == place]
                here.sort(key=lambda i: i.key, reverse=True)
                gone += here[:count]
            visitors = [Item(other, i.piece, i.s, i.place, home=r) for i in gone]
            mine = line_slots([i for i in self.items[r] if i not in gone], gone)
            theirs = line_slots(self.items[other] + visitors, [])
            score = (
                max(max(mine[0], default=0), max(theirs[0], default=0)),
                len(gone),
                max([slot for slot, i in theirs[0].items() if i.home is not None], default=0),
            )
            if best is None or score < best[0]:
                best = score, gone, mine, theirs
        _, gone, mine, theirs = best
        self.away += gone
        if gone:
            self.lines[r], self.lines[other] = mine, theirs

    def sent(self, r, c, t):
        p = self.place(c)
        ends, inner = self.lines[r]
        if p == 0:
            return None
        item = ends.get(t) if p == 1 else inner.get(t + DEPTH * (p - 1))
        return item if item is not None and item.place >= p else None

    def pairs(self, t):
        found = []
        for r in range(self.rows):
            for c in range(self.cols):
                if self.sent(r, c, t) is not None:
                    found.append((r * self.cols + c, r * self.cols + self.col(self.place(c) - 1)))
        return found

    def arrival(self, r, c, key):
        p = self.place(c)
        for i in self.items[r]:
            if i.key != key or i.place <= p:
                continue
            ends, inner = self.lines[r]
            if p == 0 and i in self.away:
                for other, _ in self.lines:
                    for slot, v in other.items():
                        if v.home == r and v.key == key:
                            return slot, True
            for slot, v in (ends if p == 0 else inner).items():
                if v is i:
                    return slot - DEPTH * p, False
        return None


def lookup(values, device):
    known = [v for v in values if v is not None]
    if len(set(known)) <= 1:
        return known[0] if known else 0
    values = [known[0] if v is None else v for v in values]
    result = jnp.uint32(0)
    place = (device % 32).astype(jnp.uint32)
    for bit in range(max(values).bit_length()):
        ones = [v >> bit & 1 for v in values]
        words = [sum(b << i for i, b in enumerate(ones[at : at + 32])) for at in range(0, len(ones), 32)]
        word = jnp.uint32(words[0])
        for i, other in enumerate(words[1:], 1):
            word = jnp.where(device // 32 == i, jnp.uint32(other), word)
        result = result | (((word >> place) & jnp.uint32(1)) << jnp.uint32(bit))
    return result.astype(jnp.int32)


def relay_kernel(at, table, x, *refs):
    *sources, out = refs
    rows, width = out.shape

    @pl.when(table[at] == 0)
    def _():
        row = pl.multiple_of(table[at + 1] * rows, rows)
        col = pl.multiple_of(table[at + 2] * width, width)
        out[...] = x[pl.ds(row, rows), pl.ds(col, width)]

    for i, source in enumerate(sources):

        @pl.when(table[at] == i + 1)
        def _(source=source):
            out[...] = source[...]


def relay(at, table, x, sources):
    return pl.pallas_call(
        functools.partial(relay_kernel, at),
        out_shape=pltpu.VMEM(sources[0].shape, sources[0].dtype),
        in_specs=[pl.BlockSpec(memory_space=pltpu.SMEM)] + [VMEM] * (1 + len(sources)),
        out_specs=VMEM,
        compiler_params=pltpu.CompilerParams(vmem_limit_bytes=RELAY_LIMIT),
        cost_estimate=pl.CostEstimate(flops=0, bytes_accessed=0, transcendentals=0),
        name="relay",
    )(table, *[in_vmem(v) for v in (x, *sources)])


def in_vmem(value):
    return pltpu.with_memory_space_constraint(value, pltpu.VMEM)


VMEM = pl.BlockSpec(memory_space=pltpu.VMEM)


def window_kernel(at, table, *refs):
    blocks = refs[:STEPS]
    factor, twice, male, out = refs[STEPS:]
    group_size, width = blocks[0].shape
    for s, block in enumerate(blocks):
        rank = table[at + s]

        @pl.loop(0, group_size // ROW_TILE)
        def _(i, s=s, block=block, rank=rank):
            here = pl.ds(pl.multiple_of(i * ROW_TILE, ROW_TILE), ROW_TILE)
            rows = pl.ds(pl.multiple_of(s * group_size + i * ROW_TILE, ROW_TILE), ROW_TILE)
            to = pl.ds(pl.multiple_of(rank * group_size + i * ROW_TILE, ROW_TILE), ROW_TILE)
            for k in range(0, width, LANES):
                value = block[here, k : k + LANES].astype(jnp.float32) - twice[rows, :]
                out[to, k : k + LANES] = (value * factor[rows, :] * male[:, k : k + LANES]).astype(out.dtype)


def standardized_window(at, table, blocks, factor, twice, male):
    group_size, n = blocks[0].shape
    depth = STEPS * group_size
    return pl.pallas_call(
        functools.partial(window_kernel, at),
        out_shape=pltpu.VMEM((depth, n), jnp.bfloat16),
        in_specs=[pl.BlockSpec(memory_space=pltpu.SMEM)] + [VMEM] * (STEPS + 3),
        out_specs=VMEM,
        compiler_params=pltpu.CompilerParams(vmem_limit_bytes=VMEM_LIMIT),
        cost_estimate=pl.CostEstimate(flops=4 * depth * n, bytes_accessed=4 * depth * n, transcendentals=0),
        name="window",
    )(table, *[in_vmem(v) for v in (*blocks, factor, twice, male)])


def standardize(table, at, candidates, x, buffers, factor, twice, male, zx, columns, first, count):
    width = columns.stop - columns.start
    place, step = table[at], table[at + 1]

    def from_source(source, col):
        @pl.loop(0, count // ROW_TILE)
        def _(i):
            here = pl.ds(pl.multiple_of(first + i * ROW_TILE, ROW_TILE), ROW_TILE)
            to = pl.ds(pl.multiple_of(i * ROW_TILE, ROW_TILE), ROW_TILE)
            for k in range(0, width, LANES):
                lanes = pl.ds(pl.multiple_of(step * width + k, LANES), LANES)
                value = source[here, pl.ds(pl.multiple_of(col + k, LANES), LANES)].astype(jnp.float32)
                value = (value - twice[:, lanes]) * factor[:, lanes] * male[here, :]
                zx[to, columns.start + k : columns.start + k + LANES] = value.astype(zx.dtype)

    for number in candidates:
        if number >= 0:

            @pl.when(place == number)
            def _(number=number):
                from_source(buffers[number], 0)

        else:

            @pl.when(place < 0)
            def _():
                from_source(x, (-1 - place) * width)


def early_kernel(at, candidates, n_buffers, table, x, *refs):
    buffers = refs[:n_buffers]
    factor, twice, male, zy, total, zx = refs[n_buffers:]
    rows, depth = zx.shape
    width = depth // (STEPS - 1)
    for rank in range(STEPS - 1):
        columns = slice(rank * width, (rank + 1) * width)
        standardize(table, at + 2 * rank, candidates[rank], x, buffers, factor, twice, male, zx, columns, 0, rows)

    @pl.loop(0, rows // ROW_BLOCK)
    def _(i):
        block = pl.ds(pl.multiple_of(i * ROW_BLOCK, ROW_BLOCK), ROW_BLOCK)
        for j in range(0, total.shape[1], COL_TILE):
            right = zy[:depth, j : j + COL_TILE]
            total[block, j : j + COL_TILE] = jnp.dot(zx[block, :], right, preferred_element_type=jnp.float32)


def early_product(at, candidates, table, x, buffers, factor, twice, male, zy):
    rows, (depth, n) = x.shape[0], zy.shape
    depth = depth // STEPS * (STEPS - 1)
    args = [in_vmem(v) for v in (x, *buffers, factor, twice, male, zy)]
    return pl.pallas_call(
        functools.partial(early_kernel, at, candidates, len(buffers)),
        out_shape=pltpu.VMEM((rows, n), jnp.float32),
        in_specs=[pl.BlockSpec(memory_space=pltpu.SMEM)] + [VMEM] * len(args),
        out_specs=VMEM,
        scratch_shapes=[pltpu.VMEM((rows, depth), jnp.bfloat16)],
        compiler_params=pltpu.CompilerParams(vmem_limit_bytes=VMEM_LIMIT),
        cost_estimate=pl.CostEstimate(flops=2 * rows * depth * n, bytes_accessed=0, transcendentals=0),
        name="early",
    )(table, *args)


def last_kernel(at, candidates, scale, n_buffers, table, x, *refs):
    buffers = refs[:n_buffers]
    factor, twice, male, zy, total, out, zx, blocks, sems = refs[n_buffers:]
    rows, n = total.shape
    width = zx.shape[1]

    def copy(i):
        return pltpu.make_async_copy(blocks.at[i % 2], out.at[pl.ds(i * ROW_BLOCK, ROW_BLOCK), :], sems.at[i % 2])

    count = rows // ROW_BLOCK
    for i in range(count):
        first = i * ROW_BLOCK
        standardize(
            table, at, candidates, x, buffers, factor, twice, male, zx, slice(0, width), first, ROW_BLOCK
        )
        if i >= 2:
            copy(i - 2).wait()
        for j in range(0, n, COL_TILE):
            right = zy[zy.shape[0] - width :, j : j + COL_TILE]
            product = jnp.dot(zx[...], right, preferred_element_type=jnp.float32)
            product = product + total[first : first + ROW_BLOCK, j : j + COL_TILE]
            blocks[i % 2, :, j : j + COL_TILE] = (product * scale).astype(blocks.dtype)
        copy(i).start()
    for i in range(max(count - 2, 0), count):
        copy(i).wait()


def last_product(at, candidates, table, x, buffers, factor, twice, male, zy, total):
    rows, (depth, n) = x.shape[0], zy.shape
    width = depth // STEPS
    scale = float(1.0 / np.sqrt(np.float32(depth)))
    args = [in_vmem(v) for v in (x, *buffers, factor, twice, male, zy, total)]
    return pl.pallas_call(
        functools.partial(last_kernel, at, candidates, scale, len(buffers)),
        out_shape=jax.ShapeDtypeStruct((rows, n), jnp.bfloat16),
        in_specs=[pl.BlockSpec(memory_space=pltpu.SMEM)] + [VMEM] * len(args),
        out_specs=pl.BlockSpec(memory_space=pl.ANY),
        scratch_shapes=[
            pltpu.VMEM((ROW_BLOCK, width), jnp.bfloat16),
            pltpu.VMEM((2, ROW_BLOCK, n), jnp.bfloat16),
            pltpu.SemaphoreType.DMA((2,)),
        ],
        compiler_params=pltpu.CompilerParams(vmem_limit_bytes=VMEM_LIMIT),
        cost_estimate=pl.CostEstimate(flops=2 * rows * width * n, bytes_accessed=2 * rows * n, transcendentals=0),
        name="last",
    )(table, *args)


def local(rows, cols, x, y, freq, weight, sex_rows, sex_cols):
    group_size = y.shape[0]
    local_vars = x.shape[1]
    groups_here = local_vars // group_size
    piece_rows = x.shape[0] // PIECES
    lanes = [Lane(rows, cols, groups_here, towards) for towards in (True, False)]
    rounds = max(lane.rounds for lane in lanes)
    devices = [(r, c) for r in range(rows) for c in range(cols)]
    both = ("row", "col")

    row_place = lax.axis_index("row")
    col_place = lax.axis_index("col")
    device = row_place * cols + col_place

    def number(r, c):
        return r * cols + c

    def group_here(item):
        return (item.owner + item.s) % rows % groups_here

    crossings = []
    crossing_of = {}
    for d, lane in enumerate(lanes):
        for r in range(rows):
            for slot, item in sorted(lane.lines[r][0].items()):
                if item.home is None:
                    continue
                source, target = (item.home, lane.col(item.place)), (r, lane.col(item.place))
                for k, crossing in enumerate(crossings):
                    if source not in crossing and target not in [to for to, _ in crossing.values()]:
                        break
                else:
                    k = len(crossings)
                    crossings.append({})
                crossings[k][source] = (target, item)
                crossing_of[d, r, item.key] = k

    def lane_of(phase, r):
        return (r + phase) % 2

    sends = [(phase, t) for t in range(1, rounds + 1) for phase in range(2)]
    pairs_of, kinds_of, own_of = {}, {}, {}
    for phase, t in sends:
        pairs, kinds, own = [], [], []
        for r, c in devices:
            lane = lanes[lane_of(phase, r)]
            item = lane.sent(r, c, t)
            if item is not None:
                pairs.append((number(r, c), number(r, lane.col(lane.place(c) - 1))))
            if item is None:
                kinds.append(None)
            elif item.place != lane.place(c):
                kinds.append("forward")
            elif item.home is not None:
                kinds.append(crossing_of[lane_of(phase, r), r, item.key])
            else:
                kinds.append("own")
            own.append(item if kinds[-1] == "own" else None)
        pairs_of[phase, t], kinds_of[phase, t], own_of[phase, t] = pairs, kinds, own

    returns = {}
    for t in range(1, rounds + 1):
        pairs, phases = [], [None] * len(devices)
        for d, lane in enumerate(lanes):
            for r in range(rows):
                item = lane.lines[r][0].get(t)
                if item is not None and item.home is not None:
                    pairs.append((number(r, lane.col(0)), number(item.home, lane.col(0))))
                    phases[pairs[-1][0]] = (r + d) % 2
        if pairs:
            returns[t] = pairs, phases

    columns = []

    def add(entries):
        columns.append(np.asarray(entries, np.int32))
        return sum(c.shape[1] for c in columns[:-1])

    relays = {}
    for key in sends:
        kinds = kinds_of[key]
        names = sorted(set(kinds) - {None, "own"}, key=str)
        if names and (len(names) > 1 or "own" in kinds):
            entries = []
            for kind, item in zip(kinds, own_of[key]):
                if kind == "own":
                    entries.append((0, item.piece, group_here(item)))
                else:
                    entries.append((1 + names.index(kind) if kind is not None else 1, 0, 0))
            relays[key] = names, add(entries)
    for t, (pairs, phases) in returns.items():
        if len(set(phases) - {None}) > 1:
            relays["back", t] = None, add([(1 + (p or 0), 0, 0) for p in phases])

    order = []
    for r, c in devices:
        arrivals = []
        for s in range(STEPS):
            when, key = 0, -1 - (r + s) % rows % groups_here
            for d, lane in enumerate(lanes):
                arrival = lane.arrival(r, c, (0, s))
                if arrival is not None:
                    t, returned = arrival
                    when, key = (t + 0.7, ("back", t)) if returned else (t, ((r + d) % 2, t))
            arrivals.append((when, s, key))
        order.append(sorted(arrivals, key=lambda a: a[:2]))
    rank_at = add([[[a[1] for a in arrivals].index(s) for s in range(STEPS)] for arrivals in order])
    used, candidates, source_at = [], [], []
    for ranks in (range(STEPS - 1), range(STEPS - 1, STEPS)):
        keys = {arrivals[k][2] for arrivals in order for k in ranks}
        used.append(sorted((k for k in keys if isinstance(k, tuple)), key=lambda k: (k[1], str(k[0]))))
        places = [
            [arrivals[k][2] if isinstance(arrivals[k][2], int) else used[-1].index(arrivals[k][2]) for k in ranks]
            for arrivals in order
        ]
        candidates.append([sorted({max(p[i], -1) for p in places}) for i in range(len(ranks))])
        source_at.append(
            add([[n for p, k in zip(row, ranks) for n in (p, arrivals[k][1])] for row, arrivals in zip(places, order)])
        )
    table = np.concatenate(columns, axis=1)
    table = lax.dynamic_slice(jnp.asarray(table), (device, 0), (1, table.shape[1]))[0]

    def own_chunk(items, x=x):
        piece = lookup([None if i is None else i.piece for i in items], device)
        group = lookup([None if i is None else group_here(i) for i in items], device)
        return lax.dynamic_slice(x, (piece * piece_rows, group * group_size), (piece_rows, group_size))

    factor = weight / jnp.sqrt(2.0 * freq * (1.0 - freq))
    twice = 2.0 * freq
    male_scale = np.float32(np.sqrt(0.5))
    male_rows = jnp.where(sex_rows > 0, male_scale, np.float32(1.0))
    male_cols = jnp.where(sex_cols > 0, male_scale, np.float32(1.0))
    wide = lambda value: jnp.broadcast_to(value[:, None], (value.shape[0], LANES))

    def in_window(value):
        span = STEPS * group_size
        return lax.dynamic_slice(jnp.concatenate([value, value]), (row_place * group_size,), (span,))

    window_factor, window_twice = in_window(factor), in_window(twice)
    male_wide = wide(male_rows)

    def own_squares():
        here = lambda value: lax.dynamic_slice(value, (col_place * local_vars,), (local_vars,))[None, :]
        zx = ((x.astype(jnp.float32) - here(twice)) * here(factor) * male_rows[:, None]).astype(jnp.bfloat16)
        return jnp.sum(jnp.square(zx.astype(jnp.float32)), axis=1)

    back = [(i, (i - 1) % rows) for i in range(rows)]
    window = [y]
    while len(window) < STEPS:
        window.append(lax.ppermute(window[-1], "row", back))
    squares = own_squares()

    starts = {}
    if any(own_of[1, 1]):
        starts[1, 1] = own_chunk(own_of[1, 1])
    later_x = x
    for k, crossing in enumerate(crossings):
        later_x = lax.optimization_barrier(later_x)
        starts["cross", k] = own_chunk([crossing[rc][1] if rc in crossing else None for rc in devices], later_x)
    later_x, squares = lax.optimization_barrier((later_x, squares))
    if any(own_of[0, 1]):
        starts[0, 1] = own_chunk(own_of[0, 1], later_x)
    bits = [1 << k for k in range(cols.bit_length() - 1)] if cols & (cols - 1) == 0 else []
    if cols & (cols - 1):
        squares = lax.psum(squares, "col")

    def sum_beside(value, squares):
        if not bits:
            return value, squares
        bit = bits.pop(0)
        other = lax.ppermute(squares, "col", [(i, i ^ bit) for i in range(cols)])
        value, other = lax.optimization_barrier((value, other))
        return value, squares + other

    buffers, crossed = {}, {}

    def bring_back(t):
        if t in returns:
            pairs, phases = returns[t]
            if ("back", t) in relays:
                held = relay(relays["back", t][1], table, x, [buffers[0, t], buffers[1, t]])
            else:
                held = buffers[next(p for p in phases if p is not None), t]
            buffers["back", t] = lax.ppermute(held, both, pairs)

    for key in sends:
        phase, t = key
        if pairs_of[key]:
            if key in relays:
                names, at = relays[key]
                sources = [buffers[phase, t - DEPTH] if name == "forward" else crossed[name] for name in names]
                held = relay(at, table, x, sources)
            elif key in starts:
                held = starts[key]
            elif "forward" in kinds_of[key]:
                held = buffers[phase, t - DEPTH]
            elif "own" in kinds_of[key]:
                held = own_chunk(own_of[key])
            else:
                held = crossed[next(k for k in kinds_of[key] if k is not None)]
            buffers[key] = lax.ppermute(held, both, pairs_of[key])
        if key == (0, 1):
            for k, crossing in enumerate(crossings):
                pairs = [(number(*rc), number(*to)) for rc, (to, _) in crossing.items()]
                crossed[k] = lax.ppermute(starts["cross", k], both, pairs)
        if phase == 1:
            bring_back(t - 1)
    bring_back(rounds)
    zy = standardized_window(rank_at, table, window, wide(window_factor), wide(window_twice), male_cols[None, :])
    zy, squares = sum_beside(zy, squares)
    shared = window_factor[None, :], window_twice[None, :], male_wide, zy
    total = early_product(source_at[0], candidates[0], table, x, [buffers[k] for k in used[0]], *shared)
    total, squares = sum_beside(total, squares)
    relation = last_product(source_at[1], candidates[1][0], table, x, [buffers[k] for k in used[1]], *shared, total)
    for bit in bits:
        squares = squares + lax.ppermute(squares, "col", [(i, i ^ bit) for i in range(cols)])
    inbreeding = squares / jnp.float32(freq.shape[0]) - 1.0
    return relation, inbreeding


def solution(mesh):
    rows, cols = mesh.shape["row"], mesh.shape["col"]
    return jax.shard_map(
        functools.partial(local, rows, cols),
        mesh=mesh,
        in_specs=(P("row", "col"), P("row", "col"), P(), P(), P("row"), P("col")),
        out_specs=(P("row", "col"), P("row")),
        check_vma=False,
    )
```

```python
import functools
import itertools

import jax
import jax.numpy as jnp
import numpy as np
from jax import lax
from jax.experimental import pallas as pl
from jax.experimental.pallas import tpu as pltpu
from jax.sharding import PartitionSpec as P

STEPS = 4
PIECES = 1
DEPTH = 1
HOP = 1
COL_TILE = 512
ROW_BLOCK = 512
ROW_TILE = 32
LANES = 128
VMEM_LIMIT = 10 * 2**20
RELAY_LIMIT = 2 * 2**20


class Item:
    def __init__(self, row, piece, s, place, home=None):
        self.row, self.piece, self.s, self.place = row, piece, s, place
        self.home = home

    @property
    def owner(self):
        return self.row if self.home is None else self.home

    @property
    def key(self):
        return self.piece, self.s


def line_slots(items, cut):
    ends, inner = {}, {}
    todo = sorted(items, key=lambda i: (i.home is None, i.piece, i.place, i.s))
    slot = 1
    while todo:
        for item in todo:
            first = 1 + DEPTH * (item.place - 1) + (HOP if item.home is not None else 0)
            if first <= slot:
                ends[slot] = item
                if item.place > 1:
                    inner[slot] = item
                todo.remove(item)
                break
        slot += 1
    for item in sorted(cut, key=lambda i: (i.place, i.key)):
        slot = 1 + DEPTH * (item.place - 1)
        if item.place > 1:
            while slot in inner:
                slot += 1
            inner[slot] = item
    return ends, inner


class Lane:
    def __init__(self, rows, cols, groups_here, towards_zero):
        self.rows, self.cols = rows, cols
        self.towards_zero = towards_zero
        self.items = []
        for r in range(rows):
            mine = [
                Item(r, piece, s, self.place((r + s) % rows // groups_here))
                for piece in range(PIECES)
                for s in range(STEPS)
            ]
            self.items.append([i for i in mine if i.place > 0])
        self.away = []
        self.lines = [line_slots(items, []) for items in self.items]
        if rows % 2 == 0 and cols > 3:
            for r in range(rows // 2):
                self.balance(r, r + rows // 2)
                self.balance(r + rows // 2, r)
        self.rounds = max(
            [max(ends, default=0) for ends, _ in self.lines] + [max(inner, default=0) - DEPTH for _, inner in self.lines]
        )

    def place(self, c):
        return c if self.towards_zero else self.cols - 1 - c

    col = place

    def balance(self, r, other):
        if len(self.items[r]) < len(self.items[other]) or any(i.row == other for i in self.away):
            return
        places = sorted({i.place for i in self.items[r]})
        best = None
        for counts in itertools.product(range(3), repeat=len(places)):
            gone = []
            for place, count in zip(places, counts):
                here = [i for i in self.items[r] if i.place == place]
                here.sort(key=lambda i: i.key, reverse=True)
                gone += here[:count]
            visitors = [Item(other, i.piece, i.s, i.place, home=r) for i in gone]
            mine = line_slots([i for i in self.items[r] if i not in gone], gone)
            theirs = line_slots(self.items[other] + visitors, [])
            score = (
                max(max(mine[0], default=0), max(theirs[0], default=0)),
                len(gone),
                max([slot for slot, i in theirs[0].items() if i.home is not None], default=0),
            )
            if best is None or score < best[0]:
                best = score, gone, mine, theirs
        _, gone, mine, theirs = best
        self.away += gone
        if gone:
            self.lines[r], self.lines[other] = mine, theirs

    def sent(self, r, c, t):
        p = self.place(c)
        ends, inner = self.lines[r]
        if p == 0:
            return None
        item = ends.get(t) if p == 1 else inner.get(t + DEPTH * (p - 1))
        return item if item is not None and item.place >= p else None

    def pairs(self, t):
        found = []
        for r in range(self.rows):
            for c in range(self.cols):
                if self.sent(r, c, t) is not None:
                    found.append((r * self.cols + c, r * self.cols + self.col(self.place(c) - 1)))
        return found

    def arrival(self, r, c, key):
        p = self.place(c)
        for i in self.items[r]:
            if i.key != key or i.place <= p:
                continue
            ends, inner = self.lines[r]
            if p == 0 and i in self.away:
                for other, _ in self.lines:
                    for slot, v in other.items():
                        if v.home == r and v.key == key:
                            return slot, True
            for slot, v in (ends if p == 0 else inner).items():
                if v is i:
                    return slot - DEPTH * p, False
        return None


def lookup(values, device):
    known = [v for v in values if v is not None]
    if len(set(known)) <= 1:
        return known[0] if known else 0
    values = [known[0] if v is None else v for v in values]
    result = jnp.uint32(0)
    place = (device % 32).astype(jnp.uint32)
    for bit in range(max(values).bit_length()):
        ones = [v >> bit & 1 for v in values]
        words = [sum(b << i for i, b in enumerate(ones[at : at + 32])) for at in range(0, len(ones), 32)]
        word = jnp.uint32(words[0])
        for i, other in enumerate(words[1:], 1):
            word = jnp.where(device // 32 == i, jnp.uint32(other), word)
        result = result | (((word >> place) & jnp.uint32(1)) << jnp.uint32(bit))
    return result.astype(jnp.int32)


def relay_kernel(at, table, x, *refs):
    *sources, out = refs
    rows, width = out.shape

    @pl.when(table[at] == 0)
    def _():
        row = pl.multiple_of(table[at + 1] * rows, rows)
        col = pl.multiple_of(table[at + 2] * width, width)
        out[...] = x[pl.ds(row, rows), pl.ds(col, width)]

    for i, source in enumerate(sources):

        @pl.when(table[at] == i + 1)
        def _(source=source):
            out[...] = source[...]


def relay(at, table, x, sources):
    return pl.pallas_call(
        functools.partial(relay_kernel, at),
        out_shape=pltpu.VMEM(sources[0].shape, sources[0].dtype),
        in_specs=[pl.BlockSpec(memory_space=pltpu.SMEM)] + [VMEM] * (1 + len(sources)),
        out_specs=VMEM,
        compiler_params=pltpu.CompilerParams(vmem_limit_bytes=RELAY_LIMIT),
        cost_estimate=pl.CostEstimate(flops=0, bytes_accessed=0, transcendentals=0),
        name="relay",
    )(table, *[in_vmem(v) for v in (x, *sources)])


def in_vmem(value):
    return pltpu.with_memory_space_constraint(value, pltpu.VMEM)


VMEM = pl.BlockSpec(memory_space=pltpu.VMEM)


def window_kernel(at, table, *refs):
    blocks = refs[:STEPS]
    factor, twice, male, out = refs[STEPS:]
    group_size, width = blocks[0].shape
    for s, block in enumerate(blocks):
        rank = table[at + s]

        @pl.loop(0, group_size // ROW_TILE)
        def _(i, s=s, block=block, rank=rank):
            here = pl.ds(pl.multiple_of(i * ROW_TILE, ROW_TILE), ROW_TILE)
            rows = pl.ds(pl.multiple_of(s * group_size + i * ROW_TILE, ROW_TILE), ROW_TILE)
            to = pl.ds(pl.multiple_of(rank * group_size + i * ROW_TILE, ROW_TILE), ROW_TILE)
            for k in range(0, width, LANES):
                value = block[here, k : k + LANES].astype(jnp.float32) - twice[rows, :]
                out[to, k : k + LANES] = (value * factor[rows, :] * male[:, k : k + LANES]).astype(out.dtype)


def standardized_window(at, table, blocks, factor, twice, male):
    group_size, n = blocks[0].shape
    depth = STEPS * group_size
    return pl.pallas_call(
        functools.partial(window_kernel, at),
        out_shape=pltpu.VMEM((depth, n), jnp.bfloat16),
        in_specs=[pl.BlockSpec(memory_space=pltpu.SMEM)] + [VMEM] * (STEPS + 3),
        out_specs=VMEM,
        compiler_params=pltpu.CompilerParams(vmem_limit_bytes=VMEM_LIMIT),
        cost_estimate=pl.CostEstimate(flops=4 * depth * n, bytes_accessed=4 * depth * n, transcendentals=0),
        name="window",
    )(table, *[in_vmem(v) for v in (*blocks, factor, twice, male)])


def standardize(table, at, candidates, x, buffers, factor, twice, male, zx, columns, first, count):
    width = columns.stop - columns.start
    place, step = table[at], table[at + 1]

    def from_source(source, col):
        @pl.loop(0, count // ROW_TILE)
        def _(i):
            here = pl.ds(pl.multiple_of(first + i * ROW_TILE, ROW_TILE), ROW_TILE)
            to = pl.ds(pl.multiple_of(i * ROW_TILE, ROW_TILE), ROW_TILE)
            for k in range(0, width, LANES):
                lanes = pl.ds(pl.multiple_of(step * width + k, LANES), LANES)
                value = source[here, pl.ds(pl.multiple_of(col + k, LANES), LANES)].astype(jnp.float32)
                value = (value - twice[:, lanes]) * factor[:, lanes] * male[here, :]
                zx[to, columns.start + k : columns.start + k + LANES] = value.astype(zx.dtype)

    for number in candidates:
        if number >= 0:

            @pl.when(place == number)
            def _(number=number):
                from_source(buffers[number], 0)

        else:

            @pl.when(place < 0)
            def _():
                from_source(x, (-1 - place) * width)


def early_kernel(at, candidates, n_buffers, table, x, *refs):
    buffers = refs[:n_buffers]
    factor, twice, male, zy, total, zx = refs[n_buffers:]
    rows, depth = zx.shape
    width = depth // (STEPS - 1)
    for rank in range(STEPS - 1):
        columns = slice(rank * width, (rank + 1) * width)
        standardize(table, at + 2 * rank, candidates[rank], x, buffers, factor, twice, male, zx, columns, 0, rows)

    @pl.loop(0, rows // ROW_BLOCK)
    def _(i):
        block = pl.ds(pl.multiple_of(i * ROW_BLOCK, ROW_BLOCK), ROW_BLOCK)
        for j in range(0, total.shape[1], COL_TILE):
            right = zy[:depth, j : j + COL_TILE]
            total[block, j : j + COL_TILE] = jnp.dot(zx[block, :], right, preferred_element_type=jnp.float32)


def early_product(at, candidates, table, x, buffers, factor, twice, male, zy):
    rows, (depth, n) = x.shape[0], zy.shape
    depth = depth // STEPS * (STEPS - 1)
    args = [in_vmem(v) for v in (x, *buffers, factor, twice, male, zy)]
    return pl.pallas_call(
        functools.partial(early_kernel, at, candidates, len(buffers)),
        out_shape=pltpu.VMEM((rows, n), jnp.float32),
        in_specs=[pl.BlockSpec(memory_space=pltpu.SMEM)] + [VMEM] * len(args),
        out_specs=VMEM,
        scratch_shapes=[pltpu.VMEM((rows, depth), jnp.bfloat16)],
        compiler_params=pltpu.CompilerParams(vmem_limit_bytes=VMEM_LIMIT),
        cost_estimate=pl.CostEstimate(flops=2 * rows * depth * n, bytes_accessed=0, transcendentals=0),
        name="early",
    )(table, *args)


def last_kernel(at, candidates, scale, n_buffers, table, x, *refs):
    buffers = refs[:n_buffers]
    factor, twice, male, zy, total, out, zx, blocks, sems = refs[n_buffers:]
    rows, n = total.shape
    width = zx.shape[1]

    def copy(i):
        return pltpu.make_async_copy(blocks.at[i % 2], out.at[pl.ds(i * ROW_BLOCK, ROW_BLOCK), :], sems.at[i % 2])

    count = rows // ROW_BLOCK
    for i in range(count):
        first = i * ROW_BLOCK
        standardize(
            table, at, candidates, x, buffers, factor, twice, male, zx, slice(0, width), first, ROW_BLOCK
        )
        if i >= 2:
            copy(i - 2).wait()
        for j in range(0, n, COL_TILE):
            right = zy[zy.shape[0] - width :, j : j + COL_TILE]
            product = jnp.dot(zx[...], right, preferred_element_type=jnp.float32)
            product = product + total[first : first + ROW_BLOCK, j : j + COL_TILE]
            blocks[i % 2, :, j : j + COL_TILE] = (product * scale).astype(blocks.dtype)
        copy(i).start()
    for i in range(max(count - 2, 0), count):
        copy(i).wait()


def last_product(at, candidates, table, x, buffers, factor, twice, male, zy, total):
    rows, (depth, n) = x.shape[0], zy.shape
    width = depth // STEPS
    scale = float(1.0 / np.sqrt(np.float32(depth)))
    args = [in_vmem(v) for v in (x, *buffers, factor, twice, male, zy, total)]
    return pl.pallas_call(
        functools.partial(last_kernel, at, candidates, scale, len(buffers)),
        out_shape=jax.ShapeDtypeStruct((rows, n), jnp.bfloat16),
        in_specs=[pl.BlockSpec(memory_space=pltpu.SMEM)] + [VMEM] * len(args),
        out_specs=pl.BlockSpec(memory_space=pl.ANY),
        scratch_shapes=[
            pltpu.VMEM((ROW_BLOCK, width), jnp.bfloat16),
            pltpu.VMEM((2, ROW_BLOCK, n), jnp.bfloat16),
            pltpu.SemaphoreType.DMA((2,)),
        ],
        compiler_params=pltpu.CompilerParams(vmem_limit_bytes=VMEM_LIMIT),
        cost_estimate=pl.CostEstimate(flops=2 * rows * width * n, bytes_accessed=2 * rows * n, transcendentals=0),
        name="last",
    )(table, *args)


def local(rows, cols, x, y, freq, weight, sex_rows, sex_cols):
    group_size = y.shape[0]
    local_vars = x.shape[1]
    groups_here = local_vars // group_size
    piece_rows = x.shape[0] // PIECES
    lanes = [Lane(rows, cols, groups_here, towards) for towards in (True, False)]
    rounds = max(lane.rounds for lane in lanes)
    devices = [(r, c) for r in range(rows) for c in range(cols)]
    both = ("row", "col")

    row_place = lax.axis_index("row")
    col_place = lax.axis_index("col")
    device = row_place * cols + col_place

    def number(r, c):
        return r * cols + c

    def group_here(item):
        return (item.owner + item.s) % rows % groups_here

    crossings = []
    crossing_of = {}
    for d, lane in enumerate(lanes):
        for r in range(rows):
            for slot, item in sorted(lane.lines[r][0].items()):
                if item.home is None:
                    continue
                source, target = (item.home, lane.col(item.place)), (r, lane.col(item.place))
                for k, crossing in enumerate(crossings):
                    if source not in crossing and target not in [to for to, _ in crossing.values()]:
                        break
                else:
                    k = len(crossings)
                    crossings.append({})
                crossings[k][source] = (target, item)
                crossing_of[d, r, item.key] = k

    def lane_of(phase, r):
        return (r + phase) % 2

    sends = [(phase, t) for t in range(1, rounds + 1) for phase in range(2)]
    pairs_of, kinds_of, own_of = {}, {}, {}
    for phase, t in sends:
        pairs, kinds, own = [], [], []
        for r, c in devices:
            lane = lanes[lane_of(phase, r)]
            item = lane.sent(r, c, t)
            if item is not None:
                pairs.append((number(r, c), number(r, lane.col(lane.place(c) - 1))))
            if item is None:
                kinds.append(None)
            elif item.place != lane.place(c):
                kinds.append("forward")
            elif item.home is not None:
                kinds.append(crossing_of[lane_of(phase, r), r, item.key])
            else:
                kinds.append("own")
            own.append(item if kinds[-1] == "own" else None)
        pairs_of[phase, t], kinds_of[phase, t], own_of[phase, t] = pairs, kinds, own

    returns = {}
    for t in range(1, rounds + 1):
        pairs, phases = [], [None] * len(devices)
        for d, lane in enumerate(lanes):
            for r in range(rows):
                item = lane.lines[r][0].get(t)
                if item is not None and item.home is not None:
                    pairs.append((number(r, lane.col(0)), number(item.home, lane.col(0))))
                    phases[pairs[-1][0]] = (r + d) % 2
        if pairs:
            returns[t] = pairs, phases

    columns = []

    def add(entries):
        columns.append(np.asarray(entries, np.int32))
        return sum(c.shape[1] for c in columns[:-1])

    relays = {}
    for key in sends:
        kinds = kinds_of[key]
        names = sorted(set(kinds) - {None, "own"}, key=str)
        if names and (len(names) > 1 or "own" in kinds):
            entries = []
            for kind, item in zip(kinds, own_of[key]):
                if kind == "own":
                    entries.append((0, item.piece, group_here(item)))
                else:
                    entries.append((1 + names.index(kind) if kind is not None else 1, 0, 0))
            relays[key] = names, add(entries)
    for t, (pairs, phases) in returns.items():
        if len(set(phases) - {None}) > 1:
            relays["back", t] = None, add([(1 + (p or 0), 0, 0) for p in phases])

    order = []
    for r, c in devices:
        arrivals = []
        for s in range(STEPS):
            when, key = 0, -1 - (r + s) % rows % groups_here
            for d, lane in enumerate(lanes):
                arrival = lane.arrival(r, c, (0, s))
                if arrival is not None:
                    t, returned = arrival
                    when, key = (t + 0.7, ("back", t)) if returned else (t, ((r + d) % 2, t))
            arrivals.append((when, s, key))
        order.append(sorted(arrivals, key=lambda a: a[:2]))
    rank_at = add([[[a[1] for a in arrivals].index(s) for s in range(STEPS)] for arrivals in order])
    used, candidates, source_at = [], [], []
    for ranks in (range(STEPS - 1), range(STEPS - 1, STEPS)):
        keys = {arrivals[k][2] for arrivals in order for k in ranks}
        used.append(sorted((k for k in keys if isinstance(k, tuple)), key=lambda k: (k[1], str(k[0]))))
        places = [
            [arrivals[k][2] if isinstance(arrivals[k][2], int) else used[-1].index(arrivals[k][2]) for k in ranks]
            for arrivals in order
        ]
        candidates.append([sorted({max(p[i], -1) for p in places}) for i in range(len(ranks))])
        source_at.append(
            add([[n for p, k in zip(row, ranks) for n in (p, arrivals[k][1])] for row, arrivals in zip(places, order)])
        )
    table = np.concatenate(columns, axis=1)
    table = lax.dynamic_slice(jnp.asarray(table), (device, 0), (1, table.shape[1]))[0]

    def own_chunk(items, x=x):
        piece = lookup([None if i is None else i.piece for i in items], device)
        group = lookup([None if i is None else group_here(i) for i in items], device)
        return lax.dynamic_slice(x, (piece * piece_rows, group * group_size), (piece_rows, group_size))

    factor = weight / jnp.sqrt(2.0 * freq * (1.0 - freq))
    twice = 2.0 * freq
    male_scale = np.float32(np.sqrt(0.5))
    male_rows = jnp.where(sex_rows > 0, male_scale, np.float32(1.0))
    male_cols = jnp.where(sex_cols > 0, male_scale, np.float32(1.0))
    wide = lambda value: jnp.broadcast_to(value[:, None], (value.shape[0], LANES))

    def in_window(value):
        span = STEPS * group_size
        return lax.dynamic_slice(jnp.concatenate([value, value]), (row_place * group_size,), (span,))

    window_factor, window_twice = in_window(factor), in_window(twice)
    male_wide = wide(male_rows)

    def own_squares():
        here = lambda value: lax.dynamic_slice(value, (col_place * local_vars,), (local_vars,))[None, :]
        zx = ((x.astype(jnp.float32) - here(twice)) * here(factor) * male_rows[:, None]).astype(jnp.bfloat16)
        return jnp.sum(jnp.square(zx.astype(jnp.float32)), axis=1)

    back = [(i, (i - 1) % rows) for i in range(rows)]
    window = [y]
    while len(window) < STEPS:
        window.append(lax.ppermute(window[-1], "row", back))
    squares = own_squares()

    starts = {}
    later_x = x
    for phase in (1, 0):
        if any(own_of[phase, 1]):
            starts[phase, 1] = own_chunk(own_of[phase, 1], later_x)
        later_x = lax.optimization_barrier(later_x)
    later_x, squares = lax.optimization_barrier((later_x, squares))
    for k, crossing in enumerate(crossings):
        starts["cross", k] = own_chunk([crossing[rc][1] if rc in crossing else None for rc in devices], later_x)
    bits = [1 << k for k in range(cols.bit_length() - 1)] if cols & (cols - 1) == 0 else []
    if cols & (cols - 1):
        squares = lax.psum(squares, "col")

    def sum_beside(value, squares):
        if not bits:
            return value, squares
        bit = bits.pop(0)
        other = lax.ppermute(squares, "col", [(i, i ^ bit) for i in range(cols)])
        value, other = lax.optimization_barrier((value, other))
        return value, squares + other

    buffers, crossed = {}, {}
    zy = None

    def window_product():
        return standardized_window(rank_at, table, window, wide(window_factor), wide(window_twice), male_cols[None, :])

    def bring_back(t):
        if t in returns:
            pairs, phases = returns[t]
            if ("back", t) in relays:
                held = relay(relays["back", t][1], table, x, [buffers[0, t], buffers[1, t]])
            else:
                held = buffers[next(p for p in phases if p is not None), t]
            buffers["back", t] = lax.ppermute(held, both, pairs)

    for key in sends:
        phase, t = key
        if pairs_of[key]:
            if key in relays:
                names, at = relays[key]
                sources = [buffers[phase, t - DEPTH] if name == "forward" else crossed[name] for name in names]
                held = relay(at, table, x, sources)
            elif key in starts:
                held = starts[key]
            elif "forward" in kinds_of[key]:
                held = buffers[phase, t - DEPTH]
            elif "own" in kinds_of[key]:
                held = own_chunk(own_of[key])
            else:
                held = crossed[next(k for k in kinds_of[key] if k is not None)]
            if key == (0, 3):
                while bits:
                    bit = bits.pop(0)
                    squares = squares + lax.ppermute(squares, "col", [(i, i ^ bit) for i in range(cols)])
                held, squares = lax.optimization_barrier((held, squares))
            buffers[key] = lax.ppermute(held, both, pairs_of[key])
        if key == (0, 1):
            for k, crossing in enumerate(crossings):
                pairs = [(number(*rc), number(*to)) for rc, (to, _) in crossing.items()]
                crossed[k] = lax.ppermute(starts["cross", k], both, pairs)
        if phase == 1:
            bring_back(t - 1)
    bring_back(rounds)
    if zy is None:
        zy = window_product()
    shared = window_factor[None, :], window_twice[None, :], male_wide, zy
    total = early_product(source_at[0], candidates[0], table, x, [buffers[k] for k in used[0]], *shared)
    relation = last_product(source_at[1], candidates[1][0], table, x, [buffers[k] for k in used[1]], *shared, total)
    for bit in bits:
        squares = squares + lax.ppermute(squares, "col", [(i, i ^ bit) for i in range(cols)])
    inbreeding = squares / jnp.float32(freq.shape[0]) - 1.0
    return relation, inbreeding


def solution(mesh):
    rows, cols = mesh.shape["row"], mesh.shape["col"]
    return jax.shard_map(
        functools.partial(local, rows, cols),
        mesh=mesh,
        in_specs=(P("row", "col"), P("row", "col"), P(), P(), P("row"), P("col")),
        out_specs=(P("row", "col"), P("row")),
        check_vma=False,
    )
```

```python
import functools
import itertools

import jax
import jax.numpy as jnp
import numpy as np
from jax import lax
from jax.experimental import pallas as pl
from jax.experimental.pallas import tpu as pltpu
from jax.sharding import PartitionSpec as P

STEPS = 4
PIECES = 1
DEPTH = 1
HOP = 1
COL_TILE = 512
ROW_BLOCK = 512
ROW_TILE = 32
LANES = 128
VMEM_LIMIT = 10 * 2**20
RELAY_LIMIT = 2 * 2**20


class Item:
    def __init__(self, row, piece, s, place, home=None):
        self.row, self.piece, self.s, self.place = row, piece, s, place
        self.home = home

    @property
    def owner(self):
        return self.row if self.home is None else self.home

    @property
    def key(self):
        return self.piece, self.s


def line_slots(items, cut):
    ends, inner = {}, {}
    todo = sorted(items, key=lambda i: (i.home is None, i.piece, i.place, i.s))
    slot = 1
    while todo:
        for item in todo:
            first = 1 + DEPTH * (item.place - 1) + (HOP if item.home is not None else 0)
            if first <= slot:
                ends[slot] = item
                if item.place > 1:
                    inner[slot] = item
                todo.remove(item)
                break
        slot += 1
    for item in sorted(cut, key=lambda i: (i.place, i.key)):
        slot = 1 + DEPTH * (item.place - 1)
        if item.place > 1:
            while slot in inner:
                slot += 1
            inner[slot] = item
    return ends, inner


class Lane:
    def __init__(self, rows, cols, groups_here, towards_zero):
        self.rows, self.cols = rows, cols
        self.towards_zero = towards_zero
        self.items = []
        for r in range(rows):
            mine = [
                Item(r, piece, s, self.place((r + s) % rows // groups_here))
                for piece in range(PIECES)
                for s in range(STEPS)
            ]
            self.items.append([i for i in mine if i.place > 0])
        self.away = []
        self.lines = [line_slots(items, []) for items in self.items]
        if rows % 2 == 0 and cols > 3:
            for r in range(rows // 2):
                self.balance(r, r + rows // 2)
                self.balance(r + rows // 2, r)
        self.rounds = max(
            [max(ends, default=0) for ends, _ in self.lines] + [max(inner, default=0) - DEPTH for _, inner in self.lines]
        )

    def place(self, c):
        return c if self.towards_zero else self.cols - 1 - c

    col = place

    def balance(self, r, other):
        if len(self.items[r]) < len(self.items[other]) or any(i.row == other for i in self.away):
            return
        places = sorted({i.place for i in self.items[r]})
        best = None
        for counts in itertools.product(range(3), repeat=len(places)):
            gone = []
            for place, count in zip(places, counts):
                here = [i for i in self.items[r] if i.place == place]
                here.sort(key=lambda i: i.key, reverse=True)
                gone += here[:count]
            visitors = [Item(other, i.piece, i.s, i.place, home=r) for i in gone]
            mine = line_slots([i for i in self.items[r] if i not in gone], gone)
            theirs = line_slots(self.items[other] + visitors, [])
            score = (
                max(max(mine[0], default=0), max(theirs[0], default=0)),
                len(gone),
                max([slot for slot, i in theirs[0].items() if i.home is not None], default=0),
            )
            if best is None or score < best[0]:
                best = score, gone, mine, theirs
        _, gone, mine, theirs = best
        self.away += gone
        if gone:
            self.lines[r], self.lines[other] = mine, theirs

    def sent(self, r, c, t):
        p = self.place(c)
        ends, inner = self.lines[r]
        if p == 0:
            return None
        item = ends.get(t) if p == 1 else inner.get(t + DEPTH * (p - 1))
        return item if item is not None and item.place >= p else None

    def pairs(self, t):
        found = []
        for r in range(self.rows):
            for c in range(self.cols):
                if self.sent(r, c, t) is not None:
                    found.append((r * self.cols + c, r * self.cols + self.col(self.place(c) - 1)))
        return found

    def arrival(self, r, c, key):
        p = self.place(c)
        for i in self.items[r]:
            if i.key != key or i.place <= p:
                continue
            ends, inner = self.lines[r]
            if p == 0 and i in self.away:
                for other, _ in self.lines:
                    for slot, v in other.items():
                        if v.home == r and v.key == key:
                            return slot, True
            for slot, v in (ends if p == 0 else inner).items():
                if v is i:
                    return slot - DEPTH * p, False
        return None


def lookup(values, device):
    known = [v for v in values if v is not None]
    if len(set(known)) <= 1:
        return known[0] if known else 0
    values = [known[0] if v is None else v for v in values]
    result = jnp.uint32(0)
    place = (device % 32).astype(jnp.uint32)
    for bit in range(max(values).bit_length()):
        ones = [v >> bit & 1 for v in values]
        words = [sum(b << i for i, b in enumerate(ones[at : at + 32])) for at in range(0, len(ones), 32)]
        word = jnp.uint32(words[0])
        for i, other in enumerate(words[1:], 1):
            word = jnp.where(device // 32 == i, jnp.uint32(other), word)
        result = result | (((word >> place) & jnp.uint32(1)) << jnp.uint32(bit))
    return result.astype(jnp.int32)


def relay_kernel(at, table, x, *refs):
    *sources, out = refs
    rows, width = out.shape

    @pl.when(table[at] == 0)
    def _():
        row = pl.multiple_of(table[at + 1] * rows, rows)
        col = pl.multiple_of(table[at + 2] * width, width)
        out[...] = x[pl.ds(row, rows), pl.ds(col, width)]

    for i, source in enumerate(sources):

        @pl.when(table[at] == i + 1)
        def _(source=source):
            out[...] = source[...]


def relay(at, table, x, sources):
    return pl.pallas_call(
        functools.partial(relay_kernel, at),
        out_shape=pltpu.VMEM(sources[0].shape, sources[0].dtype),
        in_specs=[pl.BlockSpec(memory_space=pltpu.SMEM)] + [VMEM] * (1 + len(sources)),
        out_specs=VMEM,
        compiler_params=pltpu.CompilerParams(vmem_limit_bytes=RELAY_LIMIT),
        cost_estimate=pl.CostEstimate(flops=0, bytes_accessed=0, transcendentals=0),
        name="relay",
    )(table, *[in_vmem(v) for v in (x, *sources)])


def in_vmem(value):
    return pltpu.with_memory_space_constraint(value, pltpu.VMEM)


VMEM = pl.BlockSpec(memory_space=pltpu.VMEM)


def window_kernel(at, table, *refs):
    blocks = refs[:STEPS]
    factor, twice, male, out = refs[STEPS:]
    group_size, width = blocks[0].shape
    for s, block in enumerate(blocks):
        rank = table[at + s]

        @pl.loop(0, group_size // ROW_TILE)
        def _(i, s=s, block=block, rank=rank):
            here = pl.ds(pl.multiple_of(i * ROW_TILE, ROW_TILE), ROW_TILE)
            rows = pl.ds(pl.multiple_of(s * group_size + i * ROW_TILE, ROW_TILE), ROW_TILE)
            to = pl.ds(pl.multiple_of(rank * group_size + i * ROW_TILE, ROW_TILE), ROW_TILE)
            for k in range(0, width, LANES):
                value = block[here, k : k + LANES].astype(jnp.float32) - twice[rows, :]
                out[to, k : k + LANES] = (value * factor[rows, :] * male[:, k : k + LANES]).astype(out.dtype)


def standardized_window(at, table, blocks, factor, twice, male):
    group_size, n = blocks[0].shape
    depth = STEPS * group_size
    return pl.pallas_call(
        functools.partial(window_kernel, at),
        out_shape=pltpu.VMEM((depth, n), jnp.bfloat16),
        in_specs=[pl.BlockSpec(memory_space=pltpu.SMEM)] + [VMEM] * (STEPS + 3),
        out_specs=VMEM,
        compiler_params=pltpu.CompilerParams(vmem_limit_bytes=VMEM_LIMIT),
        cost_estimate=pl.CostEstimate(flops=4 * depth * n, bytes_accessed=4 * depth * n, transcendentals=0),
        name="window",
    )(table, *[in_vmem(v) for v in (*blocks, factor, twice, male)])


def standardize(table, at, candidates, x, buffers, factor, twice, male, zx, columns, first, count):
    width = columns.stop - columns.start
    place, step = table[at], table[at + 1]

    def from_source(source, col):
        @pl.loop(0, count // ROW_TILE)
        def _(i):
            here = pl.ds(pl.multiple_of(first + i * ROW_TILE, ROW_TILE), ROW_TILE)
            to = pl.ds(pl.multiple_of(i * ROW_TILE, ROW_TILE), ROW_TILE)
            for k in range(0, width, LANES):
                lanes = pl.ds(pl.multiple_of(step * width + k, LANES), LANES)
                value = source[here, pl.ds(pl.multiple_of(col + k, LANES), LANES)].astype(jnp.float32)
                value = (value - twice[:, lanes]) * factor[:, lanes] * male[here, :]
                zx[to, columns.start + k : columns.start + k + LANES] = value.astype(zx.dtype)

    for number in candidates:
        if number >= 0:

            @pl.when(place == number)
            def _(number=number):
                from_source(buffers[number], 0)

        else:

            @pl.when(place < 0)
            def _():
                from_source(x, (-1 - place) * width)


def early_kernel(at, candidates, n_buffers, table, x, *refs):
    buffers = refs[:n_buffers]
    factor, twice, male, zy, total, zx = refs[n_buffers:]
    rows, depth = zx.shape
    width = depth // (STEPS - 1)
    for rank in range(STEPS - 1):
        columns = slice(rank * width, (rank + 1) * width)
        standardize(table, at + 2 * rank, candidates[rank], x, buffers, factor, twice, male, zx, columns, 0, rows)

    @pl.loop(0, rows // ROW_BLOCK)
    def _(i):
        block = pl.ds(pl.multiple_of(i * ROW_BLOCK, ROW_BLOCK), ROW_BLOCK)
        for j in range(0, total.shape[1], COL_TILE):
            right = zy[:depth, j : j + COL_TILE]
            total[block, j : j + COL_TILE] = jnp.dot(zx[block, :], right, preferred_element_type=jnp.float32)


def early_product(at, candidates, table, x, buffers, factor, twice, male, zy):
    rows, (depth, n) = x.shape[0], zy.shape
    depth = depth // STEPS * (STEPS - 1)
    args = [in_vmem(v) for v in (x, *buffers, factor, twice, male, zy)]
    return pl.pallas_call(
        functools.partial(early_kernel, at, candidates, len(buffers)),
        out_shape=pltpu.VMEM((rows, n), jnp.float32),
        in_specs=[pl.BlockSpec(memory_space=pltpu.SMEM)] + [VMEM] * len(args),
        out_specs=VMEM,
        scratch_shapes=[pltpu.VMEM((rows, depth), jnp.bfloat16)],
        compiler_params=pltpu.CompilerParams(vmem_limit_bytes=VMEM_LIMIT),
        cost_estimate=pl.CostEstimate(flops=2 * rows * depth * n, bytes_accessed=0, transcendentals=0),
        name="early",
    )(table, *args)


def last_kernel(at, candidates, scale, n_buffers, table, x, *refs):
    buffers = refs[:n_buffers]
    factor, twice, male, zy, total, out, zx, blocks, sems = refs[n_buffers:]
    rows, n = total.shape
    width = zx.shape[1]

    def copy(i):
        return pltpu.make_async_copy(blocks.at[i % 2], out.at[pl.ds(i * ROW_BLOCK, ROW_BLOCK), :], sems.at[i % 2])

    count = rows // ROW_BLOCK
    for i in range(count):
        first = i * ROW_BLOCK
        standardize(
            table, at, candidates, x, buffers, factor, twice, male, zx, slice(0, width), first, ROW_BLOCK
        )
        if i >= 2:
            copy(i - 2).wait()
        for j in range(0, n, COL_TILE):
            right = zy[zy.shape[0] - width :, j : j + COL_TILE]
            product = jnp.dot(zx[...], right, preferred_element_type=jnp.float32)
            product = product + total[first : first + ROW_BLOCK, j : j + COL_TILE]
            blocks[i % 2, :, j : j + COL_TILE] = (product * scale).astype(blocks.dtype)
        copy(i).start()
    for i in range(max(count - 2, 0), count):
        copy(i).wait()


def last_product(at, candidates, table, x, buffers, factor, twice, male, zy, total):
    rows, (depth, n) = x.shape[0], zy.shape
    width = depth // STEPS
    scale = float(1.0 / np.sqrt(np.float32(depth)))
    args = [in_vmem(v) for v in (x, *buffers, factor, twice, male, zy, total)]
    return pl.pallas_call(
        functools.partial(last_kernel, at, candidates, scale, len(buffers)),
        out_shape=jax.ShapeDtypeStruct((rows, n), jnp.bfloat16),
        in_specs=[pl.BlockSpec(memory_space=pltpu.SMEM)] + [VMEM] * len(args),
        out_specs=pl.BlockSpec(memory_space=pl.ANY),
        scratch_shapes=[
            pltpu.VMEM((ROW_BLOCK, width), jnp.bfloat16),
            pltpu.VMEM((2, ROW_BLOCK, n), jnp.bfloat16),
            pltpu.SemaphoreType.DMA((2,)),
        ],
        compiler_params=pltpu.CompilerParams(vmem_limit_bytes=VMEM_LIMIT),
        cost_estimate=pl.CostEstimate(flops=2 * rows * width * n, bytes_accessed=2 * rows * n, transcendentals=0),
        name="last",
    )(table, *args)


def local(rows, cols, x, y, freq, weight, sex_rows, sex_cols):
    group_size = y.shape[0]
    local_vars = x.shape[1]
    groups_here = local_vars // group_size
    piece_rows = x.shape[0] // PIECES
    lanes = [Lane(rows, cols, groups_here, towards) for towards in (True, False)]
    rounds = max(lane.rounds for lane in lanes)
    devices = [(r, c) for r in range(rows) for c in range(cols)]
    both = ("row", "col")

    row_place = lax.axis_index("row")
    col_place = lax.axis_index("col")
    device = row_place * cols + col_place

    def number(r, c):
        return r * cols + c

    def group_here(item):
        return (item.owner + item.s) % rows % groups_here

    crossings = []
    crossing_of = {}
    for d, lane in enumerate(lanes):
        for r in range(rows):
            for slot, item in sorted(lane.lines[r][0].items()):
                if item.home is None:
                    continue
                source, target = (item.home, lane.col(item.place)), (r, lane.col(item.place))
                for k, crossing in enumerate(crossings):
                    if source not in crossing and target not in [to for to, _ in crossing.values()]:
                        break
                else:
                    k = len(crossings)
                    crossings.append({})
                crossings[k][source] = (target, item)
                crossing_of[d, r, item.key] = k

    def lane_of(phase, r):
        return (r + phase) % 2

    sends = [(phase, t) for t in range(1, rounds + 1) for phase in range(2)]
    pairs_of, kinds_of, own_of = {}, {}, {}
    for phase, t in sends:
        pairs, kinds, own = [], [], []
        for r, c in devices:
            lane = lanes[lane_of(phase, r)]
            item = lane.sent(r, c, t)
            if item is not None:
                pairs.append((number(r, c), number(r, lane.col(lane.place(c) - 1))))
            if item is None:
                kinds.append(None)
            elif item.place != lane.place(c):
                kinds.append("forward")
            elif item.home is not None:
                kinds.append(crossing_of[lane_of(phase, r), r, item.key])
            else:
                kinds.append("own")
            own.append(item if kinds[-1] == "own" else None)
        pairs_of[phase, t], kinds_of[phase, t], own_of[phase, t] = pairs, kinds, own

    returns = {}
    for t in range(1, rounds + 1):
        for d, lane in enumerate(lanes):
            for r in range(rows):
                item = lane.lines[r][0].get(t)
                if item is not None and item.home is not None:
                    pair = number(r, lane.col(0)), number(item.home, lane.col(0))
                    returns.setdefault(((r + d) % 2, t), []).append(pair)

    columns = []

    def add(entries):
        columns.append(np.asarray(entries, np.int32))
        return sum(c.shape[1] for c in columns[:-1])

    relays = {}
    for key in sends:
        kinds = kinds_of[key]
        names = sorted(set(kinds) - {None, "own"}, key=str)
        if names and (len(names) > 1 or "own" in kinds):
            entries = []
            for kind, item in zip(kinds, own_of[key]):
                if kind == "own":
                    entries.append((0, item.piece, group_here(item)))
                else:
                    entries.append((1 + names.index(kind) if kind is not None else 1, 0, 0))
            relays[key] = names, add(entries)

    order = []
    for r, c in devices:
        arrivals = []
        for s in range(STEPS):
            when, key = 0, -1 - (r + s) % rows % groups_here
            for d, lane in enumerate(lanes):
                arrival = lane.arrival(r, c, (0, s))
                if arrival is not None:
                    t, returned = arrival
                    when, key = t, ((r + d) % 2, t)
                    if returned:
                        when, key = t + 0.7, ("back%d" % ((r + rows // 2 + d) % 2), t)
            arrivals.append((when, s, key))
        order.append(sorted(arrivals, key=lambda a: a[:2]))
    rank_at = add([[[a[1] for a in arrivals].index(s) for s in range(STEPS)] for arrivals in order])
    used, candidates, source_at = [], [], []
    for ranks in (range(STEPS - 1), range(STEPS - 1, STEPS)):
        keys = {arrivals[k][2] for arrivals in order for k in ranks}
        used.append(sorted((k for k in keys if isinstance(k, tuple)), key=lambda k: (k[1], str(k[0]))))
        places = [
            [arrivals[k][2] if isinstance(arrivals[k][2], int) else used[-1].index(arrivals[k][2]) for k in ranks]
            for arrivals in order
        ]
        candidates.append([sorted({max(p[i], -1) for p in places}) for i in range(len(ranks))])
        source_at.append(
            add([[n for p, k in zip(row, ranks) for n in (p, arrivals[k][1])] for row, arrivals in zip(places, order)])
        )
    table = np.concatenate(columns, axis=1)
    table = lax.dynamic_slice(jnp.asarray(table), (device, 0), (1, table.shape[1]))[0]

    def own_chunk(items, x=x):
        piece = lookup([None if i is None else i.piece for i in items], device)
        group = lookup([None if i is None else group_here(i) for i in items], device)
        return lax.dynamic_slice(x, (piece * piece_rows, group * group_size), (piece_rows, group_size))

    factor = weight / jnp.sqrt(2.0 * freq * (1.0 - freq))
    twice = 2.0 * freq
    male_scale = np.float32(np.sqrt(0.5))
    male_rows = jnp.where(sex_rows > 0, male_scale, np.float32(1.0))
    male_cols = jnp.where(sex_cols > 0, male_scale, np.float32(1.0))
    wide = lambda value: jnp.broadcast_to(value[:, None], (value.shape[0], LANES))

    def in_window(value):
        span = STEPS * group_size
        return lax.dynamic_slice(jnp.concatenate([value, value]), (row_place * group_size,), (span,))

    window_factor, window_twice = in_window(factor), in_window(twice)
    male_wide = wide(male_rows)

    def own_squares():
        here = lambda value: lax.dynamic_slice(value, (col_place * local_vars,), (local_vars,))[None, :]
        zx = ((x.astype(jnp.float32) - here(twice)) * here(factor) * male_rows[:, None]).astype(jnp.bfloat16)
        return jnp.sum(jnp.square(zx.astype(jnp.float32)), axis=1)

    back = [(i, (i - 1) % rows) for i in range(rows)]
    window = [y]
    while len(window) < STEPS:
        window.append(lax.ppermute(window[-1], "row", back))
    squares = own_squares()

    starts = {}
    if any(own_of[1, 1]):
        starts[1, 1] = own_chunk(own_of[1, 1])
    later_x = x
    for k, crossing in enumerate(crossings):
        later_x = lax.optimization_barrier(later_x)
        starts["cross", k] = own_chunk([crossing[rc][1] if rc in crossing else None for rc in devices], later_x)
    later_x, squares = lax.optimization_barrier((later_x, squares))
    if any(own_of[0, 1]):
        starts[0, 1] = own_chunk(own_of[0, 1], later_x)
    bits = [1 << k for k in range(cols.bit_length() - 1)] if cols & (cols - 1) == 0 else []
    if cols & (cols - 1):
        squares = lax.psum(squares, "col")

    def sum_beside(value, squares):
        if not bits:
            return value, squares
        bit = bits.pop(0)
        other = lax.ppermute(squares, "col", [(i, i ^ bit) for i in range(cols)])
        value, other = lax.optimization_barrier((value, other))
        return value, squares + other

    buffers, crossed = {}, {}

    def bring_back(key):
        if key in returns:
            phase, t = key
            buffers["back%d" % phase, t] = lax.ppermute(buffers[key], both, returns[key])

    for key in sends:
        phase, t = key
        if pairs_of[key]:
            if key in relays:
                names, at = relays[key]
                sources = [buffers[phase, t - DEPTH] if name == "forward" else crossed[name] for name in names]
                held = relay(at, table, x, sources)
            elif key in starts:
                held = starts[key]
            elif "forward" in kinds_of[key]:
                held = buffers[phase, t - DEPTH]
            elif "own" in kinds_of[key]:
                held = own_chunk(own_of[key])
            else:
                held = crossed[next(k for k in kinds_of[key] if k is not None)]
            buffers[key] = lax.ppermute(held, both, pairs_of[key])
        if key == (0, 1):
            for k, crossing in enumerate(crossings):
                pairs = [(number(*rc), number(*to)) for rc, (to, _) in crossing.items()]
                crossed[k] = lax.ppermute(starts["cross", k], both, pairs)
        bring_back(key)
    zy = standardized_window(rank_at, table, window, wide(window_factor), wide(window_twice), male_cols[None, :])
    shared = window_factor[None, :], window_twice[None, :], male_wide, zy
    total = early_product(source_at[0], candidates[0], table, x, [buffers[k] for k in used[0]], *shared)
    total, squares = sum_beside(total, squares)
    relation = last_product(source_at[1], candidates[1][0], table, x, [buffers[k] for k in used[1]], *shared, total)
    relation, squares = sum_beside(relation, squares)
    for bit in bits:
        squares = squares + lax.ppermute(squares, "col", [(i, i ^ bit) for i in range(cols)])
    inbreeding = squares / jnp.float32(freq.shape[0]) - 1.0
    return relation, inbreeding


def solution(mesh):
    rows, cols = mesh.shape["row"], mesh.shape["col"]
    return jax.shard_map(
        functools.partial(local, rows, cols),
        mesh=mesh,
        in_specs=(P("row", "col"), P("row", "col"), P(), P(), P("row"), P("col")),
        out_specs=(P("row", "col"), P("row")),
        check_vma=False,
    )
```

```python
import functools

import jax
import jax.numpy as jnp
import numpy as np
from jax import lax
from jax.experimental import pallas as pl
from jax.experimental.pallas import tpu as pltpu
from jax.sharding import PartitionSpec as P

STEPS = 4
EARLY = 3
DRAWS = 400
COL_TILE = 512
ROW_BLOCK = 512
ROW_TILE = 32
LANES = 128
VMEM_LIMIT = 10 * 2**20
RELAY_LIMIT = 2 * 2**20


def exchange(own):
    cols = len(own)
    rng = np.random.RandomState(0)
    best = None
    for _ in range(DRAWS):
        held = [set(o) for o in own]
        rounds, hops = [], 0
        while any(len(h) < STEPS for h in held):
            before = [set(h) for h in held]
            sends, busy = {}, set()
            draw = rng.rand(cols)
            for c in sorted(range(cols), key=lambda c: (len(before[c]), draw[c])):
                choices = []
                for other in range(cols):
                    if other not in sends:
                        for step in before[other] - before[c]:
                            rare = sum(step in h for h in before)
                            choices.append((rare + rng.rand() * 2, abs(other - c), other, step))
                if choices and c not in busy:
                    _, far, other, step = min(choices)
                    sends[other] = c, step
                    busy.add(c)
                    held[c].add(step)
                    hops += far
            rounds.append(sends)
        if best is None or (len(rounds), hops) < best[0]:
            best = (len(rounds), hops), rounds
    return best[1]


def lookup(values, device):
    known = [v for v in values if v is not None]
    if len(set(known)) <= 1:
        return known[0] if known else 0
    values = [known[0] if v is None else v for v in values]
    result = jnp.uint32(0)
    place = (device % 32).astype(jnp.uint32)
    for bit in range(max(values).bit_length()):
        ones = [v >> bit & 1 for v in values]
        words = [sum(b << i for i, b in enumerate(ones[at : at + 32])) for at in range(0, len(ones), 32)]
        word = jnp.uint32(words[0])
        for i, other in enumerate(words[1:], 1):
            word = jnp.where(device // 32 == i, jnp.uint32(other), word)
        result = result | (((word >> place) & jnp.uint32(1)) << jnp.uint32(bit))
    return result.astype(jnp.int32)


def relay_kernel(at, table, x, *refs):
    *sources, out = refs
    rows, width = out.shape

    @pl.when(table[at] == 0)
    def _():
        col = pl.multiple_of(table[at + 1] * width, width)
        out[...] = x[:, pl.ds(col, width)]

    for i, source in enumerate(sources):

        @pl.when(table[at] == i + 1)
        def _(source=source):
            out[...] = source[...]


def relay(at, table, x, sources):
    return pl.pallas_call(
        functools.partial(relay_kernel, at),
        out_shape=pltpu.VMEM(sources[0].shape, sources[0].dtype),
        in_specs=[pl.BlockSpec(memory_space=pltpu.SMEM)] + [VMEM] * (1 + len(sources)),
        out_specs=VMEM,
        compiler_params=pltpu.CompilerParams(vmem_limit_bytes=RELAY_LIMIT),
        cost_estimate=pl.CostEstimate(flops=0, bytes_accessed=0, transcendentals=0),
        name="relay",
    )(table, *[in_vmem(v) for v in (x, *sources)])


def in_vmem(value):
    return pltpu.with_memory_space_constraint(value, pltpu.VMEM)


VMEM = pl.BlockSpec(memory_space=pltpu.VMEM)


def window_kernel(at, table, *refs):
    blocks = refs[:STEPS]
    factor, twice, male, out = refs[STEPS:]
    group_size, width = blocks[0].shape
    for s, block in enumerate(blocks):
        rank = table[at + s]

        @pl.loop(0, group_size // ROW_TILE)
        def _(i, s=s, block=block, rank=rank):
            here = pl.ds(pl.multiple_of(i * ROW_TILE, ROW_TILE), ROW_TILE)
            rows = pl.ds(pl.multiple_of(s * group_size + i * ROW_TILE, ROW_TILE), ROW_TILE)
            to = pl.ds(pl.multiple_of(rank * group_size + i * ROW_TILE, ROW_TILE), ROW_TILE)
            for k in range(0, width, LANES):
                value = block[here, k : k + LANES].astype(jnp.float32) - twice[rows, :]
                out[to, k : k + LANES] = (value * factor[rows, :] * male[:, k : k + LANES]).astype(out.dtype)


def standardized_window(at, table, blocks, factor, twice, male):
    group_size, n = blocks[0].shape
    depth = STEPS * group_size
    return pl.pallas_call(
        functools.partial(window_kernel, at),
        out_shape=pltpu.VMEM((depth, n), jnp.bfloat16),
        in_specs=[pl.BlockSpec(memory_space=pltpu.SMEM)] + [VMEM] * (STEPS + 3),
        out_specs=VMEM,
        compiler_params=pltpu.CompilerParams(vmem_limit_bytes=VMEM_LIMIT),
        cost_estimate=pl.CostEstimate(flops=4 * depth * n, bytes_accessed=4 * depth * n, transcendentals=0),
        name="window",
    )(table, *[in_vmem(v) for v in (*blocks, factor, twice, male)])


def standardize(table, at, candidates, x, buffers, factor, twice, male, zx, columns, first, count):
    width = columns.stop - columns.start
    place, step = table[at], table[at + 1]

    def from_source(source, col):
        @pl.loop(0, count // ROW_TILE)
        def _(i):
            here = pl.ds(pl.multiple_of(first + i * ROW_TILE, ROW_TILE), ROW_TILE)
            to = pl.ds(pl.multiple_of(i * ROW_TILE, ROW_TILE), ROW_TILE)
            for k in range(0, width, LANES):
                lanes = pl.ds(pl.multiple_of(step * width + k, LANES), LANES)
                value = source[here, pl.ds(pl.multiple_of(col + k, LANES), LANES)].astype(jnp.float32)
                value = (value - twice[:, lanes]) * factor[:, lanes] * male[here, :]
                zx[to, columns.start + k : columns.start + k + LANES] = value.astype(zx.dtype)

    for number in candidates:
        if number >= 0:

            @pl.when(place == number)
            def _(number=number):
                from_source(buffers[number], 0)

        else:

            @pl.when(place < 0)
            def _():
                from_source(x, (-1 - place) * width)


def early_kernel(at, candidates, n_buffers, table, x, *refs):
    buffers = refs[:n_buffers]
    factor, twice, male, zy, total, zx = refs[n_buffers:]
    rows, depth = zx.shape
    width = depth // EARLY
    for rank in range(EARLY):
        columns = slice(rank * width, (rank + 1) * width)
        standardize(table, at + 2 * rank, candidates[rank], x, buffers, factor, twice, male, zx, columns, 0, rows)

    @pl.loop(0, rows // ROW_BLOCK)
    def _(i):
        block = pl.ds(pl.multiple_of(i * ROW_BLOCK, ROW_BLOCK), ROW_BLOCK)
        for j in range(0, total.shape[1], COL_TILE):
            right = zy[:depth, j : j + COL_TILE]
            total[block, j : j + COL_TILE] = jnp.dot(zx[block, :], right, preferred_element_type=jnp.float32)


def early_product(at, candidates, table, x, buffers, factor, twice, male, zy):
    rows, (depth, n) = x.shape[0], zy.shape
    depth = depth // STEPS * EARLY
    args = [in_vmem(v) for v in (x, *buffers, factor, twice, male, zy)]
    return pl.pallas_call(
        functools.partial(early_kernel, at, candidates, len(buffers)),
        out_shape=pltpu.VMEM((rows, n), jnp.float32),
        in_specs=[pl.BlockSpec(memory_space=pltpu.SMEM)] + [VMEM] * len(args),
        out_specs=VMEM,
        scratch_shapes=[pltpu.VMEM((rows, depth), jnp.bfloat16)],
        compiler_params=pltpu.CompilerParams(vmem_limit_bytes=VMEM_LIMIT),
        cost_estimate=pl.CostEstimate(flops=2 * rows * depth * n, bytes_accessed=0, transcendentals=0),
        name="early",
    )(table, *args)


def last_kernel(at, candidates, scale, n_buffers, table, x, *refs):
    buffers = refs[:n_buffers]
    factor, twice, male, zy, total, out, zx, blocks, sems = refs[n_buffers:]
    rows, n = total.shape
    depth = zx.shape[1]
    width = depth // (STEPS - EARLY)

    def copy(i):
        return pltpu.make_async_copy(blocks.at[i % 2], out.at[pl.ds(i * ROW_BLOCK, ROW_BLOCK), :], sems.at[i % 2])

    count = rows // ROW_BLOCK
    for i in range(count):
        first = i * ROW_BLOCK
        for rank in range(STEPS - EARLY):
            columns = slice(rank * width, (rank + 1) * width)
            standardize(
                table,
                at + 2 * rank,
                candidates[rank],
                x,
                buffers,
                factor,
                twice,
                male,
                zx,
                columns,
                first,
                ROW_BLOCK,
            )
        if i >= 2:
            copy(i - 2).wait()
        for j in range(0, n, COL_TILE):
            right = zy[zy.shape[0] - depth :, j : j + COL_TILE]
            product = jnp.dot(zx[...], right, preferred_element_type=jnp.float32)
            product = product + total[first : first + ROW_BLOCK, j : j + COL_TILE]
            blocks[i % 2, :, j : j + COL_TILE] = (product * scale).astype(blocks.dtype)
        copy(i).start()
    for i in range(max(count - 2, 0), count):
        copy(i).wait()


def last_product(at, candidates, table, x, buffers, factor, twice, male, zy, total):
    rows, (depth, n) = x.shape[0], zy.shape
    width = depth // STEPS * (STEPS - EARLY)
    scale = float(1.0 / np.sqrt(np.float32(depth)))
    args = [in_vmem(v) for v in (x, *buffers, factor, twice, male, zy, total)]
    return pl.pallas_call(
        functools.partial(last_kernel, at, candidates, scale, len(buffers)),
        out_shape=jax.ShapeDtypeStruct((rows, n), jnp.bfloat16),
        in_specs=[pl.BlockSpec(memory_space=pltpu.SMEM)] + [VMEM] * len(args),
        out_specs=pl.BlockSpec(memory_space=pl.ANY),
        scratch_shapes=[
            pltpu.VMEM((ROW_BLOCK, width), jnp.bfloat16),
            pltpu.VMEM((2, ROW_BLOCK, n), jnp.bfloat16),
            pltpu.SemaphoreType.DMA((2,)),
        ],
        compiler_params=pltpu.CompilerParams(vmem_limit_bytes=VMEM_LIMIT),
        cost_estimate=pl.CostEstimate(flops=2 * rows * width * n, bytes_accessed=2 * rows * n, transcendentals=0),
        name="last",
    )(table, *args)


def local(rows, cols, x, y, freq, weight, sex_rows, sex_cols):
    group_size = y.shape[0]
    local_vars = x.shape[1]
    groups_here = local_vars // group_size
    devices = [(r, c) for r in range(rows) for c in range(cols)]

    row_place = lax.axis_index("row")
    col_place = lax.axis_index("col")
    device = row_place * cols + col_place

    def group_here(r, s):
        return (r + s) % rows % groups_here

    def owner(r, s):
        return (r + s) % rows // groups_here

    plans = [exchange([[s for s in range(STEPS) if owner(r, s) == c] for c in range(cols)]) for r in range(rows)]
    rounds = max(len(plan) for plan in plans)
    arrival = {}
    for r, plan in enumerate(plans):
        for t, sends in enumerate(plan, 1):
            for receiver, s in sends.values():
                arrival[r, receiver, s] = t

    columns = []

    def add(entries):
        columns.append(np.asarray(entries, np.int32))
        return sum(c.shape[1] for c in columns[:-1])

    pairs_of, own_of, relays = {}, {}, {}
    for t in range(1, rounds + 1):
        pairs, own, came = [], [], []
        for r, c in devices:
            receiver, s = plans[r][t - 1].get(c, (None, None)) if t <= len(plans[r]) else (None, None)
            if s is not None:
                pairs.append((r * cols + c, r * cols + receiver))
            mine = s is not None and owner(r, s) == c
            own.append(group_here(r, s) if mine else None)
            came.append(None if s is None or mine else arrival[r, c, s])
        pairs_of[t], own_of[t] = pairs, own
        names = sorted(set(came) - {None})
        if names:
            entries = [(0, g) if g is not None else (1 + (names.index(n) if n else 0), 0) for g, n in zip(own, came)]
            relays[t] = names, add(entries)

    order = []
    for r, c in devices:
        arrivals = []
        for s in range(STEPS):
            t = arrival.get((r, c, s), 0)
            arrivals.append((t, s, t if t else -1 - group_here(r, s)))
        order.append(sorted(arrivals, key=lambda a: a[:2]))
    rank_at = add([[[a[1] for a in arrivals].index(s) for s in range(STEPS)] for arrivals in order])
    used, candidates, source_at = [], [], []
    for ranks in (range(EARLY), range(EARLY, STEPS)):
        used.append(sorted({arrivals[k][2] for arrivals in order for k in ranks if arrivals[k][2] > 0}))
        places = [[used[-1].index(a[k][2]) if a[k][2] > 0 else a[k][2] for k in ranks] for a in order]
        candidates.append([sorted({max(p[i], -1) for p in places}) for i in range(len(ranks))])
        source_at.append(add([[n for p, k in zip(row, ranks) for n in (p, a[k][1])] for row, a in zip(places, order)]))
    table = np.concatenate(columns, axis=1)
    table = lax.dynamic_slice(jnp.asarray(table), (device, 0), (1, table.shape[1]))[0]

    factor = weight / jnp.sqrt(2.0 * freq * (1.0 - freq))
    twice = 2.0 * freq
    male_scale = np.float32(np.sqrt(0.5))
    male_rows = jnp.where(sex_rows > 0, male_scale, np.float32(1.0))
    male_cols = jnp.where(sex_cols > 0, male_scale, np.float32(1.0))
    wide = lambda value: jnp.broadcast_to(value[:, None], (value.shape[0], LANES))

    def in_window(value):
        span = STEPS * group_size
        return lax.dynamic_slice(jnp.concatenate([value, value]), (row_place * group_size,), (span,))

    window_factor, window_twice = in_window(factor), in_window(twice)
    male_wide = wide(male_rows)

    def own_squares():
        here = lambda value: lax.dynamic_slice(value, (col_place * local_vars,), (local_vars,))[None, :]
        zx = ((x.astype(jnp.float32) - here(twice)) * here(factor) * male_rows[:, None]).astype(jnp.bfloat16)
        return jnp.sum(jnp.square(zx.astype(jnp.float32)), axis=1)

    back = [(i, (i - 1) % rows) for i in range(rows)]
    window = [y]
    while len(window) < STEPS:
        window.append(lax.ppermute(window[-1], "row", back))
    squares = own_squares()

    def col_sum_beside(value, squares):
        if cols & (cols - 1):
            return value, lax.psum(squares, "col")
        parts = [squares]
        for mask in range(1, cols):
            parts.append(lax.ppermute(squares, "col", [(i, i ^ mask) for i in range(cols)]))
        value, *parts = lax.optimization_barrier((value, *parts))
        while len(parts) > 1:
            parts = [a + b for a, b in zip(parts[::2], parts[1::2])]
        return value, parts[0]

    buffers = {}
    for t in range(1, rounds + 1):
        if t == 2:
            table, squares = lax.optimization_barrier((table, squares))
        if t in relays:
            names, at = relays[t]
            held = relay(at, table, x, [buffers[n] for n in names])
        else:
            start = (0, lookup(own_of[t], device) * group_size)
            held = lax.dynamic_slice(x, start, (x.shape[0], group_size))
        buffers[t] = lax.ppermute(held, ("row", "col"), pairs_of[t])
    zy = standardized_window(rank_at, table, window, wide(window_factor), wide(window_twice), male_cols[None, :])
    shared = window_factor[None, :], window_twice[None, :], male_wide, zy
    total = early_product(source_at[0], candidates[0], table, x, [buffers[k] for k in used[0]], *shared)
    total, squares = lax.optimization_barrier((total, squares))
    relation = last_product(source_at[1], candidates[1], table, x, [buffers[k] for k in used[1]], *shared, total)
    relation, squares = col_sum_beside(relation, squares)
    inbreeding = squares / jnp.float32(freq.shape[0]) - 1.0
    return relation, inbreeding


def solution(mesh):
    rows, cols = mesh.shape["row"], mesh.shape["col"]
    return jax.shard_map(
        functools.partial(local, rows, cols),
        mesh=mesh,
        in_specs=(P("row", "col"), P("row", "col"), P(), P(), P("row"), P("col")),
        out_specs=(P("row", "col"), P("row")),
        check_vma=False,
    )
```

```python
import functools
import itertools

import jax
import jax.numpy as jnp
import numpy as np
from jax import lax
from jax.experimental import pallas as pl
from jax.experimental.pallas import tpu as pltpu
from jax.sharding import PartitionSpec as P

STEPS = 4
PIECES = 1
DEPTH = 1
HOP = 1
COL_TILE = 512
ROW_BLOCK = 512
ROW_TILE = 32
LANES = 128
VMEM_LIMIT = 10 * 2**20
RELAY_LIMIT = 2 * 2**20


class Item:
    def __init__(self, row, piece, s, place, home=None):
        self.row, self.piece, self.s, self.place = row, piece, s, place
        self.home = home

    @property
    def owner(self):
        return self.row if self.home is None else self.home

    @property
    def key(self):
        return self.piece, self.s


def line_slots(items, cut):
    ends, inner = {}, {}
    todo = sorted(items, key=lambda i: (i.home is None, i.piece, i.place, i.s))
    slot = 1
    while todo:
        for item in todo:
            first = 1 + DEPTH * (item.place - 1) + (HOP if item.home is not None else 0)
            if first <= slot:
                ends[slot] = item
                if item.place > 1:
                    inner[slot] = item
                todo.remove(item)
                break
        slot += 1
    for item in sorted(cut, key=lambda i: (i.place, i.key)):
        slot = 1 + DEPTH * (item.place - 1)
        if item.place > 1:
            while slot in inner:
                slot += 1
            inner[slot] = item
    return ends, inner


class Lane:
    def __init__(self, rows, cols, groups_here, towards_zero):
        self.rows, self.cols = rows, cols
        self.towards_zero = towards_zero
        self.items = []
        for r in range(rows):
            mine = [
                Item(r, piece, s, self.place((r + s) % rows // groups_here))
                for piece in range(PIECES)
                for s in range(STEPS)
            ]
            self.items.append([i for i in mine if i.place > 0])
        self.away = []
        self.lines = [line_slots(items, []) for items in self.items]
        if rows % 4 == 0 and cols > 3:
            for r in range(rows // 2):
                other = r + rows // 2 if towards_zero else (r + rows // 2) ^ 1
                self.balance(r, other)
                self.balance(other, r)
        self.rounds = max(
            [max(ends, default=0) for ends, _ in self.lines] + [max(inner, default=0) - DEPTH for _, inner in self.lines]
        )

    def place(self, c):
        return c if self.towards_zero else self.cols - 1 - c

    col = place

    def balance(self, r, other):
        if len(self.items[r]) < len(self.items[other]) or any(i.row == other for i in self.away):
            return
        places = sorted({i.place for i in self.items[r]})
        best = None
        for counts in itertools.product(range(3), repeat=len(places)):
            gone = []
            for place, count in zip(places, counts):
                here = [i for i in self.items[r] if i.place == place]
                here.sort(key=lambda i: i.key, reverse=True)
                gone += here[:count]
            visitors = [Item(other, i.piece, i.s, i.place, home=r) for i in gone]
            mine = line_slots([i for i in self.items[r] if i not in gone], gone)
            theirs = line_slots(self.items[other] + visitors, [])
            score = (
                max(max(mine[0], default=0), max(theirs[0], default=0), STEPS),
                len(gone),
                max([slot for slot, i in theirs[0].items() if i.home is not None], default=0),
            )
            if best is None or score < best[0]:
                best = score, gone, mine, theirs
        _, gone, mine, theirs = best
        self.away += gone
        if gone:
            self.lines[r], self.lines[other] = mine, theirs

    def sent(self, r, c, t):
        p = self.place(c)
        ends, inner = self.lines[r]
        if p == 0:
            return None
        item = ends.get(t) if p == 1 else inner.get(t + DEPTH * (p - 1))
        return item if item is not None and item.place >= p else None

    def pairs(self, t):
        found = []
        for r in range(self.rows):
            for c in range(self.cols):
                if self.sent(r, c, t) is not None:
                    found.append((r * self.cols + c, r * self.cols + self.col(self.place(c) - 1)))
        return found

    def arrival(self, r, c, key):
        p = self.place(c)
        for i in self.items[r]:
            if i.key != key or i.place <= p:
                continue
            ends, inner = self.lines[r]
            if p == 0 and i in self.away:
                for other, _ in self.lines:
                    for slot, v in other.items():
                        if v.home == r and v.key == key:
                            return slot, True
            for slot, v in (ends if p == 0 else inner).items():
                if v is i:
                    return slot - DEPTH * p, False
        return None


def lookup(values, device):
    known = [v for v in values if v is not None]
    if len(set(known)) <= 1:
        return known[0] if known else 0
    values = [known[0] if v is None else v for v in values]
    result = jnp.uint32(0)
    place = (device % 32).astype(jnp.uint32)
    for bit in range(max(values).bit_length()):
        ones = [v >> bit & 1 for v in values]
        words = [sum(b << i for i, b in enumerate(ones[at : at + 32])) for at in range(0, len(ones), 32)]
        word = jnp.uint32(words[0])
        for i, other in enumerate(words[1:], 1):
            word = jnp.where(device // 32 == i, jnp.uint32(other), word)
        result = result | (((word >> place) & jnp.uint32(1)) << jnp.uint32(bit))
    return result.astype(jnp.int32)


def relay_kernel(at, table, x, *refs):
    *sources, out = refs
    rows, width = out.shape

    @pl.when(table[at] == 0)
    def _():
        row = pl.multiple_of(table[at + 1] * rows, rows)
        col = pl.multiple_of(table[at + 2] * width, width)
        out[...] = x[pl.ds(row, rows), pl.ds(col, width)]

    for i, source in enumerate(sources):

        @pl.when(table[at] == i + 1)
        def _(source=source):
            out[...] = source[...]


def relay(at, table, x, sources):
    return pl.pallas_call(
        functools.partial(relay_kernel, at),
        out_shape=pltpu.VMEM(sources[0].shape, sources[0].dtype),
        in_specs=[pl.BlockSpec(memory_space=pltpu.SMEM)] + [VMEM] * (1 + len(sources)),
        out_specs=VMEM,
        compiler_params=pltpu.CompilerParams(vmem_limit_bytes=RELAY_LIMIT),
        cost_estimate=pl.CostEstimate(flops=0, bytes_accessed=0, transcendentals=0),
        name="relay",
    )(table, *[in_vmem(v) for v in (x, *sources)])


def in_vmem(value):
    return pltpu.with_memory_space_constraint(value, pltpu.VMEM)


VMEM = pl.BlockSpec(memory_space=pltpu.VMEM)


def window_kernel(at, table, *refs):
    blocks = refs[:STEPS]
    factor, twice, male, out = refs[STEPS:]
    group_size, width = blocks[0].shape
    for s, block in enumerate(blocks):
        rank = table[at + s]

        @pl.loop(0, group_size // ROW_TILE)
        def _(i, s=s, block=block, rank=rank):
            here = pl.ds(pl.multiple_of(i * ROW_TILE, ROW_TILE), ROW_TILE)
            rows = pl.ds(pl.multiple_of(s * group_size + i * ROW_TILE, ROW_TILE), ROW_TILE)
            to = pl.ds(pl.multiple_of(rank * group_size + i * ROW_TILE, ROW_TILE), ROW_TILE)
            for k in range(0, width, LANES):
                value = block[here, k : k + LANES].astype(jnp.float32) - twice[rows, :]
                out[to, k : k + LANES] = (value * factor[rows, :] * male[:, k : k + LANES]).astype(out.dtype)


def standardized_window(at, table, blocks, factor, twice, male):
    group_size, n = blocks[0].shape
    depth = STEPS * group_size
    return pl.pallas_call(
        functools.partial(window_kernel, at),
        out_shape=pltpu.VMEM((depth, n), jnp.bfloat16),
        in_specs=[pl.BlockSpec(memory_space=pltpu.SMEM)] + [VMEM] * (STEPS + 3),
        out_specs=VMEM,
        compiler_params=pltpu.CompilerParams(vmem_limit_bytes=VMEM_LIMIT),
        cost_estimate=pl.CostEstimate(flops=4 * depth * n, bytes_accessed=4 * depth * n, transcendentals=0),
        name="window",
    )(table, *[in_vmem(v) for v in (*blocks, factor, twice, male)])


def standardize(table, at, candidates, x, buffers, factor, twice, male, zx, columns, first, count):
    width = columns.stop - columns.start
    place, step = table[at], table[at + 1]

    def from_source(source, col):
        @pl.loop(0, count // ROW_TILE)
        def _(i):
            here = pl.ds(pl.multiple_of(first + i * ROW_TILE, ROW_TILE), ROW_TILE)
            to = pl.ds(pl.multiple_of(i * ROW_TILE, ROW_TILE), ROW_TILE)
            for k in range(0, width, LANES):
                lanes = pl.ds(pl.multiple_of(step * width + k, LANES), LANES)
                value = source[here, pl.ds(pl.multiple_of(col + k, LANES), LANES)].astype(jnp.float32)
                value = (value - twice[:, lanes]) * factor[:, lanes] * male[here, :]
                zx[to, columns.start + k : columns.start + k + LANES] = value.astype(zx.dtype)

    for number in candidates:
        if number >= 0:

            @pl.when(place == number)
            def _(number=number):
                from_source(buffers[number], 0)

        else:

            @pl.when(place < 0)
            def _():
                from_source(x, (-1 - place) * width)


def early_kernel(at, candidates, n_buffers, table, x, *refs):
    buffers = refs[:n_buffers]
    factor, twice, male, zy, total, zx = refs[n_buffers:]
    rows, depth = zx.shape
    width = depth // (STEPS - 1)
    for rank in range(STEPS - 1):
        columns = slice(rank * width, (rank + 1) * width)
        standardize(table, at + 2 * rank, candidates[rank], x, buffers, factor, twice, male, zx, columns, 0, rows)

    @pl.loop(0, rows // ROW_BLOCK)
    def _(i):
        block = pl.ds(pl.multiple_of(i * ROW_BLOCK, ROW_BLOCK), ROW_BLOCK)
        for j in range(0, total.shape[1], COL_TILE):
            right = zy[:depth, j : j + COL_TILE]
            total[block, j : j + COL_TILE] = jnp.dot(zx[block, :], right, preferred_element_type=jnp.float32)


def early_product(at, candidates, table, x, buffers, factor, twice, male, zy):
    rows, (depth, n) = x.shape[0], zy.shape
    depth = depth // STEPS * (STEPS - 1)
    args = [in_vmem(v) for v in (x, *buffers, factor, twice, male, zy)]
    return pl.pallas_call(
        functools.partial(early_kernel, at, candidates, len(buffers)),
        out_shape=pltpu.VMEM((rows, n), jnp.float32),
        in_specs=[pl.BlockSpec(memory_space=pltpu.SMEM)] + [VMEM] * len(args),
        out_specs=VMEM,
        scratch_shapes=[pltpu.VMEM((rows, depth), jnp.bfloat16)],
        compiler_params=pltpu.CompilerParams(vmem_limit_bytes=VMEM_LIMIT),
        cost_estimate=pl.CostEstimate(flops=2 * rows * depth * n, bytes_accessed=0, transcendentals=0),
        name="early",
    )(table, *args)


def last_kernel(at, candidates, scale, n_buffers, table, x, *refs):
    buffers = refs[:n_buffers]
    factor, twice, male, zy, total, out, zx, blocks, sems = refs[n_buffers:]
    rows, n = total.shape
    width = zx.shape[1]

    def copy(i):
        return pltpu.make_async_copy(blocks.at[i % 2], out.at[pl.ds(i * ROW_BLOCK, ROW_BLOCK), :], sems.at[i % 2])

    count = rows // ROW_BLOCK
    for i in range(count):
        first = i * ROW_BLOCK
        standardize(
            table, at, candidates, x, buffers, factor, twice, male, zx, slice(0, width), first, ROW_BLOCK
        )
        if i >= 2:
            copy(i - 2).wait()
        for j in range(0, n, COL_TILE):
            right = zy[zy.shape[0] - width :, j : j + COL_TILE]
            product = jnp.dot(zx[...], right, preferred_element_type=jnp.float32)
            product = product + total[first : first + ROW_BLOCK, j : j + COL_TILE]
            blocks[i % 2, :, j : j + COL_TILE] = (product * scale).astype(blocks.dtype)
        copy(i).start()
    for i in range(max(count - 2, 0), count):
        copy(i).wait()


def last_product(at, candidates, table, x, buffers, factor, twice, male, zy, total):
    rows, (depth, n) = x.shape[0], zy.shape
    width = depth // STEPS
    scale = float(1.0 / np.sqrt(np.float32(depth)))
    args = [in_vmem(v) for v in (x, *buffers, factor, twice, male, zy, total)]
    return pl.pallas_call(
        functools.partial(last_kernel, at, candidates, scale, len(buffers)),
        out_shape=jax.ShapeDtypeStruct((rows, n), jnp.bfloat16),
        in_specs=[pl.BlockSpec(memory_space=pltpu.SMEM)] + [VMEM] * len(args),
        out_specs=pl.BlockSpec(memory_space=pl.ANY),
        scratch_shapes=[
            pltpu.VMEM((ROW_BLOCK, width), jnp.bfloat16),
            pltpu.VMEM((2, ROW_BLOCK, n), jnp.bfloat16),
            pltpu.SemaphoreType.DMA((2,)),
        ],
        compiler_params=pltpu.CompilerParams(vmem_limit_bytes=VMEM_LIMIT),
        cost_estimate=pl.CostEstimate(flops=2 * rows * width * n, bytes_accessed=2 * rows * n, transcendentals=0),
        name="last",
    )(table, *args)


def local(rows, cols, x, y, freq, weight, sex_rows, sex_cols):
    group_size = y.shape[0]
    local_vars = x.shape[1]
    groups_here = local_vars // group_size
    piece_rows = x.shape[0] // PIECES
    lanes = [Lane(rows, cols, groups_here, towards) for towards in (True, False)]
    rounds = max(lane.rounds for lane in lanes)
    devices = [(r, c) for r in range(rows) for c in range(cols)]
    both = ("row", "col")

    row_place = lax.axis_index("row")
    col_place = lax.axis_index("col")
    device = row_place * cols + col_place

    def number(r, c):
        return r * cols + c

    def group_here(item):
        return (item.owner + item.s) % rows % groups_here

    crossings = []
    crossing_of = {}
    for d, lane in enumerate(lanes):
        for r in range(rows):
            for slot, item in sorted(lane.lines[r][0].items()):
                if item.home is None:
                    continue
                source, target = (item.home, lane.col(item.place)), (r, lane.col(item.place))
                for k, crossing in enumerate(crossings):
                    if source not in crossing and target not in [to for to, _ in crossing.values()]:
                        break
                else:
                    k = len(crossings)
                    crossings.append({})
                crossings[k][source] = (target, item)
                crossing_of[d, r, item.key] = k

    def lane_of(phase, r):
        return (r + phase) % 2

    sends = [(phase, t) for t in range(1, rounds + 1) for phase in range(2)]
    pairs_of, kinds_of, own_of = {}, {}, {}
    for phase, t in sends:
        pairs, kinds, own = [], [], []
        for r, c in devices:
            lane = lanes[lane_of(phase, r)]
            item = lane.sent(r, c, t)
            if item is not None:
                pairs.append((number(r, c), number(r, lane.col(lane.place(c) - 1))))
            if item is None:
                kinds.append(None)
            elif item.place != lane.place(c):
                kinds.append("forward")
            elif item.home is not None:
                kinds.append(crossing_of[lane_of(phase, r), r, item.key])
            else:
                kinds.append("own")
            own.append(item if kinds[-1] == "own" else None)
        pairs_of[phase, t], kinds_of[phase, t], own_of[phase, t] = pairs, kinds, own

    returns = {}
    for t in range(1, rounds + 1):
        pairs, phases = [], [None] * len(devices)
        for d, lane in enumerate(lanes):
            for r in range(rows):
                item = lane.lines[r][0].get(t)
                if item is not None and item.home is not None:
                    pairs.append((number(r, lane.col(0)), number(item.home, lane.col(0))))
                    phases[pairs[-1][0]] = (r + d) % 2
        if pairs:
            returns[t] = pairs, phases

    columns = []

    def add(entries):
        columns.append(np.asarray(entries, np.int32))
        return sum(c.shape[1] for c in columns[:-1])

    relays = {}
    for key in sends:
        kinds = kinds_of[key]
        names = sorted(set(kinds) - {None, "own"}, key=str)
        if names and (len(names) > 1 or "own" in kinds):
            entries = []
            for kind, item in zip(kinds, own_of[key]):
                if kind == "own":
                    entries.append((0, item.piece, group_here(item)))
                else:
                    entries.append((1 + names.index(kind) if kind is not None else 1, 0, 0))
            relays[key] = names, add(entries)
    for t, (pairs, phases) in returns.items():
        if len(set(phases) - {None}) > 1:
            relays["back", t] = None, add([(1 + (p or 0), 0, 0) for p in phases])

    order = []
    for r, c in devices:
        arrivals = []
        for s in range(STEPS):
            when, key = 0, -1 - (r + s) % rows % groups_here
            for d, lane in enumerate(lanes):
                arrival = lane.arrival(r, c, (0, s))
                if arrival is not None:
                    t, returned = arrival
                    when, key = (t + 0.7, ("back", t)) if returned else (t, ((r + d) % 2, t))
            arrivals.append((when, s, key))
        order.append(sorted(arrivals, key=lambda a: a[:2]))
    rank_at = add([[[a[1] for a in arrivals].index(s) for s in range(STEPS)] for arrivals in order])
    used, candidates, source_at = [], [], []
    for ranks in (range(STEPS - 1), range(STEPS - 1, STEPS)):
        keys = {arrivals[k][2] for arrivals in order for k in ranks}
        used.append(sorted((k for k in keys if isinstance(k, tuple)), key=lambda k: (k[1], str(k[0]))))
        places = [
            [arrivals[k][2] if isinstance(arrivals[k][2], int) else used[-1].index(arrivals[k][2]) for k in ranks]
            for arrivals in order
        ]
        candidates.append([sorted({max(p[i], -1) for p in places}) for i in range(len(ranks))])
        source_at.append(
            add([[n for p, k in zip(row, ranks) for n in (p, arrivals[k][1])] for row, arrivals in zip(places, order)])
        )
    table = np.concatenate(columns, axis=1)
    table = lax.dynamic_slice(jnp.asarray(table), (device, 0), (1, table.shape[1]))[0]

    def own_chunk(items, x=x):
        piece = lookup([None if i is None else i.piece for i in items], device)
        group = lookup([None if i is None else group_here(i) for i in items], device)
        return lax.dynamic_slice(x, (piece * piece_rows, group * group_size), (piece_rows, group_size))

    factor = weight / jnp.sqrt(2.0 * freq * (1.0 - freq))
    twice = 2.0 * freq
    male_scale = np.float32(np.sqrt(0.5))
    male_rows = jnp.where(sex_rows > 0, male_scale, np.float32(1.0))
    male_cols = jnp.where(sex_cols > 0, male_scale, np.float32(1.0))
    wide = lambda value: jnp.broadcast_to(value[:, None], (value.shape[0], LANES))

    def in_window(value):
        span = STEPS * group_size
        return lax.dynamic_slice(jnp.concatenate([value, value]), (row_place * group_size,), (span,))

    window_factor, window_twice = in_window(factor), in_window(twice)
    male_wide = wide(male_rows)

    def own_squares():
        here = lambda value: lax.dynamic_slice(value, (col_place * local_vars,), (local_vars,))[None, :]
        zx = ((x.astype(jnp.float32) - here(twice)) * here(factor) * male_rows[:, None]).astype(jnp.bfloat16)
        return jnp.sum(jnp.square(zx.astype(jnp.float32)), axis=1)

    back = [(i, (i - 1) % rows) for i in range(rows)]
    window = [y]
    while len(window) < STEPS:
        window.append(lax.ppermute(window[-1], "row", back))
    squares = own_squares()

    starts = {}
    if any(own_of[0, 1]):
        starts[0, 1] = own_chunk(own_of[0, 1])
    later_x = x
    for k, crossing in enumerate(crossings):
        later_x = lax.optimization_barrier(later_x)
        starts["cross", k] = own_chunk([crossing[rc][1] if rc in crossing else None for rc in devices], later_x)
    later_x, squares = lax.optimization_barrier((later_x, squares))
    if any(own_of[1, 1]):
        starts[1, 1] = own_chunk(own_of[1, 1], later_x)
    bits = [1 << k for k in range(cols.bit_length() - 1)] if cols & (cols - 1) == 0 else []
    if cols & (cols - 1):
        squares = lax.psum(squares, "col")

    def sum_beside(value, squares):
        if not bits:
            return value, squares
        bit = bits.pop(0)
        other = lax.ppermute(squares, "col", [(i, i ^ bit) for i in range(cols)])
        value, other = lax.optimization_barrier((value, other))
        return value, squares + other

    buffers, crossed = {}, {}

    def bring_back(t):
        if t in returns:
            pairs, phases = returns[t]
            if ("back", t) in relays:
                held = relay(relays["back", t][1], table, x, [buffers[0, t], buffers[1, t]])
            else:
                held = buffers[next(p for p in phases if p is not None), t]
            buffers["back", t] = lax.ppermute(held, both, pairs)

    for key in sends:
        phase, t = key
        if pairs_of[key]:
            if key in relays:
                names, at = relays[key]
                sources = [buffers[phase, t - DEPTH] if name == "forward" else crossed[name] for name in names]
                held = relay(at, table, x, sources)
            elif key in starts:
                held = starts[key]
            elif "forward" in kinds_of[key]:
                held = buffers[phase, t - DEPTH]
            elif "own" in kinds_of[key]:
                held = own_chunk(own_of[key])
            else:
                held = crossed[next(k for k in kinds_of[key] if k is not None)]
            buffers[key] = lax.ppermute(held, both, pairs_of[key])
        if key == (0, 1):
            for k, crossing in enumerate(crossings):
                pairs = [(number(*rc), number(*to)) for rc, (to, _) in crossing.items()]
                crossed[k] = lax.ppermute(starts["cross", k], both, pairs)
        if phase == 1:
            bring_back(t - 1)
    bring_back(rounds)
    zy = standardized_window(rank_at, table, window, wide(window_factor), wide(window_twice), male_cols[None, :])
    zy, squares = sum_beside(zy, squares)
    shared = window_factor[None, :], window_twice[None, :], male_wide, zy
    total = early_product(source_at[0], candidates[0], table, x, [buffers[k] for k in used[0]], *shared)
    total, squares = sum_beside(total, squares)
    relation = last_product(source_at[1], candidates[1][0], table, x, [buffers[k] for k in used[1]], *shared, total)
    for bit in bits:
        squares = squares + lax.ppermute(squares, "col", [(i, i ^ bit) for i in range(cols)])
    inbreeding = squares / jnp.float32(freq.shape[0]) - 1.0
    return relation, inbreeding


def solution(mesh):
    rows, cols = mesh.shape["row"], mesh.shape["col"]
    return jax.shard_map(
        functools.partial(local, rows, cols),
        mesh=mesh,
        in_specs=(P("row", "col"), P("row", "col"), P(), P(), P("row"), P("col")),
        out_specs=(P("row", "col"), P("row")),
        check_vma=False,
    )
```

```python
import functools
import itertools

import jax
import jax.numpy as jnp
import numpy as np
from jax import lax
from jax.experimental import pallas as pl
from jax.experimental.pallas import tpu as pltpu
from jax.sharding import PartitionSpec as P

STEPS = 4
PIECES = 1
DEPTH = 1
HOP = 1
COL_TILE = 512
ROW_BLOCK = 512
ROW_TILE = 32
LANES = 128
VMEM_LIMIT = 10 * 2**20
RELAY_LIMIT = 2 * 2**20


class Item:
    def __init__(self, row, piece, s, place, home=None):
        self.row, self.piece, self.s, self.place = row, piece, s, place
        self.home = home

    @property
    def owner(self):
        return self.row if self.home is None else self.home

    @property
    def key(self):
        return self.piece, self.s


def line_slots(items):
    slots = {}
    todo = sorted(items, key=lambda i: (i.home is None, i.piece, i.place, i.s))
    slot = 1
    while todo:
        for item in todo:
            first = 1 + DEPTH * (item.place - 1) + (HOP if item.home is not None else 0)
            if first <= slot:
                slots[slot] = item
                todo.remove(item)
                break
        slot += 1
    return slots


class Lane:
    def __init__(self, rows, cols, groups_here, towards_zero):
        self.rows, self.cols = rows, cols
        self.towards_zero = towards_zero
        self.items = []
        for r in range(rows):
            mine = [
                Item(r, piece, s, self.place((r + s) % rows // groups_here))
                for piece in range(PIECES)
                for s in range(STEPS)
            ]
            self.items.append([i for i in mine if i.place > 0])
        self.away = []
        self.lines = [line_slots(items) for items in self.items]
        if rows % 4 == 0 and cols > 3:
            for r in range(rows // 2):
                other = r + rows // 2 if towards_zero else (r + rows // 2) ^ 1
                self.balance(r, other)
                self.balance(other, r)
        self.rounds = max([max(slots, default=0) for slots in self.lines])

    def place(self, c):
        return c if self.towards_zero else self.cols - 1 - c

    col = place

    def balance(self, r, other):
        if len(self.items[r]) < len(self.items[other]) or any(i.row == other for i in self.away):
            return
        places = sorted({i.place for i in self.items[r]})
        best = None
        for counts in itertools.product(range(3), repeat=len(places)):
            gone = []
            for place, count in zip(places, counts):
                here = [i for i in self.items[r] if i.place == place]
                here.sort(key=lambda i: i.key, reverse=True)
                gone += here[:count]
            visitors = [Item(other, i.piece, i.s, i.place, home=r) for i in gone]
            mine = line_slots([i for i in self.items[r] if i not in gone])
            theirs = line_slots(self.items[other] + visitors)
            score = (
                max(max(mine, default=0), max(theirs, default=0), STEPS),
                len(gone),
                max([slot for slot, i in theirs.items() if i.home is not None], default=0),
            )
            if best is None or score < best[0]:
                best = score, gone, mine, theirs
        _, gone, mine, theirs = best
        self.away += gone
        if gone:
            self.lines[r], self.lines[other] = mine, theirs

    def sent(self, r, c, t):
        p = self.place(c)
        item = self.lines[r].get(t + DEPTH * (p - 1)) if p > 0 else None
        return item if item is not None and item.place >= p else None

    def pairs(self, t):
        found = []
        for r in range(self.rows):
            for c in range(self.cols):
                if self.sent(r, c, t) is not None:
                    found.append((r * self.cols + c, r * self.cols + self.col(self.place(c) - 1)))
        return found

    def arrival(self, r, c, key):
        p = self.place(c)
        for i in self.items[r]:
            if i.key == key and i.place > p:
                for slots in self.lines:
                    for slot, v in slots.items():
                        if v is i or (v.home == r and v.key == key):
                            return slot - DEPTH * p, v is not i
        return None


def lookup(values, device):
    known = [v for v in values if v is not None]
    if len(set(known)) <= 1:
        return known[0] if known else 0
    values = [known[0] if v is None else v for v in values]
    result = jnp.uint32(0)
    place = (device % 32).astype(jnp.uint32)
    for bit in range(max(values).bit_length()):
        ones = [v >> bit & 1 for v in values]
        words = [sum(b << i for i, b in enumerate(ones[at : at + 32])) for at in range(0, len(ones), 32)]
        word = jnp.uint32(words[0])
        for i, other in enumerate(words[1:], 1):
            word = jnp.where(device // 32 == i, jnp.uint32(other), word)
        result = result | (((word >> place) & jnp.uint32(1)) << jnp.uint32(bit))
    return result.astype(jnp.int32)


def relay_kernel(at, table, x, *refs):
    *sources, out = refs
    rows, width = out.shape

    @pl.when(table[at] == 0)
    def _():
        row = pl.multiple_of(table[at + 1] * rows, rows)
        col = pl.multiple_of(table[at + 2] * width, width)
        out[...] = x[pl.ds(row, rows), pl.ds(col, width)]

    for i, source in enumerate(sources):

        @pl.when(table[at] == i + 1)
        def _(source=source):
            out[...] = source[...]


def relay(at, table, x, sources):
    return pl.pallas_call(
        functools.partial(relay_kernel, at),
        out_shape=pltpu.VMEM(sources[0].shape, sources[0].dtype),
        in_specs=[pl.BlockSpec(memory_space=pltpu.SMEM)] + [VMEM] * (1 + len(sources)),
        out_specs=VMEM,
        compiler_params=pltpu.CompilerParams(vmem_limit_bytes=RELAY_LIMIT),
        cost_estimate=pl.CostEstimate(flops=0, bytes_accessed=0, transcendentals=0),
        name="relay",
    )(table, *[in_vmem(v) for v in (x, *sources)])


def in_vmem(value):
    return pltpu.with_memory_space_constraint(value, pltpu.VMEM)


VMEM = pl.BlockSpec(memory_space=pltpu.VMEM)


def window_kernel(at, table, *refs):
    blocks = refs[:STEPS]
    factor, twice, male, out = refs[STEPS:]
    group_size, width = blocks[0].shape
    for s, block in enumerate(blocks):
        rank = table[at + s]

        @pl.loop(0, group_size // ROW_TILE)
        def _(i, s=s, block=block, rank=rank):
            here = pl.ds(pl.multiple_of(i * ROW_TILE, ROW_TILE), ROW_TILE)
            rows = pl.ds(pl.multiple_of(s * group_size + i * ROW_TILE, ROW_TILE), ROW_TILE)
            to = pl.ds(pl.multiple_of(rank * group_size + i * ROW_TILE, ROW_TILE), ROW_TILE)
            for k in range(0, width, LANES):
                value = block[here, k : k + LANES].astype(jnp.float32) - twice[rows, :]
                out[to, k : k + LANES] = (value * factor[rows, :] * male[:, k : k + LANES]).astype(out.dtype)


def standardized_window(at, table, blocks, factor, twice, male):
    group_size, n = blocks[0].shape
    depth = STEPS * group_size
    return pl.pallas_call(
        functools.partial(window_kernel, at),
        out_shape=pltpu.VMEM((depth, n), jnp.bfloat16),
        in_specs=[pl.BlockSpec(memory_space=pltpu.SMEM)] + [VMEM] * (STEPS + 3),
        out_specs=VMEM,
        compiler_params=pltpu.CompilerParams(vmem_limit_bytes=VMEM_LIMIT),
        cost_estimate=pl.CostEstimate(flops=4 * depth * n, bytes_accessed=4 * depth * n, transcendentals=0),
        name="window",
    )(table, *[in_vmem(v) for v in (*blocks, factor, twice, male)])


def standardize(table, at, candidates, x, buffers, factor, twice, male, zx, columns, first, count):
    width = columns.stop - columns.start
    place, step = table[at], table[at + 1]

    def from_source(source, col):
        @pl.loop(0, count // ROW_TILE)
        def _(i):
            here = pl.ds(pl.multiple_of(first + i * ROW_TILE, ROW_TILE), ROW_TILE)
            to = pl.ds(pl.multiple_of(i * ROW_TILE, ROW_TILE), ROW_TILE)
            for k in range(0, width, LANES):
                lanes = pl.ds(pl.multiple_of(step * width + k, LANES), LANES)
                value = source[here, pl.ds(pl.multiple_of(col + k, LANES), LANES)].astype(jnp.float32)
                value = (value - twice[:, lanes]) * factor[:, lanes] * male[here, :]
                zx[to, columns.start + k : columns.start + k + LANES] = value.astype(zx.dtype)

    for number in candidates:
        if number >= 0:

            @pl.when(place == number)
            def _(number=number):
                from_source(buffers[number], 0)

        else:

            @pl.when(place < 0)
            def _():
                from_source(x, (-1 - place) * width)


def early_kernel(at, candidates, n_buffers, table, x, *refs):
    buffers = refs[:n_buffers]
    factor, twice, male, zy, total, zx = refs[n_buffers:]
    rows, depth = zx.shape
    width = depth // (STEPS - 1)
    for rank in range(STEPS - 1):
        columns = slice(rank * width, (rank + 1) * width)
        standardize(table, at + 2 * rank, candidates[rank], x, buffers, factor, twice, male, zx, columns, 0, rows)

    @pl.loop(0, rows // ROW_BLOCK)
    def _(i):
        block = pl.ds(pl.multiple_of(i * ROW_BLOCK, ROW_BLOCK), ROW_BLOCK)
        for j in range(0, total.shape[1], COL_TILE):
            right = zy[:depth, j : j + COL_TILE]
            total[block, j : j + COL_TILE] = jnp.dot(zx[block, :], right, preferred_element_type=jnp.float32)


def early_product(at, candidates, table, x, buffers, factor, twice, male, zy):
    rows, (depth, n) = x.shape[0], zy.shape
    depth = depth // STEPS * (STEPS - 1)
    args = [in_vmem(v) for v in (x, *buffers, factor, twice, male, zy)]
    return pl.pallas_call(
        functools.partial(early_kernel, at, candidates, len(buffers)),
        out_shape=pltpu.VMEM((rows, n), jnp.float32),
        in_specs=[pl.BlockSpec(memory_space=pltpu.SMEM)] + [VMEM] * len(args),
        out_specs=VMEM,
        scratch_shapes=[pltpu.VMEM((rows, depth), jnp.bfloat16)],
        compiler_params=pltpu.CompilerParams(vmem_limit_bytes=VMEM_LIMIT),
        cost_estimate=pl.CostEstimate(flops=2 * rows * depth * n, bytes_accessed=0, transcendentals=0),
        name="early",
    )(table, *args)


def last_kernel(at, candidates, scale, n_buffers, table, x, *refs):
    buffers = refs[:n_buffers]
    factor, twice, male, zy, total, out, zx, blocks, sems = refs[n_buffers:]
    rows, n = total.shape
    width = zx.shape[1]

    def copy(i):
        return pltpu.make_async_copy(blocks.at[i % 2], out.at[pl.ds(i * ROW_BLOCK, ROW_BLOCK), :], sems.at[i % 2])

    count = rows // ROW_BLOCK
    for i in range(count):
        first = i * ROW_BLOCK
        standardize(
            table, at, candidates, x, buffers, factor, twice, male, zx, slice(0, width), first, ROW_BLOCK
        )
        if i >= 2:
            copy(i - 2).wait()
        for j in range(0, n, COL_TILE):
            right = zy[zy.shape[0] - width :, j : j + COL_TILE]
            product = jnp.dot(zx[...], right, preferred_element_type=jnp.float32)
            product = product + total[first : first + ROW_BLOCK, j : j + COL_TILE]
            blocks[i % 2, :, j : j + COL_TILE] = (product * scale).astype(blocks.dtype)
        copy(i).start()
    for i in range(max(count - 2, 0), count):
        copy(i).wait()


def last_product(at, candidates, table, x, buffers, factor, twice, male, zy, total):
    rows, (depth, n) = x.shape[0], zy.shape
    width = depth // STEPS
    scale = float(1.0 / np.sqrt(np.float32(depth)))
    args = [in_vmem(v) for v in (x, *buffers, factor, twice, male, zy, total)]
    return pl.pallas_call(
        functools.partial(last_kernel, at, candidates, scale, len(buffers)),
        out_shape=jax.ShapeDtypeStruct((rows, n), jnp.bfloat16),
        in_specs=[pl.BlockSpec(memory_space=pltpu.SMEM)] + [VMEM] * len(args),
        out_specs=pl.BlockSpec(memory_space=pl.ANY),
        scratch_shapes=[
            pltpu.VMEM((ROW_BLOCK, width), jnp.bfloat16),
            pltpu.VMEM((2, ROW_BLOCK, n), jnp.bfloat16),
            pltpu.SemaphoreType.DMA((2,)),
        ],
        compiler_params=pltpu.CompilerParams(vmem_limit_bytes=VMEM_LIMIT),
        cost_estimate=pl.CostEstimate(flops=2 * rows * width * n, bytes_accessed=2 * rows * n, transcendentals=0),
        name="last",
    )(table, *args)


def local(rows, cols, x, y, freq, weight, sex_rows, sex_cols):
    group_size = y.shape[0]
    local_vars = x.shape[1]
    groups_here = local_vars // group_size
    piece_rows = x.shape[0] // PIECES
    lanes = [Lane(rows, cols, groups_here, towards) for towards in (True, False)]
    rounds = max(lane.rounds for lane in lanes)
    devices = [(r, c) for r in range(rows) for c in range(cols)]
    both = ("row", "col")

    row_place = lax.axis_index("row")
    col_place = lax.axis_index("col")
    device = row_place * cols + col_place

    def number(r, c):
        return r * cols + c

    def group_here(item):
        return (item.owner + item.s) % rows % groups_here

    crossings = []
    crossing_of = {}
    for d, lane in enumerate(lanes):
        for r in range(rows):
            for slot, item in sorted(lane.lines[r].items()):
                if item.home is None:
                    continue
                source, target = (item.home, lane.col(item.place)), (r, lane.col(item.place))
                for k, crossing in enumerate(crossings):
                    if source not in crossing and target not in [to for to, _ in crossing.values()]:
                        break
                else:
                    k = len(crossings)
                    crossings.append({})
                crossings[k][source] = (target, item)
                crossing_of[d, r, item.key] = k

    def lane_of(phase, r):
        return (r + phase) % 2

    sends = [(phase, t) for t in range(1, rounds + 1) for phase in range(2)]
    pairs_of, kinds_of, own_of = {}, {}, {}
    for phase, t in sends:
        pairs, kinds, own = [], [], []
        for r, c in devices:
            lane = lanes[lane_of(phase, r)]
            item = lane.sent(r, c, t)
            if item is not None:
                pairs.append((number(r, c), number(r, lane.col(lane.place(c) - 1))))
            if item is None:
                kinds.append(None)
            elif item.place != lane.place(c):
                kinds.append("forward")
            elif item.home is not None:
                kinds.append(crossing_of[lane_of(phase, r), r, item.key])
            else:
                kinds.append("own")
            own.append(item if kinds[-1] == "own" else None)
        pairs_of[phase, t], kinds_of[phase, t], own_of[phase, t] = pairs, kinds, own

    returns = {}
    for d, lane in enumerate(lanes):
        for r in range(rows):
            for slot, item in lane.lines[r].items():
                if item.home is not None:
                    for p in range(item.place):
                        pair = number(r, lane.col(p)), number(item.home, lane.col(p))
                        returns.setdefault(((r + d) % 2, slot - DEPTH * p), []).append(pair)

    columns = []

    def add(entries):
        columns.append(np.asarray(entries, np.int32))
        return sum(c.shape[1] for c in columns[:-1])

    relays = {}
    for key in sends:
        kinds = kinds_of[key]
        names = sorted(set(kinds) - {None, "own"}, key=str)
        if names and (len(names) > 1 or "own" in kinds):
            entries = []
            for kind, item in zip(kinds, own_of[key]):
                if kind == "own":
                    entries.append((0, item.piece, group_here(item)))
                else:
                    entries.append((1 + names.index(kind) if kind is not None else 1, 0, 0))
            relays[key] = names, add(entries)

    order = []
    for r, c in devices:
        arrivals = []
        for s in range(STEPS):
            when, key = 0, -1 - (r + s) % rows % groups_here
            for d, lane in enumerate(lanes):
                arrival = lane.arrival(r, c, (0, s))
                if arrival is not None:
                    t, returned = arrival
                    when, key = t, ((r + d) % 2, t)
                    if returned:
                        phase = 0 if any(to == number(r, c) for _, to in returns.get((0, t), [])) else 1
                        when, key = t + 0.7, ("back%d" % phase, t)
            arrivals.append((when, s, key))
        order.append(sorted(arrivals, key=lambda a: a[:2]))
    rank_at = add([[[a[1] for a in arrivals].index(s) for s in range(STEPS)] for arrivals in order])
    used, candidates, source_at = [], [], []
    for ranks in (range(STEPS - 1), range(STEPS - 1, STEPS)):
        keys = {arrivals[k][2] for arrivals in order for k in ranks}
        used.append(sorted((k for k in keys if isinstance(k, tuple)), key=lambda k: (k[1], str(k[0]))))
        places = [
            [arrivals[k][2] if isinstance(arrivals[k][2], int) else used[-1].index(arrivals[k][2]) for k in ranks]
            for arrivals in order
        ]
        candidates.append([sorted({max(p[i], -1) for p in places}) for i in range(len(ranks))])
        source_at.append(
            add([[n for p, k in zip(row, ranks) for n in (p, arrivals[k][1])] for row, arrivals in zip(places, order)])
        )
    table = np.concatenate(columns, axis=1)
    table = lax.dynamic_slice(jnp.asarray(table), (device, 0), (1, table.shape[1]))[0]

    def own_chunk(items, x=x):
        piece = lookup([None if i is None else i.piece for i in items], device)
        group = lookup([None if i is None else group_here(i) for i in items], device)
        return lax.dynamic_slice(x, (piece * piece_rows, group * group_size), (piece_rows, group_size))

    factor = weight / jnp.sqrt(2.0 * freq * (1.0 - freq))
    twice = 2.0 * freq
    male_scale = np.float32(np.sqrt(0.5))
    male_rows = jnp.where(sex_rows > 0, male_scale, np.float32(1.0))
    male_cols = jnp.where(sex_cols > 0, male_scale, np.float32(1.0))
    wide = lambda value: jnp.broadcast_to(value[:, None], (value.shape[0], LANES))

    def in_window(value):
        span = STEPS * group_size
        return lax.dynamic_slice(jnp.concatenate([value, value]), (row_place * group_size,), (span,))

    window_factor, window_twice = in_window(factor), in_window(twice)
    male_wide = wide(male_rows)

    def own_squares():
        here = lambda value: lax.dynamic_slice(value, (col_place * local_vars,), (local_vars,))[None, :]
        zx = ((x.astype(jnp.float32) - here(twice)) * here(factor) * male_rows[:, None]).astype(jnp.bfloat16)
        return jnp.sum(jnp.square(zx.astype(jnp.float32)), axis=1)

    back = [(i, (i - 1) % rows) for i in range(rows)]
    window = [y]
    while len(window) < STEPS:
        window.append(lax.ppermute(window[-1], "row", back))
    squares = own_squares()

    starts = {}
    if any(own_of[0, 1]):
        starts[0, 1] = own_chunk(own_of[0, 1])
    later_x = x
    for k, crossing in enumerate(crossings):
        later_x = lax.optimization_barrier(later_x)
        starts["cross", k] = own_chunk([crossing[rc][1] if rc in crossing else None for rc in devices], later_x)
    later_x, squares = lax.optimization_barrier((later_x, squares))
    if any(own_of[1, 1]):
        starts[1, 1] = own_chunk(own_of[1, 1], later_x)
    def col_sum_beside(value, squares):
        if cols & (cols - 1):
            return value, lax.psum(squares, "col")
        parts = [squares]
        for mask in range(1, cols):
            parts.append(lax.ppermute(squares, "col", [(i, i ^ mask) for i in range(cols)]))
        value, *parts = lax.optimization_barrier((value, *parts))
        while len(parts) > 1:
            parts = [a + b for a, b in zip(parts[::2], parts[1::2])]
        return value, parts[0]

    buffers, crossed = {}, {}

    def bring_back(key):
        if key in returns:
            phase, t = key
            buffers["back%d" % phase, t] = lax.ppermute(buffers[key], both, returns[key])

    for key in sends:
        phase, t = key
        if pairs_of[key]:
            if key in relays:
                names, at = relays[key]
                sources = [buffers[phase, t - DEPTH] if name == "forward" else crossed[name] for name in names]
                held = relay(at, table, x, sources)
            elif key in starts:
                held = starts[key]
            elif "forward" in kinds_of[key]:
                held = buffers[phase, t - DEPTH]
            elif "own" in kinds_of[key]:
                held = own_chunk(own_of[key])
            else:
                held = crossed[next(k for k in kinds_of[key] if k is not None)]
            name = "back%d" % phase, t - 2
            if name in buffers:
                held, buffers[name] = lax.optimization_barrier((held, buffers[name]))
            buffers[key] = lax.ppermute(held, both, pairs_of[key])
        if key == (0, 1):
            for k, crossing in enumerate(crossings):
                pairs = [(number(*rc), number(*to)) for rc, (to, _) in crossing.items()]
                crossed[k] = lax.ppermute(starts["cross", k], both, pairs)
        bring_back(key)
    zy = standardized_window(rank_at, table, window, wide(window_factor), wide(window_twice), male_cols[None, :])
    shared = window_factor[None, :], window_twice[None, :], male_wide, zy
    total = early_product(source_at[0], candidates[0], table, x, [buffers[k] for k in used[0]], *shared)
    total, squares = lax.optimization_barrier((total, squares))
    relation = last_product(source_at[1], candidates[1][0], table, x, [buffers[k] for k in used[1]], *shared, total)
    relation, squares = col_sum_beside(relation, squares)
    inbreeding = squares / jnp.float32(freq.shape[0]) - 1.0
    return relation, inbreeding


def solution(mesh):
    rows, cols = mesh.shape["row"], mesh.shape["col"]
    return jax.shard_map(
        functools.partial(local, rows, cols),
        mesh=mesh,
        in_specs=(P("row", "col"), P("row", "col"), P(), P(), P("row"), P("col")),
        out_specs=(P("row", "col"), P("row")),
        check_vma=False,
    )
```

```python
import functools
import itertools

import jax
import jax.numpy as jnp
import numpy as np
from jax import lax
from jax.experimental import pallas as pl
from jax.experimental.pallas import tpu as pltpu
from jax.sharding import PartitionSpec as P

STEPS = 4
PIECES = 1
DEPTH = 1
HOP = 1
COL_TILE = 512
ROW_BLOCK = 512
ROW_TILE = 32
LANES = 128
VMEM_LIMIT = 10 * 2**20
RELAY_LIMIT = 2 * 2**20


class Item:
    def __init__(self, row, piece, s, place, home=None):
        self.row, self.piece, self.s, self.place = row, piece, s, place
        self.home = home

    @property
    def owner(self):
        return self.row if self.home is None else self.home

    @property
    def key(self):
        return self.piece, self.s


def line_slots(items):
    slots = {}
    todo = sorted(items, key=lambda i: (i.home is None, i.piece, i.place, i.s))
    slot = 1
    while todo:
        for item in todo:
            first = 1 + DEPTH * (item.place - 1) + (HOP if item.home is not None else 0)
            if first <= slot:
                slots[slot] = item
                todo.remove(item)
                break
        slot += 1
    return slots


class Lane:
    def __init__(self, rows, cols, groups_here, towards_zero):
        self.rows, self.cols = rows, cols
        self.towards_zero = towards_zero
        self.items = []
        for r in range(rows):
            mine = [
                Item(r, piece, s, self.place((r + s) % rows // groups_here))
                for piece in range(PIECES)
                for s in range(STEPS)
            ]
            self.items.append([i for i in mine if i.place > 0])
        self.away = []
        self.lines = [line_slots(items) for items in self.items]
        if rows % 4 == 0 and cols > 3:
            for r in range(rows // 2):
                other = r + rows // 2 if towards_zero else (r + rows // 2) ^ 1
                self.balance(r, other)
                self.balance(other, r)
        self.rounds = max([max(slots, default=0) for slots in self.lines])

    def place(self, c):
        return c if self.towards_zero else self.cols - 1 - c

    col = place

    def balance(self, r, other):
        if len(self.items[r]) < len(self.items[other]) or any(i.row == other for i in self.away):
            return
        places = sorted({i.place for i in self.items[r]})
        best = None
        for counts in itertools.product(range(3), repeat=len(places)):
            gone = []
            for place, count in zip(places, counts):
                here = [i for i in self.items[r] if i.place == place]
                here.sort(key=lambda i: i.key, reverse=True)
                gone += here[:count]
            visitors = [Item(other, i.piece, i.s, i.place, home=r) for i in gone]
            mine = line_slots([i for i in self.items[r] if i not in gone])
            theirs = line_slots(self.items[other] + visitors)
            score = (
                max(max(mine, default=0), max(theirs, default=0), STEPS),
                len(gone),
                max([slot for slot, i in theirs.items() if i.home is not None], default=0),
            )
            if best is None or score < best[0]:
                best = score, gone, mine, theirs
        _, gone, mine, theirs = best
        self.away += gone
        if gone:
            self.lines[r], self.lines[other] = mine, theirs

    def sent(self, r, c, t):
        p = self.place(c)
        item = self.lines[r].get(t + DEPTH * (p - 1)) if p > 0 else None
        return item if item is not None and item.place >= p else None

    def pairs(self, t):
        found = []
        for r in range(self.rows):
            for c in range(self.cols):
                if self.sent(r, c, t) is not None:
                    found.append((r * self.cols + c, r * self.cols + self.col(self.place(c) - 1)))
        return found

    def arrival(self, r, c, key):
        p = self.place(c)
        for i in self.items[r]:
            if i.key == key and i.place > p:
                for slots in self.lines:
                    for slot, v in slots.items():
                        if v is i or (v.home == r and v.key == key):
                            return slot - DEPTH * p, v is not i
        return None


def lookup(values, device):
    known = [v for v in values if v is not None]
    if len(set(known)) <= 1:
        return known[0] if known else 0
    values = [known[0] if v is None else v for v in values]
    result = jnp.uint32(0)
    place = (device % 32).astype(jnp.uint32)
    for bit in range(max(values).bit_length()):
        ones = [v >> bit & 1 for v in values]
        words = [sum(b << i for i, b in enumerate(ones[at : at + 32])) for at in range(0, len(ones), 32)]
        word = jnp.uint32(words[0])
        for i, other in enumerate(words[1:], 1):
            word = jnp.where(device // 32 == i, jnp.uint32(other), word)
        result = result | (((word >> place) & jnp.uint32(1)) << jnp.uint32(bit))
    return result.astype(jnp.int32)


def relay_kernel(at, table, x, *refs):
    *sources, out = refs
    rows, width = out.shape

    @pl.when(table[at] == 0)
    def _():
        row = pl.multiple_of(table[at + 1] * rows, rows)
        col = pl.multiple_of(table[at + 2] * width, width)
        out[...] = x[pl.ds(row, rows), pl.ds(col, width)]

    for i, source in enumerate(sources):

        @pl.when(table[at] == i + 1)
        def _(source=source):
            out[...] = source[...]


def relay(at, table, x, sources):
    return pl.pallas_call(
        functools.partial(relay_kernel, at),
        out_shape=pltpu.VMEM(sources[0].shape, sources[0].dtype),
        in_specs=[pl.BlockSpec(memory_space=pltpu.SMEM)] + [VMEM] * (1 + len(sources)),
        out_specs=VMEM,
        compiler_params=pltpu.CompilerParams(vmem_limit_bytes=RELAY_LIMIT),
        cost_estimate=pl.CostEstimate(flops=0, bytes_accessed=0, transcendentals=0),
        name="relay",
    )(table, *[in_vmem(v) for v in (x, *sources)])


def in_vmem(value):
    return pltpu.with_memory_space_constraint(value, pltpu.VMEM)


VMEM = pl.BlockSpec(memory_space=pltpu.VMEM)


def window_kernel(at, table, *refs):
    blocks = refs[:STEPS]
    factor, twice, male, out = refs[STEPS:]
    group_size, width = blocks[0].shape
    for s, block in enumerate(blocks):
        rank = table[at + s]

        @pl.loop(0, group_size // ROW_TILE)
        def _(i, s=s, block=block, rank=rank):
            here = pl.ds(pl.multiple_of(i * ROW_TILE, ROW_TILE), ROW_TILE)
            rows = pl.ds(pl.multiple_of(s * group_size + i * ROW_TILE, ROW_TILE), ROW_TILE)
            to = pl.ds(pl.multiple_of(rank * group_size + i * ROW_TILE, ROW_TILE), ROW_TILE)
            for k in range(0, width, LANES):
                value = block[here, k : k + LANES].astype(jnp.float32) - twice[rows, :]
                out[to, k : k + LANES] = (value * factor[rows, :] * male[:, k : k + LANES]).astype(out.dtype)


def standardized_window(at, table, blocks, factor, twice, male):
    group_size, n = blocks[0].shape
    depth = STEPS * group_size
    return pl.pallas_call(
        functools.partial(window_kernel, at),
        out_shape=pltpu.VMEM((depth, n), jnp.bfloat16),
        in_specs=[pl.BlockSpec(memory_space=pltpu.SMEM)] + [VMEM] * (STEPS + 3),
        out_specs=VMEM,
        compiler_params=pltpu.CompilerParams(vmem_limit_bytes=VMEM_LIMIT),
        cost_estimate=pl.CostEstimate(flops=4 * depth * n, bytes_accessed=4 * depth * n, transcendentals=0),
        name="window",
    )(table, *[in_vmem(v) for v in (*blocks, factor, twice, male)])


def standardize(table, at, candidates, x, buffers, factor, twice, male, zx, columns, first, count):
    width = columns.stop - columns.start
    place, step = table[at], table[at + 1]

    def from_source(source, col):
        @pl.loop(0, count // ROW_TILE)
        def _(i):
            here = pl.ds(pl.multiple_of(first + i * ROW_TILE, ROW_TILE), ROW_TILE)
            to = pl.ds(pl.multiple_of(i * ROW_TILE, ROW_TILE), ROW_TILE)
            for k in range(0, width, LANES):
                lanes = pl.ds(pl.multiple_of(step * width + k, LANES), LANES)
                value = source[here, pl.ds(pl.multiple_of(col + k, LANES), LANES)].astype(jnp.float32)
                value = (value - twice[:, lanes]) * factor[:, lanes] * male[here, :]
                zx[to, columns.start + k : columns.start + k + LANES] = value.astype(zx.dtype)

    for number in candidates:
        if number >= 0:

            @pl.when(place == number)
            def _(number=number):
                from_source(buffers[number], 0)

        else:

            @pl.when(place < 0)
            def _():
                from_source(x, (-1 - place) * width)


def early_kernel(at, candidates, n_buffers, table, x, *refs):
    buffers = refs[:n_buffers]
    factor, twice, male, zy, total, zx = refs[n_buffers:]
    rows, depth = zx.shape
    width = depth // (STEPS - 1)
    for rank in range(STEPS - 1):
        columns = slice(rank * width, (rank + 1) * width)
        standardize(table, at + 2 * rank, candidates[rank], x, buffers, factor, twice, male, zx, columns, 0, rows)

    @pl.loop(0, rows // ROW_BLOCK)
    def _(i):
        block = pl.ds(pl.multiple_of(i * ROW_BLOCK, ROW_BLOCK), ROW_BLOCK)
        for j in range(0, total.shape[1], COL_TILE):
            right = zy[:depth, j : j + COL_TILE]
            total[block, j : j + COL_TILE] = jnp.dot(zx[block, :], right, preferred_element_type=jnp.float32)


def early_product(at, candidates, table, x, buffers, factor, twice, male, zy):
    rows, (depth, n) = x.shape[0], zy.shape
    depth = depth // STEPS * (STEPS - 1)
    args = [in_vmem(v) for v in (x, *buffers, factor, twice, male, zy)]
    return pl.pallas_call(
        functools.partial(early_kernel, at, candidates, len(buffers)),
        out_shape=pltpu.VMEM((rows, n), jnp.float32),
        in_specs=[pl.BlockSpec(memory_space=pltpu.SMEM)] + [VMEM] * len(args),
        out_specs=VMEM,
        scratch_shapes=[pltpu.VMEM((rows, depth), jnp.bfloat16)],
        compiler_params=pltpu.CompilerParams(vmem_limit_bytes=VMEM_LIMIT),
        cost_estimate=pl.CostEstimate(flops=2 * rows * depth * n, bytes_accessed=0, transcendentals=0),
        name="early",
    )(table, *args)


def last_kernel(at, candidates, scale, n_buffers, table, x, *refs):
    buffers = refs[:n_buffers]
    factor, twice, male, zy, total, out, zx, blocks, sems = refs[n_buffers:]
    rows, n = total.shape
    width = zx.shape[1]

    def copy(i):
        return pltpu.make_async_copy(blocks.at[i % 2], out.at[pl.ds(i * ROW_BLOCK, ROW_BLOCK), :], sems.at[i % 2])

    count = rows // ROW_BLOCK
    for i in range(count):
        first = i * ROW_BLOCK
        standardize(
            table, at, candidates, x, buffers, factor, twice, male, zx, slice(0, width), first, ROW_BLOCK
        )
        if i >= 2:
            copy(i - 2).wait()
        for j in range(0, n, COL_TILE):
            right = zy[zy.shape[0] - width :, j : j + COL_TILE]
            product = jnp.dot(zx[...], right, preferred_element_type=jnp.float32)
            product = product + total[first : first + ROW_BLOCK, j : j + COL_TILE]
            blocks[i % 2, :, j : j + COL_TILE] = (product * scale).astype(blocks.dtype)
        copy(i).start()
    for i in range(max(count - 2, 0), count):
        copy(i).wait()


def last_product(at, candidates, table, x, buffers, factor, twice, male, zy, total):
    rows, (depth, n) = x.shape[0], zy.shape
    width = depth // STEPS
    scale = float(1.0 / np.sqrt(np.float32(depth)))
    args = [in_vmem(v) for v in (x, *buffers, factor, twice, male, zy, total)]
    return pl.pallas_call(
        functools.partial(last_kernel, at, candidates, scale, len(buffers)),
        out_shape=jax.ShapeDtypeStruct((rows, n), jnp.bfloat16),
        in_specs=[pl.BlockSpec(memory_space=pltpu.SMEM)] + [VMEM] * len(args),
        out_specs=pl.BlockSpec(memory_space=pl.ANY),
        scratch_shapes=[
            pltpu.VMEM((ROW_BLOCK, width), jnp.bfloat16),
            pltpu.VMEM((2, ROW_BLOCK, n), jnp.bfloat16),
            pltpu.SemaphoreType.DMA((2,)),
        ],
        compiler_params=pltpu.CompilerParams(vmem_limit_bytes=VMEM_LIMIT),
        cost_estimate=pl.CostEstimate(flops=2 * rows * width * n, bytes_accessed=2 * rows * n, transcendentals=0),
        name="last",
    )(table, *args)


def local(rows, cols, x, y, freq, weight, sex_rows, sex_cols):
    group_size = y.shape[0]
    local_vars = x.shape[1]
    groups_here = local_vars // group_size
    piece_rows = x.shape[0] // PIECES
    lanes = [Lane(rows, cols, groups_here, towards) for towards in (True, False)]
    rounds = max(lane.rounds for lane in lanes)
    devices = [(r, c) for r in range(rows) for c in range(cols)]
    both = ("row", "col")

    row_place = lax.axis_index("row")
    col_place = lax.axis_index("col")
    device = row_place * cols + col_place

    def number(r, c):
        return r * cols + c

    def group_here(item):
        return (item.owner + item.s) % rows % groups_here

    crossings = []
    crossing_of = {}
    for d, lane in enumerate(lanes):
        for r in range(rows):
            for slot, item in sorted(lane.lines[r].items()):
                if item.home is None:
                    continue
                source, target = (item.home, lane.col(item.place)), (r, lane.col(item.place))
                for k, crossing in enumerate(crossings):
                    if source not in crossing and target not in [to for to, _ in crossing.values()]:
                        break
                else:
                    k = len(crossings)
                    crossings.append({})
                crossings[k][source] = (target, item)
                crossing_of[d, r, item.key] = k

    def lane_of(phase, r):
        return (r + phase) % 2

    sends = [(phase, t) for t in range(1, rounds + 1) for phase in range(2)]
    pairs_of, kinds_of, own_of = {}, {}, {}
    for phase, t in sends:
        pairs, kinds, own = [], [], []
        for r, c in devices:
            lane = lanes[lane_of(phase, r)]
            item = lane.sent(r, c, t)
            if item is not None:
                pairs.append((number(r, c), number(r, lane.col(lane.place(c) - 1))))
            if item is None:
                kinds.append(None)
            elif item.place != lane.place(c):
                kinds.append("forward")
            elif item.home is not None:
                kinds.append(crossing_of[lane_of(phase, r), r, item.key])
            else:
                kinds.append("own")
            own.append(item if kinds[-1] == "own" else None)
        pairs_of[phase, t], kinds_of[phase, t], own_of[phase, t] = pairs, kinds, own

    returns = {}
    for d, lane in enumerate(lanes):
        for r in range(rows):
            for slot, item in lane.lines[r].items():
                if item.home is not None:
                    for p in range(item.place):
                        pair = number(r, lane.col(p)), number(item.home, lane.col(p))
                        returns.setdefault(((r + d) % 2, slot - DEPTH * p), []).append(pair)

    columns = []

    def add(entries):
        columns.append(np.asarray(entries, np.int32))
        return sum(c.shape[1] for c in columns[:-1])

    relays = {}
    for key in sends:
        kinds = kinds_of[key]
        names = sorted(set(kinds) - {None, "own"}, key=str)
        if names and (len(names) > 1 or "own" in kinds):
            entries = []
            for kind, item in zip(kinds, own_of[key]):
                if kind == "own":
                    entries.append((0, item.piece, group_here(item)))
                else:
                    entries.append((1 + names.index(kind) if kind is not None else 1, 0, 0))
            relays[key] = names, add(entries)

    order = []
    for r, c in devices:
        arrivals = []
        for s in range(STEPS):
            when, key = 0, -1 - (r + s) % rows % groups_here
            for d, lane in enumerate(lanes):
                arrival = lane.arrival(r, c, (0, s))
                if arrival is not None:
                    t, returned = arrival
                    when, key = t, ((r + d) % 2, t)
                    if returned:
                        phase = 0 if any(to == number(r, c) for _, to in returns.get((0, t), [])) else 1
                        when, key = t + 0.7, ("back%d" % phase, t)
            arrivals.append((when, s, key))
        order.append(sorted(arrivals, key=lambda a: a[:2]))
    rank_at = add([[[a[1] for a in arrivals].index(s) for s in range(STEPS)] for arrivals in order])
    used, candidates, source_at = [], [], []
    for ranks in (range(STEPS - 1), range(STEPS - 1, STEPS)):
        keys = {arrivals[k][2] for arrivals in order for k in ranks}
        used.append(sorted((k for k in keys if isinstance(k, tuple)), key=lambda k: (k[1], str(k[0]))))
        places = [
            [arrivals[k][2] if isinstance(arrivals[k][2], int) else used[-1].index(arrivals[k][2]) for k in ranks]
            for arrivals in order
        ]
        candidates.append([sorted({max(p[i], -1) for p in places}) for i in range(len(ranks))])
        source_at.append(
            add([[n for p, k in zip(row, ranks) for n in (p, arrivals[k][1])] for row, arrivals in zip(places, order)])
        )
    table = np.concatenate(columns, axis=1)
    table = lax.dynamic_slice(jnp.asarray(table), (device, 0), (1, table.shape[1]))[0]

    def own_chunk(items, x=x):
        piece = lookup([None if i is None else i.piece for i in items], device)
        group = lookup([None if i is None else group_here(i) for i in items], device)
        return lax.dynamic_slice(x, (piece * piece_rows, group * group_size), (piece_rows, group_size))

    factor = weight / jnp.sqrt(2.0 * freq * (1.0 - freq))
    twice = 2.0 * freq
    male_scale = np.float32(np.sqrt(0.5))
    male_rows = jnp.where(sex_rows > 0, male_scale, np.float32(1.0))
    male_cols = jnp.where(sex_cols > 0, male_scale, np.float32(1.0))
    wide = lambda value: jnp.broadcast_to(value[:, None], (value.shape[0], LANES))

    def in_window(value):
        span = STEPS * group_size
        return lax.dynamic_slice(jnp.concatenate([value, value]), (row_place * group_size,), (span,))

    window_factor, window_twice = in_window(factor), in_window(twice)
    male_wide = wide(male_rows)

    def own_squares():
        here = lambda value: lax.dynamic_slice(value, (col_place * local_vars,), (local_vars,))[None, :]
        zx = ((x.astype(jnp.float32) - here(twice)) * here(factor) * male_rows[:, None]).astype(jnp.bfloat16)
        return jnp.sum(jnp.square(zx.astype(jnp.float32)), axis=1)

    back = [(i, (i - 1) % rows) for i in range(rows)]
    window = [y]
    while len(window) < STEPS:
        window.append(lax.ppermute(window[-1], "row", back))
    squares = own_squares()

    starts = {}
    if any(own_of[0, 1]):
        starts[0, 1] = own_chunk(own_of[0, 1])
    later_x = x
    for k, crossing in enumerate(crossings):
        later_x = lax.optimization_barrier(later_x)
        starts["cross", k] = own_chunk([crossing[rc][1] if rc in crossing else None for rc in devices], later_x)
    later_x, squares = lax.optimization_barrier((later_x, squares))
    if any(own_of[1, 1]):
        starts[1, 1] = own_chunk(own_of[1, 1], later_x)
    bits = [1 << k for k in range(cols.bit_length() - 1)] if cols & (cols - 1) == 0 else []
    if cols & (cols - 1):
        squares = lax.psum(squares, "col")

    def sum_beside(value, squares):
        if not bits:
            return value, squares
        bit = bits.pop(0)
        other = lax.ppermute(squares, "col", [(i, i ^ bit) for i in range(cols)])
        value, other = lax.optimization_barrier((value, other))
        return value, squares + other

    buffers, crossed = {}, {}

    def bring_back(key):
        if key in returns:
            phase, t = key
            buffers["back%d" % phase, t] = lax.ppermute(buffers[key], both, returns[key])

    for key in sends:
        phase, t = key
        if pairs_of[key]:
            if key in relays:
                names, at = relays[key]
                sources = [buffers[phase, t - DEPTH] if name == "forward" else crossed[name] for name in names]
                held = relay(at, table, x, sources)
            elif key in starts:
                held = starts[key]
            elif "forward" in kinds_of[key]:
                held = buffers[phase, t - DEPTH]
            elif "own" in kinds_of[key]:
                held = own_chunk(own_of[key])
            else:
                held = crossed[next(k for k in kinds_of[key] if k is not None)]
            name = "back%d" % phase, t - 2
            if name in buffers:
                held, buffers[name] = lax.optimization_barrier((held, buffers[name]))
            buffers[key] = lax.ppermute(held, both, pairs_of[key])
        if key == (0, 1):
            for k, crossing in enumerate(crossings):
                pairs = [(number(*rc), number(*to)) for rc, (to, _) in crossing.items()]
                crossed[k] = lax.ppermute(starts["cross", k], both, pairs)
        bring_back(key)
    zy = standardized_window(rank_at, table, window, wide(window_factor), wide(window_twice), male_cols[None, :])
    zy, squares = sum_beside(zy, squares)
    shared = window_factor[None, :], window_twice[None, :], male_wide, zy
    total = early_product(source_at[0], candidates[0], table, x, [buffers[k] for k in used[0]], *shared)
    total, squares = sum_beside(total, squares)
    relation = last_product(source_at[1], candidates[1][0], table, x, [buffers[k] for k in used[1]], *shared, total)
    for bit in bits:
        squares = squares + lax.ppermute(squares, "col", [(i, i ^ bit) for i in range(cols)])
    inbreeding = squares / jnp.float32(freq.shape[0]) - 1.0
    return relation, inbreeding


def solution(mesh):
    rows, cols = mesh.shape["row"], mesh.shape["col"]
    return jax.shard_map(
        functools.partial(local, rows, cols),
        mesh=mesh,
        in_specs=(P("row", "col"), P("row", "col"), P(), P(), P("row"), P("col")),
        out_specs=(P("row", "col"), P("row")),
        check_vma=False,
    )
```

```python
import functools
import itertools

import jax
import jax.numpy as jnp
import numpy as np
from jax import lax
from jax.experimental import pallas as pl
from jax.experimental.pallas import tpu as pltpu
from jax.sharding import PartitionSpec as P

STEPS = 4
PIECES = 1
DEPTH = 1
HOP = 1
COL_TILE = 512
ROW_BLOCK = 512
ROW_TILE = 32
LANES = 128
VMEM_LIMIT = 10 * 2**20
RELAY_LIMIT = 2 * 2**20


class Item:
    def __init__(self, row, piece, s, place, home=None):
        self.row, self.piece, self.s, self.place = row, piece, s, place
        self.home = home

    @property
    def owner(self):
        return self.row if self.home is None else self.home

    @property
    def key(self):
        return self.piece, self.s


def line_slots(items):
    slots = {}
    todo = sorted(items, key=lambda i: (i.home is None, i.piece, i.place, i.s))
    slot = 1
    while todo:
        for item in todo:
            first = 1 + DEPTH * (item.place - 1) + (HOP if item.home is not None else 0)
            if first <= slot:
                slots[slot] = item
                todo.remove(item)
                break
        slot += 1
    return slots


class Lane:
    def __init__(self, rows, cols, groups_here, towards_zero):
        self.rows, self.cols = rows, cols
        self.towards_zero = towards_zero
        self.short = groups_here > 1
        self.items = []
        for r in range(rows):
            mine = [
                Item(r, piece, s, self.place((r + s) % rows // groups_here))
                for piece in range(PIECES)
                for s in range(STEPS)
            ]
            self.items.append([i for i in mine if i.place > 0])
        self.away = []
        self.lines = [line_slots(items) for items in self.items]
        if rows % 4 == 0 and cols > 3:
            for r in range(rows // 2):
                other = r + rows // 2 if towards_zero else (r + rows // 2) ^ 1
                self.balance(r, other)
                self.balance(other, r)
        self.rounds = max([max(slots, default=0) for slots in self.lines])

    def place(self, c):
        return c if self.towards_zero else self.cols - 1 - c

    col = place

    def balance(self, r, other):
        if len(self.items[r]) < len(self.items[other]) or any(i.row == other for i in self.away):
            return
        crowded = self.short and r % 2 == 0 and min(len(self.items[r]), len(self.items[r ^ 1])) >= STEPS
        places = sorted({i.place for i in self.items[r]})
        best = None
        for counts in itertools.product(range(3), repeat=len(places)):
            gone = []
            for place, count in zip(places, counts):
                here = [i for i in self.items[r] if i.place == place]
                here.sort(key=lambda i: i.key, reverse=True)
                gone += here[:count]
            visitors = [Item(other, i.piece, i.s, i.place, home=r) for i in gone]
            mine = line_slots([i for i in self.items[r] if i not in gone])
            theirs = line_slots(self.items[other] + visitors)
            score = (
                max(max(mine, default=0), max(theirs, default=0), STEPS),
                max(len(mine), STEPS - 1) if crowded else 0,
                len(gone),
                max([slot for slot, i in theirs.items() if i.home is not None], default=0),
            )
            if best is None or score < best[0]:
                best = score, gone, mine, theirs
        _, gone, mine, theirs = best
        self.away += gone
        if gone:
            self.lines[r], self.lines[other] = mine, theirs

    def sent(self, r, c, t):
        p = self.place(c)
        item = self.lines[r].get(t + DEPTH * (p - 1)) if p > 0 else None
        return item if item is not None and item.place >= p else None

    def pairs(self, t):
        found = []
        for r in range(self.rows):
            for c in range(self.cols):
                if self.sent(r, c, t) is not None:
                    found.append((r * self.cols + c, r * self.cols + self.col(self.place(c) - 1)))
        return found

    def arrival(self, r, c, key):
        p = self.place(c)
        for i in self.items[r]:
            if i.key == key and i.place > p:
                for slots in self.lines:
                    for slot, v in slots.items():
                        if v is i or (v.home == r and v.key == key):
                            return slot - DEPTH * p, v is not i
        return None


def lookup(values, device):
    known = [v for v in values if v is not None]
    if len(set(known)) <= 1:
        return known[0] if known else 0
    values = [known[0] if v is None else v for v in values]
    result = jnp.uint32(0)
    place = (device % 32).astype(jnp.uint32)
    for bit in range(max(values).bit_length()):
        ones = [v >> bit & 1 for v in values]
        words = [sum(b << i for i, b in enumerate(ones[at : at + 32])) for at in range(0, len(ones), 32)]
        word = jnp.uint32(words[0])
        for i, other in enumerate(words[1:], 1):
            word = jnp.where(device // 32 == i, jnp.uint32(other), word)
        result = result | (((word >> place) & jnp.uint32(1)) << jnp.uint32(bit))
    return result.astype(jnp.int32)


def relay_kernel(at, table, x, *refs):
    *sources, out = refs
    rows, width = out.shape

    @pl.when(table[at] == 0)
    def _():
        row = pl.multiple_of(table[at + 1] * rows, rows)
        col = pl.multiple_of(table[at + 2] * width, width)
        out[...] = x[pl.ds(row, rows), pl.ds(col, width)]

    for i, source in enumerate(sources):

        @pl.when(table[at] == i + 1)
        def _(source=source):
            out[...] = source[...]


def relay(at, table, x, sources):
    return pl.pallas_call(
        functools.partial(relay_kernel, at),
        out_shape=pltpu.VMEM(sources[0].shape, sources[0].dtype),
        in_specs=[pl.BlockSpec(memory_space=pltpu.SMEM)] + [VMEM] * (1 + len(sources)),
        out_specs=VMEM,
        compiler_params=pltpu.CompilerParams(vmem_limit_bytes=RELAY_LIMIT),
        cost_estimate=pl.CostEstimate(flops=0, bytes_accessed=0, transcendentals=0),
        name="relay",
    )(table, *[in_vmem(v) for v in (x, *sources)])


def in_vmem(value):
    return pltpu.with_memory_space_constraint(value, pltpu.VMEM)


VMEM = pl.BlockSpec(memory_space=pltpu.VMEM)


def window_kernel(at, table, *refs):
    blocks = refs[:STEPS]
    factor, twice, male, out = refs[STEPS:]
    group_size, width = blocks[0].shape
    for s, block in enumerate(blocks):
        rank = table[at + s]

        @pl.loop(0, group_size // ROW_TILE)
        def _(i, s=s, block=block, rank=rank):
            here = pl.ds(pl.multiple_of(i * ROW_TILE, ROW_TILE), ROW_TILE)
            rows = pl.ds(pl.multiple_of(s * group_size + i * ROW_TILE, ROW_TILE), ROW_TILE)
            to = pl.ds(pl.multiple_of(rank * group_size + i * ROW_TILE, ROW_TILE), ROW_TILE)
            for k in range(0, width, LANES):
                value = block[here, k : k + LANES].astype(jnp.float32) - twice[rows, :]
                out[to, k : k + LANES] = (value * factor[rows, :] * male[:, k : k + LANES]).astype(out.dtype)


def standardized_window(at, table, blocks, factor, twice, male):
    group_size, n = blocks[0].shape
    depth = STEPS * group_size
    return pl.pallas_call(
        functools.partial(window_kernel, at),
        out_shape=pltpu.VMEM((depth, n), jnp.bfloat16),
        in_specs=[pl.BlockSpec(memory_space=pltpu.SMEM)] + [VMEM] * (STEPS + 3),
        out_specs=VMEM,
        compiler_params=pltpu.CompilerParams(vmem_limit_bytes=VMEM_LIMIT),
        cost_estimate=pl.CostEstimate(flops=4 * depth * n, bytes_accessed=4 * depth * n, transcendentals=0),
        name="window",
    )(table, *[in_vmem(v) for v in (*blocks, factor, twice, male)])


def standardize(table, at, candidates, x, buffers, factor, twice, male, zx, columns, first, count):
    width = columns.stop - columns.start
    place, step = table[at], table[at + 1]

    def from_source(source, col):
        @pl.loop(0, count // ROW_TILE)
        def _(i):
            here = pl.ds(pl.multiple_of(first + i * ROW_TILE, ROW_TILE), ROW_TILE)
            to = pl.ds(pl.multiple_of(i * ROW_TILE, ROW_TILE), ROW_TILE)
            for k in range(0, width, LANES):
                lanes = pl.ds(pl.multiple_of(step * width + k, LANES), LANES)
                value = source[here, pl.ds(pl.multiple_of(col + k, LANES), LANES)].astype(jnp.float32)
                value = (value - twice[:, lanes]) * factor[:, lanes] * male[here, :]
                zx[to, columns.start + k : columns.start + k + LANES] = value.astype(zx.dtype)

    for number in candidates:
        if number >= 0:

            @pl.when(place == number)
            def _(number=number):
                from_source(buffers[number], 0)

        else:

            @pl.when(place < 0)
            def _():
                from_source(x, (-1 - place) * width)


def early_kernel(at, candidates, n_buffers, table, x, *refs):
    buffers = refs[:n_buffers]
    factor, twice, male, zy, total, zx = refs[n_buffers:]
    rows, depth = zx.shape
    width = depth // (STEPS - 1)
    for rank in range(STEPS - 1):
        columns = slice(rank * width, (rank + 1) * width)
        standardize(table, at + 2 * rank, candidates[rank], x, buffers, factor, twice, male, zx, columns, 0, rows)

    @pl.loop(0, rows // ROW_BLOCK)
    def _(i):
        block = pl.ds(pl.multiple_of(i * ROW_BLOCK, ROW_BLOCK), ROW_BLOCK)
        for j in range(0, total.shape[1], COL_TILE):
            right = zy[:depth, j : j + COL_TILE]
            total[block, j : j + COL_TILE] = jnp.dot(zx[block, :], right, preferred_element_type=jnp.float32)


def early_product(at, candidates, table, x, buffers, factor, twice, male, zy):
    rows, (depth, n) = x.shape[0], zy.shape
    depth = depth // STEPS * (STEPS - 1)
    args = [in_vmem(v) for v in (x, *buffers, factor, twice, male, zy)]
    return pl.pallas_call(
        functools.partial(early_kernel, at, candidates, len(buffers)),
        out_shape=pltpu.VMEM((rows, n), jnp.float32),
        in_specs=[pl.BlockSpec(memory_space=pltpu.SMEM)] + [VMEM] * len(args),
        out_specs=VMEM,
        scratch_shapes=[pltpu.VMEM((rows, depth), jnp.bfloat16)],
        compiler_params=pltpu.CompilerParams(vmem_limit_bytes=VMEM_LIMIT),
        cost_estimate=pl.CostEstimate(flops=2 * rows * depth * n, bytes_accessed=0, transcendentals=0),
        name="early",
    )(table, *args)


def last_kernel(at, candidates, scale, n_buffers, table, x, *refs):
    buffers = refs[:n_buffers]
    factor, twice, male, zy, total, out, zx, blocks, sems = refs[n_buffers:]
    rows, n = total.shape
    width = zx.shape[1]

    def copy(i):
        return pltpu.make_async_copy(blocks.at[i % 2], out.at[pl.ds(i * ROW_BLOCK, ROW_BLOCK), :], sems.at[i % 2])

    count = rows // ROW_BLOCK
    for i in range(count):
        first = i * ROW_BLOCK
        standardize(
            table, at, candidates, x, buffers, factor, twice, male, zx, slice(0, width), first, ROW_BLOCK
        )
        if i >= 2:
            copy(i - 2).wait()
        for j in range(0, n, COL_TILE):
            right = zy[zy.shape[0] - width :, j : j + COL_TILE]
            product = jnp.dot(zx[...], right, preferred_element_type=jnp.float32)
            product = product + total[first : first + ROW_BLOCK, j : j + COL_TILE]
            blocks[i % 2, :, j : j + COL_TILE] = (product * scale).astype(blocks.dtype)
        copy(i).start()
    for i in range(max(count - 2, 0), count):
        copy(i).wait()


def last_product(at, candidates, table, x, buffers, factor, twice, male, zy, total):
    rows, (depth, n) = x.shape[0], zy.shape
    width = depth // STEPS
    scale = float(1.0 / np.sqrt(np.float32(depth)))
    args = [in_vmem(v) for v in (x, *buffers, factor, twice, male, zy, total)]
    return pl.pallas_call(
        functools.partial(last_kernel, at, candidates, scale, len(buffers)),
        out_shape=jax.ShapeDtypeStruct((rows, n), jnp.bfloat16),
        in_specs=[pl.BlockSpec(memory_space=pltpu.SMEM)] + [VMEM] * len(args),
        out_specs=pl.BlockSpec(memory_space=pl.ANY),
        scratch_shapes=[
            pltpu.VMEM((ROW_BLOCK, width), jnp.bfloat16),
            pltpu.VMEM((2, ROW_BLOCK, n), jnp.bfloat16),
            pltpu.SemaphoreType.DMA((2,)),
        ],
        compiler_params=pltpu.CompilerParams(vmem_limit_bytes=VMEM_LIMIT),
        cost_estimate=pl.CostEstimate(flops=2 * rows * width * n, bytes_accessed=2 * rows * n, transcendentals=0),
        name="last",
    )(table, *args)


def local(rows, cols, x, y, freq, weight, sex_rows, sex_cols):
    group_size = y.shape[0]
    local_vars = x.shape[1]
    groups_here = local_vars // group_size
    piece_rows = x.shape[0] // PIECES
    lanes = [Lane(rows, cols, groups_here, towards) for towards in (True, False)]
    rounds = max(lane.rounds for lane in lanes)
    devices = [(r, c) for r in range(rows) for c in range(cols)]
    both = ("row", "col")

    row_place = lax.axis_index("row")
    col_place = lax.axis_index("col")
    device = row_place * cols + col_place

    def number(r, c):
        return r * cols + c

    def group_here(item):
        return (item.owner + item.s) % rows % groups_here

    crossings = []
    crossing_of = {}
    for d, lane in enumerate(lanes):
        for r in range(rows):
            for slot, item in sorted(lane.lines[r].items()):
                if item.home is None:
                    continue
                source, target = (item.home, lane.col(item.place)), (r, lane.col(item.place))
                for k, crossing in enumerate(crossings):
                    if source not in crossing and target not in [to for to, _ in crossing.values()]:
                        break
                else:
                    k = len(crossings)
                    crossings.append({})
                crossings[k][source] = (target, item)
                crossing_of[d, r, item.key] = k

    def lane_of(phase, r):
        return (r + phase) % 2

    sends = [(phase, t) for t in range(1, rounds + 1) for phase in range(2)]
    pairs_of, kinds_of, own_of = {}, {}, {}
    for phase, t in sends:
        pairs, kinds, own = [], [], []
        for r, c in devices:
            lane = lanes[lane_of(phase, r)]
            item = lane.sent(r, c, t)
            if item is not None:
                pairs.append((number(r, c), number(r, lane.col(lane.place(c) - 1))))
            if item is None:
                kinds.append(None)
            elif item.place != lane.place(c):
                kinds.append("forward")
            elif item.home is not None:
                kinds.append(crossing_of[lane_of(phase, r), r, item.key])
            else:
                kinds.append("own")
            own.append(item if kinds[-1] == "own" else None)
        pairs_of[phase, t], kinds_of[phase, t], own_of[phase, t] = pairs, kinds, own

    returns = {}
    for d, lane in enumerate(lanes):
        for r in range(rows):
            for slot, item in lane.lines[r].items():
                if item.home is not None:
                    for p in range(item.place):
                        pair = number(r, lane.col(p)), number(item.home, lane.col(p))
                        returns.setdefault(((r + d) % 2, slot - DEPTH * p), []).append(pair)

    columns = []

    def add(entries):
        columns.append(np.asarray(entries, np.int32))
        return sum(c.shape[1] for c in columns[:-1])

    relays = {}
    for key in sends:
        kinds = kinds_of[key]
        names = sorted(set(kinds) - {None, "own"}, key=str)
        if names and (len(names) > 1 or "own" in kinds):
            entries = []
            for kind, item in zip(kinds, own_of[key]):
                if kind == "own":
                    entries.append((0, item.piece, group_here(item)))
                else:
                    entries.append((1 + names.index(kind) if kind is not None else 1, 0, 0))
            relays[key] = names, add(entries)

    order = []
    for r, c in devices:
        arrivals = []
        for s in range(STEPS):
            when, key = 0, -1 - (r + s) % rows % groups_here
            for d, lane in enumerate(lanes):
                arrival = lane.arrival(r, c, (0, s))
                if arrival is not None:
                    t, returned = arrival
                    when, key = t, ((r + d) % 2, t)
                    if returned:
                        phase = 0 if any(to == number(r, c) for _, to in returns.get((0, t), [])) else 1
                        when, key = t + 0.7, ("back%d" % phase, t)
            arrivals.append((when, s, key))
        order.append(sorted(arrivals, key=lambda a: a[:2]))
    rank_at = add([[[a[1] for a in arrivals].index(s) for s in range(STEPS)] for arrivals in order])
    used, candidates, source_at = [], [], []
    for ranks in (range(STEPS - 1), range(STEPS - 1, STEPS)):
        keys = {arrivals[k][2] for arrivals in order for k in ranks}
        used.append(sorted((k for k in keys if isinstance(k, tuple)), key=lambda k: (k[1], str(k[0]))))
        places = [
            [arrivals[k][2] if isinstance(arrivals[k][2], int) else used[-1].index(arrivals[k][2]) for k in ranks]
            for arrivals in order
        ]
        candidates.append([sorted({max(p[i], -1) for p in places}) for i in range(len(ranks))])
        source_at.append(
            add([[n for p, k in zip(row, ranks) for n in (p, arrivals[k][1])] for row, arrivals in zip(places, order)])
        )
    table = np.concatenate(columns, axis=1)
    table = lax.dynamic_slice(jnp.asarray(table), (device, 0), (1, table.shape[1]))[0]

    def own_chunk(items, x=x):
        piece = lookup([None if i is None else i.piece for i in items], device)
        group = lookup([None if i is None else group_here(i) for i in items], device)
        return lax.dynamic_slice(x, (piece * piece_rows, group * group_size), (piece_rows, group_size))

    factor = weight / jnp.sqrt(2.0 * freq * (1.0 - freq))
    twice = 2.0 * freq
    male_scale = np.float32(np.sqrt(0.5))
    male_rows = jnp.where(sex_rows > 0, male_scale, np.float32(1.0))
    male_cols = jnp.where(sex_cols > 0, male_scale, np.float32(1.0))
    wide = lambda value: jnp.broadcast_to(value[:, None], (value.shape[0], LANES))

    def in_window(value):
        span = STEPS * group_size
        return lax.dynamic_slice(jnp.concatenate([value, value]), (row_place * group_size,), (span,))

    window_factor, window_twice = in_window(factor), in_window(twice)
    male_wide = wide(male_rows)

    def own_squares():
        here = lambda value: lax.dynamic_slice(value, (col_place * local_vars,), (local_vars,))[None, :]
        zx = ((x.astype(jnp.float32) - here(twice)) * here(factor) * male_rows[:, None]).astype(jnp.bfloat16)
        return jnp.sum(jnp.square(zx.astype(jnp.float32)), axis=1)

    back = [(i, (i - 1) % rows) for i in range(rows)]
    window = [y]
    while len(window) < STEPS:
        window.append(lax.ppermute(window[-1], "row", back))
    squares = own_squares()

    starts = {}
    if any(own_of[0, 1]):
        starts[0, 1] = own_chunk(own_of[0, 1])
    later_x = x
    for k, crossing in enumerate(crossings):
        later_x = lax.optimization_barrier(later_x)
        starts["cross", k] = own_chunk([crossing[rc][1] if rc in crossing else None for rc in devices], later_x)
    later_x, squares = lax.optimization_barrier((later_x, squares))
    if any(own_of[1, 1]):
        starts[1, 1] = own_chunk(own_of[1, 1], later_x)
    bits = [1 << k for k in range(cols.bit_length() - 1)] if cols & (cols - 1) == 0 else []
    if cols & (cols - 1):
        squares = lax.psum(squares, "col")

    def sum_beside(value, squares):
        if not bits:
            return value, squares
        bit = bits.pop(0)
        other = lax.ppermute(squares, "col", [(i, i ^ bit) for i in range(cols)])
        value, other = lax.optimization_barrier((value, other))
        return value, squares + other

    buffers, crossed = {}, {}

    def bring_back(key):
        if key in returns:
            phase, t = key
            buffers["back%d" % phase, t] = lax.ppermute(buffers[key], both, returns[key])

    for key in sends:
        phase, t = key
        if pairs_of[key]:
            if key in relays:
                names, at = relays[key]
                sources = [buffers[phase, t - DEPTH] if name == "forward" else crossed[name] for name in names]
                held = relay(at, table, x, sources)
            elif key in starts:
                held = starts[key]
            elif "forward" in kinds_of[key]:
                held = buffers[phase, t - DEPTH]
            elif "own" in kinds_of[key]:
                held = own_chunk(own_of[key])
            else:
                held = crossed[next(k for k in kinds_of[key] if k is not None)]
            name = "back%d" % phase, t - 2
            if name in buffers:
                held, buffers[name] = lax.optimization_barrier((held, buffers[name]))
            buffers[key] = lax.ppermute(held, both, pairs_of[key])
        if key == (0, 1):
            for k, crossing in enumerate(crossings):
                pairs = [(number(*rc), number(*to)) for rc, (to, _) in crossing.items()]
                crossed[k] = lax.ppermute(starts["cross", k], both, pairs)
        bring_back(key)
    zy = standardized_window(rank_at, table, window, wide(window_factor), wide(window_twice), male_cols[None, :])
    zy, squares = sum_beside(zy, squares)
    shared = window_factor[None, :], window_twice[None, :], male_wide, zy
    total = early_product(source_at[0], candidates[0], table, x, [buffers[k] for k in used[0]], *shared)
    total, squares = sum_beside(total, squares)
    relation = last_product(source_at[1], candidates[1][0], table, x, [buffers[k] for k in used[1]], *shared, total)
    for bit in bits:
        squares = squares + lax.ppermute(squares, "col", [(i, i ^ bit) for i in range(cols)])
    inbreeding = squares / jnp.float32(freq.shape[0]) - 1.0
    return relation, inbreeding


def solution(mesh):
    rows, cols = mesh.shape["row"], mesh.shape["col"]
    return jax.shard_map(
        functools.partial(local, rows, cols),
        mesh=mesh,
        in_specs=(P("row", "col"), P("row", "col"), P(), P(), P("row"), P("col")),
        out_specs=(P("row", "col"), P("row")),
        check_vma=False,
    )
```

```python
import functools
import itertools

import jax
import jax.numpy as jnp
import numpy as np
from jax import lax
from jax.experimental import pallas as pl
from jax.experimental.pallas import tpu as pltpu
from jax.sharding import PartitionSpec as P

STEPS = 4
PIECES = 1
DEPTH = 1
HOP = 1
COL_TILE = 512
ROW_BLOCK = 512
ROW_TILE = 32
LANES = 128
VMEM_LIMIT = 10 * 2**20
RELAY_LIMIT = 2 * 2**20


class Item:
    def __init__(self, row, piece, s, place, home=None):
        self.row, self.piece, self.s, self.place = row, piece, s, place
        self.home = home

    @property
    def owner(self):
        return self.row if self.home is None else self.home

    @property
    def key(self):
        return self.piece, self.s


def line_slots(items):
    slots = {}
    todo = sorted(items, key=lambda i: (i.home is None, i.piece, i.place, i.s))
    slot = 1
    while todo:
        for item in todo:
            first = 1 + DEPTH * (item.place - 1) + (HOP if item.home is not None else 0)
            if first <= slot:
                slots[slot] = item
                todo.remove(item)
                break
        slot += 1
    return slots


class Lane:
    def __init__(self, rows, cols, groups_here, towards_zero):
        self.rows, self.cols = rows, cols
        self.towards_zero = towards_zero
        self.short = groups_here > 1
        self.items = []
        for r in range(rows):
            mine = [
                Item(r, piece, s, self.place((r + s) % rows // groups_here))
                for piece in range(PIECES)
                for s in range(STEPS)
            ]
            self.items.append([i for i in mine if i.place > 0])
        self.away = []
        self.lines = [line_slots(items) for items in self.items]
        if rows % 4 == 0 and cols > 3:
            for r in range(rows // 2):
                other = r + rows // 2 if towards_zero else (r + rows // 2) ^ 1
                self.balance(r, other)
                self.balance(other, r)
        self.rounds = max([max(slots, default=0) for slots in self.lines])

    def place(self, c):
        return c if self.towards_zero else self.cols - 1 - c

    col = place

    def balance(self, r, other):
        if len(self.items[r]) < len(self.items[other]) or any(i.row == other for i in self.away):
            return
        crowded = self.short and r % 2 == 0 and min(len(self.items[r]), len(self.items[r ^ 1])) >= STEPS
        places = sorted({i.place for i in self.items[r]})
        best = None
        for counts in itertools.product(range(3), repeat=len(places)):
            gone = []
            for place, count in zip(places, counts):
                here = [i for i in self.items[r] if i.place == place]
                here.sort(key=lambda i: i.key, reverse=True)
                gone += here[:count]
            visitors = [Item(other, i.piece, i.s, i.place, home=r) for i in gone]
            mine = line_slots([i for i in self.items[r] if i not in gone])
            theirs = line_slots(self.items[other] + visitors)
            score = (
                max(max(mine, default=0), max(theirs, default=0), STEPS),
                max(len(mine), STEPS - 1) if crowded else 0,
                len(gone),
                max([slot for slot, i in theirs.items() if i.home is not None], default=0),
            )
            if best is None or score < best[0]:
                best = score, gone, mine, theirs
        _, gone, mine, theirs = best
        self.away += gone
        if gone:
            self.lines[r], self.lines[other] = mine, theirs

    def sent(self, r, c, t):
        p = self.place(c)
        item = self.lines[r].get(t + DEPTH * (p - 1)) if p > 0 else None
        return item if item is not None and item.place >= p else None

    def pairs(self, t):
        found = []
        for r in range(self.rows):
            for c in range(self.cols):
                if self.sent(r, c, t) is not None:
                    found.append((r * self.cols + c, r * self.cols + self.col(self.place(c) - 1)))
        return found

    def arrival(self, r, c, key):
        p = self.place(c)
        for i in self.items[r]:
            if i.key == key and i.place > p:
                for slots in self.lines:
                    for slot, v in slots.items():
                        if v is i or (v.home == r and v.key == key):
                            return slot - DEPTH * p, v is not i
        return None


def lookup(values, device):
    known = [v for v in values if v is not None]
    if len(set(known)) <= 1:
        return known[0] if known else 0
    values = [known[0] if v is None else v for v in values]
    result = jnp.uint32(0)
    place = (device % 32).astype(jnp.uint32)
    for bit in range(max(values).bit_length()):
        ones = [v >> bit & 1 for v in values]
        words = [sum(b << i for i, b in enumerate(ones[at : at + 32])) for at in range(0, len(ones), 32)]
        word = jnp.uint32(words[0])
        for i, other in enumerate(words[1:], 1):
            word = jnp.where(device // 32 == i, jnp.uint32(other), word)
        result = result | (((word >> place) & jnp.uint32(1)) << jnp.uint32(bit))
    return result.astype(jnp.int32)


def relay_kernel(at, table, x, *refs):
    *sources, out = refs
    rows, width = out.shape

    @pl.when(table[at] == 0)
    def _():
        row = pl.multiple_of(table[at + 1] * rows, rows)
        col = pl.multiple_of(table[at + 2] * width, width)
        out[...] = x[pl.ds(row, rows), pl.ds(col, width)]

    for i, source in enumerate(sources):

        @pl.when(table[at] == i + 1)
        def _(source=source):
            out[...] = source[...]


def relay(at, table, x, sources):
    return pl.pallas_call(
        functools.partial(relay_kernel, at),
        out_shape=pltpu.VMEM(sources[0].shape, sources[0].dtype),
        in_specs=[pl.BlockSpec(memory_space=pltpu.SMEM)] + [VMEM] * (1 + len(sources)),
        out_specs=VMEM,
        compiler_params=pltpu.CompilerParams(vmem_limit_bytes=RELAY_LIMIT),
        cost_estimate=pl.CostEstimate(flops=0, bytes_accessed=0, transcendentals=0),
        name="relay",
    )(table, *[in_vmem(v) for v in (x, *sources)])


def in_vmem(value):
    return pltpu.with_memory_space_constraint(value, pltpu.VMEM)


VMEM = pl.BlockSpec(memory_space=pltpu.VMEM)


def window_kernel(at, table, *refs):
    blocks = refs[:STEPS]
    factor, twice, male, out = refs[STEPS:]
    group_size, width = blocks[0].shape
    for s, block in enumerate(blocks):
        rank = table[at + s]

        @pl.loop(0, group_size // ROW_TILE)
        def _(i, s=s, block=block, rank=rank):
            here = pl.ds(pl.multiple_of(i * ROW_TILE, ROW_TILE), ROW_TILE)
            rows = pl.ds(pl.multiple_of(s * group_size + i * ROW_TILE, ROW_TILE), ROW_TILE)
            to = pl.ds(pl.multiple_of(rank * group_size + i * ROW_TILE, ROW_TILE), ROW_TILE)
            for k in range(0, width, LANES):
                value = block[here, k : k + LANES].astype(jnp.float32) - twice[rows, :]
                out[to, k : k + LANES] = (value * factor[rows, :] * male[:, k : k + LANES]).astype(out.dtype)


def standardized_window(at, table, blocks, factor, twice, male):
    group_size, n = blocks[0].shape
    depth = STEPS * group_size
    return pl.pallas_call(
        functools.partial(window_kernel, at),
        out_shape=pltpu.VMEM((depth, n), jnp.bfloat16),
        in_specs=[pl.BlockSpec(memory_space=pltpu.SMEM)] + [VMEM] * (STEPS + 3),
        out_specs=VMEM,
        compiler_params=pltpu.CompilerParams(vmem_limit_bytes=VMEM_LIMIT),
        cost_estimate=pl.CostEstimate(flops=4 * depth * n, bytes_accessed=4 * depth * n, transcendentals=0),
        name="window",
    )(table, *[in_vmem(v) for v in (*blocks, factor, twice, male)])


def standardize(table, at, candidates, x, buffers, factor, twice, male, zx, columns, first, count):
    width = columns.stop - columns.start
    place, step = table[at], table[at + 1]

    def from_source(source, col):
        @pl.loop(0, count // ROW_TILE)
        def _(i):
            here = pl.ds(pl.multiple_of(first + i * ROW_TILE, ROW_TILE), ROW_TILE)
            to = pl.ds(pl.multiple_of(i * ROW_TILE, ROW_TILE), ROW_TILE)
            for k in range(0, width, LANES):
                lanes = pl.ds(pl.multiple_of(step * width + k, LANES), LANES)
                value = source[here, pl.ds(pl.multiple_of(col + k, LANES), LANES)].astype(jnp.float32)
                value = (value - twice[:, lanes]) * factor[:, lanes] * male[here, :]
                zx[to, columns.start + k : columns.start + k + LANES] = value.astype(zx.dtype)

    for number in candidates:
        if number >= 0:

            @pl.when(place == number)
            def _(number=number):
                from_source(buffers[number], 0)

        else:

            @pl.when(place < 0)
            def _():
                from_source(x, (-1 - place) * width)


def early_kernel(at, candidates, n_buffers, table, x, *refs):
    buffers = refs[:n_buffers]
    factor, twice, male, zy, total, zx = refs[n_buffers:]
    rows, depth = zx.shape
    width = depth // (STEPS - 1)
    for rank in range(STEPS - 1):
        columns = slice(rank * width, (rank + 1) * width)
        standardize(table, at + 2 * rank, candidates[rank], x, buffers, factor, twice, male, zx, columns, 0, rows)

    @pl.loop(0, rows // ROW_BLOCK)
    def _(i):
        block = pl.ds(pl.multiple_of(i * ROW_BLOCK, ROW_BLOCK), ROW_BLOCK)
        for j in range(0, total.shape[1], COL_TILE):
            right = zy[:depth, j : j + COL_TILE]
            total[block, j : j + COL_TILE] = jnp.dot(zx[block, :], right, preferred_element_type=jnp.float32)


def early_product(at, candidates, table, x, buffers, factor, twice, male, zy):
    rows, (depth, n) = x.shape[0], zy.shape
    depth = depth // STEPS * (STEPS - 1)
    args = [in_vmem(v) for v in (x, *buffers, factor, twice, male, zy)]
    return pl.pallas_call(
        functools.partial(early_kernel, at, candidates, len(buffers)),
        out_shape=pltpu.VMEM((rows, n), jnp.float32),
        in_specs=[pl.BlockSpec(memory_space=pltpu.SMEM)] + [VMEM] * len(args),
        out_specs=VMEM,
        scratch_shapes=[pltpu.VMEM((rows, depth), jnp.bfloat16)],
        compiler_params=pltpu.CompilerParams(vmem_limit_bytes=VMEM_LIMIT),
        cost_estimate=pl.CostEstimate(flops=2 * rows * depth * n, bytes_accessed=0, transcendentals=0),
        name="early",
    )(table, *args)


def last_kernel(at, candidates, scale, n_buffers, table, x, *refs):
    buffers = refs[:n_buffers]
    factor, twice, male, zy, total, out, zx, blocks, sems = refs[n_buffers:]
    rows, n = total.shape
    width = zx.shape[1]

    def copy(i):
        return pltpu.make_async_copy(blocks.at[i % 2], out.at[pl.ds(i * ROW_BLOCK, ROW_BLOCK), :], sems.at[i % 2])

    count = rows // ROW_BLOCK
    for i in range(count):
        first = i * ROW_BLOCK
        standardize(
            table, at, candidates, x, buffers, factor, twice, male, zx, slice(0, width), first, ROW_BLOCK
        )
        if i >= 2:
            copy(i - 2).wait()
        for j in range(0, n, COL_TILE):
            right = zy[zy.shape[0] - width :, j : j + COL_TILE]
            product = jnp.dot(zx[...], right, preferred_element_type=jnp.float32)
            product = product + total[first : first + ROW_BLOCK, j : j + COL_TILE]
            blocks[i % 2, :, j : j + COL_TILE] = (product * scale).astype(blocks.dtype)
        copy(i).start()
    for i in range(max(count - 2, 0), count):
        copy(i).wait()


def last_product(at, candidates, table, x, buffers, factor, twice, male, zy, total):
    rows, (depth, n) = x.shape[0], zy.shape
    width = depth // STEPS
    scale = float(1.0 / np.sqrt(np.float32(depth)))
    args = [in_vmem(v) for v in (x, *buffers, factor, twice, male, zy, total)]
    return pl.pallas_call(
        functools.partial(last_kernel, at, candidates, scale, len(buffers)),
        out_shape=jax.ShapeDtypeStruct((rows, n), jnp.bfloat16),
        in_specs=[pl.BlockSpec(memory_space=pltpu.SMEM)] + [VMEM] * len(args),
        out_specs=pl.BlockSpec(memory_space=pl.ANY),
        scratch_shapes=[
            pltpu.VMEM((ROW_BLOCK, width), jnp.bfloat16),
            pltpu.VMEM((2, ROW_BLOCK, n), jnp.bfloat16),
            pltpu.SemaphoreType.DMA((2,)),
        ],
        compiler_params=pltpu.CompilerParams(vmem_limit_bytes=VMEM_LIMIT),
        cost_estimate=pl.CostEstimate(flops=2 * rows * width * n, bytes_accessed=2 * rows * n, transcendentals=0),
        name="last",
    )(table, *args)


def local(rows, cols, x, y, freq, weight, sex_rows, sex_cols):
    group_size = y.shape[0]
    local_vars = x.shape[1]
    groups_here = local_vars // group_size
    piece_rows = x.shape[0] // PIECES
    lanes = [Lane(rows, cols, groups_here, towards) for towards in (True, False)]
    rounds = max(lane.rounds for lane in lanes)
    devices = [(r, c) for r in range(rows) for c in range(cols)]
    both = ("row", "col")

    row_place = lax.axis_index("row")
    col_place = lax.axis_index("col")
    device = row_place * cols + col_place

    def number(r, c):
        return r * cols + c

    def group_here(item):
        return (item.owner + item.s) % rows % groups_here

    crossings = []
    crossing_of = {}
    for d, lane in enumerate(lanes):
        for r in range(rows):
            for slot, item in sorted(lane.lines[r].items()):
                if item.home is None:
                    continue
                source, target = (item.home, lane.col(item.place)), (r, lane.col(item.place))
                for k, crossing in enumerate(crossings):
                    if source not in crossing and target not in [to for to, _ in crossing.values()]:
                        break
                else:
                    k = len(crossings)
                    crossings.append({})
                crossings[k][source] = (target, item)
                crossing_of[d, r, item.key] = k

    def lane_of(phase, r):
        return (r + phase) % 2

    sends = [(phase, t) for t in range(1, rounds + 1) for phase in range(2)]
    pairs_of, kinds_of, own_of = {}, {}, {}
    for phase, t in sends:
        pairs, kinds, own = [], [], []
        for r, c in devices:
            lane = lanes[lane_of(phase, r)]
            item = lane.sent(r, c, t)
            if item is not None:
                pairs.append((number(r, c), number(r, lane.col(lane.place(c) - 1))))
            if item is None:
                kinds.append(None)
            elif item.place != lane.place(c):
                kinds.append("forward")
            elif item.home is not None:
                kinds.append(crossing_of[lane_of(phase, r), r, item.key])
            else:
                kinds.append("own")
            own.append(item if kinds[-1] == "own" else None)
        pairs_of[phase, t], kinds_of[phase, t], own_of[phase, t] = pairs, kinds, own

    returns = {}
    for d, lane in enumerate(lanes):
        for r in range(rows):
            for slot, item in lane.lines[r].items():
                if item.home is not None:
                    for p in range(item.place):
                        pair = number(r, lane.col(p)), number(item.home, lane.col(p))
                        returns.setdefault(((r + d) % 2, slot - DEPTH * p), []).append(pair)

    columns = []

    def add(entries):
        columns.append(np.asarray(entries, np.int32))
        return sum(c.shape[1] for c in columns[:-1])

    relays = {}
    for key in sends:
        kinds = kinds_of[key]
        names = sorted(set(kinds) - {None, "own"}, key=str)
        if names and (len(names) > 1 or "own" in kinds):
            entries = []
            for kind, item in zip(kinds, own_of[key]):
                if kind == "own":
                    entries.append((0, item.piece, group_here(item)))
                else:
                    entries.append((1 + names.index(kind) if kind is not None else 1, 0, 0))
            relays[key] = names, add(entries)

    order = []
    for r, c in devices:
        arrivals = []
        for s in range(STEPS):
            when, key = 0, -1 - (r + s) % rows % groups_here
            for d, lane in enumerate(lanes):
                arrival = lane.arrival(r, c, (0, s))
                if arrival is not None:
                    t, returned = arrival
                    when, key = t, ((r + d) % 2, t)
                    if returned:
                        phase = 0 if any(to == number(r, c) for _, to in returns.get((0, t), [])) else 1
                        when, key = t + 0.7, ("back%d" % phase, t)
            arrivals.append((when, s, key))
        order.append(sorted(arrivals, key=lambda a: a[:2]))
    rank_at = add([[[a[1] for a in arrivals].index(s) for s in range(STEPS)] for arrivals in order])
    used, candidates, source_at = [], [], []
    for ranks in (range(STEPS - 1), range(STEPS - 1, STEPS)):
        keys = {arrivals[k][2] for arrivals in order for k in ranks}
        used.append(sorted((k for k in keys if isinstance(k, tuple)), key=lambda k: (k[1], str(k[0]))))
        places = [
            [arrivals[k][2] if isinstance(arrivals[k][2], int) else used[-1].index(arrivals[k][2]) for k in ranks]
            for arrivals in order
        ]
        candidates.append([sorted({max(p[i], -1) for p in places}) for i in range(len(ranks))])
        source_at.append(
            add([[n for p, k in zip(row, ranks) for n in (p, arrivals[k][1])] for row, arrivals in zip(places, order)])
        )
    table = np.concatenate(columns, axis=1)
    table = lax.dynamic_slice(jnp.asarray(table), (device, 0), (1, table.shape[1]))[0]

    def own_chunk(items, x=x):
        piece = lookup([None if i is None else i.piece for i in items], device)
        group = lookup([None if i is None else group_here(i) for i in items], device)
        return lax.dynamic_slice(x, (piece * piece_rows, group * group_size), (piece_rows, group_size))

    factor = weight / jnp.sqrt(2.0 * freq * (1.0 - freq))
    twice = 2.0 * freq
    male_scale = np.float32(np.sqrt(0.5))
    male_rows = jnp.where(sex_rows > 0, male_scale, np.float32(1.0))
    male_cols = jnp.where(sex_cols > 0, male_scale, np.float32(1.0))
    wide = lambda value: jnp.broadcast_to(value[:, None], (value.shape[0], LANES))

    def in_window(value):
        span = STEPS * group_size
        return lax.dynamic_slice(jnp.concatenate([value, value]), (row_place * group_size,), (span,))

    window_factor, window_twice = in_window(factor), in_window(twice)
    male_wide = wide(male_rows)

    def own_squares():
        here = lambda value: lax.dynamic_slice(value, (col_place * local_vars,), (local_vars,))[None, :]
        zx = ((x.astype(jnp.float32) - here(twice)) * here(factor) * male_rows[:, None]).astype(jnp.bfloat16)
        return jnp.sum(jnp.square(zx.astype(jnp.float32)), axis=1)

    back = [(i, (i - 1) % rows) for i in range(rows)]
    squares = own_squares()

    starts = {}
    if any(own_of[0, 1]):
        starts[0, 1] = own_chunk(own_of[0, 1])
    later_x = x
    for k, crossing in enumerate(crossings):
        later_x = lax.optimization_barrier(later_x)
        starts["cross", k] = own_chunk([crossing[rc][1] if rc in crossing else None for rc in devices], later_x)
    later_x, squares = lax.optimization_barrier((later_x, squares))
    if any(own_of[1, 1]):
        starts[1, 1] = own_chunk(own_of[1, 1], later_x)
    bits = [1 << k for k in range(cols.bit_length() - 1)] if cols & (cols - 1) == 0 else []
    if cols & (cols - 1):
        squares = lax.psum(squares, "col")

    def sum_beside(value, squares):
        if not bits:
            return value, squares
        bit = bits.pop(0)
        other = lax.ppermute(squares, "col", [(i, i ^ bit) for i in range(cols)])
        value, other = lax.optimization_barrier((value, other))
        return value, squares + other

    crossed = {}
    for k, crossing in enumerate(crossings):
        pairs = [(number(*rc), number(*to)) for rc, (to, _) in crossing.items()]
        crossed[k] = lax.ppermute(starts["cross", k], both, pairs)
    window = [y]
    if crossed:
        window[0], crossed[0] = lax.optimization_barrier((y, crossed[0]))
    while len(window) < STEPS:
        window.append(lax.ppermute(window[-1], "row", back))

    buffers = {}

    def bring_back(key):
        if key in returns:
            phase, t = key
            buffers["back%d" % phase, t] = lax.ppermute(buffers[key], both, returns[key])

    for key in sends:
        phase, t = key
        if pairs_of[key]:
            if key in relays:
                names, at = relays[key]
                sources = [buffers[phase, t - DEPTH] if name == "forward" else crossed[name] for name in names]
                held = relay(at, table, x, sources)
            elif key in starts:
                held = starts[key]
            elif "forward" in kinds_of[key]:
                held = buffers[phase, t - DEPTH]
            elif "own" in kinds_of[key]:
                held = own_chunk(own_of[key])
            else:
                held = crossed[next(k for k in kinds_of[key] if k is not None)]
            name = "back%d" % phase, t - 2
            if name in buffers:
                held, buffers[name] = lax.optimization_barrier((held, buffers[name]))
            buffers[key] = lax.ppermute(held, both, pairs_of[key])
        bring_back(key)
    zy = standardized_window(rank_at, table, window, wide(window_factor), wide(window_twice), male_cols[None, :])
    zy, squares = sum_beside(zy, squares)
    shared = window_factor[None, :], window_twice[None, :], male_wide, zy
    total = early_product(source_at[0], candidates[0], table, x, [buffers[k] for k in used[0]], *shared)
    total, squares = sum_beside(total, squares)
    relation = last_product(source_at[1], candidates[1][0], table, x, [buffers[k] for k in used[1]], *shared, total)
    for bit in bits:
        squares = squares + lax.ppermute(squares, "col", [(i, i ^ bit) for i in range(cols)])
    inbreeding = squares / jnp.float32(freq.shape[0]) - 1.0
    return relation, inbreeding


def solution(mesh):
    rows, cols = mesh.shape["row"], mesh.shape["col"]
    return jax.shard_map(
        functools.partial(local, rows, cols),
        mesh=mesh,
        in_specs=(P("row", "col"), P("row", "col"), P(), P(), P("row"), P("col")),
        out_specs=(P("row", "col"), P("row")),
        check_vma=False,
    )
```

```python
import functools
import itertools

import jax
import jax.numpy as jnp
import numpy as np
from jax import lax
from jax.experimental import pallas as pl
from jax.experimental.pallas import tpu as pltpu
from jax.sharding import PartitionSpec as P

STEPS = 4
PIECES = 1
DEPTH = 1
HOP = 1
COL_TILE = 512
ROW_BLOCK = 512
ROW_TILE = 32
TALL_TILE = 128
LANES = 128
VMEM_LIMIT = 10 * 2**20
RELAY_LIMIT = 2 * 2**20


class Item:
    def __init__(self, row, piece, s, place, home=None):
        self.row, self.piece, self.s, self.place = row, piece, s, place
        self.home = home

    @property
    def owner(self):
        return self.row if self.home is None else self.home

    @property
    def key(self):
        return self.piece, self.s


def line_slots(items):
    slots = {}
    todo = sorted(items, key=lambda i: (i.home is None, i.piece, i.place, i.s))
    slot = 1
    while todo:
        for item in todo:
            first = 1 + DEPTH * (item.place - 1) + (HOP if item.home is not None else 0)
            if first <= slot:
                slots[slot] = item
                todo.remove(item)
                break
        slot += 1
    return slots


class Lane:
    def __init__(self, rows, cols, groups_here, towards_zero):
        self.rows, self.cols = rows, cols
        self.towards_zero = towards_zero
        self.short = groups_here > 1
        self.items = []
        for r in range(rows):
            mine = [
                Item(r, piece, s, self.place((r + s) % rows // groups_here))
                for piece in range(PIECES)
                for s in range(STEPS)
            ]
            self.items.append([i for i in mine if i.place > 0])
        self.away = []
        self.lines = [line_slots(items) for items in self.items]
        if rows % 4 == 0 and cols > 3:
            for r in range(rows // 2):
                other = r + rows // 2 if towards_zero else (r + rows // 2) ^ 1
                self.balance(r, other)
                self.balance(other, r)
        self.rounds = max([max(slots, default=0) for slots in self.lines])

    def place(self, c):
        return c if self.towards_zero else self.cols - 1 - c

    col = place

    def balance(self, r, other):
        if len(self.items[r]) < len(self.items[other]) or any(i.row == other for i in self.away):
            return
        crowded = self.short and r % 2 == 0 and min(len(self.items[r]), len(self.items[r ^ 1])) >= STEPS
        places = sorted({i.place for i in self.items[r]})
        best = None
        for counts in itertools.product(range(3), repeat=len(places)):
            gone = []
            for place, count in zip(places, counts):
                here = [i for i in self.items[r] if i.place == place]
                here.sort(key=lambda i: i.key, reverse=True)
                gone += here[:count]
            visitors = [Item(other, i.piece, i.s, i.place, home=r) for i in gone]
            mine = line_slots([i for i in self.items[r] if i not in gone])
            theirs = line_slots(self.items[other] + visitors)
            score = (
                max(max(mine, default=0), max(theirs, default=0), STEPS),
                max(len(mine), STEPS - 1) if crowded else 0,
                len(gone),
                max([slot for slot, i in theirs.items() if i.home is not None], default=0),
            )
            if best is None or score < best[0]:
                best = score, gone, mine, theirs
        _, gone, mine, theirs = best
        self.away += gone
        if gone:
            self.lines[r], self.lines[other] = mine, theirs

    def sent(self, r, c, t):
        p = self.place(c)
        item = self.lines[r].get(t + DEPTH * (p - 1)) if p > 0 else None
        return item if item is not None and item.place >= p else None

    def pairs(self, t):
        found = []
        for r in range(self.rows):
            for c in range(self.cols):
                if self.sent(r, c, t) is not None:
                    found.append((r * self.cols + c, r * self.cols + self.col(self.place(c) - 1)))
        return found

    def arrival(self, r, c, key):
        p = self.place(c)
        for i in self.items[r]:
            if i.key == key and i.place > p:
                for slots in self.lines:
                    for slot, v in slots.items():
                        if v is i or (v.home == r and v.key == key):
                            return slot - DEPTH * p, v is not i
        return None


def lookup(values, device):
    known = [v for v in values if v is not None]
    if len(set(known)) <= 1:
        return known[0] if known else 0
    values = [known[0] if v is None else v for v in values]
    result = jnp.uint32(0)
    place = (device % 32).astype(jnp.uint32)
    for bit in range(max(values).bit_length()):
        ones = [v >> bit & 1 for v in values]
        words = [sum(b << i for i, b in enumerate(ones[at : at + 32])) for at in range(0, len(ones), 32)]
        word = jnp.uint32(words[0])
        for i, other in enumerate(words[1:], 1):
            word = jnp.where(device // 32 == i, jnp.uint32(other), word)
        result = result | (((word >> place) & jnp.uint32(1)) << jnp.uint32(bit))
    return result.astype(jnp.int32)


def relay_kernel(at, table, x, *refs):
    *sources, out = refs
    rows, width = out.shape

    @pl.when(table[at] == 0)
    def _():
        row = pl.multiple_of(table[at + 1] * rows, rows)
        col = pl.multiple_of(table[at + 2] * width, width)
        out[...] = x[pl.ds(row, rows), pl.ds(col, width)]

    for i, source in enumerate(sources):

        @pl.when(table[at] == i + 1)
        def _(source=source):
            out[...] = source[...]


def relay(at, table, x, sources):
    return pl.pallas_call(
        functools.partial(relay_kernel, at),
        out_shape=pltpu.VMEM(sources[0].shape, sources[0].dtype),
        in_specs=[pl.BlockSpec(memory_space=pltpu.SMEM)] + [VMEM] * (1 + len(sources)),
        out_specs=VMEM,
        compiler_params=pltpu.CompilerParams(vmem_limit_bytes=RELAY_LIMIT),
        cost_estimate=pl.CostEstimate(flops=0, bytes_accessed=0, transcendentals=0),
        name="relay",
    )(table, *[in_vmem(v) for v in (x, *sources)])


def in_vmem(value):
    return pltpu.with_memory_space_constraint(value, pltpu.VMEM)


VMEM = pl.BlockSpec(memory_space=pltpu.VMEM)


def window_kernel(at, table, *refs):
    blocks = refs[:STEPS]
    factor, twice, male, out = refs[STEPS:]
    group_size, width = blocks[0].shape
    for s, block in enumerate(blocks):
        rank = table[at + s]

        @pl.loop(0, group_size // ROW_TILE)
        def _(i, s=s, block=block, rank=rank):
            here = pl.ds(pl.multiple_of(i * ROW_TILE, ROW_TILE), ROW_TILE)
            rows = pl.ds(pl.multiple_of(s * group_size + i * ROW_TILE, ROW_TILE), ROW_TILE)
            to = pl.ds(pl.multiple_of(rank * group_size + i * ROW_TILE, ROW_TILE), ROW_TILE)
            for k in range(0, width, LANES):
                value = block[here, k : k + LANES].astype(jnp.float32) - twice[rows, :]
                out[to, k : k + LANES] = (value * factor[rows, :] * male[:, k : k + LANES]).astype(out.dtype)


def standardized_window(at, table, blocks, factor, twice, male):
    group_size, n = blocks[0].shape
    depth = STEPS * group_size
    return pl.pallas_call(
        functools.partial(window_kernel, at),
        out_shape=pltpu.VMEM((depth, n), jnp.bfloat16),
        in_specs=[pl.BlockSpec(memory_space=pltpu.SMEM)] + [VMEM] * (STEPS + 3),
        out_specs=VMEM,
        compiler_params=pltpu.CompilerParams(vmem_limit_bytes=VMEM_LIMIT),
        cost_estimate=pl.CostEstimate(flops=4 * depth * n, bytes_accessed=4 * depth * n, transcendentals=0),
        name="window",
    )(table, *[in_vmem(v) for v in (*blocks, factor, twice, male)])


def standardize(table, at, candidates, x, buffers, factor, twice, male, zx, columns, first, count):
    width = columns.stop - columns.start
    place, step = table[at], table[at + 1]

    def from_source(source, col):
        @pl.loop(0, count // TALL_TILE)
        def _(i):
            here = pl.ds(pl.multiple_of(first + i * TALL_TILE, TALL_TILE), TALL_TILE)
            to = pl.ds(pl.multiple_of(i * TALL_TILE, TALL_TILE), TALL_TILE)
            for k in range(0, width, LANES):
                lanes = pl.ds(pl.multiple_of(step * width + k, LANES), LANES)
                value = source[here, pl.ds(pl.multiple_of(col + k, LANES), LANES)].astype(jnp.float32)
                value = (value - twice[:, lanes]) * factor[:, lanes] * male[here, :]
                zx[to, columns.start + k : columns.start + k + LANES] = value.astype(zx.dtype)

    for number in candidates:
        if number >= 0:

            @pl.when(place == number)
            def _(number=number):
                from_source(buffers[number], 0)

        else:

            @pl.when(place < 0)
            def _():
                from_source(x, (-1 - place) * width)


def early_kernel(at, candidates, n_buffers, table, x, *refs):
    buffers = refs[:n_buffers]
    factor, twice, male, zy, total, zx = refs[n_buffers:]
    rows, depth = zx.shape
    width = depth // (STEPS - 1)
    for rank in range(STEPS - 1):
        columns = slice(rank * width, (rank + 1) * width)
        standardize(table, at + 2 * rank, candidates[rank], x, buffers, factor, twice, male, zx, columns, 0, rows)

    @pl.loop(0, rows // ROW_BLOCK)
    def _(i):
        block = pl.ds(pl.multiple_of(i * ROW_BLOCK, ROW_BLOCK), ROW_BLOCK)
        for j in range(0, total.shape[1], COL_TILE):
            right = zy[:depth, j : j + COL_TILE]
            total[block, j : j + COL_TILE] = jnp.dot(zx[block, :], right, preferred_element_type=jnp.float32)


def early_product(at, candidates, table, x, buffers, factor, twice, male, zy):
    rows, (depth, n) = x.shape[0], zy.shape
    depth = depth // STEPS * (STEPS - 1)
    args = [in_vmem(v) for v in (x, *buffers, factor, twice, male, zy)]
    return pl.pallas_call(
        functools.partial(early_kernel, at, candidates, len(buffers)),
        out_shape=pltpu.VMEM((rows, n), jnp.float32),
        in_specs=[pl.BlockSpec(memory_space=pltpu.SMEM)] + [VMEM] * len(args),
        out_specs=VMEM,
        scratch_shapes=[pltpu.VMEM((rows, depth), jnp.bfloat16)],
        compiler_params=pltpu.CompilerParams(vmem_limit_bytes=VMEM_LIMIT),
        cost_estimate=pl.CostEstimate(flops=2 * rows * depth * n, bytes_accessed=0, transcendentals=0),
        name="early",
    )(table, *args)


def last_kernel(at, candidates, scale, n_buffers, table, x, *refs):
    buffers = refs[:n_buffers]
    factor, twice, male, zy, total, out, zx, blocks, sems = refs[n_buffers:]
    rows, n = total.shape
    width = zx.shape[1]

    def copy(i):
        return pltpu.make_async_copy(blocks.at[i % 2], out.at[pl.ds(i * ROW_BLOCK, ROW_BLOCK), :], sems.at[i % 2])

    count = rows // ROW_BLOCK
    for i in range(count):
        first = i * ROW_BLOCK
        standardize(
            table, at, candidates, x, buffers, factor, twice, male, zx, slice(0, width), first, ROW_BLOCK
        )
        if i >= 2:
            copy(i - 2).wait()
        for j in range(0, n, COL_TILE):
            right = zy[zy.shape[0] - width :, j : j + COL_TILE]
            product = jnp.dot(zx[...], right, preferred_element_type=jnp.float32)
            product = product + total[first : first + ROW_BLOCK, j : j + COL_TILE]
            blocks[i % 2, :, j : j + COL_TILE] = (product * scale).astype(blocks.dtype)
        copy(i).start()
    for i in range(max(count - 2, 0), count):
        copy(i).wait()


def last_product(at, candidates, table, x, buffers, factor, twice, male, zy, total):
    rows, (depth, n) = x.shape[0], zy.shape
    width = depth // STEPS
    scale = float(1.0 / np.sqrt(np.float32(depth)))
    args = [in_vmem(v) for v in (x, *buffers, factor, twice, male, zy, total)]
    return pl.pallas_call(
        functools.partial(last_kernel, at, candidates, scale, len(buffers)),
        out_shape=jax.ShapeDtypeStruct((rows, n), jnp.bfloat16),
        in_specs=[pl.BlockSpec(memory_space=pltpu.SMEM)] + [VMEM] * len(args),
        out_specs=pl.BlockSpec(memory_space=pl.ANY),
        scratch_shapes=[
            pltpu.VMEM((ROW_BLOCK, width), jnp.bfloat16),
            pltpu.VMEM((2, ROW_BLOCK, n), jnp.bfloat16),
            pltpu.SemaphoreType.DMA((2,)),
        ],
        compiler_params=pltpu.CompilerParams(vmem_limit_bytes=VMEM_LIMIT),
        cost_estimate=pl.CostEstimate(flops=2 * rows * width * n, bytes_accessed=2 * rows * n, transcendentals=0),
        name="last",
    )(table, *args)


def local(rows, cols, x, y, freq, weight, sex_rows, sex_cols):
    group_size = y.shape[0]
    local_vars = x.shape[1]
    groups_here = local_vars // group_size
    piece_rows = x.shape[0] // PIECES
    lanes = [Lane(rows, cols, groups_here, towards) for towards in (True, False)]
    rounds = max(lane.rounds for lane in lanes)
    devices = [(r, c) for r in range(rows) for c in range(cols)]
    both = ("row", "col")

    row_place = lax.axis_index("row")
    col_place = lax.axis_index("col")
    device = row_place * cols + col_place

    def number(r, c):
        return r * cols + c

    def group_here(item):
        return (item.owner + item.s) % rows % groups_here

    crossings = []
    crossing_of = {}
    for d, lane in enumerate(lanes):
        for r in range(rows):
            for slot, item in sorted(lane.lines[r].items()):
                if item.home is None:
                    continue
                source, target = (item.home, lane.col(item.place)), (r, lane.col(item.place))
                for k, crossing in enumerate(crossings):
                    if source not in crossing and target not in [to for to, _ in crossing.values()]:
                        break
                else:
                    k = len(crossings)
                    crossings.append({})
                crossings[k][source] = (target, item)
                crossing_of[d, r, item.key] = k

    def lane_of(phase, r):
        return (r + phase) % 2

    sends = [(phase, t) for t in range(1, rounds + 1) for phase in range(2)]
    pairs_of, kinds_of, own_of = {}, {}, {}
    for phase, t in sends:
        pairs, kinds, own = [], [], []
        for r, c in devices:
            lane = lanes[lane_of(phase, r)]
            item = lane.sent(r, c, t)
            if item is not None:
                pairs.append((number(r, c), number(r, lane.col(lane.place(c) - 1))))
            if item is None:
                kinds.append(None)
            elif item.place != lane.place(c):
                kinds.append("forward")
            elif item.home is not None:
                kinds.append(crossing_of[lane_of(phase, r), r, item.key])
            else:
                kinds.append("own")
            own.append(item if kinds[-1] == "own" else None)
        pairs_of[phase, t], kinds_of[phase, t], own_of[phase, t] = pairs, kinds, own

    returns = {}
    for d, lane in enumerate(lanes):
        for r in range(rows):
            for slot, item in lane.lines[r].items():
                if item.home is not None:
                    for p in range(item.place):
                        pair = number(r, lane.col(p)), number(item.home, lane.col(p))
                        returns.setdefault(((r + d) % 2, slot - DEPTH * p), []).append(pair)

    columns = []

    def add(entries):
        columns.append(np.asarray(entries, np.int32))
        return sum(c.shape[1] for c in columns[:-1])

    relays = {}
    for key in sends:
        kinds = kinds_of[key]
        names = sorted(set(kinds) - {None, "own"}, key=str)
        if names and (len(names) > 1 or "own" in kinds):
            entries = []
            for kind, item in zip(kinds, own_of[key]):
                if kind == "own":
                    entries.append((0, item.piece, group_here(item)))
                else:
                    entries.append((1 + names.index(kind) if kind is not None else 1, 0, 0))
            relays[key] = names, add(entries)

    order = []
    for r, c in devices:
        arrivals = []
        for s in range(STEPS):
            when, key = 0, -1 - (r + s) % rows % groups_here
            for d, lane in enumerate(lanes):
                arrival = lane.arrival(r, c, (0, s))
                if arrival is not None:
                    t, returned = arrival
                    when, key = t, ((r + d) % 2, t)
                    if returned:
                        phase = 0 if any(to == number(r, c) for _, to in returns.get((0, t), [])) else 1
                        when, key = t + 0.7, ("back%d" % phase, t)
            arrivals.append((when, s, key))
        order.append(sorted(arrivals, key=lambda a: a[:2]))
    rank_at = add([[[a[1] for a in arrivals].index(s) for s in range(STEPS)] for arrivals in order])
    used, candidates, source_at = [], [], []
    for ranks in (range(STEPS - 1), range(STEPS - 1, STEPS)):
        keys = {arrivals[k][2] for arrivals in order for k in ranks}
        used.append(sorted((k for k in keys if isinstance(k, tuple)), key=lambda k: (k[1], str(k[0]))))
        places = [
            [arrivals[k][2] if isinstance(arrivals[k][2], int) else used[-1].index(arrivals[k][2]) for k in ranks]
            for arrivals in order
        ]
        candidates.append([sorted({max(p[i], -1) for p in places}) for i in range(len(ranks))])
        source_at.append(
            add([[n for p, k in zip(row, ranks) for n in (p, arrivals[k][1])] for row, arrivals in zip(places, order)])
        )
    table = np.concatenate(columns, axis=1)
    table = lax.dynamic_slice(jnp.asarray(table), (device, 0), (1, table.shape[1]))[0]

    def own_chunk(items, x=x):
        piece = lookup([None if i is None else i.piece for i in items], device)
        group = lookup([None if i is None else group_here(i) for i in items], device)
        return lax.dynamic_slice(x, (piece * piece_rows, group * group_size), (piece_rows, group_size))

    factor = weight / jnp.sqrt(2.0 * freq * (1.0 - freq))
    twice = 2.0 * freq
    male_scale = np.float32(np.sqrt(0.5))
    male_rows = jnp.where(sex_rows > 0, male_scale, np.float32(1.0))
    male_cols = jnp.where(sex_cols > 0, male_scale, np.float32(1.0))
    wide = lambda value: jnp.broadcast_to(value[:, None], (value.shape[0], LANES))

    def in_window(value):
        span = STEPS * group_size
        return lax.dynamic_slice(jnp.concatenate([value, value]), (row_place * group_size,), (span,))

    window_factor, window_twice = in_window(factor), in_window(twice)
    male_wide = wide(male_rows)

    def own_squares():
        here = lambda value: lax.dynamic_slice(value, (col_place * local_vars,), (local_vars,))[None, :]
        zx = ((x.astype(jnp.float32) - here(twice)) * here(factor) * male_rows[:, None]).astype(jnp.bfloat16)
        return jnp.sum(jnp.square(zx.astype(jnp.float32)), axis=1)

    back = [(i, (i - 1) % rows) for i in range(rows)]
    squares = own_squares()

    starts = {}
    if any(own_of[0, 1]):
        starts[0, 1] = own_chunk(own_of[0, 1])
    later_x = x
    for k, crossing in enumerate(crossings):
        later_x = lax.optimization_barrier(later_x)
        starts["cross", k] = own_chunk([crossing[rc][1] if rc in crossing else None for rc in devices], later_x)
    later_x, squares = lax.optimization_barrier((later_x, squares))
    if any(own_of[1, 1]):
        starts[1, 1] = own_chunk(own_of[1, 1], later_x)
    bits = [1 << k for k in range(cols.bit_length() - 1)] if cols & (cols - 1) == 0 else []
    if cols & (cols - 1):
        squares = lax.psum(squares, "col")

    def sum_beside(value, squares):
        if not bits:
            return value, squares
        bit = bits.pop(0)
        other = lax.ppermute(squares, "col", [(i, i ^ bit) for i in range(cols)])
        value, other = lax.optimization_barrier((value, other))
        return value, squares + other

    crossed = {}
    for k, crossing in enumerate(crossings):
        pairs = [(number(*rc), number(*to)) for rc, (to, _) in crossing.items()]
        crossed[k] = lax.ppermute(starts["cross", k], both, pairs)
    window = [y]
    if crossed:
        window[0], crossed[0] = lax.optimization_barrier((y, crossed[0]))
    while len(window) < STEPS:
        window.append(lax.ppermute(window[-1], "row", back))

    buffers = {}

    def bring_back(key):
        if key in returns:
            phase, t = key
            buffers["back%d" % phase, t] = lax.ppermute(buffers[key], both, returns[key])

    for key in sends:
        phase, t = key
        if pairs_of[key]:
            if key in relays:
                names, at = relays[key]
                sources = [buffers[phase, t - DEPTH] if name == "forward" else crossed[name] for name in names]
                held = relay(at, table, x, sources)
            elif key in starts:
                held = starts[key]
            elif "forward" in kinds_of[key]:
                held = buffers[phase, t - DEPTH]
            elif "own" in kinds_of[key]:
                held = own_chunk(own_of[key])
            else:
                held = crossed[next(k for k in kinds_of[key] if k is not None)]
            name = "back%d" % phase, t - 2
            if name in buffers:
                held, buffers[name] = lax.optimization_barrier((held, buffers[name]))
            buffers[key] = lax.ppermute(held, both, pairs_of[key])
        bring_back(key)
    zy = standardized_window(rank_at, table, window, wide(window_factor), wide(window_twice), male_cols[None, :])
    zy, squares = sum_beside(zy, squares)
    shared = window_factor[None, :], window_twice[None, :], male_wide, zy
    total = early_product(source_at[0], candidates[0], table, x, [buffers[k] for k in used[0]], *shared)
    total, squares = sum_beside(total, squares)
    relation = last_product(source_at[1], candidates[1][0], table, x, [buffers[k] for k in used[1]], *shared, total)
    for bit in bits:
        squares = squares + lax.ppermute(squares, "col", [(i, i ^ bit) for i in range(cols)])
    inbreeding = squares / jnp.float32(freq.shape[0]) - 1.0
    return relation, inbreeding


def solution(mesh):
    rows, cols = mesh.shape["row"], mesh.shape["col"]
    return jax.shard_map(
        functools.partial(local, rows, cols),
        mesh=mesh,
        in_specs=(P("row", "col"), P("row", "col"), P(), P(), P("row"), P("col")),
        out_specs=(P("row", "col"), P("row")),
        check_vma=False,
    )
```

```python
import functools
import itertools

import jax
import jax.numpy as jnp
import numpy as np
from jax import lax
from jax.experimental import pallas as pl
from jax.experimental.pallas import tpu as pltpu
from jax.sharding import PartitionSpec as P

STEPS = 4
PIECES = 1
DEPTH = 1
HOP = 1
COL_TILE = 512
ROW_BLOCK = 512
EARLY_BLOCK = 1024
ROW_TILE = 32
TALL_TILE = 128
LANES = 128
VMEM_LIMIT = 10 * 2**20
RELAY_LIMIT = 2 * 2**20


class Item:
    def __init__(self, row, piece, s, place, home=None):
        self.row, self.piece, self.s, self.place = row, piece, s, place
        self.home = home

    @property
    def owner(self):
        return self.row if self.home is None else self.home

    @property
    def key(self):
        return self.piece, self.s


def line_slots(items):
    slots = {}
    todo = sorted(items, key=lambda i: (i.home is None, i.piece, i.place, i.s))
    slot = 1
    while todo:
        for item in todo:
            first = 1 + DEPTH * (item.place - 1) + (HOP if item.home is not None else 0)
            if first <= slot:
                slots[slot] = item
                todo.remove(item)
                break
        slot += 1
    return slots


class Lane:
    def __init__(self, rows, cols, groups_here, towards_zero):
        self.rows, self.cols = rows, cols
        self.towards_zero = towards_zero
        self.short = groups_here > 1
        self.items = []
        for r in range(rows):
            mine = [
                Item(r, piece, s, self.place((r + s) % rows // groups_here))
                for piece in range(PIECES)
                for s in range(STEPS)
            ]
            self.items.append([i for i in mine if i.place > 0])
        self.away = []
        self.lines = [line_slots(items) for items in self.items]
        if rows % 4 == 0 and cols > 3:
            for r in range(rows // 2):
                other = r + rows // 2 if towards_zero else (r + rows // 2) ^ 1
                self.balance(r, other)
                self.balance(other, r)
        self.rounds = max([max(slots, default=0) for slots in self.lines])

    def place(self, c):
        return c if self.towards_zero else self.cols - 1 - c

    col = place

    def balance(self, r, other):
        if len(self.items[r]) < len(self.items[other]) or any(i.row == other for i in self.away):
            return
        crowded = self.short and r % 2 == 0 and min(len(self.items[r]), len(self.items[r ^ 1])) >= STEPS
        places = sorted({i.place for i in self.items[r]})
        best = None
        for counts in itertools.product(range(3), repeat=len(places)):
            gone = []
            for place, count in zip(places, counts):
                here = [i for i in self.items[r] if i.place == place]
                here.sort(key=lambda i: i.key, reverse=True)
                gone += here[:count]
            visitors = [Item(other, i.piece, i.s, i.place, home=r) for i in gone]
            mine = line_slots([i for i in self.items[r] if i not in gone])
            theirs = line_slots(self.items[other] + visitors)
            score = (
                max(max(mine, default=0), max(theirs, default=0), STEPS),
                max(len(mine), STEPS - 1) if crowded else 0,
                len(gone),
                max([slot for slot, i in theirs.items() if i.home is not None], default=0),
            )
            if best is None or score < best[0]:
                best = score, gone, mine, theirs
        _, gone, mine, theirs = best
        self.away += gone
        if gone:
            self.lines[r], self.lines[other] = mine, theirs

    def sent(self, r, c, t):
        p = self.place(c)
        item = self.lines[r].get(t + DEPTH * (p - 1)) if p > 0 else None
        return item if item is not None and item.place >= p else None

    def pairs(self, t):
        found = []
        for r in range(self.rows):
            for c in range(self.cols):
                if self.sent(r, c, t) is not None:
                    found.append((r * self.cols + c, r * self.cols + self.col(self.place(c) - 1)))
        return found

    def arrival(self, r, c, key):
        p = self.place(c)
        for i in self.items[r]:
            if i.key == key and i.place > p:
                for slots in self.lines:
                    for slot, v in slots.items():
                        if v is i or (v.home == r and v.key == key):
                            return slot - DEPTH * p, v is not i
        return None


def lookup(values, device):
    known = [v for v in values if v is not None]
    if len(set(known)) <= 1:
        return known[0] if known else 0
    values = [known[0] if v is None else v for v in values]
    result = jnp.uint32(0)
    place = (device % 32).astype(jnp.uint32)
    for bit in range(max(values).bit_length()):
        ones = [v >> bit & 1 for v in values]
        words = [sum(b << i for i, b in enumerate(ones[at : at + 32])) for at in range(0, len(ones), 32)]
        word = jnp.uint32(words[0])
        for i, other in enumerate(words[1:], 1):
            word = jnp.where(device // 32 == i, jnp.uint32(other), word)
        result = result | (((word >> place) & jnp.uint32(1)) << jnp.uint32(bit))
    return result.astype(jnp.int32)


def relay_kernel(at, table, x, *refs):
    *sources, out = refs
    rows, width = out.shape

    @pl.when(table[at] == 0)
    def _():
        row = pl.multiple_of(table[at + 1] * rows, rows)
        col = pl.multiple_of(table[at + 2] * width, width)
        out[...] = x[pl.ds(row, rows), pl.ds(col, width)]

    for i, source in enumerate(sources):

        @pl.when(table[at] == i + 1)
        def _(source=source):
            out[...] = source[...]


def relay(at, table, x, sources):
    return pl.pallas_call(
        functools.partial(relay_kernel, at),
        out_shape=pltpu.VMEM(sources[0].shape, sources[0].dtype),
        in_specs=[pl.BlockSpec(memory_space=pltpu.SMEM)] + [VMEM] * (1 + len(sources)),
        out_specs=VMEM,
        compiler_params=pltpu.CompilerParams(vmem_limit_bytes=RELAY_LIMIT),
        cost_estimate=pl.CostEstimate(flops=0, bytes_accessed=0, transcendentals=0),
        name="relay",
    )(table, *[in_vmem(v) for v in (x, *sources)])


def in_vmem(value):
    return pltpu.with_memory_space_constraint(value, pltpu.VMEM)


VMEM = pl.BlockSpec(memory_space=pltpu.VMEM)


def window_kernel(at, table, *refs):
    blocks = refs[:STEPS]
    factor, twice, male, out = refs[STEPS:]
    group_size, width = blocks[0].shape
    for s, block in enumerate(blocks):
        rank = table[at + s]

        @pl.loop(0, group_size // ROW_TILE)
        def _(i, s=s, block=block, rank=rank):
            here = pl.ds(pl.multiple_of(i * ROW_TILE, ROW_TILE), ROW_TILE)
            rows = pl.ds(pl.multiple_of(s * group_size + i * ROW_TILE, ROW_TILE), ROW_TILE)
            to = pl.ds(pl.multiple_of(rank * group_size + i * ROW_TILE, ROW_TILE), ROW_TILE)
            for k in range(0, width, LANES):
                value = block[here, k : k + LANES].astype(jnp.float32) - twice[rows, :]
                out[to, k : k + LANES] = (value * factor[rows, :] * male[:, k : k + LANES]).astype(out.dtype)


def standardized_window(at, table, blocks, factor, twice, male):
    group_size, n = blocks[0].shape
    depth = STEPS * group_size
    return pl.pallas_call(
        functools.partial(window_kernel, at),
        out_shape=pltpu.VMEM((depth, n), jnp.bfloat16),
        in_specs=[pl.BlockSpec(memory_space=pltpu.SMEM)] + [VMEM] * (STEPS + 3),
        out_specs=VMEM,
        compiler_params=pltpu.CompilerParams(vmem_limit_bytes=VMEM_LIMIT),
        cost_estimate=pl.CostEstimate(flops=4 * depth * n, bytes_accessed=4 * depth * n, transcendentals=0),
        name="window",
    )(table, *[in_vmem(v) for v in (*blocks, factor, twice, male)])


def standardize(table, at, candidates, x, buffers, factor, twice, male, zx, columns, first, count):
    width = columns.stop - columns.start
    place, step = table[at], table[at + 1]

    def from_source(source, col):
        @pl.loop(0, count // TALL_TILE)
        def _(i):
            here = pl.ds(pl.multiple_of(first + i * TALL_TILE, TALL_TILE), TALL_TILE)
            to = pl.ds(pl.multiple_of(i * TALL_TILE, TALL_TILE), TALL_TILE)
            for k in range(0, width, LANES):
                lanes = pl.ds(pl.multiple_of(step * width + k, LANES), LANES)
                value = source[here, pl.ds(pl.multiple_of(col + k, LANES), LANES)].astype(jnp.float32)
                value = (value - twice[:, lanes]) * factor[:, lanes] * male[here, :]
                zx[to, columns.start + k : columns.start + k + LANES] = value.astype(zx.dtype)

    for number in candidates:
        if number >= 0:

            @pl.when(place == number)
            def _(number=number):
                from_source(buffers[number], 0)

        else:

            @pl.when(place < 0)
            def _():
                from_source(x, (-1 - place) * width)


def early_kernel(at, candidates, n_buffers, table, x, *refs):
    buffers = refs[:n_buffers]
    factor, twice, male, zy, total, zx = refs[n_buffers:]
    rows, depth = zx.shape
    width = depth // (STEPS - 1)
    for rank in range(STEPS - 1):
        columns = slice(rank * width, (rank + 1) * width)
        standardize(table, at + 2 * rank, candidates[rank], x, buffers, factor, twice, male, zx, columns, 0, rows)

    @pl.loop(0, rows // EARLY_BLOCK)
    def _(i):
        block = pl.ds(pl.multiple_of(i * EARLY_BLOCK, EARLY_BLOCK), EARLY_BLOCK)
        for j in range(0, total.shape[1], COL_TILE):
            right = zy[:depth, j : j + COL_TILE]
            total[block, j : j + COL_TILE] = jnp.dot(zx[block, :], right, preferred_element_type=jnp.float32)


def early_product(at, candidates, table, x, buffers, factor, twice, male, zy):
    rows, (depth, n) = x.shape[0], zy.shape
    depth = depth // STEPS * (STEPS - 1)
    args = [in_vmem(v) for v in (x, *buffers, factor, twice, male, zy)]
    return pl.pallas_call(
        functools.partial(early_kernel, at, candidates, len(buffers)),
        out_shape=pltpu.VMEM((rows, n), jnp.float32),
        in_specs=[pl.BlockSpec(memory_space=pltpu.SMEM)] + [VMEM] * len(args),
        out_specs=VMEM,
        scratch_shapes=[pltpu.VMEM((rows, depth), jnp.bfloat16)],
        compiler_params=pltpu.CompilerParams(vmem_limit_bytes=VMEM_LIMIT),
        cost_estimate=pl.CostEstimate(flops=2 * rows * depth * n, bytes_accessed=0, transcendentals=0),
        name="early",
    )(table, *args)


def last_kernel(at, candidates, scale, n_buffers, table, x, *refs):
    buffers = refs[:n_buffers]
    factor, twice, male, zy, total, out, zx, blocks, sems = refs[n_buffers:]
    rows, n = total.shape
    width = zx.shape[1]

    def copy(i):
        return pltpu.make_async_copy(blocks.at[i % 2], out.at[pl.ds(i * ROW_BLOCK, ROW_BLOCK), :], sems.at[i % 2])

    count = rows // ROW_BLOCK
    for i in range(count):
        first = i * ROW_BLOCK
        standardize(
            table, at, candidates, x, buffers, factor, twice, male, zx, slice(0, width), first, ROW_BLOCK
        )
        if i >= 2:
            copy(i - 2).wait()
        for j in range(0, n, COL_TILE):
            right = zy[zy.shape[0] - width :, j : j + COL_TILE]
            product = jnp.dot(zx[...], right, preferred_element_type=jnp.float32)
            product = product + total[first : first + ROW_BLOCK, j : j + COL_TILE]
            blocks[i % 2, :, j : j + COL_TILE] = (product * scale).astype(blocks.dtype)
        copy(i).start()
    for i in range(max(count - 2, 0), count):
        copy(i).wait()


def last_product(at, candidates, table, x, buffers, factor, twice, male, zy, total):
    rows, (depth, n) = x.shape[0], zy.shape
    width = depth // STEPS
    scale = float(1.0 / np.sqrt(np.float32(depth)))
    args = [in_vmem(v) for v in (x, *buffers, factor, twice, male, zy, total)]
    return pl.pallas_call(
        functools.partial(last_kernel, at, candidates, scale, len(buffers)),
        out_shape=jax.ShapeDtypeStruct((rows, n), jnp.bfloat16),
        in_specs=[pl.BlockSpec(memory_space=pltpu.SMEM)] + [VMEM] * len(args),
        out_specs=pl.BlockSpec(memory_space=pl.ANY),
        scratch_shapes=[
            pltpu.VMEM((ROW_BLOCK, width), jnp.bfloat16),
            pltpu.VMEM((2, ROW_BLOCK, n), jnp.bfloat16),
            pltpu.SemaphoreType.DMA((2,)),
        ],
        compiler_params=pltpu.CompilerParams(vmem_limit_bytes=VMEM_LIMIT),
        cost_estimate=pl.CostEstimate(flops=2 * rows * width * n, bytes_accessed=2 * rows * n, transcendentals=0),
        name="last",
    )(table, *args)


def local(rows, cols, x, y, freq, weight, sex_rows, sex_cols):
    group_size = y.shape[0]
    local_vars = x.shape[1]
    groups_here = local_vars // group_size
    piece_rows = x.shape[0] // PIECES
    lanes = [Lane(rows, cols, groups_here, towards) for towards in (True, False)]
    rounds = max(lane.rounds for lane in lanes)
    devices = [(r, c) for r in range(rows) for c in range(cols)]
    both = ("row", "col")

    row_place = lax.axis_index("row")
    col_place = lax.axis_index("col")
    device = row_place * cols + col_place

    def number(r, c):
        return r * cols + c

    def group_here(item):
        return (item.owner + item.s) % rows % groups_here

    crossings = []
    crossing_of = {}
    for d, lane in enumerate(lanes):
        for r in range(rows):
            for slot, item in sorted(lane.lines[r].items()):
                if item.home is None:
                    continue
                source, target = (item.home, lane.col(item.place)), (r, lane.col(item.place))
                for k, crossing in enumerate(crossings):
                    if source not in crossing and target not in [to for to, _ in crossing.values()]:
                        break
                else:
                    k = len(crossings)
                    crossings.append({})
                crossings[k][source] = (target, item)
                crossing_of[d, r, item.key] = k

    def lane_of(phase, r):
        return (r + phase) % 2

    sends = [(phase, t) for t in range(1, rounds + 1) for phase in range(2)]
    pairs_of, kinds_of, own_of = {}, {}, {}
    for phase, t in sends:
        pairs, kinds, own = [], [], []
        for r, c in devices:
            lane = lanes[lane_of(phase, r)]
            item = lane.sent(r, c, t)
            if item is not None:
                pairs.append((number(r, c), number(r, lane.col(lane.place(c) - 1))))
            if item is None:
                kinds.append(None)
            elif item.place != lane.place(c):
                kinds.append("forward")
            elif item.home is not None:
                kinds.append(crossing_of[lane_of(phase, r), r, item.key])
            else:
                kinds.append("own")
            own.append(item if kinds[-1] == "own" else None)
        pairs_of[phase, t], kinds_of[phase, t], own_of[phase, t] = pairs, kinds, own

    returns = {}
    for d, lane in enumerate(lanes):
        for r in range(rows):
            for slot, item in lane.lines[r].items():
                if item.home is not None:
                    for p in range(item.place):
                        pair = number(r, lane.col(p)), number(item.home, lane.col(p))
                        returns.setdefault(((r + d) % 2, slot - DEPTH * p), []).append(pair)

    columns = []

    def add(entries):
        columns.append(np.asarray(entries, np.int32))
        return sum(c.shape[1] for c in columns[:-1])

    relays = {}
    for key in sends:
        kinds = kinds_of[key]
        names = sorted(set(kinds) - {None, "own"}, key=str)
        if names and (len(names) > 1 or "own" in kinds):
            entries = []
            for kind, item in zip(kinds, own_of[key]):
                if kind == "own":
                    entries.append((0, item.piece, group_here(item)))
                else:
                    entries.append((1 + names.index(kind) if kind is not None else 1, 0, 0))
            relays[key] = names, add(entries)

    order = []
    for r, c in devices:
        arrivals = []
        for s in range(STEPS):
            when, key = 0, -1 - (r + s) % rows % groups_here
            for d, lane in enumerate(lanes):
                arrival = lane.arrival(r, c, (0, s))
                if arrival is not None:
                    t, returned = arrival
                    when, key = t, ((r + d) % 2, t)
                    if returned:
                        phase = 0 if any(to == number(r, c) for _, to in returns.get((0, t), [])) else 1
                        when, key = t + 0.7, ("back%d" % phase, t)
            arrivals.append((when, s, key))
        order.append(sorted(arrivals, key=lambda a: a[:2]))
    rank_at = add([[[a[1] for a in arrivals].index(s) for s in range(STEPS)] for arrivals in order])
    used, candidates, source_at = [], [], []
    for ranks in (range(STEPS - 1), range(STEPS - 1, STEPS)):
        keys = {arrivals[k][2] for arrivals in order for k in ranks}
        used.append(sorted((k for k in keys if isinstance(k, tuple)), key=lambda k: (k[1], str(k[0]))))
        places = [
            [arrivals[k][2] if isinstance(arrivals[k][2], int) else used[-1].index(arrivals[k][2]) for k in ranks]
            for arrivals in order
        ]
        candidates.append([sorted({max(p[i], -1) for p in places}) for i in range(len(ranks))])
        source_at.append(
            add([[n for p, k in zip(row, ranks) for n in (p, arrivals[k][1])] for row, arrivals in zip(places, order)])
        )
    table = np.concatenate(columns, axis=1)
    table = lax.dynamic_slice(jnp.asarray(table), (device, 0), (1, table.shape[1]))[0]

    def own_chunk(items, x=x):
        piece = lookup([None if i is None else i.piece for i in items], device)
        group = lookup([None if i is None else group_here(i) for i in items], device)
        return lax.dynamic_slice(x, (piece * piece_rows, group * group_size), (piece_rows, group_size))

    factor = weight / jnp.sqrt(2.0 * freq * (1.0 - freq))
    twice = 2.0 * freq
    male_scale = np.float32(np.sqrt(0.5))
    male_rows = jnp.where(sex_rows > 0, male_scale, np.float32(1.0))
    male_cols = jnp.where(sex_cols > 0, male_scale, np.float32(1.0))
    wide = lambda value: jnp.broadcast_to(value[:, None], (value.shape[0], LANES))

    def in_window(value):
        span = STEPS * group_size
        return lax.dynamic_slice(jnp.concatenate([value, value]), (row_place * group_size,), (span,))

    window_factor, window_twice = in_window(factor), in_window(twice)
    male_wide = wide(male_rows)

    def own_squares():
        here = lambda value: lax.dynamic_slice(value, (col_place * local_vars,), (local_vars,))[None, :]
        zx = ((x.astype(jnp.float32) - here(twice)) * here(factor) * male_rows[:, None]).astype(jnp.bfloat16)
        return jnp.sum(jnp.square(zx.astype(jnp.float32)), axis=1)

    back = [(i, (i - 1) % rows) for i in range(rows)]
    squares = own_squares()

    starts = {}
    if any(own_of[0, 1]):
        starts[0, 1] = own_chunk(own_of[0, 1])
    later_x = x
    for k, crossing in enumerate(crossings):
        later_x = lax.optimization_barrier(later_x)
        starts["cross", k] = own_chunk([crossing[rc][1] if rc in crossing else None for rc in devices], later_x)
    later_x, squares = lax.optimization_barrier((later_x, squares))
    if any(own_of[1, 1]):
        starts[1, 1] = own_chunk(own_of[1, 1], later_x)
    bits = [1 << k for k in range(cols.bit_length() - 1)] if cols & (cols - 1) == 0 else []
    if cols & (cols - 1):
        squares = lax.psum(squares, "col")

    def sum_beside(value, squares):
        if not bits:
            return value, squares
        bit = bits.pop(0)
        other = lax.ppermute(squares, "col", [(i, i ^ bit) for i in range(cols)])
        value, other = lax.optimization_barrier((value, other))
        return value, squares + other

    crossed = {}
    for k, crossing in enumerate(crossings):
        pairs = [(number(*rc), number(*to)) for rc, (to, _) in crossing.items()]
        crossed[k] = lax.ppermute(starts["cross", k], both, pairs)
    window = [y]
    if crossed:
        window[0], crossed[0] = lax.optimization_barrier((y, crossed[0]))
    while len(window) < STEPS:
        window.append(lax.ppermute(window[-1], "row", back))

    buffers = {}

    def bring_back(key):
        if key in returns:
            phase, t = key
            buffers["back%d" % phase, t] = lax.ppermute(buffers[key], both, returns[key])

    for key in sends:
        phase, t = key
        if pairs_of[key]:
            if key in relays:
                names, at = relays[key]
                sources = [buffers[phase, t - DEPTH] if name == "forward" else crossed[name] for name in names]
                held = relay(at, table, x, sources)
            elif key in starts:
                held = starts[key]
            elif "forward" in kinds_of[key]:
                held = buffers[phase, t - DEPTH]
            elif "own" in kinds_of[key]:
                held = own_chunk(own_of[key])
            else:
                held = crossed[next(k for k in kinds_of[key] if k is not None)]
            name = "back%d" % phase, t - 2
            if name in buffers:
                held, buffers[name] = lax.optimization_barrier((held, buffers[name]))
            buffers[key] = lax.ppermute(held, both, pairs_of[key])
        bring_back(key)
    zy = standardized_window(rank_at, table, window, wide(window_factor), wide(window_twice), male_cols[None, :])
    zy, squares = sum_beside(zy, squares)
    shared = window_factor[None, :], window_twice[None, :], male_wide, zy
    total = early_product(source_at[0], candidates[0], table, x, [buffers[k] for k in used[0]], *shared)
    total, squares = sum_beside(total, squares)
    relation = last_product(source_at[1], candidates[1][0], table, x, [buffers[k] for k in used[1]], *shared, total)
    for bit in bits:
        squares = squares + lax.ppermute(squares, "col", [(i, i ^ bit) for i in range(cols)])
    inbreeding = squares / jnp.float32(freq.shape[0]) - 1.0
    return relation, inbreeding


def solution(mesh):
    rows, cols = mesh.shape["row"], mesh.shape["col"]
    return jax.shard_map(
        functools.partial(local, rows, cols),
        mesh=mesh,
        in_specs=(P("row", "col"), P("row", "col"), P(), P(), P("row"), P("col")),
        out_specs=(P("row", "col"), P("row")),
        check_vma=False,
    )
```

```python
import functools
import itertools

import jax
import jax.numpy as jnp
import numpy as np
from jax import lax
from jax.experimental import pallas as pl
from jax.experimental.pallas import tpu as pltpu
from jax.sharding import PartitionSpec as P

STEPS = 4
PIECES = 1
DEPTH = 1
HOP = 1
COL_TILE = 1024
ROW_BLOCK = 512
EARLY_BLOCK = 1024
ROW_TILE = 32
TALL_TILE = 128
LANES = 128
VMEM_LIMIT = 10 * 2**20
RELAY_LIMIT = 2 * 2**20


class Item:
    def __init__(self, row, piece, s, place, home=None):
        self.row, self.piece, self.s, self.place = row, piece, s, place
        self.home = home

    @property
    def owner(self):
        return self.row if self.home is None else self.home

    @property
    def key(self):
        return self.piece, self.s


def line_slots(items):
    slots = {}
    todo = sorted(items, key=lambda i: (i.home is None, i.piece, i.place, i.s))
    slot = 1
    while todo:
        for item in todo:
            first = 1 + DEPTH * (item.place - 1) + (HOP if item.home is not None else 0)
            if first <= slot:
                slots[slot] = item
                todo.remove(item)
                break
        slot += 1
    return slots


class Lane:
    def __init__(self, rows, cols, groups_here, towards_zero):
        self.rows, self.cols = rows, cols
        self.towards_zero = towards_zero
        self.short = groups_here > 1
        self.items = []
        for r in range(rows):
            mine = [
                Item(r, piece, s, self.place((r + s) % rows // groups_here))
                for piece in range(PIECES)
                for s in range(STEPS)
            ]
            self.items.append([i for i in mine if i.place > 0])
        self.away = []
        self.lines = [line_slots(items) for items in self.items]
        if rows % 4 == 0 and cols > 3:
            for r in range(rows // 2):
                other = r + rows // 2 if towards_zero else (r + rows // 2) ^ 1
                self.balance(r, other)
                self.balance(other, r)
        self.rounds = max([max(slots, default=0) for slots in self.lines])

    def place(self, c):
        return c if self.towards_zero else self.cols - 1 - c

    col = place

    def balance(self, r, other):
        if len(self.items[r]) < len(self.items[other]) or any(i.row == other for i in self.away):
            return
        crowded = self.short and r % 2 == 0 and min(len(self.items[r]), len(self.items[r ^ 1])) >= STEPS
        places = sorted({i.place for i in self.items[r]})
        best = None
        for counts in itertools.product(range(3), repeat=len(places)):
            gone = []
            for place, count in zip(places, counts):
                here = [i for i in self.items[r] if i.place == place]
                here.sort(key=lambda i: i.key, reverse=True)
                gone += here[:count]
            visitors = [Item(other, i.piece, i.s, i.place, home=r) for i in gone]
            mine = line_slots([i for i in self.items[r] if i not in gone])
            theirs = line_slots(self.items[other] + visitors)
            score = (
                max(max(mine, default=0), max(theirs, default=0), STEPS),
                max(len(mine), STEPS - 1) if crowded else 0,
                len(gone),
                max([slot for slot, i in theirs.items() if i.home is not None], default=0),
            )
            if best is None or score < best[0]:
                best = score, gone, mine, theirs
        _, gone, mine, theirs = best
        self.away += gone
        if gone:
            self.lines[r], self.lines[other] = mine, theirs

    def sent(self, r, c, t):
        p = self.place(c)
        item = self.lines[r].get(t + DEPTH * (p - 1)) if p > 0 else None
        return item if item is not None and item.place >= p else None

    def pairs(self, t):
        found = []
        for r in range(self.rows):
            for c in range(self.cols):
                if self.sent(r, c, t) is not None:
                    found.append((r * self.cols + c, r * self.cols + self.col(self.place(c) - 1)))
        return found

    def arrival(self, r, c, key):
        p = self.place(c)
        for i in self.items[r]:
            if i.key == key and i.place > p:
                for slots in self.lines:
                    for slot, v in slots.items():
                        if v is i or (v.home == r and v.key == key):
                            return slot - DEPTH * p, v is not i
        return None


def lookup(values, device):
    known = [v for v in values if v is not None]
    if len(set(known)) <= 1:
        return known[0] if known else 0
    values = [known[0] if v is None else v for v in values]
    result = jnp.uint32(0)
    place = (device % 32).astype(jnp.uint32)
    for bit in range(max(values).bit_length()):
        ones = [v >> bit & 1 for v in values]
        words = [sum(b << i for i, b in enumerate(ones[at : at + 32])) for at in range(0, len(ones), 32)]
        word = jnp.uint32(words[0])
        for i, other in enumerate(words[1:], 1):
            word = jnp.where(device // 32 == i, jnp.uint32(other), word)
        result = result | (((word >> place) & jnp.uint32(1)) << jnp.uint32(bit))
    return result.astype(jnp.int32)


def relay_kernel(at, table, x, *refs):
    *sources, out = refs
    rows, width = out.shape

    @pl.when(table[at] == 0)
    def _():
        row = pl.multiple_of(table[at + 1] * rows, rows)
        col = pl.multiple_of(table[at + 2] * width, width)
        out[...] = x[pl.ds(row, rows), pl.ds(col, width)]

    for i, source in enumerate(sources):

        @pl.when(table[at] == i + 1)
        def _(source=source):
            out[...] = source[...]


def relay(at, table, x, sources):
    return pl.pallas_call(
        functools.partial(relay_kernel, at),
        out_shape=pltpu.VMEM(sources[0].shape, sources[0].dtype),
        in_specs=[pl.BlockSpec(memory_space=pltpu.SMEM)] + [VMEM] * (1 + len(sources)),
        out_specs=VMEM,
        compiler_params=pltpu.CompilerParams(vmem_limit_bytes=RELAY_LIMIT),
        cost_estimate=pl.CostEstimate(flops=0, bytes_accessed=0, transcendentals=0),
        name="relay",
    )(table, *[in_vmem(v) for v in (x, *sources)])


def in_vmem(value):
    return pltpu.with_memory_space_constraint(value, pltpu.VMEM)


VMEM = pl.BlockSpec(memory_space=pltpu.VMEM)


def window_kernel(at, table, *refs):
    blocks = refs[:STEPS]
    factor, twice, male, out = refs[STEPS:]
    group_size, width = blocks[0].shape
    for s, block in enumerate(blocks):
        rank = table[at + s]

        @pl.loop(0, group_size // ROW_TILE)
        def _(i, s=s, block=block, rank=rank):
            here = pl.ds(pl.multiple_of(i * ROW_TILE, ROW_TILE), ROW_TILE)
            rows = pl.ds(pl.multiple_of(s * group_size + i * ROW_TILE, ROW_TILE), ROW_TILE)
            to = pl.ds(pl.multiple_of(rank * group_size + i * ROW_TILE, ROW_TILE), ROW_TILE)
            for k in range(0, width, LANES):
                value = block[here, k : k + LANES].astype(jnp.float32) - twice[rows, :]
                out[to, k : k + LANES] = (value * factor[rows, :] * male[:, k : k + LANES]).astype(out.dtype)


def standardized_window(at, table, blocks, factor, twice, male):
    group_size, n = blocks[0].shape
    depth = STEPS * group_size
    return pl.pallas_call(
        functools.partial(window_kernel, at),
        out_shape=pltpu.VMEM((depth, n), jnp.bfloat16),
        in_specs=[pl.BlockSpec(memory_space=pltpu.SMEM)] + [VMEM] * (STEPS + 3),
        out_specs=VMEM,
        compiler_params=pltpu.CompilerParams(vmem_limit_bytes=VMEM_LIMIT),
        cost_estimate=pl.CostEstimate(flops=4 * depth * n, bytes_accessed=4 * depth * n, transcendentals=0),
        name="window",
    )(table, *[in_vmem(v) for v in (*blocks, factor, twice, male)])


def standardize(table, at, candidates, x, buffers, factor, twice, male, zx, columns, first, count):
    width = columns.stop - columns.start
    place, step = table[at], table[at + 1]

    def from_source(source, col):
        @pl.loop(0, count // TALL_TILE)
        def _(i):
            here = pl.ds(pl.multiple_of(first + i * TALL_TILE, TALL_TILE), TALL_TILE)
            to = pl.ds(pl.multiple_of(i * TALL_TILE, TALL_TILE), TALL_TILE)
            for k in range(0, width, LANES):
                lanes = pl.ds(pl.multiple_of(step * width + k, LANES), LANES)
                value = source[here, pl.ds(pl.multiple_of(col + k, LANES), LANES)].astype(jnp.float32)
                value = (value - twice[:, lanes]) * factor[:, lanes] * male[here, :]
                zx[to, columns.start + k : columns.start + k + LANES] = value.astype(zx.dtype)

    for number in candidates:
        if number >= 0:

            @pl.when(place == number)
            def _(number=number):
                from_source(buffers[number], 0)

        else:

            @pl.when(place < 0)
            def _():
                from_source(x, (-1 - place) * width)


def early_kernel(at, candidates, n_buffers, table, x, *refs):
    buffers = refs[:n_buffers]
    factor, twice, male, zy, total, zx = refs[n_buffers:]
    rows, depth = zx.shape
    width = depth // (STEPS - 1)
    for rank in range(STEPS - 1):
        columns = slice(rank * width, (rank + 1) * width)
        standardize(table, at + 2 * rank, candidates[rank], x, buffers, factor, twice, male, zx, columns, 0, rows)

    @pl.loop(0, rows // EARLY_BLOCK)
    def _(i):
        block = pl.ds(pl.multiple_of(i * EARLY_BLOCK, EARLY_BLOCK), EARLY_BLOCK)
        for j in range(0, total.shape[1], COL_TILE):
            right = zy[:depth, j : j + COL_TILE]
            total[block, j : j + COL_TILE] = jnp.dot(zx[block, :], right, preferred_element_type=jnp.float32)


def early_product(at, candidates, table, x, buffers, factor, twice, male, zy):
    rows, (depth, n) = x.shape[0], zy.shape
    depth = depth // STEPS * (STEPS - 1)
    args = [in_vmem(v) for v in (x, *buffers, factor, twice, male, zy)]
    return pl.pallas_call(
        functools.partial(early_kernel, at, candidates, len(buffers)),
        out_shape=pltpu.VMEM((rows, n), jnp.float32),
        in_specs=[pl.BlockSpec(memory_space=pltpu.SMEM)] + [VMEM] * len(args),
        out_specs=VMEM,
        scratch_shapes=[pltpu.VMEM((rows, depth), jnp.bfloat16)],
        compiler_params=pltpu.CompilerParams(vmem_limit_bytes=VMEM_LIMIT),
        cost_estimate=pl.CostEstimate(flops=2 * rows * depth * n, bytes_accessed=0, transcendentals=0),
        name="early",
    )(table, *args)


def last_kernel(at, candidates, scale, n_buffers, table, x, *refs):
    buffers = refs[:n_buffers]
    factor, twice, male, zy, total, out, zx, blocks, sems = refs[n_buffers:]
    rows, n = total.shape
    width = zx.shape[1]

    def copy(i):
        return pltpu.make_async_copy(blocks.at[i % 2], out.at[pl.ds(i * ROW_BLOCK, ROW_BLOCK), :], sems.at[i % 2])

    count = rows // ROW_BLOCK
    for i in range(count):
        first = i * ROW_BLOCK
        standardize(
            table, at, candidates, x, buffers, factor, twice, male, zx, slice(0, width), first, ROW_BLOCK
        )
        if i >= 2:
            copy(i - 2).wait()
        for j in range(0, n, COL_TILE):
            right = zy[zy.shape[0] - width :, j : j + COL_TILE]
            product = jnp.dot(zx[...], right, preferred_element_type=jnp.float32)
            product = product + total[first : first + ROW_BLOCK, j : j + COL_TILE]
            blocks[i % 2, :, j : j + COL_TILE] = (product * scale).astype(blocks.dtype)
        copy(i).start()
    for i in range(max(count - 2, 0), count):
        copy(i).wait()


def last_product(at, candidates, table, x, buffers, factor, twice, male, zy, total):
    rows, (depth, n) = x.shape[0], zy.shape
    width = depth // STEPS
    scale = float(1.0 / np.sqrt(np.float32(depth)))
    args = [in_vmem(v) for v in (x, *buffers, factor, twice, male, zy, total)]
    return pl.pallas_call(
        functools.partial(last_kernel, at, candidates, scale, len(buffers)),
        out_shape=jax.ShapeDtypeStruct((rows, n), jnp.bfloat16),
        in_specs=[pl.BlockSpec(memory_space=pltpu.SMEM)] + [VMEM] * len(args),
        out_specs=pl.BlockSpec(memory_space=pl.ANY),
        scratch_shapes=[
            pltpu.VMEM((ROW_BLOCK, width), jnp.bfloat16),
            pltpu.VMEM((2, ROW_BLOCK, n), jnp.bfloat16),
            pltpu.SemaphoreType.DMA((2,)),
        ],
        compiler_params=pltpu.CompilerParams(vmem_limit_bytes=VMEM_LIMIT),
        cost_estimate=pl.CostEstimate(flops=2 * rows * width * n, bytes_accessed=2 * rows * n, transcendentals=0),
        name="last",
    )(table, *args)


def local(rows, cols, x, y, freq, weight, sex_rows, sex_cols):
    group_size = y.shape[0]
    local_vars = x.shape[1]
    groups_here = local_vars // group_size
    piece_rows = x.shape[0] // PIECES
    lanes = [Lane(rows, cols, groups_here, towards) for towards in (True, False)]
    rounds = max(lane.rounds for lane in lanes)
    devices = [(r, c) for r in range(rows) for c in range(cols)]
    both = ("row", "col")

    row_place = lax.axis_index("row")
    col_place = lax.axis_index("col")
    device = row_place * cols + col_place

    def number(r, c):
        return r * cols + c

    def group_here(item):
        return (item.owner + item.s) % rows % groups_here

    crossings = []
    crossing_of = {}
    for d, lane in enumerate(lanes):
        for r in range(rows):
            for slot, item in sorted(lane.lines[r].items()):
                if item.home is None:
                    continue
                source, target = (item.home, lane.col(item.place)), (r, lane.col(item.place))
                for k, crossing in enumerate(crossings):
                    if source not in crossing and target not in [to for to, _ in crossing.values()]:
                        break
                else:
                    k = len(crossings)
                    crossings.append({})
                crossings[k][source] = (target, item)
                crossing_of[d, r, item.key] = k

    def lane_of(phase, r):
        return (r + phase) % 2

    sends = [(phase, t) for t in range(1, rounds + 1) for phase in range(2)]
    pairs_of, kinds_of, own_of = {}, {}, {}
    for phase, t in sends:
        pairs, kinds, own = [], [], []
        for r, c in devices:
            lane = lanes[lane_of(phase, r)]
            item = lane.sent(r, c, t)
            if item is not None:
                pairs.append((number(r, c), number(r, lane.col(lane.place(c) - 1))))
            if item is None:
                kinds.append(None)
            elif item.place != lane.place(c):
                kinds.append("forward")
            elif item.home is not None:
                kinds.append(crossing_of[lane_of(phase, r), r, item.key])
            else:
                kinds.append("own")
            own.append(item if kinds[-1] == "own" else None)
        pairs_of[phase, t], kinds_of[phase, t], own_of[phase, t] = pairs, kinds, own

    returns = {}
    for d, lane in enumerate(lanes):
        for r in range(rows):
            for slot, item in lane.lines[r].items():
                if item.home is not None:
                    for p in range(item.place):
                        pair = number(r, lane.col(p)), number(item.home, lane.col(p))
                        returns.setdefault(((r + d) % 2, slot - DEPTH * p), []).append(pair)

    columns = []

    def add(entries):
        columns.append(np.asarray(entries, np.int32))
        return sum(c.shape[1] for c in columns[:-1])

    relays = {}
    for key in sends:
        kinds = kinds_of[key]
        names = sorted(set(kinds) - {None, "own"}, key=str)
        if names and (len(names) > 1 or "own" in kinds):
            entries = []
            for kind, item in zip(kinds, own_of[key]):
                if kind == "own":
                    entries.append((0, item.piece, group_here(item)))
                else:
                    entries.append((1 + names.index(kind) if kind is not None else 1, 0, 0))
            relays[key] = names, add(entries)

    order = []
    for r, c in devices:
        arrivals = []
        for s in range(STEPS):
            when, key = 0, -1 - (r + s) % rows % groups_here
            for d, lane in enumerate(lanes):
                arrival = lane.arrival(r, c, (0, s))
                if arrival is not None:
                    t, returned = arrival
                    when, key = t, ((r + d) % 2, t)
                    if returned:
                        phase = 0 if any(to == number(r, c) for _, to in returns.get((0, t), [])) else 1
                        when, key = t + 0.7, ("back%d" % phase, t)
            arrivals.append((when, s, key))
        order.append(sorted(arrivals, key=lambda a: a[:2]))
    rank_at = add([[[a[1] for a in arrivals].index(s) for s in range(STEPS)] for arrivals in order])
    used, candidates, source_at = [], [], []
    for ranks in (range(STEPS - 1), range(STEPS - 1, STEPS)):
        keys = {arrivals[k][2] for arrivals in order for k in ranks}
        used.append(sorted((k for k in keys if isinstance(k, tuple)), key=lambda k: (k[1], str(k[0]))))
        places = [
            [arrivals[k][2] if isinstance(arrivals[k][2], int) else used[-1].index(arrivals[k][2]) for k in ranks]
            for arrivals in order
        ]
        candidates.append([sorted({max(p[i], -1) for p in places}) for i in range(len(ranks))])
        source_at.append(
            add([[n for p, k in zip(row, ranks) for n in (p, arrivals[k][1])] for row, arrivals in zip(places, order)])
        )
    table = np.concatenate(columns, axis=1)
    table = lax.dynamic_slice(jnp.asarray(table), (device, 0), (1, table.shape[1]))[0]

    def own_chunk(items, x=x):
        piece = lookup([None if i is None else i.piece for i in items], device)
        group = lookup([None if i is None else group_here(i) for i in items], device)
        return lax.dynamic_slice(x, (piece * piece_rows, group * group_size), (piece_rows, group_size))

    factor = weight / jnp.sqrt(2.0 * freq * (1.0 - freq))
    twice = 2.0 * freq
    male_scale = np.float32(np.sqrt(0.5))
    male_rows = jnp.where(sex_rows > 0, male_scale, np.float32(1.0))
    male_cols = jnp.where(sex_cols > 0, male_scale, np.float32(1.0))
    wide = lambda value: jnp.broadcast_to(value[:, None], (value.shape[0], LANES))

    def in_window(value):
        span = STEPS * group_size
        return lax.dynamic_slice(jnp.concatenate([value, value]), (row_place * group_size,), (span,))

    window_factor, window_twice = in_window(factor), in_window(twice)
    male_wide = wide(male_rows)

    def own_squares():
        here = lambda value: lax.dynamic_slice(value, (col_place * local_vars,), (local_vars,))[None, :]
        zx = ((x.astype(jnp.float32) - here(twice)) * here(factor) * male_rows[:, None]).astype(jnp.bfloat16)
        return jnp.sum(jnp.square(zx.astype(jnp.float32)), axis=1)

    back = [(i, (i - 1) % rows) for i in range(rows)]
    squares = own_squares()

    starts = {}
    if any(own_of[0, 1]):
        starts[0, 1] = own_chunk(own_of[0, 1])
    later_x = x
    for k, crossing in enumerate(crossings):
        later_x = lax.optimization_barrier(later_x)
        starts["cross", k] = own_chunk([crossing[rc][1] if rc in crossing else None for rc in devices], later_x)
    later_x, squares = lax.optimization_barrier((later_x, squares))
    if any(own_of[1, 1]):
        starts[1, 1] = own_chunk(own_of[1, 1], later_x)
    bits = [1 << k for k in range(cols.bit_length() - 1)] if cols & (cols - 1) == 0 else []
    if cols & (cols - 1):
        squares = lax.psum(squares, "col")

    def sum_beside(value, squares):
        if not bits:
            return value, squares
        bit = bits.pop(0)
        other = lax.ppermute(squares, "col", [(i, i ^ bit) for i in range(cols)])
        value, other = lax.optimization_barrier((value, other))
        return value, squares + other

    crossed = {}
    for k, crossing in enumerate(crossings):
        pairs = [(number(*rc), number(*to)) for rc, (to, _) in crossing.items()]
        crossed[k] = lax.ppermute(starts["cross", k], both, pairs)
    window = [y]
    if crossed:
        window[0], crossed[0] = lax.optimization_barrier((y, crossed[0]))
    while len(window) < STEPS:
        window.append(lax.ppermute(window[-1], "row", back))

    buffers = {}

    def bring_back(key):
        if key in returns:
            phase, t = key
            buffers["back%d" % phase, t] = lax.ppermute(buffers[key], both, returns[key])

    for key in sends:
        phase, t = key
        if pairs_of[key]:
            if key in relays:
                names, at = relays[key]
                sources = [buffers[phase, t - DEPTH] if name == "forward" else crossed[name] for name in names]
                held = relay(at, table, x, sources)
            elif key in starts:
                held = starts[key]
            elif "forward" in kinds_of[key]:
                held = buffers[phase, t - DEPTH]
            elif "own" in kinds_of[key]:
                held = own_chunk(own_of[key])
            else:
                held = crossed[next(k for k in kinds_of[key] if k is not None)]
            name = "back%d" % phase, t - 2
            if name in buffers:
                held, buffers[name] = lax.optimization_barrier((held, buffers[name]))
            buffers[key] = lax.ppermute(held, both, pairs_of[key])
        bring_back(key)
    zy = standardized_window(rank_at, table, window, wide(window_factor), wide(window_twice), male_cols[None, :])
    zy, squares = sum_beside(zy, squares)
    shared = window_factor[None, :], window_twice[None, :], male_wide, zy
    total = early_product(source_at[0], candidates[0], table, x, [buffers[k] for k in used[0]], *shared)
    total, squares = sum_beside(total, squares)
    relation = last_product(source_at[1], candidates[1][0], table, x, [buffers[k] for k in used[1]], *shared, total)
    for bit in bits:
        squares = squares + lax.ppermute(squares, "col", [(i, i ^ bit) for i in range(cols)])
    inbreeding = squares / jnp.float32(freq.shape[0]) - 1.0
    return relation, inbreeding


def solution(mesh):
    rows, cols = mesh.shape["row"], mesh.shape["col"]
    return jax.shard_map(
        functools.partial(local, rows, cols),
        mesh=mesh,
        in_specs=(P("row", "col"), P("row", "col"), P(), P(), P("row"), P("col")),
        out_specs=(P("row", "col"), P("row")),
        check_vma=False,
    )
```
